32 devices in a mesh: dp: 8 (over z, core), fsdp: 4 (over y, x).
Axes of the slice: x: 2, y: 2, z: 4, core: 2. Of those that a mesh axis runs over, the one named last changes fastest.
Arguments:
- tokens: bfloat16 [8, 2624, 1536], P('dp', 'fsdp'), may hold values from -6 to 6
- cotangent: bfloat16 [8, 2624, 1536], P('dp', 'fsdp'), may hold values from -6 to 6
- text_states: bfloat16 [8, 2, 256, 4096], P('dp', None, 'fsdp'), may hold values from -6 to 6
- conditioning: bfloat16 [8, 2, 1024], P('dp'), may hold values from -6 to 6
- image_sizes: int32 [8, 2, 2], P('dp'), may hold values from 6 to 96, as said below
- ada_weight: bfloat16 [1024, 6144], P('fsdp'), may hold values from -0.1875 to 0.1875
- ada_bias: float32 [6144], replicated, may hold values from -3 to 3
- qkv_weight: bfloat16 [1536, 4608], P('fsdp'), may hold values from -0.15625 to 0.15625
- out_weight: bfloat16 [1536, 1536], P('fsdp'), may hold values from -0.15625 to 0.15625
- text_weight: bfloat16 [4096, 3072], P('fsdp'), may hold values from -0.09375 to 0.09375
- gate_up_weight: bfloat16 [1536, 8192], P('fsdp'), may hold values from -0.15625 to 0.15625
- down_weight: bfloat16 [4096, 1536], P('fsdp'), may hold values from -0.09375 to 0.09375
- norm_gains: float32 [7, 1536], replicated, may hold values from 0.1 to 1.9
- norm_shifts: float32 [2, 1536], replicated, may hold values from -3 to 3
- text_gain: float32 [4096], replicated, may hold values from 0.1 to 1.9
- head_gate: float32 [24], replicated, may hold values from 0.2 to 0.8
Outputs:
- block_out: bfloat16 [8, 2624, 1536], P('dp', 'fsdp')
- tokens_grad: bfloat16 [8, 2624, 1536], P('dp', 'fsdp')
- text_grad: bfloat16 [8, 2, 256, 4096], P('dp', None, 'fsdp')
- ada_weight_grad: float32 [1024, 6144], P(('dp', 'fsdp'))
- qkv_weight_grad: float32 [1536, 4608], P(('dp', 'fsdp'))
- out_weight_grad: float32 [1536, 1536], P(('dp', 'fsdp'))
- text_weight_grad: float32 [4096, 3072], P(('dp', 'fsdp'))
- gate_up_weight_grad: float32 [1536, 8192], P(('dp', 'fsdp'))
- down_weight_grad: float32 [4096, 1536], P(('dp', 'fsdp'))
- ada_bias_grad: float32 [6144], replicated
- norm_gains_grad: float32 [7, 1536], replicated
- norm_shifts_grad: float32 [2, 1536], replicated
- text_gain_grad: float32 [4096], replicated
- head_gate_grad: float32 [24], replicated
The draws below stay inside these ranges and needn't reach their ends.
Inputs may be any that keep to these rules, and one draw needn't show every extreme that they name: `image_sizes`: in every group image 0 has 16 * 12**2 patches and image 1 has 12**2; an image is square or has rows and columns in the ratio 1:4 or 4:1.
All inputs are finite; a program needn't handle non-finite values.
Results may differ from the reference program's by a relative error of at most 0.023.
Values may be sent and summed in bfloat16 or wider, within the bound.
A program may use at most 512 MiB of HBM per device.

```python
import jax
import jax.numpy as jnp
from jax import lax

D = 1536
HEADS = 24
HD = 64
FF = 4096
CAPD = 4096
CONDD = 1024
CAP = 256
IMGS = 2
SIDE = 12
GROUP_TOK = 2624
GROUPS = 8


def draw_image_sizes(key, part):
    aspect_key = jax.random.fold_in(key, 11)
    group_key = jax.random.fold_in(key, 12)
    aspect = jax.random.randint(aspect_key, (GROUPS, IMGS), 0, 3)
    chosen = jax.random.randint(group_key, (), 0, GROUPS)
    group_index = jnp.arange(GROUPS, dtype=jnp.int32)[:, None]
    slot_index = jnp.arange(IMGS, dtype=jnp.int32)[None, :]
    aspect = jnp.where((group_index == chosen) & (slot_index <= 1), 2, aspect)
    side_length = jnp.where(slot_index == 0, 4 * SIDE, SIDE)
    patch_rows = jnp.where(aspect == 0, side_length, jnp.where(aspect == 1, side_length // 2, side_length * 2))
    patch_cols = jnp.where(aspect == 0, side_length, jnp.where(aspect == 1, side_length * 2, side_length // 2))
    return jnp.stack([patch_rows, patch_cols], axis=-1).astype(jnp.int32)


def block_scale(key, extent, shards, least, largest):
    loudness, own = 1.0, jax.random.fold_in(key, 6)
    for dim, blocks in shards:
        draws = jnp.exp(jax.random.uniform(jax.random.fold_in(own, dim), (blocks,), jnp.float32, least / len(shards), largest / len(shards)))
        loudness = loudness * jnp.repeat(draws, extent[dim] // blocks).reshape([-1 if axis == dim else 1 for axis in range(len(extent))])
    return loudness


def bell_draw(stream_key, extent, scale, most, shards=(), held_as=jnp.bfloat16):
    array = scale * jax.random.normal(stream_key, extent, jnp.float32)
    if shards:
        array = array * block_scale(stream_key, extent, shards, -0.22, 0.18)
    return jnp.clip(array, -most, most).astype(held_as)


def setup_inputs(seed: int = 0) -> dict:
    arg_keys = jax.random.split(jax.random.key(seed), 17)
    return {
        "tokens": bell_draw(arg_keys[0], (GROUPS, GROUP_TOK, D), 1.0, 6.0, ((0, 8), (1, 4))),
        "cotangent": bell_draw(arg_keys[1], (GROUPS, GROUP_TOK, D), 1.0, 6.0, ((0, 8), (1, 4))),
        "text_states": bell_draw(arg_keys[2], (GROUPS, IMGS, CAP, CAPD), 1.0, 6.0, ((0, 8), (2, 4))),
        "conditioning": bell_draw(arg_keys[3], (GROUPS, IMGS, CONDD), 1.0, 6.0, ((0, 8),)),
        "image_sizes": draw_image_sizes(jax.random.fold_in(arg_keys[16], 71), 0),
        "ada_weight": bell_draw(arg_keys[5], (CONDD, 4 * D), CONDD ** -0.5, 0.1875, ((0, 4),)),
        "ada_bias": bell_draw(arg_keys[6], (4 * D,), 0.5, 3.0, (), jnp.float32),
        "qkv_weight": bell_draw(arg_keys[7], (D, 3 * D), D ** -0.5, 0.15625, ((0, 4),)),
        "out_weight": bell_draw(arg_keys[8], (D, D), D ** -0.5, 0.15625, ((0, 4),)),
        "text_weight": bell_draw(arg_keys[9], (CAPD, 2 * D), CAPD ** -0.5, 0.09375, ((0, 4),)),
        "gate_up_weight": bell_draw(arg_keys[10], (D, 2 * FF), D ** -0.5, 0.15625, ((0, 4),)),
        "down_weight": bell_draw(arg_keys[11], (FF, D), FF ** -0.5, 0.09375, ((0, 4),)),
        "norm_gains": jnp.clip(1.0 + 0.18 * jax.random.normal(arg_keys[12], (7, D), jnp.float32), 0.1, 1.9),
        "norm_shifts": bell_draw(arg_keys[13], (2, D), 0.5, 3.0, (), jnp.float32),
        "text_gain": jnp.clip(1.0 + 0.18 * jax.random.normal(arg_keys[14], (CAPD,), jnp.float32), 0.1, 1.9),
        "head_gate": jnp.clip(jax.random.uniform(arg_keys[15], (HEADS,), jnp.float32, 0.2, 0.8), 0.2, 0.8),
    }


EPS = 1e-05
HIGHEST_PRECISION = lax.Precision.HIGHEST
MASKED = -1e+30

@jax.custom_vjp
def low(v):
    return lax.optimization_barrier(v.astype(jnp.bfloat16)).astype(jnp.float32)

@jax.custom_vjp
def low_back(v):
    return v

def low_keep(v):
    return (low(v), None)

def low_pass(kept, grad):
    return (grad,)

def back_keep(v):
    return (v, None)

def back_low(kept, grad):
    return (low(grad),)
low.defvjp(low_keep, low_pass)
low_back.defvjp(back_keep, back_low)

def matmul(left, right):
    return jnp.dot(left, right, precision=HIGHEST_PRECISION, preferred_element_type=jnp.float32)

def rms_norm(value, gain):
    return value * lax.rsqrt(lax.optimization_barrier(jnp.mean(value * value, axis=-1, keepdims=True)) + EPS) * gain

def layer_norm(value, weight, shift):
    centred = value - lax.optimization_barrier(jnp.mean(value, axis=-1, keepdims=True))
    return centred * lax.rsqrt(lax.optimization_barrier(jnp.mean(centred * centred, axis=-1, keepdims=True)) + EPS) * weight + shift

def token_layout(image_sizes, first_token, token_count, image_count):
    patch_rows = image_sizes[:, 0].astype(jnp.int32)
    patch_cols = image_sizes[:, 1].astype(jnp.int32)
    image_tokens = patch_rows * (patch_cols + 1)
    image_ends = jnp.cumsum(image_tokens).astype(jnp.int32)
    image_starts = image_ends - image_tokens
    position = first_token + jnp.arange(token_count, dtype=jnp.int32)
    member_of = (position[:, None] >= image_starts[None, :]) & (position[:, None] < image_ends[None, :])
    member_int = member_of.astype(jnp.int32)
    in_image = lax.optimization_barrier(jnp.sum(member_int, axis=1)).astype(jnp.int32)
    slot_ids = jnp.arange(image_count, dtype=jnp.int32)
    image_index = (lax.optimization_barrier(jnp.sum(member_int * slot_ids[None, :], axis=1)) + image_count * (1 - in_image)).astype(jnp.int32)
    offset_in = (position - lax.optimization_barrier(jnp.sum(member_int * image_starts[None, :], axis=1))).astype(jnp.int32)
    line_width = (lax.optimization_barrier(jnp.sum(member_int * (patch_cols + 1)[None, :], axis=1)) + (1 - in_image)).astype(jnp.int32)
    token_row = (offset_in // line_width * in_image).astype(jnp.int32)
    token_col = (offset_in % line_width * in_image).astype(jnp.int32)
    return (member_of.astype(jnp.float32), image_index, token_row, token_col)

def rope_tables(token_row, token_col, head_dim):
    quarter = head_dim // 4
    frequency = 10000.0 ** (-jnp.arange(quarter, dtype=jnp.float32) / quarter)
    angles = jnp.concatenate([token_row.astype(jnp.float32)[:, None] * frequency[None, :], token_col.astype(jnp.float32)[:, None] * frequency[None, :]], axis=1)
    return (jnp.cos(angles), jnp.sin(angles))

def rotate(value, cosine, sine_table):
    paired = value.reshape(value.shape[0], value.shape[1], value.shape[2] // 2, 2)
    real_part = paired[..., 0]
    imag_part = paired[..., 1]
    cos_b = cosine[:, None, :]
    sin_b = sine_table[:, None, :]
    turned = jnp.stack([real_part * cos_b - imag_part * sin_b, real_part * sin_b + imag_part * cos_b], axis=-1)
    return turned.reshape(value.shape)

def head_attention(queries, key_block, value_block, allowed):
    scores = low_back(matmul(queries, key_block.T) * HD ** (-0.5))
    scores = jnp.where(allowed, scores, MASKED)
    maximum = lax.optimization_barrier(jnp.max(scores, axis=1, keepdims=True))
    exponent = jnp.exp(scores - maximum)
    attn_probs = low(exponent / lax.optimization_barrier(jnp.sum(exponent, axis=1, keepdims=True)))
    return matmul(attn_probs, value_block)

def attention(queries, key_block, value_block, allowed):

    def one_head(packed):
        return head_attention(packed[0], packed[1], packed[2], allowed)
    result = lax.map(jax.checkpoint(one_head), (queries.transpose(1, 0, 2), key_block.transpose(1, 0, 2), value_block.transpose(1, 0, 2)))
    return result.transpose(1, 0, 2)

def block_forward(params, tokens, text_states, conditioning, image_sizes):
    ada_weight, ada_bias, qkv_weight, out_weight, text_weight, gate_up_weight, down_weight, norm_gains, norm_shifts, text_gain, head_gate = params
    token_count = tokens.shape[0]
    onehot, image_index, token_row, token_col = token_layout(image_sizes, 0, token_count, IMGS)
    modulation = matmul(low(jax.nn.silu(conditioning)), ada_weight) + ada_bias
    per_token = matmul(onehot, modulation)
    scale_attend = per_token[:, :D]
    gate_attend = per_token[:, D:2 * D]
    scale_feed = per_token[:, 2 * D:3 * D]
    gate_feed = per_token[:, 3 * D:]
    normed = low(rms_norm(tokens, norm_gains[0]) * (1.0 + scale_attend))
    projected = low_back(matmul(normed, qkv_weight))
    cosine, sine_table = rope_tables(token_row, token_col, HD)
    queries = low(rotate(layer_norm(projected[:, :D], norm_gains[2], norm_shifts[0]).reshape(token_count, HEADS, HD), cosine, sine_table))
    key_rows = low(rotate(layer_norm(projected[:, D:2 * D], norm_gains[3], norm_shifts[1]).reshape(token_count, HEADS, HD), cosine, sine_table))
    value_rows = low(projected[:, 2 * D:]).reshape(token_count, HEADS, HD)
    text_normed = low(rms_norm(text_states, text_gain)).reshape(IMGS * CAP, CAPD)
    text_projected = low_back(matmul(text_normed, text_weight))
    text_keys = low(layer_norm(text_projected[:, :D], norm_gains[4], 0.0)).reshape(IMGS * CAP, HEADS, HD)
    text_values = low(text_projected[:, D:]).reshape(IMGS * CAP, HEADS, HD)
    same_image = image_index[:, None] == image_index[None, :]
    text_image = jnp.arange(IMGS * CAP, dtype=jnp.int32) // CAP
    linked = (image_index[:, None] == text_image[None, :]) | (image_index[:, None] == IMGS)
    self_out = low_back(attention(queries, key_rows, value_rows, same_image))
    cross_out = low_back(attention(queries, text_keys, text_values, linked))
    mixed = low((self_out + jnp.tanh(head_gate)[None, :, None] * cross_out).reshape(token_count, D))
    branch = low_back(matmul(mixed, out_weight))
    hidden = tokens + jnp.tanh(gate_attend) * rms_norm(branch, norm_gains[1])
    normed_feed = low(rms_norm(hidden, norm_gains[5]) * (1.0 + scale_feed))
    gate_up = low_back(matmul(normed_feed, gate_up_weight))
    activated = low(jax.nn.silu(gate_up[:, :FF]) * gate_up[:, FF:])
    down_out = low_back(matmul(activated, down_weight))
    return hidden + jnp.tanh(gate_feed) * rms_norm(down_out, norm_gains[6])

def reference(tokens, cotangent, text_states, conditioning, image_sizes, ada_weight, ada_bias, qkv_weight, out_weight, text_weight, gate_up_weight, down_weight, norm_gains, norm_shifts, text_gain, head_gate):
    params = (ada_weight.astype(jnp.float32), ada_bias.astype(jnp.float32), qkv_weight.astype(jnp.float32), out_weight.astype(jnp.float32), text_weight.astype(jnp.float32), gate_up_weight.astype(jnp.float32), down_weight.astype(jnp.float32), norm_gains.astype(jnp.float32), norm_shifts.astype(jnp.float32), text_gain.astype(jnp.float32), head_gate.astype(jnp.float32))

    def per_group(running, member):
        group_tokens, group_cot, group_text, group_cond, group_sizes = member

        def forward_fn(param_set, token_in, text_in):
            return block_forward(param_set, token_in, text_in, group_cond, group_sizes)
        result, pull = jax.vjp(forward_fn, params, group_tokens, group_text)
        param_grads, token_grads, text_grads = pull(group_cot)
        running = jax.tree.map(lambda total, extra: total + extra, running, param_grads)
        return (running, (result.astype(jnp.bfloat16), token_grads.astype(jnp.bfloat16), text_grads.astype(jnp.bfloat16)))
    zeros = jax.tree.map(jnp.zeros_like, params)
    summed, stacked = lax.scan(per_group, zeros, (tokens.astype(jnp.float32), cotangent.astype(jnp.float32), text_states.astype(jnp.float32), conditioning.astype(jnp.float32), image_sizes))
    block_out, tokens_grad, text_grad = stacked
    return (block_out, tokens_grad, text_grad, summed[0], summed[2], summed[3], summed[4], summed[5], summed[6], summed[1], summed[7], summed[8], summed[9], summed[10])
```

```python
import functools

import jax
import jax.numpy as jnp
from jax import lax
from jax.experimental import pallas as pl
from jax.experimental.pallas import tpu as pltpu
from jax.sharding import Mesh
from jax.sharding import PartitionSpec as P

EPS = 1e-05
HIGHEST_PRECISION = lax.Precision.HIGHEST
MASKED = -1e30
LOG2E = 1.4426950408889634
FIRST_PATCHES = 16 * 12**2
FIRST_MOST = FIRST_PATCHES + 96
QBLOCK = 256
BF16 = jnp.bfloat16
F32 = jnp.float32
VMEM_LIMIT = 60 * 1024 * 1024


def round_up(value, step):
    return -(-value // step) * step


def low_product(left, right):
    return jnp.dot(left, right, preferred_element_type=F32)


def times_transposed(left, right):
    return lax.dot_general(left, right, (((1,), (1,)), ((), ())), preferred_element_type=F32)


def outer_sum(left, right):
    return lax.dot_general(left, right, (((0,), (0,)), ((), ())), preferred_element_type=F32)


def exact_outer(left, right):
    return lax.dot_general(
        left, right, (((0,), (0,)), ((), ())), precision=HIGHEST_PRECISION, preferred_element_type=F32
    )


def exact_transposed(left, right):
    return lax.dot_general(
        left, right, (((1,), (1,)), ((), ())), precision=HIGHEST_PRECISION, preferred_element_type=F32
    )


def row_mean(value):
    return jnp.mean(value, axis=-1, keepdims=True)


def inverse_rms(value):
    return lax.rsqrt(row_mean(value * value) + EPS)


def norm_pull(grad, unit, inverse):
    return (grad - unit * row_mean(grad * unit)) * inverse


def token_layout(image_sizes, position, image_count):
    start = jnp.int32(0)
    image_index = jnp.full(position.shape, image_count, jnp.int32)
    token_row = jnp.zeros(position.shape, jnp.int32)
    token_col = jnp.zeros(position.shape, jnp.int32)
    for i in range(image_count):
        width = image_sizes[i, 1] + 1
        end = start + image_sizes[i, 0] * width
        inside = (position >= start) & (position < end)
        offset = position - start
        image_index = jnp.where(inside, i, image_index)
        token_row = jnp.where(inside, offset // width, token_row)
        token_col = jnp.where(inside, offset % width, token_col)
        start = end
    return image_index, token_row, token_col


def rope_tables(token_row, token_col, head_dim):
    quarter = head_dim // 4
    pair = (jnp.arange(128, dtype=jnp.int32) % head_dim) // 2
    frequency = 10000.0 ** (-(pair % quarter).astype(F32) / quarter)
    place = jnp.where(
        (pair < quarter)[None, :], token_row.astype(F32)[:, None], token_col.astype(F32)[:, None]
    )
    angles = place * frequency[None, :]
    even = (jnp.arange(128, dtype=jnp.int32) % 2 == 0)[None, :]
    return jnp.cos(angles), jnp.where(even, -jnp.sin(angles), jnp.sin(angles))


def swap_pairs(value):
    width = value.shape[1]
    even = lax.broadcasted_iota(jnp.int32, value.shape, 1) % 2 == 0
    return jnp.where(even, pltpu.roll(value, width - 1, 1), pltpu.roll(value, 1, 1))


def wide_table(table, width):
    return jnp.concatenate([table] * (width // table.shape[1]), axis=1)


def pack_columns(columns):
    rows = columns[0].shape[0]
    lane = lax.broadcasted_iota(jnp.int32, (rows, 128), 1)
    packed = jnp.zeros((rows, 128), F32)
    for i, column in enumerate(columns):
        packed = jnp.where(lane == i, column, packed)
    return jnp.transpose(packed)[:8, :]


def as_columns(rows_list):
    width = rows_list[0].shape[1]
    stacked = jnp.concatenate(
        rows_list + [jnp.zeros((128 - len(rows_list), width), F32)], axis=0
    )
    return jnp.transpose(stacked)


def real_lanes(shape, part):
    return lax.broadcasted_iota(jnp.int32, shape, 1) < part


def own_stats(value, part):
    mean = jnp.sum(value, axis=1, keepdims=True) * (1.0 / part)
    centred = value - mean
    if value.shape[1] != part:
        centred = jnp.where(real_lanes(value.shape, part), centred, 0.0)
    return mean, jnp.sum(centred * centred, axis=1, keepdims=True)


def joined_stats(stats_ref, part, slot):
    narrow = stats_ref.shape[0]
    means = [stats_ref[i, 2 * slot : 2 * slot + 1, :] for i in range(narrow)]
    squares = [stats_ref[i, 2 * slot + 1 : 2 * slot + 2, :] for i in range(narrow)]
    mean = functools.reduce(jnp.add, means) * (1.0 / narrow)
    square = functools.reduce(jnp.add, squares)
    square = square + part * functools.reduce(jnp.add, [(m - mean) * (m - mean) for m in means])
    return mean, lax.rsqrt(square * (1.0 / (narrow * part)) + EPS)


def stats_kernel(part, slots, projected_ref, out_ref):
    padded = projected_ref.shape[1] // slots
    columns = []
    for slot in range(slots):
        columns += own_stats(projected_ref[:, slot * padded : (slot + 1) * padded], part)
    out_ref[...] = pack_columns(columns)


def column_stats(projected, part, padded, slots):
    rows = projected.shape[0]
    return pl.pallas_call(
        functools.partial(stats_kernel, part, slots),
        grid=(pl.cdiv(rows, QBLOCK),),
        in_specs=[pl.BlockSpec((QBLOCK, slots * padded), lambda i: (i, 0))],
        out_specs=pl.BlockSpec((8, QBLOCK), lambda i: (0, i)),
        out_shape=jax.ShapeDtypeStruct((8, rows), F32),
        compiler_params=pltpu.CompilerParams(vmem_limit_bytes=VMEM_LIMIT),
        cost_estimate=pl.CostEstimate(flops=10 * rows * slots * padded, bytes_accessed=4 * rows * slots * padded, transcendentals=0),
    )(projected)


def heads_kernel(part, query_scale, projected_ref, stats_ref, cos_ref, sin_ref, gains_ref, shifts_ref, out_ref):
    padded = projected_ref.shape[1] // 3
    cosine = wide_table(cos_ref[...], padded)
    sine = wide_table(sin_ref[...], padded)
    columns = as_columns([*joined_stats(stats_ref, part, 0), *joined_stats(stats_ref, part, 1)])
    for slot in range(3):
        place = slice(slot * padded, (slot + 1) * padded)
        value = projected_ref[:, place]
        if slot < 2:
            value = (value - columns[:, 2 * slot : 2 * slot + 1]) * columns[:, 2 * slot + 1 : 2 * slot + 2]
            value = value * gains_ref[slot : slot + 1, :] + shifts_ref[slot : slot + 1, :]
            value = value * cosine + swap_pairs(value) * sine
            if slot == 0:
                value = value * query_scale
        out_ref[:, place] = value.astype(BF16)


def make_heads(projected, stats, cosine, sine, gains, shifts, part, query_scale):
    rows, triple = projected.shape
    padded = triple // 3
    narrow = stats.shape[0]
    return pl.pallas_call(
        functools.partial(heads_kernel, part, query_scale),
        grid=(pl.cdiv(rows, QBLOCK),),
        in_specs=[
            pl.BlockSpec((QBLOCK, triple), lambda i: (i, 0)),
            pl.BlockSpec((narrow, 8, QBLOCK), lambda i: (0, 0, i)),
            pl.BlockSpec((QBLOCK, 128), lambda i: (i, 0)),
            pl.BlockSpec((QBLOCK, 128), lambda i: (i, 0)),
            pl.BlockSpec((2, padded), lambda i: (0, 0)),
            pl.BlockSpec((2, padded), lambda i: (0, 0)),
        ],
        out_specs=pl.BlockSpec((QBLOCK, triple), lambda i: (i, 0)),
        out_shape=jax.ShapeDtypeStruct((rows, triple), BF16),
        compiler_params=pltpu.CompilerParams(vmem_limit_bytes=VMEM_LIMIT),
        cost_estimate=pl.CostEstimate(flops=40 * rows * triple, bytes_accessed=6 * rows * triple, transcendentals=0),
    )(projected, stats, cosine, sine, gains, shifts)


def turned_back(refs, cosine, sine):
    grad = jnp.concatenate([ref[...].astype(F32) for ref in refs], axis=1)
    return grad * cosine - swap_pairs(grad) * sine


def grad_stats_kernel(rows, part, pairs, *refs):
    dq_refs, dk_refs = refs[:pairs], refs[pairs : 2 * pairs]
    projected_ref, stats_ref, cos_ref, sin_ref, gains_ref, out_ref, sums_ref = refs[2 * pairs :]
    step = pl.program_id(0)
    padded = 128 * pairs
    cosine = wide_table(cos_ref[...], padded)
    sine = wide_table(sin_ref[...], padded)
    height = cos_ref.shape[0]
    inside = step * height + lax.broadcasted_iota(jnp.int32, (height, 1), 0) < rows

    @pl.when(step == 0)
    def _():
        sums_ref[...] = jnp.zeros_like(sums_ref)

    columns = as_columns([*joined_stats(stats_ref, part, 0), *joined_stats(stats_ref, part, 1)])
    packed = []
    for slot, grads in enumerate((dq_refs, dk_refs)):
        grad = jnp.where(inside, turned_back(grads, cosine, sine), 0.0)
        unit = (projected_ref[:, slot * padded : (slot + 1) * padded] - columns[:, 2 * slot : 2 * slot + 1])
        unit = jnp.where(inside, unit * columns[:, 2 * slot + 1 : 2 * slot + 2], 0.0)
        both = grad * unit
        sums_ref[2 * slot : 2 * slot + 1, :] += jnp.sum(both, axis=0, keepdims=True)
        sums_ref[2 * slot + 1 : 2 * slot + 2, :] += jnp.sum(grad, axis=0, keepdims=True)
        gain = gains_ref[slot : slot + 1, :]
        packed.append(jnp.sum(grad * gain, axis=1, keepdims=True))
        packed.append(jnp.sum(both * gain, axis=1, keepdims=True))
    out_ref[...] = pack_columns(packed)


def heads_back_kernel(part, pairs, *refs):
    dq_refs, dk_refs, dv_refs = refs[:pairs], refs[pairs : 2 * pairs], refs[2 * pairs : 3 * pairs]
    projected_ref, stats_ref, totals_ref, cos_ref, sin_ref, gains_ref, out_ref = refs[3 * pairs :]
    padded = 128 * pairs
    narrow = stats_ref.shape[0]
    cosine = wide_table(cos_ref[...], padded)
    sine = wide_table(sin_ref[...], padded)
    means = [
        functools.reduce(jnp.add, [totals_ref[i, j : j + 1, :] for i in range(narrow)]) * (1.0 / (narrow * part))
        for j in range(4)
    ]
    columns = as_columns([*joined_stats(stats_ref, part, 0), *joined_stats(stats_ref, part, 1), *means])
    for slot, grads in enumerate((dq_refs, dk_refs)):
        grad = turned_back(grads, cosine, sine) * gains_ref[slot : slot + 1, :]
        inverse = columns[:, 2 * slot + 1 : 2 * slot + 2]
        unit = (projected_ref[:, slot * padded : (slot + 1) * padded] - columns[:, 2 * slot : 2 * slot + 1]) * inverse
        grad = grad - columns[:, 4 + 2 * slot : 5 + 2 * slot] - unit * columns[:, 5 + 2 * slot : 6 + 2 * slot]
        grad = grad * inverse
        if padded != part:
            grad = jnp.where(real_lanes(grad.shape, part), grad, 0.0)
        out_ref[:, slot * padded : (slot + 1) * padded] = grad.astype(BF16)
    for pair, ref in enumerate(dv_refs):
        out_ref[:, 2 * padded + 128 * pair : 2 * padded + 128 * (pair + 1)] = ref[...]


def heads_back(grads, projected, stats, cosine, sine, gains, part, share):
    rows, triple = projected.shape
    padded = triple // 3
    pairs = padded // 128
    narrow = stats.shape[0]
    pair_spec = pl.BlockSpec((QBLOCK, 128), lambda i: (i, 0))
    two_spec = pl.BlockSpec((QBLOCK, 2 * padded), lambda i: (i, 0))
    stat_spec = pl.BlockSpec((narrow, 8, QBLOCK), lambda i: (0, 0, i))
    gain_spec = pl.BlockSpec((2, padded), lambda i: (0, 0))
    own, sums = pl.pallas_call(
        functools.partial(grad_stats_kernel, rows, part, pairs),
        grid=(pl.cdiv(rows, QBLOCK),),
        in_specs=[pair_spec] * (2 * pairs) + [two_spec, stat_spec, pair_spec, pair_spec, gain_spec],
        out_specs=[
            pl.BlockSpec((8, QBLOCK), lambda i: (0, i)),
            pl.BlockSpec((8, padded), lambda i: (0, 0)),
        ],
        out_shape=[jax.ShapeDtypeStruct((8, rows), F32), jax.ShapeDtypeStruct((8, padded), F32)],
        compiler_params=pltpu.CompilerParams(vmem_limit_bytes=VMEM_LIMIT),
        cost_estimate=pl.CostEstimate(flops=40 * rows * triple, bytes_accessed=5 * rows * triple, transcendentals=0),
    )(*grads[0], *grads[1], projected, stats, cosine, sine, gains)
    totals = share(own)
    out = pl.pallas_call(
        functools.partial(heads_back_kernel, part, pairs),
        grid=(pl.cdiv(rows, QBLOCK),),
        in_specs=[pair_spec] * (3 * pairs) + [two_spec, stat_spec, stat_spec, pair_spec, pair_spec, gain_spec],
        out_specs=pl.BlockSpec((QBLOCK, triple), lambda i: (i, 0)),
        out_shape=jax.ShapeDtypeStruct((rows, triple), BF16),
        compiler_params=pltpu.CompilerParams(vmem_limit_bytes=VMEM_LIMIT),
        cost_estimate=pl.CostEstimate(flops=40 * rows * triple, bytes_accessed=7 * rows * triple, transcendentals=0),
    )(*grads[0], *grads[1], *grads[2], projected, stats, totals, cosine, sine, gains)
    return out, sums


def head_lanes(rows, half, head_dim):
    lane = lax.broadcasted_iota(jnp.int32, (rows, 128), 1)
    return (lane >= half * head_dim) & (lane < (half + 1) * head_dim)


def softmax_product(pieces):
    maximum = functools.reduce(jnp.maximum, [jnp.max(s, axis=1, keepdims=True) for s, _ in pieces])
    total, result = 0.0, 0.0
    for scores, values in pieces:
        weight = jnp.exp2(scores - maximum)
        total = total + jnp.sum(weight, axis=1, keepdims=True)
        result = result + low_product(weight.astype(BF16), values)
    return result * (1.0 / total), maximum + jnp.log2(total)


def attend_kernel(
    head_dim, first, most, caption, image_count,
    gate_ref, q_ref, k_ref, v_ref, tk_ref, tv_ref, column_ref, row_ref,
    mixed_ref, self_ref, cross_ref, stats_ref,
):
    count = q_ref.shape[0]
    halves = 128 // head_dim

    def emit(at, rows, outs):
        lanes = [head_lanes(rows, half, head_dim) for half in range(halves)]
        own, cross, gated = 0.0, 0.0, 0.0
        columns = []
        for half, (own_out, own_total, cross_out, cross_total) in enumerate(outs):
            gate = gate_ref[0, half]
            own = own + jnp.where(lanes[half], own_out, 0.0)
            cross = cross + jnp.where(lanes[half], cross_out, 0.0)
            gated = gated + jnp.where(lanes[half], gate * cross_out, 0.0)
            columns += [own_total, cross_total]
        self_ref[pl.ds(at, rows), :] = own
        cross_ref[pl.ds(at, rows), :] = cross
        mixed_ref[pl.ds(at, rows), :] = (own + gated).astype(BF16)
        lane = lax.broadcasted_iota(jnp.int32, (rows, 128), 1)
        packed = jnp.zeros((rows, 128), F32)
        for i, column in enumerate(columns):
            packed = jnp.where(lane == i, column, packed)
        stats_ref[:, pl.ds(at, rows)] = jnp.transpose(packed)[:8, :]

    def clean(block, carry):
        at = pl.multiple_of(block * QBLOCK, QBLOCK)
        queries = q_ref[pl.ds(at, QBLOCK), :]
        outs = []
        for half in range(halves):
            q = jnp.where(head_lanes(QBLOCK, half, head_dim), queries, jnp.zeros_like(queries))
            bias = jnp.where(row_ref[0:1, first:most] == 0, 0.0, MASKED)
            own_out, own_total = softmax_product([
                (times_transposed(q, k_ref[0:first, :]), v_ref[0:first, :]),
                (times_transposed(q, k_ref[first:most, :]) + bias, v_ref[first:most, :]),
            ])
            cross_out, cross_total = softmax_product(
                [(times_transposed(q, tk_ref[0:caption, :]), tv_ref[0:caption, :])]
            )
            outs.append((own_out, own_total, cross_out, cross_total))
        emit(at, QBLOCK, outs)
        return carry

    lax.fori_loop(0, first // QBLOCK, clean, 0)
    rest = count - first
    queries = q_ref[first:count, :]
    image = column_ref[first:count, :]
    outs = []
    for half in range(halves):
        q = jnp.where(head_lanes(rest, half, head_dim), queries, jnp.zeros_like(queries))
        own_out, own_total = softmax_product([
            (jnp.where(image == row_ref[0:1, :], times_transposed(q, k_ref[...]), MASKED), v_ref[...])
        ])
        scores = times_transposed(q, tk_ref[...])
        owner = lax.broadcasted_iota(jnp.int32, (1, scores.shape[1]), 1) // caption
        scores = jnp.where((image == owner) | (image == image_count), scores, MASKED)
        cross_out, cross_total = softmax_product([(scores, tv_ref[...])])
        outs.append((own_out, own_total, cross_out, cross_total))
    emit(first, rest, outs)


def attention_specs(count, texts, pairs):
    return [
        pl.BlockSpec((1, 128 // 64), lambda p: (p, 0), memory_space=pltpu.SMEM),
        pl.BlockSpec((count, 128), lambda p: (0, p)),
        pl.BlockSpec((count, 128), lambda p: (0, pairs + p)),
        pl.BlockSpec((count, 128), lambda p: (0, 2 * pairs + p)),
        pl.BlockSpec((texts, 128), lambda p: (0, p)),
        pl.BlockSpec((texts, 128), lambda p: (0, pairs + p)),
        pl.BlockSpec((count, 1), lambda p: (0, 0)),
        pl.BlockSpec((1, count), lambda p: (0, 0)),
    ]


def attend(gates, packed, text_packed, column, row, head_dim, image_count):
    count, texts = packed.shape[0], text_packed.shape[0]
    pairs = packed.shape[1] // 384
    halves = 128 // head_dim
    specs = attention_specs(count, texts, pairs)
    specs[0] = pl.BlockSpec((None, 1, halves), lambda p: (p, 0, 0), memory_space=pltpu.SMEM)
    most = min(round_up(FIRST_MOST, 128), count)
    flops = 4 * count * (count + texts) * 128 * pairs * halves
    return pl.pallas_call(
        functools.partial(
            attend_kernel, head_dim, FIRST_PATCHES, most, texts // image_count, image_count
        ),
        grid=(pairs,),
        in_specs=specs,
        out_specs=[
            pl.BlockSpec((count, 128), lambda p: (0, p)),
            pl.BlockSpec((count, 128), lambda p: (0, p)),
            pl.BlockSpec((count, 128), lambda p: (0, p)),
            pl.BlockSpec((None, 8, count), lambda p: (p, 0, 0)),
        ],
        out_shape=[
            jax.ShapeDtypeStruct((count, 128 * pairs), BF16),
            jax.ShapeDtypeStruct((count, 128 * pairs), F32),
            jax.ShapeDtypeStruct((count, 128 * pairs), F32),
            jax.ShapeDtypeStruct((pairs, 8, count), F32),
        ],
        compiler_params=pltpu.CompilerParams(vmem_limit_bytes=VMEM_LIMIT),
        cost_estimate=pl.CostEstimate(flops=flops, bytes_accessed=20 * count * 128 * pairs, transcendentals=count * count * pairs * halves),
    )(gates.reshape(pairs, 1, halves), packed, packed, packed, text_packed, text_packed, column, row)


def gate_lanes(gate_ref, head_dim):
    lane = lax.broadcasted_iota(jnp.int32, (1, 128), 1)
    gates = jnp.zeros((1, 128), F32)
    for half in range(128 // head_dim):
        gates = jnp.where(lane // head_dim == half, gate_ref[0, half], gates)
    return gates


def head_picks(head_dim):
    return (
        lax.broadcasted_iota(jnp.int32, (8, 128), 1) // head_dim
        == lax.broadcasted_iota(jnp.int32, (8, 128), 0)
    ).astype(F32)


def rows_back(head_dim, queries, outs, delta, stats, offset, keys, values, key_sum, value_sum, spans):
    rows = queries.shape[0]
    halves = 128 // head_dim
    zero = jnp.zeros((rows, 128), BF16)
    lanes = [head_lanes(rows, half, head_dim) for half in range(halves)]
    q_heads = [jnp.where(lane, queries, zero) for lane in lanes]
    out_heads = [jnp.where(lane, outs, zero) for lane in lanes]
    q_stack = jnp.concatenate(q_heads, axis=0)
    out_stack = jnp.concatenate(out_heads, axis=0)
    dq = [0.0] * halves
    for low, high, mask in spans:
        key_part = keys[low:high, :]
        value_part = values[low:high, :]
        probs, grads = [], []
        for half in range(halves):
            scores = mask(times_transposed(key_part, q_heads[half]))
            prob = jnp.exp2(scores - stats[2 * half + offset : 2 * half + offset + 1, :])
            dprob = times_transposed(value_part, out_heads[half])
            dscore = (prob * (dprob - delta[half : half + 1, :])).astype(BF16)
            probs.append(prob.astype(BF16))
            grads.append(dscore)
            dq[half] = dq[half] + outer_sum(dscore, key_part)
        value_sum[low:high, :] += low_product(jnp.concatenate(probs, axis=1), out_stack)
        key_sum[low:high, :] += low_product(jnp.concatenate(grads, axis=1), q_stack)
    total = 0.0
    for half in range(halves):
        total = total + jnp.where(lanes[half], dq[half], 0.0)
    return total


def cross_back_kernel(
    head_dim, first, caption, image_count, scale,
    gate_ref, q_ref, tk_ref, tv_ref, row_ref, grad_ref, cross_ref, stats_ref,
    dq_ref, dtk_ref, dtv_ref, gate_grad_ref, dtk_sum, dtv_sum,
):
    count = q_ref.shape[0]
    for total in (dtk_sum, dtv_sum, gate_grad_ref):
        total[...] = jnp.zeros_like(total)
    gates = gate_lanes(gate_ref, head_dim)
    picks = head_picks(head_dim)

    def part(at, rows, spans):
        wide = grad_ref[pl.ds(at, rows), :].astype(F32)
        cross = cross_ref[pl.ds(at, rows), :]
        gate_grad_ref[0:1, :] += jnp.sum(wide * cross, axis=0, keepdims=True)
        gated = (wide * gates).astype(BF16)
        delta = exact_transposed(picks, gated.astype(F32) * cross)
        dq = rows_back(
            head_dim, q_ref[pl.ds(at, rows), :], gated, delta, stats_ref[:, pl.ds(at, rows)], 1,
            tk_ref, tv_ref, dtk_sum, dtv_sum, spans,
        )
        dq_ref[pl.ds(at, rows), :] = (dq * scale).astype(BF16)

    def clean(block, carry):
        part(pl.multiple_of(block * QBLOCK, QBLOCK), QBLOCK, [(0, caption, lambda scores: scores)])
        return carry

    lax.fori_loop(0, first // QBLOCK, clean, 0)
    image = row_ref[0:1, first:count]
    owner = lax.broadcasted_iota(jnp.int32, (tk_ref.shape[0], 1), 0) // caption
    allowed = (owner == image) | (image == image_count)
    part(first, count - first, [(0, tk_ref.shape[0], lambda scores: jnp.where(allowed, scores, MASKED))])
    dtk_ref[...] = (dtk_sum[...] * (1.0 / LOG2E)).astype(BF16)
    dtv_ref[...] = dtv_sum[...].astype(BF16)


def cross_back(gates, packed, text_packed, row, grad, cross, stats, head_dim, image_count, scale):
    count, texts = packed.shape[0], text_packed.shape[0]
    pairs = packed.shape[1] // 384
    halves = 128 // head_dim
    tokens = pl.BlockSpec((count, 128), lambda p: (0, p))
    captions = pl.BlockSpec((texts, 128), lambda p: (0, p))
    flops = 10 * count * texts * 64 * pairs * halves
    return pl.pallas_call(
        functools.partial(cross_back_kernel, head_dim, FIRST_PATCHES, texts // image_count, image_count, scale),
        grid=(pairs,),
        in_specs=[
            pl.BlockSpec((None, 1, halves), lambda p: (p, 0, 0), memory_space=pltpu.SMEM),
            tokens,
            captions,
            pl.BlockSpec((texts, 128), lambda p: (0, pairs + p)),
            pl.BlockSpec((1, count), lambda p: (0, 0)),
            tokens,
            tokens,
            pl.BlockSpec((None, 8, count), lambda p: (p, 0, 0)),
        ],
        out_specs=[tokens, captions, captions, pl.BlockSpec((None, 8, 128), lambda p: (p, 0, 0))],
        out_shape=[jax.ShapeDtypeStruct((count, 128 * pairs), BF16)]
        + [jax.ShapeDtypeStruct((texts, 128 * pairs), BF16)] * 2
        + [jax.ShapeDtypeStruct((pairs, 8, 128), F32)],
        scratch_shapes=[pltpu.VMEM((texts, 128), F32), pltpu.VMEM((texts, 128), F32)],
        compiler_params=pltpu.CompilerParams(vmem_limit_bytes=VMEM_LIMIT),
        cost_estimate=pl.CostEstimate(flops=flops, bytes_accessed=12 * count * 128 * pairs, transcendentals=count * texts * pairs),
    )(gates.reshape(pairs, 1, halves), packed, text_packed, text_packed, row, grad, cross, stats)


def self_back_kernel(
    head_dim, first, most, scale,
    q_ref, k_ref, v_ref, column_ref, row_ref, grad_ref, self_ref, stats_ref, more_ref,
    dq_ref, dk_ref, dv_ref, dk_sum, dv_sum,
):
    count = q_ref.shape[0]
    dk_sum[...] = jnp.zeros_like(dk_sum)
    dv_sum[...] = jnp.zeros_like(dv_sum)
    picks = head_picks(head_dim)

    def part(at, rows, spans):
        grad = grad_ref[pl.ds(at, rows), :]
        delta = exact_transposed(picks, grad.astype(F32) * self_ref[pl.ds(at, rows), :])
        dq = rows_back(
            head_dim, q_ref[pl.ds(at, rows), :], grad, delta, stats_ref[:, pl.ds(at, rows)], 0,
            k_ref, v_ref, dk_sum, dv_sum, spans,
        )
        dq_ref[pl.ds(at, rows), :] = (dq * scale + more_ref[pl.ds(at, rows), :].astype(F32)).astype(BF16)

    def clean(block, carry):
        bias = jnp.where(column_ref[first:most, :] == 0, 0.0, MASKED)
        part(
            pl.multiple_of(block * QBLOCK, QBLOCK), QBLOCK,
            [(0, first, lambda scores: scores), (first, most, lambda scores: scores + bias)],
        )
        return carry

    lax.fori_loop(0, first // QBLOCK, clean, 0)
    image = row_ref[0:1, first:count]
    part(first, count - first, [(0, count, lambda scores: jnp.where(column_ref[...] == image, scores, MASKED))])
    dk_ref[...] = (dk_sum[...] * (1.0 / LOG2E)).astype(BF16)
    dv_ref[...] = dv_sum[...].astype(BF16)


def self_back(pair, packed, column, row, grad, own, stats, more, head_dim, scale):
    count = packed.shape[0]
    pairs = packed.shape[1] // 384
    tokens = pl.BlockSpec((count, 128), lambda i: (0, pair))
    out = pl.BlockSpec((count, 128), lambda i: (0, 0))
    most = min(round_up(FIRST_MOST, 128), count)
    flops = 10 * count * count * 128
    return pl.pallas_call(
        functools.partial(self_back_kernel, head_dim, FIRST_PATCHES, most, scale),
        grid=(1,),
        in_specs=[
            tokens,
            pl.BlockSpec((count, 128), lambda i: (0, pairs + pair)),
            pl.BlockSpec((count, 128), lambda i: (0, 2 * pairs + pair)),
            pl.BlockSpec((count, 1), lambda i: (0, 0)),
            pl.BlockSpec((1, count), lambda i: (0, 0)),
            tokens,
            tokens,
            pl.BlockSpec((None, 8, count), lambda i: (pair, 0, 0)),
            tokens,
        ],
        out_specs=[out, out, out],
        out_shape=[jax.ShapeDtypeStruct((count, 128), BF16)] * 3,
        scratch_shapes=[pltpu.VMEM((count, 128), F32), pltpu.VMEM((count, 128), F32)],
        compiler_params=pltpu.CompilerParams(vmem_limit_bytes=VMEM_LIMIT),
        cost_estimate=pl.CostEstimate(flops=flops, bytes_accessed=30 * count * 128, transcendentals=2 * count * count),
    )(packed, packed, packed, column, row, grad, own, stats, more)


def fsdp_share_kernel(narrow, x_ref, out_ref, send_sem, recv_sem):
    me = lax.axis_index("fsdp")
    barrier = pltpu.get_barrier_semaphore()
    for step in range(1, narrow):
        pl.semaphore_signal(
            barrier, inc=1, device_id={"fsdp": lax.rem(me + step, narrow)}, device_id_type=pl.DeviceIdType.MESH
        )
    pl.semaphore_wait(barrier, narrow - 1)
    copies = []
    for step in range(1, narrow):
        copy = pltpu.make_async_remote_copy(
            src_ref=x_ref,
            dst_ref=out_ref.at[me],
            send_sem=send_sem.at[step],
            recv_sem=recv_sem.at[step],
            device_id={"fsdp": lax.rem(me + step, narrow)},
            device_id_type=pl.DeviceIdType.MESH,
        )
        copy.start()
        copies.append(copy)
    out_ref[me] = x_ref[...]
    for copy in copies:
        copy.wait()


def fsdp_share(value, narrow, collective_id):
    return pl.pallas_call(
        functools.partial(fsdp_share_kernel, narrow),
        in_specs=[pl.BlockSpec(memory_space=pltpu.VMEM)],
        out_specs=pl.BlockSpec(memory_space=pltpu.VMEM),
        out_shape=jax.ShapeDtypeStruct((narrow,) + value.shape, value.dtype),
        scratch_shapes=[pltpu.SemaphoreType.DMA((narrow,)), pltpu.SemaphoreType.DMA((narrow,))],
        compiler_params=pltpu.CompilerParams(collective_id=collective_id, has_side_effects=True),
        cost_estimate=pl.CostEstimate(flops=0, bytes_accessed=8 * narrow * value.size, transcendentals=0),
    )(value)


def finish_kernel(narrow, wide, sum_rows, x_ref, out_ref, first_ref, second_ref, sends, recvs):
    me = lax.axis_index("fsdp")
    group = lax.axis_index("z") * 2 + lax.axis_index("core")
    rows = x_ref.shape[1]
    rest = rows - sum_rows
    barrier = pltpu.get_barrier_semaphore()
    places = [{"fsdp": lax.rem(me + step, narrow)} for step in range(1, narrow)]
    peers = [lax.rem(group + step, wide) for step in range(1, wide)]
    partners = [{"z": peer // 2, "core": peer % 2} for peer in peers]
    for place in places + partners:
        pl.semaphore_signal(barrier, inc=1, device_id=place, device_id_type=pl.DeviceIdType.MESH)
    pl.semaphore_wait(barrier, narrow + wide - 2)

    def send_all(targets, source, target, base):
        copies = []
        for i, place in enumerate(targets):
            copy = pltpu.make_async_remote_copy(
                src_ref=source(i),
                dst_ref=target,
                send_sem=sends.at[base + i],
                recv_sem=recvs.at[base + i],
                device_id=place,
                device_id_type=pl.DeviceIdType.MESH,
            )
            copy.start()
            copies.append(copy)
        return copies

    copies = send_all(places, lambda i: x_ref.at[lax.rem(me + i + 1, narrow)], first_ref.at[me], 0)
    first_ref[me] = x_ref[me]
    for copy in copies:
        copy.wait()
    total = first_ref[0]
    for i in range(1, narrow):
        total = total + first_ref[i]
    second_ref[group] = total
    copies = send_all(partners, lambda i: second_ref.at[group], second_ref.at[group], narrow)
    for copy in copies:
        copy.wait()
    total = second_ref[0, :sum_rows, :]
    for i in range(1, wide):
        total = total + second_ref[i, :sum_rows, :]
    out_ref[me, :sum_rows, :] = total
    for i in range(wide):
        out_ref[me, sum_rows + i * rest : sum_rows + (i + 1) * rest, :] = second_ref[i, sum_rows:, :]
    copies = send_all(places, lambda i: out_ref.at[me], out_ref.at[me], narrow + wide)
    for copy in copies:
        copy.wait()


def finish(summed, kept, narrow, wide, collective_id):
    sum_rows = round_up(-(-summed.size // (128 * narrow)), 8)
    kept_rows = round_up(-(-kept.size // (128 * narrow)), 8)

    def chunked(value, rows):
        return jnp.pad(value, (0, narrow * rows * 128 - value.size)).reshape(narrow, rows, 128)

    joined = jnp.concatenate([chunked(summed, sum_rows), chunked(kept, kept_rows)], axis=1)
    rows = sum_rows + kept_rows
    count = 2 * narrow + wide
    out = pl.pallas_call(
        functools.partial(finish_kernel, narrow, wide, sum_rows),
        in_specs=[pl.BlockSpec(memory_space=pltpu.VMEM)],
        out_specs=pl.BlockSpec(memory_space=pltpu.VMEM),
        out_shape=jax.ShapeDtypeStruct((narrow, sum_rows + wide * kept_rows, 128), F32),
        scratch_shapes=[
            pltpu.VMEM((narrow, rows, 128), F32),
            pltpu.VMEM((wide, rows, 128), F32),
            pltpu.SemaphoreType.DMA((count,)),
            pltpu.SemaphoreType.DMA((count,)),
        ],
        compiler_params=pltpu.CompilerParams(collective_id=collective_id, has_side_effects=True),
    )(joined)
    total = out[:, :sum_rows, :].reshape(-1)[: summed.size]
    groups = out[:, sum_rows:, :].reshape(narrow, wide, kept_rows * 128).transpose(1, 0, 2)
    return total, groups.reshape(wide, -1)[:, : kept.size]


def exchange(blocks, axis):
    return lax.all_to_all(blocks, axis, 0, 0, tiled=True)


def core_swap(value):
    return lax.ppermute(value, "core", [(0, 1), (1, 0)])


def by_core(low, high):
    first = lax.axis_index("core") == 0
    return jnp.where(first, low, high), jnp.where(first, high, low)


def in_core_order(own, other):
    first = lax.axis_index("core") == 0
    return jnp.where(first, own, other), jnp.where(first, other, own)


def reduced(own_left, other_left, right):
    came = core_swap(outer_sum(other_left, right).astype(BF16))
    both = (outer_sum(own_left, right) + came.astype(F32)).astype(BF16)
    part = lax.psum_scatter(both, "fsdp", scatter_dimension=0, tiled=True)
    return lax.psum_scatter(part, "z", scatter_dimension=0, tiled=True).astype(F32)


def device_columns(value, deep, narrow):
    rows, width = value.shape
    block = width // (2 * deep * narrow)
    core = lax.axis_index("core")
    if block % 128 == 0:
        blocks = value.reshape(rows, deep, 2, narrow, block).transpose(2, 0, 3, 1, 4).reshape(2, rows, width // 2)
        return tuple(lax.dynamic_index_in_dim(blocks, i, 0, keepdims=False) for i in (core, 1 - core))
    target = jnp.arange(width, dtype=jnp.int32)
    c, f, z, r = (
        target // (narrow * deep * block), target // (deep * block) % narrow, target // block % deep, target % block,
    )
    c = (c + core) % 2
    source = ((z * 2 + c) * narrow + f) * block + r
    pick = (jnp.arange(width, dtype=jnp.int32)[:, None] == source[None, :]).astype(BF16)
    moved = low_product(value, pick).astype(BF16)
    return moved[:, : width // 2], moved[:, width // 2 :]


def whole_weight(shard):
    rows = shard.shape[0] // 2
    half = lax.dynamic_slice_in_dim(shard, lax.axis_index("core") * rows, rows, 0)
    return lax.all_gather(half, ("fsdp", "core"), axis=0, tiled=True)


def shards(
    tokens,
    cotangent,
    text_states,
    conditioning,
    image_sizes,
    ada_weight,
    ada_bias,
    qkv_weight,
    out_weight,
    text_weight,
    gate_up_weight,
    down_weight,
    norm_gains,
    norm_shifts,
    text_gain,
    head_gate,
):
    model_width = tokens.shape[2]
    head_count = head_gate.shape[0]
    head_dim = model_width // head_count
    image_count = text_states.shape[1]
    caption_local = text_states.shape[2]
    caption_width = text_states.shape[3]
    local_tok = tokens.shape[1]
    deep = lax.axis_size("z")
    narrow = lax.axis_size("fsdp")
    wide = 2 * deep
    me = lax.axis_index("fsdp")
    group_tok = local_tok * narrow
    caption_full = caption_local * narrow
    score_scale = head_dim ** (-0.5)
    text_total = image_count * caption_full
    text_local = image_count * caption_local
    part = model_width // narrow
    part_pad = round_up(part, 128)
    heads_here = head_count // narrow
    pairs = part_pad // 128
    halves = 128 // head_dim

    group_sizes = image_sizes[0]
    position = me * local_tok + jnp.arange(local_tok, dtype=jnp.int32)
    image_index = token_layout(group_sizes, position, image_count)[0]
    key_image, key_row, key_col = token_layout(
        group_sizes, jnp.arange(group_tok, dtype=jnp.int32), image_count
    )
    member = [(image_index == i).astype(F32)[:, None] for i in range(image_count)]
    cosine, sine = rope_tables(key_row, key_col, head_dim)

    cond_low = jax.nn.silu(conditioning[0].astype(F32)).astype(BF16)
    cond_rows = ada_weight.shape[0]
    cond_part = lax.dynamic_slice_in_dim(cond_low, me * cond_rows, cond_rows, 1)
    modulation_part = low_product(cond_part, ada_weight)
    modulation = (
        jnp.sum(fsdp_share(modulation_part.reshape(-1, 128), narrow, 0), axis=0).reshape(modulation_part.shape)
        + ada_bias
    )

    def per_token(index):
        rows = modulation[:, index * model_width : (index + 1) * model_width]
        return functools.reduce(
            jnp.add, [member[i] * rows[i : i + 1, :] for i in range(image_count)]
        )

    def per_image(value):
        return jnp.stack([jnp.sum(member[i] * value, axis=0) for i in range(image_count)])

    token_in = tokens[0].astype(F32)
    token_inverse = inverse_rms(token_in)
    normed_low = (
        token_in * token_inverse * norm_gains[0] * (1.0 + per_token(0))
    ).astype(BF16)
    normed_all = lax.all_gather(normed_low, "fsdp", axis=0, tiled=True)

    def widened(value, slots):
        if part == part_pad:
            return value
        lead = value.shape[:-1]
        value = value.reshape(*lead, slots, part)
        pads = [(0, 0)] * (len(lead) + 1) + [(0, part_pad - part)]
        return jnp.pad(value, pads).reshape(*lead, slots * part_pad)

    def narrowed(value, slots):
        if part == part_pad:
            return value
        lead = value.shape[:-1]
        return value.reshape(*lead, slots, part_pad)[..., :part].reshape(*lead, slots * part)

    def own_columns(value):
        return widened(lax.dynamic_slice_in_dim(value, me * part, part, value.ndim - 1), 1)

    qkv_rows = qkv_weight.shape[0] // 2
    qkv_half = lax.dynamic_slice_in_dim(qkv_weight, lax.axis_index("core") * qkv_rows, qkv_rows, 0)
    qkv_half = exchange(
        qkv_half.reshape(qkv_rows, 3, narrow, part).transpose(2, 0, 1, 3).reshape(narrow, qkv_rows, 3 * part), "fsdp"
    )
    own_qkv = widened(
        jnp.concatenate(in_core_order(qkv_half, core_swap(qkv_half)), axis=1).reshape(model_width, 3 * part), 3
    )

    full_out = whole_weight(out_weight)
    full_gate_up = whole_weight(gate_up_weight)
    full_down = whole_weight(down_weight)

    text_in = text_states[0].astype(F32).reshape(text_local, caption_width)
    text_inverse = inverse_rms(text_in)
    text_low = (text_in * text_inverse * text_gain).astype(BF16)
    text_cols = caption_width // narrow
    text_slice = (
        exchange(text_low.reshape(text_local, narrow, text_cols).transpose(1, 0, 2), "fsdp")
        .reshape(narrow, image_count, caption_local, text_cols)
        .transpose(1, 0, 2, 3)
        .reshape(text_total, text_cols)
    )
    own_text_weight = (
        text_weight.reshape(text_cols, 2, narrow, part).transpose(2, 0, 1, 3).reshape(narrow, text_cols, 2 * part)
    )
    text_partial = jnp.stack([low_product(text_slice, own_text_weight[i]).astype(BF16) for i in range(narrow)])
    text_projected = widened(jnp.sum(exchange(text_partial, "fsdp").astype(F32), axis=0), 2)
    text_parts = fsdp_share(column_stats(text_projected[:, :part_pad], part, part_pad, 1), narrow, 1)
    text_means = text_parts[:, 0, :]
    text_mean = jnp.mean(text_means, axis=0)
    text_square = jnp.sum(text_parts[:, 1, :], axis=0) + part * jnp.sum((text_means - text_mean) ** 2, axis=0)
    text_key_inverse = lax.rsqrt(text_square / model_width + EPS)[:, None]
    text_unit = (text_projected[:, :part_pad] - text_mean[:, None]) * text_key_inverse
    text_gains = own_columns(norm_gains[4])
    text_packed = jnp.concatenate(
        [(text_unit * text_gains).astype(BF16), text_projected[:, part_pad:].astype(BF16)], axis=1
    )

    projected = low_product(normed_all, own_qkv)
    stats_all = fsdp_share(column_stats(projected[:, : 2 * part_pad], part, part_pad, 2), narrow, 2)
    head_gains = own_columns(norm_gains[2:4])
    packed = make_heads(
        projected, stats_all, cosine, sine, head_gains, own_columns(norm_shifts), part, score_scale * LOG2E
    )
    gate_tanh = jnp.tanh(head_gate)
    own_gates = lax.dynamic_slice_in_dim(gate_tanh, me * heads_here, heads_here, 0)
    own_gates = jnp.concatenate([own_gates, jnp.ones((pairs * halves - heads_here,), F32)])
    column = key_image[:, None]
    row = key_image[None, :]
    mixed_heads, self_out, cross_out, stats = attend(
        own_gates, packed, text_packed, column, row, head_dim, image_count
    )
    mixed_low = (
        exchange(narrowed(mixed_heads, 1).reshape(narrow, local_tok, part), "fsdp")
        .transpose(1, 0, 2)
        .reshape(local_tok, model_width)
    )

    branch = low_product(mixed_low, full_out)
    branch_inverse = inverse_rms(branch)
    branch_unit = branch * branch_inverse
    gate_attend = jnp.tanh(per_token(1))
    hidden = token_in + gate_attend * (branch_unit * norm_gains[1])
    hidden_inverse = inverse_rms(hidden)
    hidden_unit = hidden * hidden_inverse
    scale_feed = 1.0 + per_token(2)
    normed_feed_low = (hidden_unit * norm_gains[5] * scale_feed).astype(BF16)
    gate_up = low_product(normed_feed_low, full_gate_up)
    hidden_units = gate_up.shape[1] // 2
    gate_half = gate_up[:, :hidden_units]
    up_half = gate_up[:, hidden_units:]
    sigmoid = jax.nn.sigmoid(gate_half)
    activated_low = (gate_half * sigmoid * up_half).astype(BF16)
    down_out = low_product(activated_low, full_down)
    down_inverse = inverse_rms(down_out)
    down_unit = down_out * down_inverse
    gate_feed = jnp.tanh(per_token(3))
    down_normed = down_unit * norm_gains[6]
    result = (hidden + gate_feed * down_normed).astype(BF16)

    grad_result = cotangent[0].astype(F32)
    grad_down_y = grad_result * gate_feed
    grad_gain_six = jnp.sum(grad_down_y * down_unit, axis=0)
    grad_gate_feed = per_image(grad_result * down_normed * (1.0 - gate_feed * gate_feed))
    grad_down_low = norm_pull(grad_down_y * norm_gains[6], down_unit, down_inverse).astype(BF16)
    grad_down_weight = reduced(*device_columns(activated_low, deep, narrow), grad_down_low)
    grad_activated = times_transposed(grad_down_low, full_down)
    grad_gate_up_low = jnp.concatenate(
        [
            (grad_activated * up_half * sigmoid * (1.0 + gate_half * (1.0 - sigmoid))).astype(BF16),
            (grad_activated * gate_half * sigmoid).astype(BF16),
        ],
        axis=1,
    )
    grad_gate_up_weight = reduced(*device_columns(normed_feed_low, deep, narrow), grad_gate_up_low)
    grad_normed_feed = times_transposed(grad_gate_up_low, full_gate_up)
    grad_feed_y = grad_normed_feed * scale_feed
    grad_gain_five = jnp.sum(grad_feed_y * hidden_unit, axis=0)
    grad_scale_feed = per_image(grad_normed_feed * hidden_unit * norm_gains[5])
    grad_hidden = grad_result + norm_pull(grad_feed_y * norm_gains[5], hidden_unit, hidden_inverse)
    grad_branch_y = grad_hidden * gate_attend
    grad_gain_one = jnp.sum(grad_branch_y * branch_unit, axis=0)
    grad_gate_attend = per_image(
        grad_hidden * branch_unit * norm_gains[1] * (1.0 - gate_attend * gate_attend)
    )
    grad_branch_low = norm_pull(grad_branch_y * norm_gains[1], branch_unit, branch_inverse).astype(BF16)
    grad_out_weight = reduced(*device_columns(mixed_low, deep, narrow), grad_branch_low)
    grad_mixed = times_transposed(grad_branch_low, full_out).astype(BF16)
    grad_heads = widened(
        exchange(grad_mixed.reshape(local_tok, narrow, part).transpose(1, 0, 2), "fsdp").reshape(group_tok, part), 1
    )
    dq_cross, dtk, dtv, gate_sums = cross_back(
        own_gates, packed, text_packed, row, grad_heads, cross_out, stats, head_dim, image_count, score_scale
    )

    grad_text_keys = dtk.astype(F32)
    own_gain_four = jnp.sum(grad_text_keys * text_unit, axis=0)
    grad_text_unit = grad_text_keys * text_gains
    text_sums = jnp.stack([jnp.sum(grad_text_unit, axis=1), jnp.sum(grad_text_unit * text_unit, axis=1)])
    text_sums = jnp.sum(
        fsdp_share(jnp.pad(text_sums, ((0, 6), (0, 0))), narrow, 3), axis=0
    ) * (1.0 / model_width)
    grad_text_key_in = (grad_text_unit - text_sums[0][:, None] - text_unit * text_sums[1][:, None]) * text_key_inverse
    grad_text_own = jnp.concatenate(
        [narrowed(grad_text_key_in.astype(BF16), 1), narrowed(dtv, 1)], axis=1
    )
    grad_text_all = lax.all_gather(grad_text_own, "fsdp", axis=0)
    grad_text_columns = (
        grad_text_all.reshape(narrow, text_total, 2, part).transpose(1, 2, 0, 3).reshape(text_total, 2 * model_width)
    )
    text_half = text_cols // 2
    own_text, other_text = by_core(text_slice[:, :text_half], text_slice[:, text_half:])
    came_text = core_swap(outer_sum(other_text, grad_text_columns).astype(BF16))
    text_part = lax.psum_scatter(
        (outer_sum(own_text, grad_text_columns) + came_text.astype(F32)).astype(BF16),
        "z", scatter_dimension=0, tiled=True,
    )
    everyone = ("z", "core", "fsdp")
    grad_text_weight = lax.ppermute(
        text_part,
        everyone,
        [
            ((z * 2 + c) * narrow + f, f * wide + c * deep + z)
            for z in range(deep) for c in range(2) for f in range(narrow)
        ],
    ).astype(F32)
    grad_text_slice = times_transposed(grad_text_columns, text_weight).astype(BF16)
    grad_text_normed = (
        exchange(
            grad_text_slice.reshape(image_count, narrow, caption_local, text_cols)
            .transpose(1, 0, 2, 3)
            .reshape(narrow, text_local, text_cols),
            "fsdp",
        )
        .transpose(1, 0, 2)
        .reshape(text_local, caption_width)
        .astype(F32)
    )
    text_state_unit = text_in * text_inverse
    grad_text_gain = jnp.sum(grad_text_normed * text_state_unit, axis=0)
    grad_text = (
        norm_pull(grad_text_normed * text_gain, text_state_unit, text_inverse)
        .astype(BF16)
        .reshape(image_count, caption_local, caption_width)
    )

    backs = [
        self_back(pair, packed, column, row, grad_heads, self_out, stats, dq_cross, head_dim, score_scale)
        for pair in range(pairs)
    ]
    own_gate_grad = jnp.sum(gate_sums[:, 0, :].reshape(pairs * halves, head_dim), axis=1)[:heads_here]
    grad_head_gate = lax.dynamic_update_slice_in_dim(
        jnp.zeros((head_count,), F32), own_gate_grad, me * heads_here, 0
    ) * (1.0 - gate_tanh * gate_tanh)
    grad_projected_low, head_sums = heads_back(
        list(zip(*backs)), projected, stats_all, cosine, sine, head_gains, part,
        lambda value: fsdp_share(value, narrow, 4),
    )
    grad_normed = lax.psum_scatter(
        times_transposed(grad_projected_low, own_qkv).astype(BF16), "fsdp", scatter_dimension=0, tiled=True
    ).astype(F32)

    qkv_grad = outer_sum(normed_all, grad_projected_low).astype(BF16).reshape(deep, 2, model_width // wide, 3 * part_pad)
    own_grad, other_grad = by_core(qkv_grad[:, 0], qkv_grad[:, 1])
    own_grad = own_grad.astype(F32) + core_swap(other_grad).astype(F32)
    own_grad = jnp.sum(exchange(own_grad.astype(BF16), "z").astype(F32), axis=0)
    grad_qkv_weight = (
        exchange(narrowed(own_grad.astype(BF16), 3).reshape(narrow, -1, 3 * part), "fsdp")
        .reshape(narrow, -1, 3, part)
        .transpose(1, 2, 0, 3)
        .reshape(-1, 3 * model_width)
        .astype(F32)
    )

    token_unit = token_in * token_inverse
    scale_attend = 1.0 + per_token(0)
    grad_normed_y = grad_normed * scale_attend
    grad_gain_zero = jnp.sum(grad_normed_y * token_unit, axis=0)
    grad_scale_attend = per_image(grad_normed * token_unit * norm_gains[0])
    grad_tokens = (
        grad_hidden + norm_pull(grad_normed_y * norm_gains[0], token_unit, token_inverse)
    ).astype(BF16)

    def placed_columns(value):
        return lax.dynamic_update_slice_in_dim(
            jnp.zeros((model_width,), F32), narrowed(value, 1), me * part, 0
        )

    grad_modulation = jnp.concatenate(
        [grad_scale_attend, grad_gate_attend, grad_scale_feed, grad_gate_feed], axis=1
    )
    group = lax.axis_index("z") * 2 + lax.axis_index("core")
    summed = jnp.concatenate(
        [
            grad_gain_zero,
            grad_gain_one,
            placed_columns(head_sums[0]),
            placed_columns(head_sums[2]),
            placed_columns(own_gain_four),
            grad_gain_five,
            grad_gain_six,
            placed_columns(head_sums[1]),
            placed_columns(head_sums[3]),
            grad_text_gain,
            grad_head_gate,
        ]
    )
    kept = jnp.concatenate(
        [grad_modulation.reshape(-1), jnp.where(me == 0, cond_low.astype(F32), 0.0).reshape(-1)]
    )
    summed, kept = finish(summed, kept, narrow, wide, 5)
    gain_count = norm_gains.size
    shift_end = gain_count + norm_shifts.size
    text_end = shift_end + text_gain.size
    grad_gains = summed[:gain_count].reshape(norm_gains.shape)
    grad_shifts = summed[gain_count:shift_end].reshape(norm_shifts.shape)
    grad_text_gain = summed[shift_end:text_end]
    grad_head_gate = summed[text_end:]
    every_image = wide * image_count
    slots = kept[:, : grad_modulation.size].reshape(every_image, grad_modulation.shape[1])
    cond_slots = kept[:, grad_modulation.size :].reshape(every_image, cond_low.shape[1])
    grad_ada_bias = jnp.sum(slots, axis=0)
    ada_rows = cond_rows // wide
    own_cond = lax.dynamic_slice_in_dim(cond_slots, (group * narrow + me) * ada_rows, ada_rows, 1)
    grad_ada_weight = exact_outer(own_cond, slots)
    return (
        result[None],
        grad_tokens[None],
        grad_text[None],
        grad_ada_weight,
        grad_qkv_weight,
        grad_out_weight,
        grad_text_weight,
        grad_gate_up_weight,
        grad_down_weight,
        grad_ada_bias,
        grad_gains,
        grad_shifts,
        grad_text_gain,
        grad_head_gate,
    )


def solution(mesh):
    wide, narrow = mesh.devices.shape
    fine = Mesh(mesh.devices.reshape(wide // 2, 2, narrow), ("z", "core", "fsdp"))
    groups = ("z", "core")
    every = ("z", "core", "fsdp")
    placed = (
        P(groups, "fsdp", None),
        P(groups, "fsdp", None),
        P(groups, None, "fsdp", None),
        P(groups, None, None),
        P(groups, None, None),
        P("fsdp", None),
        P(),
        P("fsdp", None),
        P("fsdp", None),
        P("fsdp", None),
        P("fsdp", None),
        P("fsdp", None),
        P(),
        P(),
        P(),
        P(),
    )
    return jax.shard_map(
        shards,
        mesh=fine,
        in_specs=placed,
        out_specs=(
            P(groups, "fsdp", None),
            P(groups, "fsdp", None),
            P(groups, None, "fsdp", None),
            P(every, None),
            P(every, None),
            P(every, None),
            P(every, None),
            P(every, None),
            P(every, None),
            P(),
            P(),
            P(),
            P(),
            P(),
        ),
        check_vma=False,
    )
```

```python
import functools

import jax
import jax.numpy as jnp
from jax import lax
from jax.experimental import pallas as pl
from jax.experimental.pallas import tpu as pltpu
from jax.sharding import Mesh
from jax.sharding import PartitionSpec as P

EPS = 1e-05
HIGHEST_PRECISION = lax.Precision.HIGHEST
MASKED = -1e30
LOG2E = 1.4426950408889634
FIRST_PATCHES = 16 * 12**2
FIRST_MOST = FIRST_PATCHES + 96
QBLOCK = 256
BF16 = jnp.bfloat16
F32 = jnp.float32
VMEM_LIMIT = 60 * 1024 * 1024


def round_up(value, step):
    return -(-value // step) * step


def low_product(left, right):
    return jnp.dot(left, right, preferred_element_type=F32)


def times_transposed(left, right):
    return lax.dot_general(left, right, (((1,), (1,)), ((), ())), preferred_element_type=F32)


def outer_sum(left, right):
    return lax.dot_general(left, right, (((0,), (0,)), ((), ())), preferred_element_type=F32)


def exact_outer(left, right):
    return lax.dot_general(
        left, right, (((0,), (0,)), ((), ())), precision=HIGHEST_PRECISION, preferred_element_type=F32
    )


def exact_transposed(left, right):
    return lax.dot_general(
        left, right, (((1,), (1,)), ((), ())), precision=HIGHEST_PRECISION, preferred_element_type=F32
    )


def row_mean(value):
    return jnp.mean(value, axis=-1, keepdims=True)


def inverse_rms(value):
    return lax.rsqrt(row_mean(value * value) + EPS)


def norm_pull(grad, unit, inverse):
    return (grad - unit * row_mean(grad * unit)) * inverse


def token_layout(image_sizes, position, image_count):
    start = jnp.int32(0)
    image_index = jnp.full(position.shape, image_count, jnp.int32)
    token_row = jnp.zeros(position.shape, jnp.int32)
    token_col = jnp.zeros(position.shape, jnp.int32)
    for i in range(image_count):
        width = image_sizes[i, 1] + 1
        end = start + image_sizes[i, 0] * width
        inside = (position >= start) & (position < end)
        offset = position - start
        image_index = jnp.where(inside, i, image_index)
        token_row = jnp.where(inside, offset // width, token_row)
        token_col = jnp.where(inside, offset % width, token_col)
        start = end
    return image_index, token_row, token_col


def rope_tables(token_row, token_col, head_dim):
    quarter = head_dim // 4
    pair = (jnp.arange(128, dtype=jnp.int32) % head_dim) // 2
    frequency = 10000.0 ** (-(pair % quarter).astype(F32) / quarter)
    place = jnp.where(
        (pair < quarter)[None, :], token_row.astype(F32)[:, None], token_col.astype(F32)[:, None]
    )
    angles = place * frequency[None, :]
    even = (jnp.arange(128, dtype=jnp.int32) % 2 == 0)[None, :]
    return jnp.cos(angles), jnp.where(even, -jnp.sin(angles), jnp.sin(angles))


def swap_pairs(value):
    width = value.shape[1]
    even = lax.broadcasted_iota(jnp.int32, value.shape, 1) % 2 == 0
    return jnp.where(even, pltpu.roll(value, width - 1, 1), pltpu.roll(value, 1, 1))


def wide_table(table, width):
    return jnp.concatenate([table] * (width // table.shape[1]), axis=1)


def pack_columns(columns):
    rows = columns[0].shape[0]
    lane = lax.broadcasted_iota(jnp.int32, (rows, 128), 1)
    packed = jnp.zeros((rows, 128), F32)
    for i, column in enumerate(columns):
        packed = jnp.where(lane == i, column, packed)
    return jnp.transpose(packed)[:8, :]


def as_columns(rows_list):
    width = rows_list[0].shape[1]
    stacked = jnp.concatenate(
        rows_list + [jnp.zeros((128 - len(rows_list), width), F32)], axis=0
    )
    return jnp.transpose(stacked)


def real_lanes(shape, part):
    return lax.broadcasted_iota(jnp.int32, shape, 1) < part


def own_stats(value, part):
    mean = jnp.sum(value, axis=1, keepdims=True) * (1.0 / part)
    centred = value - mean
    if value.shape[1] != part:
        centred = jnp.where(real_lanes(value.shape, part), centred, 0.0)
    return mean, jnp.sum(centred * centred, axis=1, keepdims=True)


def joined_stats(stats_ref, part, slot):
    narrow = stats_ref.shape[0]
    means = [stats_ref[i, 2 * slot : 2 * slot + 1, :] for i in range(narrow)]
    squares = [stats_ref[i, 2 * slot + 1 : 2 * slot + 2, :] for i in range(narrow)]
    mean = functools.reduce(jnp.add, means) * (1.0 / narrow)
    square = functools.reduce(jnp.add, squares)
    square = square + part * functools.reduce(jnp.add, [(m - mean) * (m - mean) for m in means])
    return mean, lax.rsqrt(square * (1.0 / (narrow * part)) + EPS)


def stats_kernel(part, slots, projected_ref, out_ref):
    padded = projected_ref.shape[1] // slots
    columns = []
    for slot in range(slots):
        columns += own_stats(projected_ref[:, slot * padded : (slot + 1) * padded], part)
    out_ref[...] = pack_columns(columns)


def column_stats(projected, part, padded, slots):
    rows = projected.shape[0]
    return pl.pallas_call(
        functools.partial(stats_kernel, part, slots),
        grid=(pl.cdiv(rows, QBLOCK),),
        in_specs=[pl.BlockSpec((QBLOCK, slots * padded), lambda i: (i, 0))],
        out_specs=pl.BlockSpec((8, QBLOCK), lambda i: (0, i)),
        out_shape=jax.ShapeDtypeStruct((8, rows), F32),
        compiler_params=pltpu.CompilerParams(vmem_limit_bytes=VMEM_LIMIT),
        cost_estimate=pl.CostEstimate(flops=10 * rows * slots * padded, bytes_accessed=4 * rows * slots * padded, transcendentals=0),
    )(projected)


def heads_kernel(part, query_scale, projected_ref, stats_ref, cos_ref, sin_ref, gains_ref, shifts_ref, out_ref):
    padded = projected_ref.shape[1] // 3
    cosine = wide_table(cos_ref[...], padded)
    sine = wide_table(sin_ref[...], padded)
    columns = as_columns([*joined_stats(stats_ref, part, 0), *joined_stats(stats_ref, part, 1)])
    for slot in range(3):
        place = slice(slot * padded, (slot + 1) * padded)
        value = projected_ref[:, place]
        if slot < 2:
            value = (value - columns[:, 2 * slot : 2 * slot + 1]) * columns[:, 2 * slot + 1 : 2 * slot + 2]
            value = value * gains_ref[slot : slot + 1, :] + shifts_ref[slot : slot + 1, :]
            value = value * cosine + swap_pairs(value) * sine
            if slot == 0:
                value = value * query_scale
        out_ref[:, place] = value.astype(BF16)


def make_heads(projected, stats, cosine, sine, gains, shifts, part, query_scale):
    rows, triple = projected.shape
    padded = triple // 3
    narrow = stats.shape[0]
    return pl.pallas_call(
        functools.partial(heads_kernel, part, query_scale),
        grid=(pl.cdiv(rows, QBLOCK),),
        in_specs=[
            pl.BlockSpec((QBLOCK, triple), lambda i: (i, 0)),
            pl.BlockSpec((narrow, 8, QBLOCK), lambda i: (0, 0, i)),
            pl.BlockSpec((QBLOCK, 128), lambda i: (i, 0)),
            pl.BlockSpec((QBLOCK, 128), lambda i: (i, 0)),
            pl.BlockSpec((2, padded), lambda i: (0, 0)),
            pl.BlockSpec((2, padded), lambda i: (0, 0)),
        ],
        out_specs=pl.BlockSpec((QBLOCK, triple), lambda i: (i, 0)),
        out_shape=jax.ShapeDtypeStruct((rows, triple), BF16),
        compiler_params=pltpu.CompilerParams(vmem_limit_bytes=VMEM_LIMIT),
        cost_estimate=pl.CostEstimate(flops=40 * rows * triple, bytes_accessed=6 * rows * triple, transcendentals=0),
    )(projected, stats, cosine, sine, gains, shifts)


def turned_back(refs, cosine, sine):
    grad = jnp.concatenate([ref[...].astype(F32) for ref in refs], axis=1)
    return grad * cosine - swap_pairs(grad) * sine


def grad_stats_kernel(rows, part, pairs, *refs):
    dq_refs, dk_refs = refs[:pairs], refs[pairs : 2 * pairs]
    projected_ref, stats_ref, cos_ref, sin_ref, gains_ref, out_ref, sums_ref = refs[2 * pairs :]
    step = pl.program_id(0)
    padded = 128 * pairs
    cosine = wide_table(cos_ref[...], padded)
    sine = wide_table(sin_ref[...], padded)
    height = cos_ref.shape[0]
    inside = step * height + lax.broadcasted_iota(jnp.int32, (height, 1), 0) < rows

    @pl.when(step == 0)
    def _():
        sums_ref[...] = jnp.zeros_like(sums_ref)

    columns = as_columns([*joined_stats(stats_ref, part, 0), *joined_stats(stats_ref, part, 1)])
    packed = []
    for slot, grads in enumerate((dq_refs, dk_refs)):
        grad = jnp.where(inside, turned_back(grads, cosine, sine), 0.0)
        unit = (projected_ref[:, slot * padded : (slot + 1) * padded] - columns[:, 2 * slot : 2 * slot + 1])
        unit = jnp.where(inside, unit * columns[:, 2 * slot + 1 : 2 * slot + 2], 0.0)
        both = grad * unit
        sums_ref[2 * slot : 2 * slot + 1, :] += jnp.sum(both, axis=0, keepdims=True)
        sums_ref[2 * slot + 1 : 2 * slot + 2, :] += jnp.sum(grad, axis=0, keepdims=True)
        gain = gains_ref[slot : slot + 1, :]
        packed.append(jnp.sum(grad * gain, axis=1, keepdims=True))
        packed.append(jnp.sum(both * gain, axis=1, keepdims=True))
    out_ref[...] = pack_columns(packed)


def heads_back_kernel(part, pairs, *refs):
    dq_refs, dk_refs, dv_refs = refs[:pairs], refs[pairs : 2 * pairs], refs[2 * pairs : 3 * pairs]
    projected_ref, stats_ref, totals_ref, cos_ref, sin_ref, gains_ref, out_ref = refs[3 * pairs :]
    padded = 128 * pairs
    narrow = stats_ref.shape[0]
    cosine = wide_table(cos_ref[...], padded)
    sine = wide_table(sin_ref[...], padded)
    means = [
        functools.reduce(jnp.add, [totals_ref[i, j : j + 1, :] for i in range(narrow)]) * (1.0 / (narrow * part))
        for j in range(4)
    ]
    columns = as_columns([*joined_stats(stats_ref, part, 0), *joined_stats(stats_ref, part, 1), *means])
    for slot, grads in enumerate((dq_refs, dk_refs)):
        grad = turned_back(grads, cosine, sine) * gains_ref[slot : slot + 1, :]
        inverse = columns[:, 2 * slot + 1 : 2 * slot + 2]
        unit = (projected_ref[:, slot * padded : (slot + 1) * padded] - columns[:, 2 * slot : 2 * slot + 1]) * inverse
        grad = grad - columns[:, 4 + 2 * slot : 5 + 2 * slot] - unit * columns[:, 5 + 2 * slot : 6 + 2 * slot]
        grad = grad * inverse
        if padded != part:
            grad = jnp.where(real_lanes(grad.shape, part), grad, 0.0)
        out_ref[:, slot * padded : (slot + 1) * padded] = grad.astype(BF16)
    for pair, ref in enumerate(dv_refs):
        out_ref[:, 2 * padded + 128 * pair : 2 * padded + 128 * (pair + 1)] = ref[...]


def heads_back(grads, projected, stats, cosine, sine, gains, part, share):
    rows, triple = projected.shape
    padded = triple // 3
    pairs = padded // 128
    narrow = stats.shape[0]
    pair_spec = pl.BlockSpec((QBLOCK, 128), lambda i: (i, 0))
    two_spec = pl.BlockSpec((QBLOCK, 2 * padded), lambda i: (i, 0))
    stat_spec = pl.BlockSpec((narrow, 8, QBLOCK), lambda i: (0, 0, i))
    gain_spec = pl.BlockSpec((2, padded), lambda i: (0, 0))
    own, sums = pl.pallas_call(
        functools.partial(grad_stats_kernel, rows, part, pairs),
        grid=(pl.cdiv(rows, QBLOCK),),
        in_specs=[pair_spec] * (2 * pairs) + [two_spec, stat_spec, pair_spec, pair_spec, gain_spec],
        out_specs=[
            pl.BlockSpec((8, QBLOCK), lambda i: (0, i)),
            pl.BlockSpec((8, padded), lambda i: (0, 0)),
        ],
        out_shape=[jax.ShapeDtypeStruct((8, rows), F32), jax.ShapeDtypeStruct((8, padded), F32)],
        compiler_params=pltpu.CompilerParams(vmem_limit_bytes=VMEM_LIMIT),
        cost_estimate=pl.CostEstimate(flops=40 * rows * triple, bytes_accessed=5 * rows * triple, transcendentals=0),
    )(*grads[0], *grads[1], projected, stats, cosine, sine, gains)
    totals = share(own)
    out = pl.pallas_call(
        functools.partial(heads_back_kernel, part, pairs),
        grid=(pl.cdiv(rows, QBLOCK),),
        in_specs=[pair_spec] * (3 * pairs) + [two_spec, stat_spec, stat_spec, pair_spec, pair_spec, gain_spec],
        out_specs=pl.BlockSpec((QBLOCK, triple), lambda i: (i, 0)),
        out_shape=jax.ShapeDtypeStruct((rows, triple), BF16),
        compiler_params=pltpu.CompilerParams(vmem_limit_bytes=VMEM_LIMIT),
        cost_estimate=pl.CostEstimate(flops=40 * rows * triple, bytes_accessed=7 * rows * triple, transcendentals=0),
    )(*grads[0], *grads[1], *grads[2], projected, stats, totals, cosine, sine, gains)
    return out, sums


def head_lanes(rows, half, head_dim):
    lane = lax.broadcasted_iota(jnp.int32, (rows, 128), 1)
    return (lane >= half * head_dim) & (lane < (half + 1) * head_dim)


def softmax_product(pieces):
    maximum = functools.reduce(jnp.maximum, [jnp.max(s, axis=1, keepdims=True) for s, _ in pieces])
    total, result = 0.0, 0.0
    for scores, values in pieces:
        weight = jnp.exp2(scores - maximum)
        total = total + jnp.sum(weight, axis=1, keepdims=True)
        result = result + low_product(weight.astype(BF16), values)
    return result * (1.0 / total), maximum + jnp.log2(total)


def attend_kernel(
    head_dim, first, most, caption, image_count,
    gate_ref, q_ref, k_ref, v_ref, tk_ref, tv_ref, column_ref, row_ref,
    mixed_ref, self_ref, cross_ref, stats_ref,
):
    count = q_ref.shape[0]
    halves = 128 // head_dim

    def emit(at, rows, outs):
        lanes = [head_lanes(rows, half, head_dim) for half in range(halves)]
        own, cross, gated = 0.0, 0.0, 0.0
        columns = []
        for half, (own_out, own_total, cross_out, cross_total) in enumerate(outs):
            gate = gate_ref[0, half]
            own = own + jnp.where(lanes[half], own_out, 0.0)
            cross = cross + jnp.where(lanes[half], cross_out, 0.0)
            gated = gated + jnp.where(lanes[half], gate * cross_out, 0.0)
            columns += [own_total, cross_total]
        self_ref[pl.ds(at, rows), :] = own
        cross_ref[pl.ds(at, rows), :] = cross
        mixed_ref[pl.ds(at, rows), :] = (own + gated).astype(BF16)
        lane = lax.broadcasted_iota(jnp.int32, (rows, 128), 1)
        packed = jnp.zeros((rows, 128), F32)
        for i, column in enumerate(columns):
            packed = jnp.where(lane == i, column, packed)
        stats_ref[:, pl.ds(at, rows)] = jnp.transpose(packed)[:8, :]

    def clean(block, carry):
        at = pl.multiple_of(block * QBLOCK, QBLOCK)
        queries = q_ref[pl.ds(at, QBLOCK), :]
        outs = []
        for half in range(halves):
            q = jnp.where(head_lanes(QBLOCK, half, head_dim), queries, jnp.zeros_like(queries))
            bias = jnp.where(row_ref[0:1, first:most] == 0, 0.0, MASKED)
            own_out, own_total = softmax_product([
                (times_transposed(q, k_ref[0:first, :]), v_ref[0:first, :]),
                (times_transposed(q, k_ref[first:most, :]) + bias, v_ref[first:most, :]),
            ])
            cross_out, cross_total = softmax_product(
                [(times_transposed(q, tk_ref[0:caption, :]), tv_ref[0:caption, :])]
            )
            outs.append((own_out, own_total, cross_out, cross_total))
        emit(at, QBLOCK, outs)
        return carry

    lax.fori_loop(0, first // QBLOCK, clean, 0)
    rest = count - first
    queries = q_ref[first:count, :]
    image = column_ref[first:count, :]
    outs = []
    for half in range(halves):
        q = jnp.where(head_lanes(rest, half, head_dim), queries, jnp.zeros_like(queries))
        own_out, own_total = softmax_product([
            (jnp.where(image == row_ref[0:1, :], times_transposed(q, k_ref[...]), MASKED), v_ref[...])
        ])
        scores = times_transposed(q, tk_ref[...])
        owner = lax.broadcasted_iota(jnp.int32, (1, scores.shape[1]), 1) // caption
        scores = jnp.where((image == owner) | (image == image_count), scores, MASKED)
        cross_out, cross_total = softmax_product([(scores, tv_ref[...])])
        outs.append((own_out, own_total, cross_out, cross_total))
    emit(first, rest, outs)


def attend(pair, gates, packed, text_packed, column, row, head_dim, image_count):
    count, texts = packed.shape[0], text_packed.shape[0]
    pairs = packed.shape[1] // 384
    halves = 128 // head_dim
    out = pl.BlockSpec((count, 128), lambda i: (0, 0))
    most = min(round_up(FIRST_MOST, 128), count)
    flops = 4 * count * (count + texts) * 128
    return pl.pallas_call(
        functools.partial(
            attend_kernel, head_dim, FIRST_PATCHES, most, texts // image_count, image_count
        ),
        grid=(1,),
        in_specs=[
            pl.BlockSpec((None, 1, halves), lambda i: (pair, 0, 0), memory_space=pltpu.SMEM),
            pl.BlockSpec((count, 128), lambda i: (0, pair)),
            pl.BlockSpec((count, 128), lambda i: (0, pairs + pair)),
            pl.BlockSpec((count, 128), lambda i: (0, 2 * pairs + pair)),
            pl.BlockSpec((texts, 128), lambda i: (0, pair)),
            pl.BlockSpec((texts, 128), lambda i: (0, pairs + pair)),
            pl.BlockSpec((count, 1), lambda i: (0, 0)),
            pl.BlockSpec((1, count), lambda i: (0, 0)),
        ],
        out_specs=[out, out, out, pl.BlockSpec((8, count), lambda i: (0, 0))],
        out_shape=[
            jax.ShapeDtypeStruct((count, 128), BF16),
            jax.ShapeDtypeStruct((count, 128), F32),
            jax.ShapeDtypeStruct((count, 128), F32),
            jax.ShapeDtypeStruct((8, count), F32),
        ],
        compiler_params=pltpu.CompilerParams(vmem_limit_bytes=VMEM_LIMIT),
        cost_estimate=pl.CostEstimate(flops=flops, bytes_accessed=20 * count * 128, transcendentals=2 * count * count),
    )(gates.reshape(pairs, 1, halves), packed, packed, packed, text_packed, text_packed, column, row)


def gate_lanes(gate_ref, head_dim):
    lane = lax.broadcasted_iota(jnp.int32, (1, 128), 1)
    gates = jnp.zeros((1, 128), F32)
    for half in range(128 // head_dim):
        gates = jnp.where(lane // head_dim == half, gate_ref[0, half], gates)
    return gates


def head_picks(head_dim):
    return (
        lax.broadcasted_iota(jnp.int32, (8, 128), 1) // head_dim
        == lax.broadcasted_iota(jnp.int32, (8, 128), 0)
    ).astype(F32)


def rows_back(head_dim, queries, outs, delta, stats, offset, keys, values, key_sum, value_sum, spans):
    rows = queries.shape[0]
    halves = 128 // head_dim
    zero = jnp.zeros((rows, 128), BF16)
    lanes = [head_lanes(rows, half, head_dim) for half in range(halves)]
    q_heads = [jnp.where(lane, queries, zero) for lane in lanes]
    out_heads = [jnp.where(lane, outs, zero) for lane in lanes]
    q_stack = jnp.concatenate(q_heads, axis=0)
    out_stack = jnp.concatenate(out_heads, axis=0)
    dq = [0.0] * halves
    for low, high, mask in spans:
        key_part = keys[low:high, :]
        value_part = values[low:high, :]
        probs, grads = [], []
        for half in range(halves):
            scores = mask(times_transposed(key_part, q_heads[half]))
            prob = jnp.exp2(scores - stats[2 * half + offset : 2 * half + offset + 1, :])
            dprob = times_transposed(value_part, out_heads[half])
            dscore = (prob * (dprob - delta[half : half + 1, :])).astype(BF16)
            probs.append(prob.astype(BF16))
            grads.append(dscore)
            dq[half] = dq[half] + outer_sum(dscore, key_part)
        value_sum[low:high, :] += low_product(jnp.concatenate(probs, axis=1), out_stack)
        key_sum[low:high, :] += low_product(jnp.concatenate(grads, axis=1), q_stack)
    total = 0.0
    for half in range(halves):
        total = total + jnp.where(lanes[half], dq[half], 0.0)
    return total


def cross_back_kernel(
    head_dim, first, caption, image_count, scale,
    gate_ref, q_ref, tk_ref, tv_ref, row_ref, grad_ref, cross_ref, stats_ref,
    dq_ref, dtk_ref, dtv_ref, gate_grad_ref, dtk_sum, dtv_sum,
):
    count = q_ref.shape[0]
    for total in (dtk_sum, dtv_sum, gate_grad_ref):
        total[...] = jnp.zeros_like(total)
    gates = gate_lanes(gate_ref, head_dim)
    picks = head_picks(head_dim)

    def part(at, rows, spans):
        wide = grad_ref[pl.ds(at, rows), :].astype(F32)
        cross = cross_ref[pl.ds(at, rows), :]
        gate_grad_ref[0:1, :] += jnp.sum(wide * cross, axis=0, keepdims=True)
        gated = (wide * gates).astype(BF16)
        delta = exact_transposed(picks, gated.astype(F32) * cross)
        dq = rows_back(
            head_dim, q_ref[pl.ds(at, rows), :], gated, delta, stats_ref[:, pl.ds(at, rows)], 1,
            tk_ref, tv_ref, dtk_sum, dtv_sum, spans,
        )
        dq_ref[pl.ds(at, rows), :] = (dq * scale).astype(BF16)

    def clean(block, carry):
        part(pl.multiple_of(block * QBLOCK, QBLOCK), QBLOCK, [(0, caption, lambda scores: scores)])
        return carry

    lax.fori_loop(0, first // QBLOCK, clean, 0)
    image = row_ref[0:1, first:count]
    owner = lax.broadcasted_iota(jnp.int32, (tk_ref.shape[0], 1), 0) // caption
    allowed = (owner == image) | (image == image_count)
    part(first, count - first, [(0, tk_ref.shape[0], lambda scores: jnp.where(allowed, scores, MASKED))])
    dtk_ref[...] = (dtk_sum[...] * (1.0 / LOG2E)).astype(BF16)
    dtv_ref[...] = dtv_sum[...].astype(BF16)


def cross_back(pair, gates, packed, text_packed, row, grad, cross, stats, head_dim, image_count, scale):
    count, texts = packed.shape[0], text_packed.shape[0]
    pairs = packed.shape[1] // 384
    halves = 128 // head_dim
    tokens = pl.BlockSpec((count, 128), lambda i: (0, pair))
    own_tokens = pl.BlockSpec((count, 128), lambda i: (0, 0))
    captions = pl.BlockSpec((texts, 128), lambda i: (0, 0))
    flops = 10 * count * texts * 128
    return pl.pallas_call(
        functools.partial(cross_back_kernel, head_dim, FIRST_PATCHES, texts // image_count, image_count, scale),
        grid=(1,),
        in_specs=[
            pl.BlockSpec((None, 1, halves), lambda i: (pair, 0, 0), memory_space=pltpu.SMEM),
            tokens,
            pl.BlockSpec((texts, 128), lambda i: (0, pair)),
            pl.BlockSpec((texts, 128), lambda i: (0, pairs + pair)),
            pl.BlockSpec((1, count), lambda i: (0, 0)),
            own_tokens,
            own_tokens,
            pl.BlockSpec((8, count), lambda i: (0, 0)),
        ],
        out_specs=[own_tokens, captions, captions, pl.BlockSpec((8, 128), lambda i: (0, 0))],
        out_shape=[
            jax.ShapeDtypeStruct((count, 128), BF16),
            jax.ShapeDtypeStruct((texts, 128), BF16),
            jax.ShapeDtypeStruct((texts, 128), BF16),
            jax.ShapeDtypeStruct((8, 128), F32),
        ],
        scratch_shapes=[pltpu.VMEM((texts, 128), F32), pltpu.VMEM((texts, 128), F32)],
        compiler_params=pltpu.CompilerParams(vmem_limit_bytes=VMEM_LIMIT),
        cost_estimate=pl.CostEstimate(flops=flops, bytes_accessed=12 * count * 128, transcendentals=count * texts),
    )(gates.reshape(pairs, 1, halves), packed, text_packed, text_packed, row, grad, cross, stats)


def self_back_kernel(
    head_dim, first, most, scale,
    q_ref, k_ref, v_ref, column_ref, row_ref, grad_ref, self_ref, stats_ref, more_ref,
    dq_ref, dk_ref, dv_ref, dk_sum, dv_sum,
):
    count = q_ref.shape[0]
    dk_sum[...] = jnp.zeros_like(dk_sum)
    dv_sum[...] = jnp.zeros_like(dv_sum)
    picks = head_picks(head_dim)

    def part(at, rows, spans):
        grad = grad_ref[pl.ds(at, rows), :]
        delta = exact_transposed(picks, grad.astype(F32) * self_ref[pl.ds(at, rows), :])
        dq = rows_back(
            head_dim, q_ref[pl.ds(at, rows), :], grad, delta, stats_ref[:, pl.ds(at, rows)], 0,
            k_ref, v_ref, dk_sum, dv_sum, spans,
        )
        dq_ref[pl.ds(at, rows), :] = (dq * scale + more_ref[pl.ds(at, rows), :].astype(F32)).astype(BF16)

    def clean(block, carry):
        bias = jnp.where(column_ref[first:most, :] == 0, 0.0, MASKED)
        part(
            pl.multiple_of(block * QBLOCK, QBLOCK), QBLOCK,
            [(0, first, lambda scores: scores), (first, most, lambda scores: scores + bias)],
        )
        return carry

    lax.fori_loop(0, first // QBLOCK, clean, 0)
    image = row_ref[0:1, first:count]
    part(first, count - first, [(0, count, lambda scores: jnp.where(column_ref[...] == image, scores, MASKED))])
    dk_ref[...] = (dk_sum[...] * (1.0 / LOG2E)).astype(BF16)
    dv_ref[...] = dv_sum[...].astype(BF16)


def self_back(pair, packed, column, row, grad, own, stats, more, head_dim, scale):
    count = packed.shape[0]
    pairs = packed.shape[1] // 384
    tokens = pl.BlockSpec((count, 128), lambda i: (0, pair))
    out = pl.BlockSpec((count, 128), lambda i: (0, 0))
    most = min(round_up(FIRST_MOST, 128), count)
    flops = 10 * count * count * 128
    return pl.pallas_call(
        functools.partial(self_back_kernel, head_dim, FIRST_PATCHES, most, scale),
        grid=(1,),
        in_specs=[
            tokens,
            pl.BlockSpec((count, 128), lambda i: (0, pairs + pair)),
            pl.BlockSpec((count, 128), lambda i: (0, 2 * pairs + pair)),
            pl.BlockSpec((count, 1), lambda i: (0, 0)),
            pl.BlockSpec((1, count), lambda i: (0, 0)),
            out,
            out,
            pl.BlockSpec((8, count), lambda i: (0, 0)),
            out,
        ],
        out_specs=[out, out, out],
        out_shape=[jax.ShapeDtypeStruct((count, 128), BF16)] * 3,
        scratch_shapes=[pltpu.VMEM((count, 128), F32), pltpu.VMEM((count, 128), F32)],
        compiler_params=pltpu.CompilerParams(vmem_limit_bytes=VMEM_LIMIT),
        cost_estimate=pl.CostEstimate(flops=flops, bytes_accessed=30 * count * 128, transcendentals=2 * count * count),
    )(packed, packed, packed, column, row, grad, own, stats, more)


def fsdp_share_kernel(narrow, x_ref, out_ref, send_sem, recv_sem):
    me = lax.axis_index("fsdp")
    barrier = pltpu.get_barrier_semaphore()
    for step in range(1, narrow):
        pl.semaphore_signal(
            barrier, inc=1, device_id={"fsdp": lax.rem(me + step, narrow)}, device_id_type=pl.DeviceIdType.MESH
        )
    pl.semaphore_wait(barrier, narrow - 1)
    copies = []
    for step in range(1, narrow):
        copy = pltpu.make_async_remote_copy(
            src_ref=x_ref,
            dst_ref=out_ref.at[me],
            send_sem=send_sem.at[step],
            recv_sem=recv_sem.at[step],
            device_id={"fsdp": lax.rem(me + step, narrow)},
            device_id_type=pl.DeviceIdType.MESH,
        )
        copy.start()
        copies.append(copy)
    out_ref[me] = x_ref[...]
    for copy in copies:
        copy.wait()


def fsdp_share(value, narrow, collective_id):
    return pl.pallas_call(
        functools.partial(fsdp_share_kernel, narrow),
        in_specs=[pl.BlockSpec(memory_space=pltpu.VMEM)],
        out_specs=pl.BlockSpec(memory_space=pltpu.VMEM),
        out_shape=jax.ShapeDtypeStruct((narrow,) + value.shape, value.dtype),
        scratch_shapes=[pltpu.SemaphoreType.DMA((narrow,)), pltpu.SemaphoreType.DMA((narrow,))],
        compiler_params=pltpu.CompilerParams(collective_id=collective_id, has_side_effects=True),
        cost_estimate=pl.CostEstimate(flops=0, bytes_accessed=8 * narrow * value.size, transcendentals=0),
    )(value)


def finish_kernel(narrow, wide, sum_rows, x_ref, out_ref, first_ref, second_ref, sends, recvs):
    me = lax.axis_index("fsdp")
    group = lax.axis_index("z") * 2 + lax.axis_index("core")
    rows = x_ref.shape[1]
    rest = rows - sum_rows
    barrier = pltpu.get_barrier_semaphore()
    places = [{"fsdp": lax.rem(me + step, narrow)} for step in range(1, narrow)]
    peers = [lax.rem(group + step, wide) for step in range(1, wide)]
    partners = [{"z": peer // 2, "core": peer % 2} for peer in peers]
    for place in places + partners:
        pl.semaphore_signal(barrier, inc=1, device_id=place, device_id_type=pl.DeviceIdType.MESH)
    pl.semaphore_wait(barrier, narrow + wide - 2)

    def send_all(targets, source, target, base):
        copies = []
        for i, place in enumerate(targets):
            copy = pltpu.make_async_remote_copy(
                src_ref=source(i),
                dst_ref=target,
                send_sem=sends.at[base + i],
                recv_sem=recvs.at[base + i],
                device_id=place,
                device_id_type=pl.DeviceIdType.MESH,
            )
            copy.start()
            copies.append(copy)
        return copies

    copies = send_all(places, lambda i: x_ref.at[lax.rem(me + i + 1, narrow)], first_ref.at[me], 0)
    first_ref[me] = x_ref[me]
    for copy in copies:
        copy.wait()
    total = first_ref[0]
    for i in range(1, narrow):
        total = total + first_ref[i]
    second_ref[group] = total
    copies = send_all(partners, lambda i: second_ref.at[group], second_ref.at[group], narrow)
    for copy in copies:
        copy.wait()
    total = second_ref[0, :sum_rows, :]
    for i in range(1, wide):
        total = total + second_ref[i, :sum_rows, :]
    out_ref[me, :sum_rows, :] = total
    for i in range(wide):
        out_ref[me, sum_rows + i * rest : sum_rows + (i + 1) * rest, :] = second_ref[i, sum_rows:, :]
    copies = send_all(places, lambda i: out_ref.at[me], out_ref.at[me], narrow + wide)
    for copy in copies:
        copy.wait()


def finish(summed, kept, narrow, wide, collective_id):
    sum_rows = round_up(-(-summed.size // (128 * narrow)), 8)
    kept_rows = round_up(-(-kept.size // (128 * narrow)), 8)

    def chunked(value, rows):
        return jnp.pad(value, (0, narrow * rows * 128 - value.size)).reshape(narrow, rows, 128)

    joined = jnp.concatenate([chunked(summed, sum_rows), chunked(kept, kept_rows)], axis=1)
    rows = sum_rows + kept_rows
    count = 2 * narrow + wide
    out = pl.pallas_call(
        functools.partial(finish_kernel, narrow, wide, sum_rows),
        in_specs=[pl.BlockSpec(memory_space=pltpu.VMEM)],
        out_specs=pl.BlockSpec(memory_space=pltpu.VMEM),
        out_shape=jax.ShapeDtypeStruct((narrow, sum_rows + wide * kept_rows, 128), F32),
        scratch_shapes=[
            pltpu.VMEM((narrow, rows, 128), F32),
            pltpu.VMEM((wide, rows, 128), F32),
            pltpu.SemaphoreType.DMA((count,)),
            pltpu.SemaphoreType.DMA((count,)),
        ],
        compiler_params=pltpu.CompilerParams(collective_id=collective_id, has_side_effects=True),
    )(joined)
    total = out[:, :sum_rows, :].reshape(-1)[: summed.size]
    groups = out[:, sum_rows:, :].reshape(narrow, wide, kept_rows * 128).transpose(1, 0, 2)
    return total, groups.reshape(wide, -1)[:, : kept.size]


def exchange(blocks, axis):
    return lax.all_to_all(blocks, axis, 0, 0, tiled=True)


def core_swap(value):
    return lax.ppermute(value, "core", [(0, 1), (1, 0)])


def by_core(low, high):
    first = lax.axis_index("core") == 0
    return jnp.where(first, low, high), jnp.where(first, high, low)


def in_core_order(own, other):
    first = lax.axis_index("core") == 0
    return jnp.where(first, own, other), jnp.where(first, other, own)


def chip_sum(own_left, other_left, right):
    came = core_swap(outer_sum(other_left, right).astype(BF16))
    return (outer_sum(own_left, right) + came.astype(F32)).astype(BF16)


def fsdp_sum(both):
    return lax.psum_scatter(both, "fsdp", scatter_dimension=0, tiled=True)


def z_sum(part, deep):
    return jnp.sum(exchange(part.reshape(deep, -1, part.shape[1]), "z").astype(F32), axis=0)


def device_columns(value, deep, narrow):
    rows, width = value.shape
    block = width // (2 * deep * narrow)
    core = lax.axis_index("core")
    if block % 128 == 0:
        low, high = (
            jnp.concatenate(
                [
                    value[:, ((z * 2 + c) * narrow + f) * block : ((z * 2 + c) * narrow + f + 1) * block]
                    for f in range(narrow)
                    for z in range(deep)
                ],
                axis=1,
            )
            for c in range(2)
        )
        return by_core(low, high)
    target = jnp.arange(width, dtype=jnp.int32)
    c, f, z, r = (
        target // (narrow * deep * block), target // (deep * block) % narrow, target // block % deep, target % block,
    )
    c = (c + core) % 2
    source = ((z * 2 + c) * narrow + f) * block + r
    pick = (jnp.arange(width, dtype=jnp.int32)[:, None] == source[None, :]).astype(BF16)
    moved = low_product(value, pick).astype(BF16)
    return moved[:, : width // 2], moved[:, width // 2 :]


def whole_weight(shard):
    rows = shard.shape[0] // 2
    half = lax.dynamic_slice_in_dim(shard, lax.axis_index("core") * rows, rows, 0)
    return lax.all_gather(half, ("fsdp", "core"), axis=0, tiled=True)


def shards(
    tokens,
    cotangent,
    text_states,
    conditioning,
    image_sizes,
    ada_weight,
    ada_bias,
    qkv_weight,
    out_weight,
    text_weight,
    gate_up_weight,
    down_weight,
    norm_gains,
    norm_shifts,
    text_gain,
    head_gate,
):
    model_width = tokens.shape[2]
    head_count = head_gate.shape[0]
    head_dim = model_width // head_count
    image_count = text_states.shape[1]
    caption_local = text_states.shape[2]
    caption_width = text_states.shape[3]
    local_tok = tokens.shape[1]
    deep = lax.axis_size("z")
    narrow = lax.axis_size("fsdp")
    wide = 2 * deep
    me = lax.axis_index("fsdp")
    group_tok = local_tok * narrow
    caption_full = caption_local * narrow
    score_scale = head_dim ** (-0.5)
    text_total = image_count * caption_full
    text_local = image_count * caption_local
    part = model_width // narrow
    part_pad = round_up(part, 128)
    heads_here = head_count // narrow
    pairs = part_pad // 128
    halves = 128 // head_dim

    group_sizes = image_sizes[0]
    position = me * local_tok + jnp.arange(local_tok, dtype=jnp.int32)
    image_index = token_layout(group_sizes, position, image_count)[0]
    key_image, key_row, key_col = token_layout(
        group_sizes, jnp.arange(group_tok, dtype=jnp.int32), image_count
    )
    member = [(image_index == i).astype(F32)[:, None] for i in range(image_count)]
    cosine, sine = rope_tables(key_row, key_col, head_dim)

    cond_low = jax.nn.silu(conditioning[0].astype(F32)).astype(BF16)
    cond_rows = ada_weight.shape[0]
    cond_part = lax.dynamic_slice_in_dim(cond_low, me * cond_rows, cond_rows, 1)
    modulation_part = low_product(cond_part, ada_weight)
    modulation = (
        jnp.sum(fsdp_share(modulation_part.reshape(-1, 128), narrow, 0), axis=0).reshape(modulation_part.shape)
        + ada_bias
    )

    def per_token(index):
        rows = modulation[:, index * model_width : (index + 1) * model_width]
        return functools.reduce(
            jnp.add, [member[i] * rows[i : i + 1, :] for i in range(image_count)]
        )

    def per_image(value):
        return jnp.stack([jnp.sum(member[i] * value, axis=0) for i in range(image_count)])

    token_in = tokens[0].astype(F32)
    token_inverse = inverse_rms(token_in)
    tokens_all = lax.all_gather(tokens[0], "fsdp", axis=0, tiled=True)
    def widened(value, slots):
        if part == part_pad:
            return value
        lead = value.shape[:-1]
        value = value.reshape(*lead, slots, part)
        pads = [(0, 0)] * (len(lead) + 1) + [(0, part_pad - part)]
        return jnp.pad(value, pads).reshape(*lead, slots * part_pad)

    def narrowed(value, slots):
        if part == part_pad:
            return value
        lead = value.shape[:-1]
        return value.reshape(*lead, slots, part_pad)[..., :part].reshape(*lead, slots * part)

    def own_columns(value):
        return widened(lax.dynamic_slice_in_dim(value, me * part, part, value.ndim - 1), 1)

    qkv_rows = qkv_weight.shape[0] // 2
    qkv_half = lax.dynamic_slice_in_dim(qkv_weight, lax.axis_index("core") * qkv_rows, qkv_rows, 0)
    qkv_half = exchange(
        qkv_half.reshape(qkv_rows, 3, narrow, part).transpose(2, 0, 1, 3).reshape(narrow, qkv_rows, 3 * part), "fsdp"
    )
    own_qkv = widened(
        jnp.concatenate(in_core_order(qkv_half, core_swap(qkv_half)), axis=1).reshape(model_width, 3 * part), 3
    )

    full_out = whole_weight(out_weight)
    full_gate_up = whole_weight(gate_up_weight)
    full_down = whole_weight(down_weight)

    text_in = text_states[0].astype(F32).reshape(text_local, caption_width)
    text_inverse = inverse_rms(text_in)
    text_low = (text_in * text_inverse * text_gain).astype(BF16)
    text_cols = caption_width // narrow
    text_slice = (
        exchange(text_low.reshape(text_local, narrow, text_cols).transpose(1, 0, 2), "fsdp")
        .reshape(narrow, image_count, caption_local, text_cols)
        .transpose(1, 0, 2, 3)
        .reshape(text_total, text_cols)
    )
    own_text_weight = (
        text_weight.reshape(text_cols, 2, narrow, part).transpose(2, 0, 1, 3).reshape(narrow, text_cols, 2 * part)
    )
    text_partial = jnp.stack([low_product(text_slice, own_text_weight[i]).astype(BF16) for i in range(narrow)])
    text_partial, tokens_all = lax.optimization_barrier((text_partial, tokens_all))
    text_projected = widened(jnp.sum(exchange(text_partial, "fsdp").astype(F32), axis=0), 2)
    text_parts = fsdp_share(column_stats(text_projected[:, :part_pad], part, part_pad, 1), narrow, 1)
    text_means = text_parts[:, 0, :]
    text_mean = jnp.mean(text_means, axis=0)
    text_square = jnp.sum(text_parts[:, 1, :], axis=0) + part * jnp.sum((text_means - text_mean) ** 2, axis=0)
    text_key_inverse = lax.rsqrt(text_square / model_width + EPS)[:, None]
    text_unit = (text_projected[:, :part_pad] - text_mean[:, None]) * text_key_inverse
    text_gains = own_columns(norm_gains[4])
    text_packed = jnp.concatenate(
        [(text_unit * text_gains).astype(BF16), text_projected[:, part_pad:].astype(BF16)], axis=1
    )

    wide_tokens = tokens_all.astype(F32)
    wide_scale = functools.reduce(
        jnp.add,
        [(key_image == i).astype(F32)[:, None] * modulation[i : i + 1, :model_width] for i in range(image_count)],
    )
    normed_all = (wide_tokens * inverse_rms(wide_tokens) * norm_gains[0] * (1.0 + wide_scale)).astype(BF16)

    projected = low_product(normed_all, own_qkv)
    stats_all = fsdp_share(column_stats(projected[:, : 2 * part_pad], part, part_pad, 2), narrow, 2)
    head_gains = own_columns(norm_gains[2:4])
    packed = make_heads(
        projected, stats_all, cosine, sine, head_gains, own_columns(norm_shifts), part, score_scale * LOG2E
    )
    gate_tanh = jnp.tanh(head_gate)
    own_gates = lax.dynamic_slice_in_dim(gate_tanh, me * heads_here, heads_here, 0)
    own_gates = jnp.concatenate([own_gates, jnp.ones((pairs * halves - heads_here,), F32)])
    column = key_image[:, None]
    row = key_image[None, :]
    attended = [
        attend(pair, own_gates, packed, text_packed, column, row, head_dim, image_count) for pair in range(pairs)
    ]
    mixed_pairs = [exchange(one[0].reshape(narrow, local_tok, 128), "fsdp") for one in attended]
    self_outs = [one[1] for one in attended]
    cross_outs = [one[2] for one in attended]
    stats = [one[3] for one in attended]
    mixed_low = (
        narrowed(jnp.concatenate(mixed_pairs, axis=2), 1).transpose(1, 0, 2).reshape(local_tok, model_width)
    )

    branch = low_product(mixed_low, full_out)
    branch_inverse = inverse_rms(branch)
    branch_unit = branch * branch_inverse
    gate_attend = jnp.tanh(per_token(1))
    hidden = token_in + gate_attend * (branch_unit * norm_gains[1])
    hidden_inverse = inverse_rms(hidden)
    hidden_unit = hidden * hidden_inverse
    scale_feed = 1.0 + per_token(2)
    normed_feed_low = (hidden_unit * norm_gains[5] * scale_feed).astype(BF16)
    gate_up = low_product(normed_feed_low, full_gate_up)
    hidden_units = gate_up.shape[1] // 2
    gate_half = gate_up[:, :hidden_units]
    up_half = gate_up[:, hidden_units:]
    sigmoid = jax.nn.sigmoid(gate_half)
    activated_low = (gate_half * sigmoid * up_half).astype(BF16)
    down_out = low_product(activated_low, full_down)
    down_inverse = inverse_rms(down_out)
    down_unit = down_out * down_inverse
    gate_feed = jnp.tanh(per_token(3))
    down_normed = down_unit * norm_gains[6]
    result = (hidden + gate_feed * down_normed).astype(BF16)

    grad_result = cotangent[0].astype(F32)
    grad_down_y = grad_result * gate_feed
    grad_gain_six = jnp.sum(grad_down_y * down_unit, axis=0)
    grad_gate_feed = per_image(grad_result * down_normed * (1.0 - gate_feed * gate_feed))
    grad_down_low = norm_pull(grad_down_y * norm_gains[6], down_unit, down_inverse).astype(BF16)
    down_both = chip_sum(*device_columns(activated_low, deep, narrow), grad_down_low)
    grad_activated = times_transposed(grad_down_low, full_down)
    grad_gate_up_low = jnp.concatenate(
        [
            (grad_activated * up_half * sigmoid * (1.0 + gate_half * (1.0 - sigmoid))).astype(BF16),
            (grad_activated * gate_half * sigmoid).astype(BF16),
        ],
        axis=1,
    )
    gate_up_both = chip_sum(*device_columns(normed_feed_low, deep, narrow), grad_gate_up_low)
    grad_gate_up_low, down_both, gate_up_both = lax.optimization_barrier((grad_gate_up_low, down_both, gate_up_both))
    down_part = fsdp_sum(down_both)
    gate_up_part = fsdp_sum(gate_up_both)
    grad_normed_feed = times_transposed(grad_gate_up_low, full_gate_up)
    grad_feed_y = grad_normed_feed * scale_feed
    grad_gain_five = jnp.sum(grad_feed_y * hidden_unit, axis=0)
    grad_scale_feed = per_image(grad_normed_feed * hidden_unit * norm_gains[5])
    grad_hidden = grad_result + norm_pull(grad_feed_y * norm_gains[5], hidden_unit, hidden_inverse)
    grad_branch_y = grad_hidden * gate_attend
    grad_gain_one = jnp.sum(grad_branch_y * branch_unit, axis=0)
    grad_gate_attend = per_image(
        grad_hidden * branch_unit * norm_gains[1] * (1.0 - gate_attend * gate_attend)
    )
    grad_branch_low = norm_pull(grad_branch_y * norm_gains[1], branch_unit, branch_inverse).astype(BF16)
    out_both = chip_sum(*device_columns(mixed_low, deep, narrow), grad_branch_low)
    out_part = fsdp_sum(out_both)
    grad_mixed = times_transposed(grad_branch_low, full_out).astype(BF16)
    grad_blocks = widened(grad_mixed.reshape(local_tok, narrow, part).transpose(1, 0, 2), 1)
    grad_heads = [
        exchange(grad_blocks[:, :, 128 * pair : 128 * (pair + 1)], "fsdp").reshape(group_tok, 128)
        for pair in range(pairs)
    ]
    grad_heads[0], down_part = lax.optimization_barrier((grad_heads[0], down_part))
    crossed = [
        cross_back(
            pair, own_gates, packed, text_packed, row, grad_heads[pair], cross_outs[pair], stats[pair],
            head_dim, image_count, score_scale,
        )
        for pair in range(pairs)
    ]
    grad_down_weight = z_sum(down_part, deep)
    dtk = jnp.concatenate([one[1] for one in crossed], axis=1)
    dtv = jnp.concatenate([one[2] for one in crossed], axis=1)
    gate_sums = jnp.stack([one[3] for one in crossed])

    grad_text_keys = dtk.astype(F32)
    own_gain_four = jnp.sum(grad_text_keys * text_unit, axis=0)
    grad_text_unit = grad_text_keys * text_gains
    text_sums = jnp.stack([jnp.sum(grad_text_unit, axis=1), jnp.sum(grad_text_unit * text_unit, axis=1)])
    text_sums = jnp.sum(
        fsdp_share(jnp.pad(text_sums, ((0, 6), (0, 0))), narrow, 3), axis=0
    ) * (1.0 / model_width)
    grad_text_key_in = (grad_text_unit - text_sums[0][:, None] - text_unit * text_sums[1][:, None]) * text_key_inverse
    grad_text_own = jnp.concatenate(
        [narrowed(grad_text_key_in.astype(BF16), 1), narrowed(dtv, 1)], axis=1
    )
    backs = []
    for pair in range(pairs):
        backs.append(
            self_back(
                pair, packed, column, row, grad_heads[pair], self_outs[pair], stats[pair], crossed[pair][0],
                head_dim, score_scale,
            )
        )
        if pair == 0:
            grad_heads[1], gate_up_part, grad_down_weight, first, grad_text_own = lax.optimization_barrier(
                (grad_heads[1], gate_up_part, grad_down_weight, backs[0][0], grad_text_own)
            )
            backs[0] = (first, *backs[0][1:])
            grad_gate_up_weight = z_sum(gate_up_part, deep)
        if pair == 1 and pairs > 2:
            grad_heads[2], out_part, second = lax.optimization_barrier((grad_heads[2], out_part, backs[1][0]))
            backs[1] = (second, *backs[1][1:])
    grad_out_weight = z_sum(out_part, deep)

    grad_text_all = lax.all_gather(grad_text_own, "fsdp", axis=0)
    grad_text_columns = (
        grad_text_all.reshape(narrow, text_total, 2, part).transpose(1, 2, 0, 3).reshape(text_total, 2 * model_width)
    )
    text_half = text_cols // 2
    own_text, other_text = by_core(text_slice[:, :text_half], text_slice[:, text_half:])
    came_text = core_swap(outer_sum(other_text, grad_text_columns).astype(BF16))
    text_both = (outer_sum(own_text, grad_text_columns) + came_text.astype(F32)).astype(BF16)
    text_part = jnp.sum(
        exchange(text_both.reshape(deep, -1, 2 * model_width), "z").astype(F32), axis=0
    ).astype(BF16)
    everyone = ("z", "core", "fsdp")
    grad_text_weight = lax.ppermute(
        text_part,
        everyone,
        [
            ((z * 2 + c) * narrow + f, f * wide + c * deep + z)
            for z in range(deep) for c in range(2) for f in range(narrow)
        ],
    ).astype(F32)
    grad_text_slice = times_transposed(grad_text_columns, text_weight).astype(BF16)
    grad_text_normed = (
        exchange(
            grad_text_slice.reshape(image_count, narrow, caption_local, text_cols)
            .transpose(1, 0, 2, 3)
            .reshape(narrow, text_local, text_cols),
            "fsdp",
        )
        .transpose(1, 0, 2)
        .reshape(text_local, caption_width)
        .astype(F32)
    )
    text_state_unit = text_in * text_inverse
    grad_text_gain = jnp.sum(grad_text_normed * text_state_unit, axis=0)
    grad_text = (
        norm_pull(grad_text_normed * text_gain, text_state_unit, text_inverse)
        .astype(BF16)
        .reshape(image_count, caption_local, caption_width)
    )

    own_gate_grad = jnp.sum(gate_sums[:, 0, :].reshape(pairs * halves, head_dim), axis=1)[:heads_here]
    grad_head_gate = lax.dynamic_update_slice_in_dim(
        jnp.zeros((head_count,), F32), own_gate_grad, me * heads_here, 0
    ) * (1.0 - gate_tanh * gate_tanh)
    grad_projected_low, head_sums = heads_back(
        list(zip(*backs)), projected, stats_all, cosine, sine, head_gains, part,
        lambda value: fsdp_share(value, narrow, 4),
    )
    grad_normed = lax.psum_scatter(
        times_transposed(grad_projected_low, own_qkv).astype(BF16), "fsdp", scatter_dimension=0, tiled=True
    ).astype(F32)

    qkv_grad = outer_sum(normed_all, grad_projected_low).astype(BF16).reshape(deep, 2, model_width // wide, 3 * part_pad)
    own_grad, other_grad = by_core(qkv_grad[:, 0], qkv_grad[:, 1])
    own_grad = own_grad.astype(F32) + core_swap(other_grad).astype(F32)
    own_grad = jnp.sum(exchange(own_grad.astype(BF16), "z").astype(F32), axis=0)
    grad_qkv_weight = (
        exchange(narrowed(own_grad.astype(BF16), 3).reshape(narrow, -1, 3 * part), "fsdp")
        .reshape(narrow, -1, 3, part)
        .transpose(1, 2, 0, 3)
        .reshape(-1, 3 * model_width)
        .astype(F32)
    )

    token_unit = token_in * token_inverse
    scale_attend = 1.0 + per_token(0)
    grad_normed_y = grad_normed * scale_attend
    grad_gain_zero = jnp.sum(grad_normed_y * token_unit, axis=0)
    grad_scale_attend = per_image(grad_normed * token_unit * norm_gains[0])
    grad_tokens = (
        grad_hidden + norm_pull(grad_normed_y * norm_gains[0], token_unit, token_inverse)
    ).astype(BF16)

    def placed_columns(value):
        return lax.dynamic_update_slice_in_dim(
            jnp.zeros((model_width,), F32), narrowed(value, 1), me * part, 0
        )

    grad_modulation = jnp.concatenate(
        [grad_scale_attend, grad_gate_attend, grad_scale_feed, grad_gate_feed], axis=1
    )
    group = lax.axis_index("z") * 2 + lax.axis_index("core")
    summed = jnp.concatenate(
        [
            grad_gain_zero,
            grad_gain_one,
            placed_columns(head_sums[0]),
            placed_columns(head_sums[2]),
            placed_columns(own_gain_four),
            grad_gain_five,
            grad_gain_six,
            placed_columns(head_sums[1]),
            placed_columns(head_sums[3]),
            grad_text_gain,
            grad_head_gate,
        ]
    )
    kept = jnp.concatenate(
        [grad_modulation.reshape(-1), jnp.where(me == 0, cond_low.astype(F32), 0.0).reshape(-1)]
    )
    summed, kept = finish(summed, kept, narrow, wide, 5)
    gain_count = norm_gains.size
    shift_end = gain_count + norm_shifts.size
    text_end = shift_end + text_gain.size
    grad_gains = summed[:gain_count].reshape(norm_gains.shape)
    grad_shifts = summed[gain_count:shift_end].reshape(norm_shifts.shape)
    grad_text_gain = summed[shift_end:text_end]
    grad_head_gate = summed[text_end:]
    every_image = wide * image_count
    slots = kept[:, : grad_modulation.size].reshape(every_image, grad_modulation.shape[1])
    cond_slots = kept[:, grad_modulation.size :].reshape(every_image, cond_low.shape[1])
    grad_ada_bias = jnp.sum(slots, axis=0)
    ada_rows = cond_rows // wide
    own_cond = lax.dynamic_slice_in_dim(cond_slots, (group * narrow + me) * ada_rows, ada_rows, 1)
    grad_ada_weight = exact_outer(own_cond, slots)
    return (
        result[None],
        grad_tokens[None],
        grad_text[None],
        grad_ada_weight,
        grad_qkv_weight,
        grad_out_weight,
        grad_text_weight,
        grad_gate_up_weight,
        grad_down_weight,
        grad_ada_bias,
        grad_gains,
        grad_shifts,
        grad_text_gain,
        grad_head_gate,
    )


def solution(mesh):
    wide, narrow = mesh.devices.shape
    fine = Mesh(mesh.devices.reshape(wide // 2, 2, narrow), ("z", "core", "fsdp"))
    groups = ("z", "core")
    every = ("z", "core", "fsdp")
    placed = (
        P(groups, "fsdp", None),
        P(groups, "fsdp", None),
        P(groups, None, "fsdp", None),
        P(groups, None, None),
        P(groups, None, None),
        P("fsdp", None),
        P(),
        P("fsdp", None),
        P("fsdp", None),
        P("fsdp", None),
        P("fsdp", None),
        P("fsdp", None),
        P(),
        P(),
        P(),
        P(),
    )
    return jax.shard_map(
        shards,
        mesh=fine,
        in_specs=placed,
        out_specs=(
            P(groups, "fsdp", None),
            P(groups, "fsdp", None),
            P(groups, None, "fsdp", None),
            P(every, None),
            P(every, None),
            P(every, None),
            P(every, None),
            P(every, None),
            P(every, None),
            P(),
            P(),
            P(),
            P(),
            P(),
        ),
        check_vma=False,
    )
```

```python
import functools

import jax
import jax.numpy as jnp
from jax import lax
from jax.experimental import pallas as pl
from jax.experimental.pallas import tpu as pltpu
from jax.sharding import Mesh
from jax.sharding import PartitionSpec as P

EPS = 1e-05
HIGHEST_PRECISION = lax.Precision.HIGHEST
MASKED = -1e30
LOG2E = 1.4426950408889634
FIRST_PATCHES = 16 * 12**2
FIRST_MOST = FIRST_PATCHES + 96
QBLOCK = 256
BF16 = jnp.bfloat16
F32 = jnp.float32
VMEM_LIMIT = 60 * 1024 * 1024


def round_up(value, step):
    return -(-value // step) * step


def low_product(left, right):
    return jnp.dot(left, right, preferred_element_type=F32)


def times_transposed(left, right):
    return lax.dot_general(left, right, (((1,), (1,)), ((), ())), preferred_element_type=F32)


def outer_sum(left, right):
    return lax.dot_general(left, right, (((0,), (0,)), ((), ())), preferred_element_type=F32)


def exact_outer(left, right):
    return lax.dot_general(
        left, right, (((0,), (0,)), ((), ())), precision=HIGHEST_PRECISION, preferred_element_type=F32
    )


def exact_transposed(left, right):
    return lax.dot_general(
        left, right, (((1,), (1,)), ((), ())), precision=HIGHEST_PRECISION, preferred_element_type=F32
    )


def row_mean(value):
    return jnp.mean(value, axis=-1, keepdims=True)


def inverse_rms(value):
    return lax.rsqrt(row_mean(value * value) + EPS)


def norm_pull(grad, unit, inverse):
    return (grad - unit * row_mean(grad * unit)) * inverse


def token_layout(image_sizes, position, image_count):
    start = jnp.int32(0)
    image_index = jnp.full(position.shape, image_count, jnp.int32)
    token_row = jnp.zeros(position.shape, jnp.int32)
    token_col = jnp.zeros(position.shape, jnp.int32)
    for i in range(image_count):
        width = image_sizes[i, 1] + 1
        end = start + image_sizes[i, 0] * width
        inside = (position >= start) & (position < end)
        offset = position - start
        image_index = jnp.where(inside, i, image_index)
        token_row = jnp.where(inside, offset // width, token_row)
        token_col = jnp.where(inside, offset % width, token_col)
        start = end
    return image_index, token_row, token_col


def rope_tables(token_row, token_col, head_dim):
    quarter = head_dim // 4
    pair = (jnp.arange(128, dtype=jnp.int32) % head_dim) // 2
    frequency = 10000.0 ** (-(pair % quarter).astype(F32) / quarter)
    place = jnp.where(
        (pair < quarter)[None, :], token_row.astype(F32)[:, None], token_col.astype(F32)[:, None]
    )
    angles = place * frequency[None, :]
    even = (jnp.arange(128, dtype=jnp.int32) % 2 == 0)[None, :]
    return jnp.cos(angles), jnp.where(even, -jnp.sin(angles), jnp.sin(angles))


def swap_pairs(value):
    width = value.shape[1]
    even = lax.broadcasted_iota(jnp.int32, value.shape, 1) % 2 == 0
    return jnp.where(even, pltpu.roll(value, width - 1, 1), pltpu.roll(value, 1, 1))


def wide_table(table, width):
    return jnp.concatenate([table] * (width // table.shape[1]), axis=1)


def pack_columns(columns):
    rows = columns[0].shape[0]
    lane = lax.broadcasted_iota(jnp.int32, (rows, 128), 1)
    packed = jnp.zeros((rows, 128), F32)
    for i, column in enumerate(columns):
        packed = jnp.where(lane == i, column, packed)
    return jnp.transpose(packed)[:8, :]


def as_columns(rows_list):
    width = rows_list[0].shape[1]
    stacked = jnp.concatenate(
        rows_list + [jnp.zeros((128 - len(rows_list), width), F32)], axis=0
    )
    return jnp.transpose(stacked)


def real_lanes(shape, part):
    return lax.broadcasted_iota(jnp.int32, shape, 1) < part


def own_stats(value, part):
    mean = jnp.sum(value, axis=1, keepdims=True) * (1.0 / part)
    centred = value - mean
    if value.shape[1] != part:
        centred = jnp.where(real_lanes(value.shape, part), centred, 0.0)
    return mean, jnp.sum(centred * centred, axis=1, keepdims=True)


def joined_stats(stats_ref, part, slot):
    narrow = stats_ref.shape[0]
    means = [stats_ref[i, 2 * slot : 2 * slot + 1, :] for i in range(narrow)]
    squares = [stats_ref[i, 2 * slot + 1 : 2 * slot + 2, :] for i in range(narrow)]
    mean = functools.reduce(jnp.add, means) * (1.0 / narrow)
    square = functools.reduce(jnp.add, squares)
    square = square + part * functools.reduce(jnp.add, [(m - mean) * (m - mean) for m in means])
    return mean, lax.rsqrt(square * (1.0 / (narrow * part)) + EPS)


def stats_kernel(part, slots, projected_ref, out_ref):
    padded = projected_ref.shape[1] // slots
    columns = []
    for slot in range(slots):
        columns += own_stats(projected_ref[:, slot * padded : (slot + 1) * padded], part)
    out_ref[...] = pack_columns(columns)


def column_stats(projected, part, padded, slots):
    rows = projected.shape[0]
    return pl.pallas_call(
        functools.partial(stats_kernel, part, slots),
        grid=(pl.cdiv(rows, QBLOCK),),
        in_specs=[pl.BlockSpec((QBLOCK, slots * padded), lambda i: (i, 0))],
        out_specs=pl.BlockSpec((8, QBLOCK), lambda i: (0, i)),
        out_shape=jax.ShapeDtypeStruct((8, rows), F32),
        compiler_params=pltpu.CompilerParams(vmem_limit_bytes=VMEM_LIMIT),
        cost_estimate=pl.CostEstimate(flops=10 * rows * slots * padded, bytes_accessed=4 * rows * slots * padded, transcendentals=0),
    )(projected)


def heads_kernel(part, query_scale, projected_ref, stats_ref, cos_ref, sin_ref, gains_ref, shifts_ref, out_ref):
    padded = projected_ref.shape[1] // 3
    cosine = wide_table(cos_ref[...], padded)
    sine = wide_table(sin_ref[...], padded)
    columns = as_columns([*joined_stats(stats_ref, part, 0), *joined_stats(stats_ref, part, 1)])
    for slot in range(3):
        place = slice(slot * padded, (slot + 1) * padded)
        value = projected_ref[:, place]
        if slot < 2:
            value = (value - columns[:, 2 * slot : 2 * slot + 1]) * columns[:, 2 * slot + 1 : 2 * slot + 2]
            value = value * gains_ref[slot : slot + 1, :] + shifts_ref[slot : slot + 1, :]
            value = value * cosine + swap_pairs(value) * sine
            if slot == 0:
                value = value * query_scale
        out_ref[:, place] = value.astype(BF16)


def make_heads(projected, stats, cosine, sine, gains, shifts, part, query_scale):
    rows, triple = projected.shape
    padded = triple // 3
    narrow = stats.shape[0]
    return pl.pallas_call(
        functools.partial(heads_kernel, part, query_scale),
        grid=(pl.cdiv(rows, QBLOCK),),
        in_specs=[
            pl.BlockSpec((QBLOCK, triple), lambda i: (i, 0)),
            pl.BlockSpec((narrow, 8, QBLOCK), lambda i: (0, 0, i)),
            pl.BlockSpec((QBLOCK, 128), lambda i: (i, 0)),
            pl.BlockSpec((QBLOCK, 128), lambda i: (i, 0)),
            pl.BlockSpec((2, padded), lambda i: (0, 0)),
            pl.BlockSpec((2, padded), lambda i: (0, 0)),
        ],
        out_specs=pl.BlockSpec((QBLOCK, triple), lambda i: (i, 0)),
        out_shape=jax.ShapeDtypeStruct((rows, triple), BF16),
        compiler_params=pltpu.CompilerParams(vmem_limit_bytes=VMEM_LIMIT),
        cost_estimate=pl.CostEstimate(flops=40 * rows * triple, bytes_accessed=6 * rows * triple, transcendentals=0),
    )(projected, stats, cosine, sine, gains, shifts)


def turned_back(refs, cosine, sine):
    grad = jnp.concatenate([ref[...].astype(F32) for ref in refs], axis=1)
    return grad * cosine - swap_pairs(grad) * sine


def grad_stats_kernel(rows, part, pairs, *refs):
    dq_refs, dk_refs = refs[:pairs], refs[pairs : 2 * pairs]
    projected_ref, stats_ref, cos_ref, sin_ref, gains_ref, out_ref, sums_ref = refs[2 * pairs :]
    step = pl.program_id(0)
    padded = 128 * pairs
    cosine = wide_table(cos_ref[...], padded)
    sine = wide_table(sin_ref[...], padded)
    height = cos_ref.shape[0]
    inside = step * height + lax.broadcasted_iota(jnp.int32, (height, 1), 0) < rows

    @pl.when(step == 0)
    def _():
        sums_ref[...] = jnp.zeros_like(sums_ref)

    columns = as_columns([*joined_stats(stats_ref, part, 0), *joined_stats(stats_ref, part, 1)])
    packed = []
    for slot, grads in enumerate((dq_refs, dk_refs)):
        grad = jnp.where(inside, turned_back(grads, cosine, sine), 0.0)
        unit = (projected_ref[:, slot * padded : (slot + 1) * padded] - columns[:, 2 * slot : 2 * slot + 1])
        unit = jnp.where(inside, unit * columns[:, 2 * slot + 1 : 2 * slot + 2], 0.0)
        both = grad * unit
        sums_ref[2 * slot : 2 * slot + 1, :] += jnp.sum(both, axis=0, keepdims=True)
        sums_ref[2 * slot + 1 : 2 * slot + 2, :] += jnp.sum(grad, axis=0, keepdims=True)
        gain = gains_ref[slot : slot + 1, :]
        packed.append(jnp.sum(grad * gain, axis=1, keepdims=True))
        packed.append(jnp.sum(both * gain, axis=1, keepdims=True))
    out_ref[...] = pack_columns(packed)


def heads_back_kernel(part, pairs, *refs):
    dq_refs, dk_refs, dv_refs = refs[:pairs], refs[pairs : 2 * pairs], refs[2 * pairs : 3 * pairs]
    projected_ref, stats_ref, totals_ref, cos_ref, sin_ref, gains_ref, out_ref = refs[3 * pairs :]
    padded = 128 * pairs
    narrow = stats_ref.shape[0]
    cosine = wide_table(cos_ref[...], padded)
    sine = wide_table(sin_ref[...], padded)
    means = [
        functools.reduce(jnp.add, [totals_ref[i, j : j + 1, :] for i in range(narrow)]) * (1.0 / (narrow * part))
        for j in range(4)
    ]
    columns = as_columns([*joined_stats(stats_ref, part, 0), *joined_stats(stats_ref, part, 1), *means])
    for slot, grads in enumerate((dq_refs, dk_refs)):
        grad = turned_back(grads, cosine, sine) * gains_ref[slot : slot + 1, :]
        inverse = columns[:, 2 * slot + 1 : 2 * slot + 2]
        unit = (projected_ref[:, slot * padded : (slot + 1) * padded] - columns[:, 2 * slot : 2 * slot + 1]) * inverse
        grad = grad - columns[:, 4 + 2 * slot : 5 + 2 * slot] - unit * columns[:, 5 + 2 * slot : 6 + 2 * slot]
        grad = grad * inverse
        if padded != part:
            grad = jnp.where(real_lanes(grad.shape, part), grad, 0.0)
        out_ref[:, slot * padded : (slot + 1) * padded] = grad.astype(BF16)
    for pair, ref in enumerate(dv_refs):
        out_ref[:, 2 * padded + 128 * pair : 2 * padded + 128 * (pair + 1)] = ref[...]


def heads_back(grads, projected, stats, cosine, sine, gains, part, share):
    rows, triple = projected.shape
    padded = triple // 3
    pairs = padded // 128
    narrow = stats.shape[0]
    pair_spec = pl.BlockSpec((QBLOCK, 128), lambda i: (i, 0))
    two_spec = pl.BlockSpec((QBLOCK, 2 * padded), lambda i: (i, 0))
    stat_spec = pl.BlockSpec((narrow, 8, QBLOCK), lambda i: (0, 0, i))
    gain_spec = pl.BlockSpec((2, padded), lambda i: (0, 0))
    own, sums = pl.pallas_call(
        functools.partial(grad_stats_kernel, rows, part, pairs),
        grid=(pl.cdiv(rows, QBLOCK),),
        in_specs=[pair_spec] * (2 * pairs) + [two_spec, stat_spec, pair_spec, pair_spec, gain_spec],
        out_specs=[
            pl.BlockSpec((8, QBLOCK), lambda i: (0, i)),
            pl.BlockSpec((8, padded), lambda i: (0, 0)),
        ],
        out_shape=[jax.ShapeDtypeStruct((8, rows), F32), jax.ShapeDtypeStruct((8, padded), F32)],
        compiler_params=pltpu.CompilerParams(vmem_limit_bytes=VMEM_LIMIT),
        cost_estimate=pl.CostEstimate(flops=40 * rows * triple, bytes_accessed=5 * rows * triple, transcendentals=0),
    )(*grads[0], *grads[1], projected, stats, cosine, sine, gains)
    totals = share(own)
    out = pl.pallas_call(
        functools.partial(heads_back_kernel, part, pairs),
        grid=(pl.cdiv(rows, QBLOCK),),
        in_specs=[pair_spec] * (3 * pairs) + [two_spec, stat_spec, stat_spec, pair_spec, pair_spec, gain_spec],
        out_specs=pl.BlockSpec((QBLOCK, triple), lambda i: (i, 0)),
        out_shape=jax.ShapeDtypeStruct((rows, triple), BF16),
        compiler_params=pltpu.CompilerParams(vmem_limit_bytes=VMEM_LIMIT),
        cost_estimate=pl.CostEstimate(flops=40 * rows * triple, bytes_accessed=7 * rows * triple, transcendentals=0),
    )(*grads[0], *grads[1], *grads[2], projected, stats, totals, cosine, sine, gains)
    return out, sums


def head_lanes(rows, half, head_dim):
    lane = lax.broadcasted_iota(jnp.int32, (rows, 128), 1)
    return (lane >= half * head_dim) & (lane < (half + 1) * head_dim)


def softmax_product(pieces):
    maximum = functools.reduce(jnp.maximum, [jnp.max(s, axis=1, keepdims=True) for s, _ in pieces])
    total, result = 0.0, 0.0
    for scores, values in pieces:
        weight = jnp.exp2(scores - maximum)
        total = total + jnp.sum(weight, axis=1, keepdims=True)
        result = result + low_product(weight.astype(BF16), values)
    return result * (1.0 / total), maximum + jnp.log2(total)


def attend_kernel(
    head_dim, first, most, caption, image_count,
    gate_ref, q_ref, k_ref, v_ref, tk_ref, tv_ref, column_ref, row_ref,
    mixed_ref, self_ref, cross_ref, stats_ref,
):
    count = q_ref.shape[0]
    halves = 128 // head_dim

    def emit(at, rows, outs):
        lanes = [head_lanes(rows, half, head_dim) for half in range(halves)]
        own, cross, gated = 0.0, 0.0, 0.0
        columns = []
        for half, (own_out, own_total, cross_out, cross_total) in enumerate(outs):
            gate = gate_ref[0, half]
            own = own + jnp.where(lanes[half], own_out, 0.0)
            cross = cross + jnp.where(lanes[half], cross_out, 0.0)
            gated = gated + jnp.where(lanes[half], gate * cross_out, 0.0)
            columns += [own_total, cross_total]
        self_ref[pl.ds(at, rows), :] = own
        cross_ref[pl.ds(at, rows), :] = cross
        mixed_ref[pl.ds(at, rows), :] = (own + gated).astype(BF16)
        lane = lax.broadcasted_iota(jnp.int32, (rows, 128), 1)
        packed = jnp.zeros((rows, 128), F32)
        for i, column in enumerate(columns):
            packed = jnp.where(lane == i, column, packed)
        stats_ref[:, pl.ds(at, rows)] = jnp.transpose(packed)[:8, :]

    def clean(block, carry):
        at = pl.multiple_of(block * QBLOCK, QBLOCK)
        queries = q_ref[pl.ds(at, QBLOCK), :]
        outs = []
        for half in range(halves):
            q = jnp.where(head_lanes(QBLOCK, half, head_dim), queries, jnp.zeros_like(queries))
            bias = jnp.where(row_ref[0:1, first:most] == 0, 0.0, MASKED)
            own_out, own_total = softmax_product([
                (times_transposed(q, k_ref[0:first, :]), v_ref[0:first, :]),
                (times_transposed(q, k_ref[first:most, :]) + bias, v_ref[first:most, :]),
            ])
            cross_out, cross_total = softmax_product(
                [(times_transposed(q, tk_ref[0:caption, :]), tv_ref[0:caption, :])]
            )
            outs.append((own_out, own_total, cross_out, cross_total))
        emit(at, QBLOCK, outs)
        return carry

    lax.fori_loop(0, first // QBLOCK, clean, 0)
    rest = count - first
    queries = q_ref[first:count, :]
    image = column_ref[first:count, :]
    outs = []
    for half in range(halves):
        q = jnp.where(head_lanes(rest, half, head_dim), queries, jnp.zeros_like(queries))
        own_out, own_total = softmax_product([
            (jnp.where(image == row_ref[0:1, :], times_transposed(q, k_ref[...]), MASKED), v_ref[...])
        ])
        scores = times_transposed(q, tk_ref[...])
        owner = lax.broadcasted_iota(jnp.int32, (1, scores.shape[1]), 1) // caption
        scores = jnp.where((image == owner) | (image == image_count), scores, MASKED)
        cross_out, cross_total = softmax_product([(scores, tv_ref[...])])
        outs.append((own_out, own_total, cross_out, cross_total))
    emit(first, rest, outs)


def attend(pair, gates, packed, text_packed, column, row, head_dim, image_count):
    count, texts = packed.shape[0], text_packed.shape[0]
    pairs = packed.shape[1] // 384
    halves = 128 // head_dim
    out = pl.BlockSpec((count, 128), lambda i: (0, 0))
    most = min(round_up(FIRST_MOST, 128), count)
    flops = 4 * count * (count + texts) * 128
    return pl.pallas_call(
        functools.partial(
            attend_kernel, head_dim, FIRST_PATCHES, most, texts // image_count, image_count
        ),
        grid=(1,),
        in_specs=[
            pl.BlockSpec((None, 1, halves), lambda i: (pair, 0, 0), memory_space=pltpu.SMEM),
            pl.BlockSpec((count, 128), lambda i: (0, pair)),
            pl.BlockSpec((count, 128), lambda i: (0, pairs + pair)),
            pl.BlockSpec((count, 128), lambda i: (0, 2 * pairs + pair)),
            pl.BlockSpec((texts, 128), lambda i: (0, pair)),
            pl.BlockSpec((texts, 128), lambda i: (0, pairs + pair)),
            pl.BlockSpec((count, 1), lambda i: (0, 0)),
            pl.BlockSpec((1, count), lambda i: (0, 0)),
        ],
        out_specs=[out, out, out, pl.BlockSpec((8, count), lambda i: (0, 0))],
        out_shape=[
            jax.ShapeDtypeStruct((count, 128), BF16),
            jax.ShapeDtypeStruct((count, 128), F32),
            jax.ShapeDtypeStruct((count, 128), F32),
            jax.ShapeDtypeStruct((8, count), F32),
        ],
        compiler_params=pltpu.CompilerParams(vmem_limit_bytes=VMEM_LIMIT),
        cost_estimate=pl.CostEstimate(flops=flops, bytes_accessed=20 * count * 128, transcendentals=2 * count * count),
    )(gates.reshape(pairs, 1, halves), packed, packed, packed, text_packed, text_packed, column, row)


def gate_lanes(gate_ref, head_dim):
    lane = lax.broadcasted_iota(jnp.int32, (1, 128), 1)
    gates = jnp.zeros((1, 128), F32)
    for half in range(128 // head_dim):
        gates = jnp.where(lane // head_dim == half, gate_ref[0, half], gates)
    return gates


def head_picks(head_dim):
    return (
        lax.broadcasted_iota(jnp.int32, (8, 128), 1) // head_dim
        == lax.broadcasted_iota(jnp.int32, (8, 128), 0)
    ).astype(F32)


def rows_back(head_dim, queries, outs, delta, stats, offset, keys, values, key_sum, value_sum, spans):
    rows = queries.shape[0]
    halves = 128 // head_dim
    zero = jnp.zeros((rows, 128), BF16)
    lanes = [head_lanes(rows, half, head_dim) for half in range(halves)]
    q_heads = [jnp.where(lane, queries, zero) for lane in lanes]
    out_heads = [jnp.where(lane, outs, zero) for lane in lanes]
    q_stack = jnp.concatenate(q_heads, axis=0)
    out_stack = jnp.concatenate(out_heads, axis=0)
    dq = [0.0] * halves
    for low, high, mask in spans:
        key_part = keys[low:high, :]
        value_part = values[low:high, :]
        probs, grads = [], []
        for half in range(halves):
            scores = mask(times_transposed(key_part, q_heads[half]))
            prob = jnp.exp2(scores - stats[2 * half + offset : 2 * half + offset + 1, :])
            dprob = times_transposed(value_part, out_heads[half])
            dscore = (prob * (dprob - delta[half : half + 1, :])).astype(BF16)
            probs.append(prob.astype(BF16))
            grads.append(dscore)
            dq[half] = dq[half] + outer_sum(dscore, key_part)
        value_sum[low:high, :] += low_product(jnp.concatenate(probs, axis=1), out_stack)
        key_sum[low:high, :] += low_product(jnp.concatenate(grads, axis=1), q_stack)
    total = 0.0
    for half in range(halves):
        total = total + jnp.where(lanes[half], dq[half], 0.0)
    return total


def cross_back_kernel(
    head_dim, first, caption, image_count, scale,
    gate_ref, q_ref, tk_ref, tv_ref, row_ref, grad_ref, cross_ref, stats_ref,
    dq_ref, dtk_ref, dtv_ref, gate_grad_ref, dtk_sum, dtv_sum,
):
    count = q_ref.shape[0]
    for total in (dtk_sum, dtv_sum, gate_grad_ref):
        total[...] = jnp.zeros_like(total)
    gates = gate_lanes(gate_ref, head_dim)
    picks = head_picks(head_dim)

    def part(at, rows, spans):
        wide = grad_ref[pl.ds(at, rows), :].astype(F32)
        cross = cross_ref[pl.ds(at, rows), :]
        gate_grad_ref[0:1, :] += jnp.sum(wide * cross, axis=0, keepdims=True)
        gated = (wide * gates).astype(BF16)
        delta = exact_transposed(picks, gated.astype(F32) * cross)
        dq = rows_back(
            head_dim, q_ref[pl.ds(at, rows), :], gated, delta, stats_ref[:, pl.ds(at, rows)], 1,
            tk_ref, tv_ref, dtk_sum, dtv_sum, spans,
        )
        dq_ref[pl.ds(at, rows), :] = (dq * scale).astype(BF16)

    def clean(block, carry):
        part(pl.multiple_of(block * QBLOCK, QBLOCK), QBLOCK, [(0, caption, lambda scores: scores)])
        return carry

    lax.fori_loop(0, first // QBLOCK, clean, 0)
    image = row_ref[0:1, first:count]
    owner = lax.broadcasted_iota(jnp.int32, (tk_ref.shape[0], 1), 0) // caption
    allowed = (owner == image) | (image == image_count)
    part(first, count - first, [(0, tk_ref.shape[0], lambda scores: jnp.where(allowed, scores, MASKED))])
    dtk_ref[...] = (dtk_sum[...] * (1.0 / LOG2E)).astype(BF16)
    dtv_ref[...] = dtv_sum[...].astype(BF16)


def cross_back(pair, gates, packed, text_packed, row, grad, cross, stats, head_dim, image_count, scale):
    count, texts = packed.shape[0], text_packed.shape[0]
    pairs = packed.shape[1] // 384
    halves = 128 // head_dim
    tokens = pl.BlockSpec((count, 128), lambda i: (0, pair))
    own_tokens = pl.BlockSpec((count, 128), lambda i: (0, 0))
    captions = pl.BlockSpec((texts, 128), lambda i: (0, 0))
    flops = 10 * count * texts * 128
    return pl.pallas_call(
        functools.partial(cross_back_kernel, head_dim, FIRST_PATCHES, texts // image_count, image_count, scale),
        grid=(1,),
        in_specs=[
            pl.BlockSpec((None, 1, halves), lambda i: (pair, 0, 0), memory_space=pltpu.SMEM),
            tokens,
            pl.BlockSpec((texts, 128), lambda i: (0, pair)),
            pl.BlockSpec((texts, 128), lambda i: (0, pairs + pair)),
            pl.BlockSpec((1, count), lambda i: (0, 0)),
            tokens,
            own_tokens,
            pl.BlockSpec((8, count), lambda i: (0, 0)),
        ],
        out_specs=[own_tokens, captions, captions, pl.BlockSpec((8, 128), lambda i: (0, 0))],
        out_shape=[
            jax.ShapeDtypeStruct((count, 128), BF16),
            jax.ShapeDtypeStruct((texts, 128), BF16),
            jax.ShapeDtypeStruct((texts, 128), BF16),
            jax.ShapeDtypeStruct((8, 128), F32),
        ],
        scratch_shapes=[pltpu.VMEM((texts, 128), F32), pltpu.VMEM((texts, 128), F32)],
        compiler_params=pltpu.CompilerParams(vmem_limit_bytes=VMEM_LIMIT),
        cost_estimate=pl.CostEstimate(flops=flops, bytes_accessed=12 * count * 128, transcendentals=count * texts),
    )(gates.reshape(pairs, 1, halves), packed, text_packed, text_packed, row, grad, cross, stats)


def self_back_kernel(
    head_dim, first, most, scale,
    q_ref, k_ref, v_ref, column_ref, row_ref, grad_ref, self_ref, stats_ref, more_ref,
    dq_ref, dk_ref, dv_ref, dk_sum, dv_sum,
):
    count = q_ref.shape[0]
    dk_sum[...] = jnp.zeros_like(dk_sum)
    dv_sum[...] = jnp.zeros_like(dv_sum)
    picks = head_picks(head_dim)

    def part(at, rows, spans):
        grad = grad_ref[pl.ds(at, rows), :]
        delta = exact_transposed(picks, grad.astype(F32) * self_ref[pl.ds(at, rows), :])
        dq = rows_back(
            head_dim, q_ref[pl.ds(at, rows), :], grad, delta, stats_ref[:, pl.ds(at, rows)], 0,
            k_ref, v_ref, dk_sum, dv_sum, spans,
        )
        dq_ref[pl.ds(at, rows), :] = (dq * scale + more_ref[pl.ds(at, rows), :].astype(F32)).astype(BF16)

    def clean(block, carry):
        bias = jnp.where(column_ref[first:most, :] == 0, 0.0, MASKED)
        part(
            pl.multiple_of(block * QBLOCK, QBLOCK), QBLOCK,
            [(0, first, lambda scores: scores), (first, most, lambda scores: scores + bias)],
        )
        return carry

    lax.fori_loop(0, first // QBLOCK, clean, 0)
    image = row_ref[0:1, first:count]
    part(first, count - first, [(0, count, lambda scores: jnp.where(column_ref[...] == image, scores, MASKED))])
    dk_ref[...] = (dk_sum[...] * (1.0 / LOG2E)).astype(BF16)
    dv_ref[...] = dv_sum[...].astype(BF16)


def self_back(pair, packed, column, row, grad, own, stats, more, head_dim, scale):
    count = packed.shape[0]
    pairs = packed.shape[1] // 384
    tokens = pl.BlockSpec((count, 128), lambda i: (0, pair))
    out = pl.BlockSpec((count, 128), lambda i: (0, 0))
    most = min(round_up(FIRST_MOST, 128), count)
    flops = 10 * count * count * 128
    return pl.pallas_call(
        functools.partial(self_back_kernel, head_dim, FIRST_PATCHES, most, scale),
        grid=(1,),
        in_specs=[
            tokens,
            pl.BlockSpec((count, 128), lambda i: (0, pairs + pair)),
            pl.BlockSpec((count, 128), lambda i: (0, 2 * pairs + pair)),
            pl.BlockSpec((count, 1), lambda i: (0, 0)),
            pl.BlockSpec((1, count), lambda i: (0, 0)),
            tokens,
            out,
            pl.BlockSpec((8, count), lambda i: (0, 0)),
            out,
        ],
        out_specs=[out, out, out],
        out_shape=[jax.ShapeDtypeStruct((count, 128), BF16)] * 3,
        scratch_shapes=[pltpu.VMEM((count, 128), F32), pltpu.VMEM((count, 128), F32)],
        compiler_params=pltpu.CompilerParams(vmem_limit_bytes=VMEM_LIMIT),
        cost_estimate=pl.CostEstimate(flops=flops, bytes_accessed=30 * count * 128, transcendentals=2 * count * count),
    )(packed, packed, packed, column, row, grad, own, stats, more)


def swiglu_kernel(core_ref, gate_ref, up_ref, out_ref, moved_ref):
    gate = gate_ref[...]
    value = (gate * up_ref[...] / (1.0 + jnp.exp(-gate))).astype(BF16)
    out_ref[...] = value
    moved_ref[...] = value


def swiglu(gate_up, core, deep, narrow):
    rows, double = gate_up.shape
    width = double // 2
    blocks = 2 * deep * narrow
    block = width // blocks

    def moved_place(i, core_ref):
        z, c, f = i // (2 * narrow), (i // narrow) % 2, i % narrow
        return (0, ((c + core_ref[0]) % 2) * (deep * narrow) + f * deep + z)

    return pl.pallas_call(
        swiglu_kernel,
        grid_spec=pltpu.PrefetchScalarGridSpec(
            num_scalar_prefetch=1,
            grid=(blocks,),
            in_specs=[
                pl.BlockSpec((rows, block), lambda i, core_ref: (0, i)),
                pl.BlockSpec((rows, block), lambda i, core_ref: (0, blocks + i)),
            ],
            out_specs=[
                pl.BlockSpec((rows, block), lambda i, core_ref: (0, i)),
                pl.BlockSpec((rows, block), moved_place),
            ],
        ),
        out_shape=[jax.ShapeDtypeStruct((rows, width), BF16)] * 2,
        compiler_params=pltpu.CompilerParams(vmem_limit_bytes=VMEM_LIMIT),
        cost_estimate=pl.CostEstimate(flops=6 * rows * width, bytes_accessed=12 * rows * width, transcendentals=rows * width),
    )(core.reshape(1), gate_up, gate_up)


def fsdp_share_kernel(narrow, x_ref, out_ref, send_sem, recv_sem):
    me = lax.axis_index("fsdp")
    barrier = pltpu.get_barrier_semaphore()
    for step in range(1, narrow):
        pl.semaphore_signal(
            barrier, inc=1, device_id={"fsdp": lax.rem(me + step, narrow)}, device_id_type=pl.DeviceIdType.MESH
        )
    pl.semaphore_wait(barrier, narrow - 1)
    copies = []
    for step in range(1, narrow):
        copy = pltpu.make_async_remote_copy(
            src_ref=x_ref,
            dst_ref=out_ref.at[me],
            send_sem=send_sem.at[step],
            recv_sem=recv_sem.at[step],
            device_id={"fsdp": lax.rem(me + step, narrow)},
            device_id_type=pl.DeviceIdType.MESH,
        )
        copy.start()
        copies.append(copy)
    out_ref[me] = x_ref[...]
    for copy in copies:
        copy.wait()


def fsdp_share(value, narrow, collective_id):
    return pl.pallas_call(
        functools.partial(fsdp_share_kernel, narrow),
        in_specs=[pl.BlockSpec(memory_space=pltpu.VMEM)],
        out_specs=pl.BlockSpec(memory_space=pltpu.VMEM),
        out_shape=jax.ShapeDtypeStruct((narrow,) + value.shape, value.dtype),
        scratch_shapes=[pltpu.SemaphoreType.DMA((narrow,)), pltpu.SemaphoreType.DMA((narrow,))],
        compiler_params=pltpu.CompilerParams(collective_id=collective_id, has_side_effects=True),
        cost_estimate=pl.CostEstimate(flops=0, bytes_accessed=8 * narrow * value.size, transcendentals=0),
    )(value)


def finish_kernel(narrow, wide, sum_rows, x_ref, out_ref, first_ref, second_ref, sends, recvs):
    me = lax.axis_index("fsdp")
    group = lax.axis_index("z") * 2 + lax.axis_index("core")
    rows = x_ref.shape[1]
    rest = rows - sum_rows
    barrier = pltpu.get_barrier_semaphore()
    places = [{"fsdp": lax.rem(me + step, narrow)} for step in range(1, narrow)]
    peers = [lax.rem(group + step, wide) for step in range(1, wide)]
    partners = [{"z": peer // 2, "core": peer % 2} for peer in peers]
    for place in places + partners:
        pl.semaphore_signal(barrier, inc=1, device_id=place, device_id_type=pl.DeviceIdType.MESH)
    pl.semaphore_wait(barrier, narrow + wide - 2)

    def send_all(targets, source, target, base):
        copies = []
        for i, place in enumerate(targets):
            copy = pltpu.make_async_remote_copy(
                src_ref=source(i),
                dst_ref=target,
                send_sem=sends.at[base + i],
                recv_sem=recvs.at[base + i],
                device_id=place,
                device_id_type=pl.DeviceIdType.MESH,
            )
            copy.start()
            copies.append(copy)
        return copies

    copies = send_all(places, lambda i: x_ref.at[lax.rem(me + i + 1, narrow)], first_ref.at[me], 0)
    first_ref[me] = x_ref[me]
    for copy in copies:
        copy.wait()
    total = first_ref[0]
    for i in range(1, narrow):
        total = total + first_ref[i]
    second_ref[group] = total
    copies = send_all(partners, lambda i: second_ref.at[group], second_ref.at[group], narrow)
    for copy in copies:
        copy.wait()
    total = second_ref[0, :sum_rows, :]
    for i in range(1, wide):
        total = total + second_ref[i, :sum_rows, :]
    out_ref[me, :sum_rows, :] = total
    for i in range(wide):
        out_ref[me, sum_rows + i * rest : sum_rows + (i + 1) * rest, :] = second_ref[i, sum_rows:, :]
    copies = send_all(places, lambda i: out_ref.at[me], out_ref.at[me], narrow + wide)
    for copy in copies:
        copy.wait()


def finish(summed, kept, narrow, wide, collective_id):
    sum_rows = round_up(-(-summed.size // (128 * narrow)), 8)
    kept_rows = round_up(-(-kept.size // (128 * narrow)), 8)

    def chunked(value, rows):
        return jnp.pad(value, (0, narrow * rows * 128 - value.size)).reshape(narrow, rows, 128)

    joined = jnp.concatenate([chunked(summed, sum_rows), chunked(kept, kept_rows)], axis=1)
    rows = sum_rows + kept_rows
    count = 2 * narrow + wide
    out = pl.pallas_call(
        functools.partial(finish_kernel, narrow, wide, sum_rows),
        in_specs=[pl.BlockSpec(memory_space=pltpu.VMEM)],
        out_specs=pl.BlockSpec(memory_space=pltpu.VMEM),
        out_shape=jax.ShapeDtypeStruct((narrow, sum_rows + wide * kept_rows, 128), F32),
        scratch_shapes=[
            pltpu.VMEM((narrow, rows, 128), F32),
            pltpu.VMEM((wide, rows, 128), F32),
            pltpu.SemaphoreType.DMA((count,)),
            pltpu.SemaphoreType.DMA((count,)),
        ],
        compiler_params=pltpu.CompilerParams(collective_id=collective_id, has_side_effects=True),
    )(joined)
    total = out[:, :sum_rows, :].reshape(-1)[: summed.size]
    groups = out[:, sum_rows:, :].reshape(narrow, wide, kept_rows * 128).transpose(1, 0, 2)
    return total, groups.reshape(wide, -1)[:, : kept.size]


def exchange(blocks, axis):
    return lax.all_to_all(blocks, axis, 0, 0, tiled=True)


def core_swap(value):
    return lax.ppermute(value, "core", [(0, 1), (1, 0)])


def by_core(low, high):
    first = lax.axis_index("core") == 0
    return jnp.where(first, low, high), jnp.where(first, high, low)


def in_core_order(own, other):
    first = lax.axis_index("core") == 0
    return jnp.where(first, own, other), jnp.where(first, other, own)


def chip_sum(own_left, other_left, right):
    came = core_swap(outer_sum(other_left, right).astype(BF16))
    return (outer_sum(own_left, right) + came.astype(F32)).astype(BF16)


def fsdp_sum(both):
    return lax.psum_scatter(both, "fsdp", scatter_dimension=0, tiled=True)


def z_sum(blocks, deep):
    me = lax.axis_index("z")
    total = lax.dynamic_index_in_dim(blocks, me, 0, keepdims=False).astype(F32)
    for step in range(1, deep):
        sent = lax.dynamic_index_in_dim(blocks, me ^ step, 0, keepdims=False)
        total = total + lax.ppermute(sent, "z", [(i, i ^ step) for i in range(deep)]).astype(F32)
    return total


def to_all(block, narrow):
    return [
        lax.ppermute(block, "fsdp", [(i, i ^ step) for i in range(narrow)]) for step in range(1, narrow)
    ]


def in_order(block, came):
    me = lax.axis_index("fsdp")
    narrow = len(came) + 1
    result = lax.dynamic_update_slice_in_dim(
        jnp.zeros((narrow,) + block.shape, block.dtype), block[None], me, 0
    )
    for step in range(1, narrow):
        result = lax.dynamic_update_slice_in_dim(result, came[step - 1][None], me ^ step, 0)
    return result


def device_columns(value, deep, narrow):
    rows, width = value.shape
    block = width // (2 * deep * narrow)
    core = lax.axis_index("core")
    target = jnp.arange(width, dtype=jnp.int32)
    c, f, z, r = (
        target // (narrow * deep * block), target // (deep * block) % narrow, target // block % deep, target % block,
    )
    c = (c + core) % 2
    source = ((z * 2 + c) * narrow + f) * block + r
    pick = (jnp.arange(width, dtype=jnp.int32)[:, None] == source[None, :]).astype(BF16)
    moved = low_product(value, pick).astype(BF16)
    return moved[:, : width // 2], moved[:, width // 2 :]


def whole_weight(shard):
    rows = shard.shape[0] // 2
    half = lax.dynamic_slice_in_dim(shard, lax.axis_index("core") * rows, rows, 0)
    return lax.all_gather(half, ("fsdp", "core"), axis=0, tiled=True)


def shards(
    tokens,
    cotangent,
    text_states,
    conditioning,
    image_sizes,
    ada_weight,
    ada_bias,
    qkv_weight,
    out_weight,
    text_weight,
    gate_up_weight,
    down_weight,
    norm_gains,
    norm_shifts,
    text_gain,
    head_gate,
):
    model_width = tokens.shape[2]
    head_count = head_gate.shape[0]
    head_dim = model_width // head_count
    image_count = text_states.shape[1]
    caption_local = text_states.shape[2]
    caption_width = text_states.shape[3]
    local_tok = tokens.shape[1]
    deep = lax.axis_size("z")
    narrow = lax.axis_size("fsdp")
    wide = 2 * deep
    me = lax.axis_index("fsdp")
    group_tok = local_tok * narrow
    caption_full = caption_local * narrow
    score_scale = head_dim ** (-0.5)
    text_total = image_count * caption_full
    text_local = image_count * caption_local
    part = model_width // narrow
    part_pad = round_up(part, 128)
    heads_here = head_count // narrow
    pairs = part_pad // 128
    halves = 128 // head_dim

    group_sizes = image_sizes[0]
    position = me * local_tok + jnp.arange(local_tok, dtype=jnp.int32)
    image_index = token_layout(group_sizes, position, image_count)[0]
    key_image, key_row, key_col = token_layout(
        group_sizes, jnp.arange(group_tok, dtype=jnp.int32), image_count
    )
    member = [(image_index == i).astype(F32)[:, None] for i in range(image_count)]
    cosine, sine = rope_tables(key_row, key_col, head_dim)

    cond_low = jax.nn.silu(conditioning[0].astype(F32)).astype(BF16)
    cond_rows = ada_weight.shape[0]
    cond_part = lax.dynamic_slice_in_dim(cond_low, me * cond_rows, cond_rows, 1)
    modulation_part = low_product(cond_part, ada_weight)
    modulation = (
        jnp.sum(fsdp_share(modulation_part.reshape(-1, 128), narrow, 0), axis=0).reshape(modulation_part.shape)
        + ada_bias
    )

    def per_token(index):
        rows = modulation[:, index * model_width : (index + 1) * model_width]
        return functools.reduce(
            jnp.add, [member[i] * rows[i : i + 1, :] for i in range(image_count)]
        )

    def per_image(value):
        return jnp.stack([jnp.sum(member[i] * value, axis=0) for i in range(image_count)])

    token_in = tokens[0].astype(F32)
    token_inverse = inverse_rms(token_in)
    tokens_all = lax.all_gather(tokens[0], "fsdp", axis=0, tiled=True)
    def widened(value, slots):
        if part == part_pad:
            return value
        lead = value.shape[:-1]
        value = value.reshape(*lead, slots, part)
        pads = [(0, 0)] * (len(lead) + 1) + [(0, part_pad - part)]
        return jnp.pad(value, pads).reshape(*lead, slots * part_pad)

    def narrowed(value, slots):
        if part == part_pad:
            return value
        lead = value.shape[:-1]
        return value.reshape(*lead, slots, part_pad)[..., :part].reshape(*lead, slots * part)

    def own_columns(value):
        return widened(lax.dynamic_slice_in_dim(value, me * part, part, value.ndim - 1), 1)

    qkv_rows = qkv_weight.shape[0] // 2
    qkv_half = lax.dynamic_slice_in_dim(qkv_weight, lax.axis_index("core") * qkv_rows, qkv_rows, 0)
    qkv_half = exchange(
        qkv_half.reshape(qkv_rows, 3, narrow, part).transpose(2, 0, 1, 3).reshape(narrow, qkv_rows, 3 * part), "fsdp"
    )
    own_qkv = widened(
        jnp.concatenate(in_core_order(qkv_half, core_swap(qkv_half)), axis=1).reshape(model_width, 3 * part), 3
    )

    full_out = whole_weight(out_weight)
    full_gate_up = whole_weight(gate_up_weight)
    full_down = whole_weight(down_weight)

    text_in = text_states[0].astype(F32).reshape(text_local, caption_width)
    text_inverse = inverse_rms(text_in)
    text_low = (text_in * text_inverse * text_gain).astype(BF16)
    text_cols = caption_width // narrow
    text_slice = (
        exchange(text_low.reshape(text_local, narrow, text_cols).transpose(1, 0, 2), "fsdp")
        .reshape(narrow, image_count, caption_local, text_cols)
        .transpose(1, 0, 2, 3)
        .reshape(text_total, text_cols)
    )
    own_text_weight = (
        text_weight.reshape(text_cols, 2, narrow, part).transpose(2, 0, 1, 3).reshape(narrow, text_cols, 2 * part)
    )
    text_partial = jnp.stack([low_product(text_slice, own_text_weight[i]).astype(BF16) for i in range(narrow)])
    text_partial, tokens_all = lax.optimization_barrier((text_partial, tokens_all))
    text_projected = widened(jnp.sum(exchange(text_partial, "fsdp").astype(F32), axis=0), 2)
    text_parts = fsdp_share(column_stats(text_projected, part, part_pad, 1), narrow, 1)
    text_means = text_parts[:, 0, :]
    text_mean = jnp.mean(text_means, axis=0)
    text_square = jnp.sum(text_parts[:, 1, :], axis=0) + part * jnp.sum((text_means - text_mean) ** 2, axis=0)
    text_key_inverse = lax.rsqrt(text_square / model_width + EPS)[:, None]
    text_unit = (text_projected[:, :part_pad] - text_mean[:, None]) * text_key_inverse
    text_gains = own_columns(norm_gains[4])
    text_packed = jnp.concatenate(
        [(text_unit * text_gains).astype(BF16), text_projected[:, part_pad:].astype(BF16)], axis=1
    )

    wide_tokens = tokens_all.astype(F32)
    wide_scale = functools.reduce(
        jnp.add,
        [(key_image == i).astype(F32)[:, None] * modulation[i : i + 1, :model_width] for i in range(image_count)],
    )
    normed_all = (wide_tokens * inverse_rms(wide_tokens) * norm_gains[0] * (1.0 + wide_scale)).astype(BF16)

    projected = low_product(normed_all, own_qkv)
    stats_all = fsdp_share(column_stats(projected, part, part_pad, 2), narrow, 2)
    head_gains = own_columns(norm_gains[2:4])
    packed = make_heads(
        projected, stats_all, cosine, sine, head_gains, own_columns(norm_shifts), part, score_scale * LOG2E
    )
    gate_tanh = jnp.tanh(head_gate)
    own_gates = lax.dynamic_slice_in_dim(gate_tanh, me * heads_here, heads_here, 0)
    own_gates = jnp.concatenate([own_gates, jnp.ones((pairs * halves - heads_here,), F32)])
    column = key_image[:, None]
    row = key_image[None, :]
    attended = [
        attend(pair, own_gates, packed, text_packed, column, row, head_dim, image_count) for pair in range(pairs)
    ]
    mixed_pairs = [exchange(one[0].reshape(narrow, local_tok, 128), "fsdp") for one in attended]
    self_outs = [one[1] for one in attended]
    cross_outs = [one[2] for one in attended]
    stats = [one[3] for one in attended]
    mixed_low = (
        narrowed(jnp.concatenate(mixed_pairs, axis=2), 1).transpose(1, 0, 2).reshape(local_tok, model_width)
    )

    branch = low_product(mixed_low, full_out)
    branch_inverse = inverse_rms(branch)
    branch_unit = branch * branch_inverse
    gate_attend = jnp.tanh(per_token(1))
    hidden = token_in + gate_attend * (branch_unit * norm_gains[1])
    hidden_inverse = inverse_rms(hidden)
    hidden_unit = hidden * hidden_inverse
    scale_feed = 1.0 + per_token(2)
    normed_feed_low = (hidden_unit * norm_gains[5] * scale_feed).astype(BF16)
    gate_up = low_product(normed_feed_low, full_gate_up)
    hidden_units = gate_up.shape[1] // 2
    gate_half = gate_up[:, :hidden_units]
    up_half = gate_up[:, hidden_units:]
    sigmoid = jax.nn.sigmoid(gate_half)
    if hidden_units // (wide * narrow) % 128 == 0:
        activated_low, moved = swiglu(gate_up, lax.axis_index("core"), deep, narrow)
        down_columns = (moved[:, : hidden_units // 2], moved[:, hidden_units // 2 :])
    else:
        activated_low = (gate_half * sigmoid * up_half).astype(BF16)
        down_columns = device_columns(activated_low, deep, narrow)
    down_out = low_product(activated_low, full_down)
    down_inverse = inverse_rms(down_out)
    down_unit = down_out * down_inverse
    gate_feed = jnp.tanh(per_token(3))
    down_normed = down_unit * norm_gains[6]
    result = (hidden + gate_feed * down_normed).astype(BF16)

    grad_result = cotangent[0].astype(F32)
    grad_down_y = grad_result * gate_feed
    grad_gain_six = jnp.sum(grad_down_y * down_unit, axis=0)
    grad_gate_feed = per_image(grad_result * down_normed * (1.0 - gate_feed * gate_feed))
    grad_down_low = norm_pull(grad_down_y * norm_gains[6], down_unit, down_inverse).astype(BF16)
    grad_activated = times_transposed(grad_down_low, full_down)
    grad_gate_up_low = jnp.concatenate(
        [
            (grad_activated * up_half * sigmoid * (1.0 + gate_half * (1.0 - sigmoid))).astype(BF16),
            (grad_activated * gate_half * sigmoid).astype(BF16),
        ],
        axis=1,
    )
    grad_normed_feed = times_transposed(grad_gate_up_low, full_gate_up)
    grad_feed_y = grad_normed_feed * scale_feed
    grad_gain_five = jnp.sum(grad_feed_y * hidden_unit, axis=0)
    grad_scale_feed = per_image(grad_normed_feed * hidden_unit * norm_gains[5])
    grad_hidden = grad_result + norm_pull(grad_feed_y * norm_gains[5], hidden_unit, hidden_inverse)
    grad_branch_y = grad_hidden * gate_attend
    grad_gain_one = jnp.sum(grad_branch_y * branch_unit, axis=0)
    grad_gate_attend = per_image(
        grad_hidden * branch_unit * norm_gains[1] * (1.0 - gate_attend * gate_attend)
    )
    grad_branch_low = norm_pull(grad_branch_y * norm_gains[1], branch_unit, branch_inverse).astype(BF16)
    grad_mixed = times_transposed(grad_branch_low, full_out).astype(BF16)
    grad_blocks = widened(grad_mixed.reshape(local_tok, narrow, part).transpose(1, 0, 2), 1)
    grad_heads = exchange(grad_blocks, "fsdp").reshape(group_tok, part_pad)
    def by_z(value):
        return value.reshape(deep, -1, value.shape[1])

    down_both = chip_sum(*down_columns, grad_down_low)
    gate_up_both = chip_sum(*device_columns(normed_feed_low, deep, narrow), grad_gate_up_low)
    out_both = chip_sum(*device_columns(mixed_low, deep, narrow), grad_branch_low)
    down_part = fsdp_sum(down_both)
    grad_heads, gate_up_both, out_both, down_part = lax.optimization_barrier(
        (grad_heads, gate_up_both, out_both, down_part)
    )
    came_downs = exchange(by_z(down_part), "z")
    gate_up_part = fsdp_sum(gate_up_both)
    out_part = fsdp_sum(out_both)
    crossed = [
        cross_back(
            pair, own_gates, packed, text_packed, row, grad_heads, cross_outs[pair], stats[pair],
            head_dim, image_count, score_scale,
        )
        for pair in range(pairs)
    ]
    dtk = jnp.concatenate([one[1] for one in crossed], axis=1)
    dtv = jnp.concatenate([one[2] for one in crossed], axis=1)
    gate_sums = jnp.stack([one[3] for one in crossed])

    grad_text_keys = dtk.astype(F32)
    own_gain_four = jnp.sum(grad_text_keys * text_unit, axis=0)
    grad_text_unit = grad_text_keys * text_gains
    text_sums = jnp.stack([jnp.sum(grad_text_unit, axis=1), jnp.sum(grad_text_unit * text_unit, axis=1)])
    text_sums = jnp.sum(
        fsdp_share(jnp.pad(text_sums, ((0, 6), (0, 0))), narrow, 3), axis=0
    ) * (1.0 / model_width)
    grad_text_key_in = (grad_text_unit - text_sums[0][:, None] - text_unit * text_sums[1][:, None]) * text_key_inverse
    grad_text_own = jnp.concatenate(
        [narrowed(grad_text_key_in.astype(BF16), 1), narrowed(dtv, 1)], axis=1
    )
    def self_pair(pair):
        return self_back(
            pair, packed, column, row, grad_heads, self_outs[pair], stats[pair], crossed[pair][0], head_dim, score_scale
        )

    came_texts = to_all(grad_text_own, narrow)
    backs = [self_pair(0)]
    first, came_downs, *came_texts = lax.optimization_barrier((backs[0][0], came_downs, *came_texts))
    grad_down_weight = jnp.sum(came_downs.astype(F32), axis=0)
    backs[0] = (first, *backs[0][1:])
    grad_text_all = in_order(grad_text_own, came_texts)
    grad_text_columns = (
        grad_text_all.reshape(narrow, text_total, 2, part).transpose(1, 2, 0, 3).reshape(text_total, 2 * model_width)
    )
    text_half = text_cols // 2
    own_text, other_text = by_core(text_slice[:, :text_half], text_slice[:, text_half:])
    came_text = core_swap(outer_sum(other_text, grad_text_columns).astype(BF16))
    text_both = (outer_sum(own_text, grad_text_columns) + came_text.astype(F32)).astype(BF16)
    grad_heads, text_both, first = lax.optimization_barrier((grad_heads, text_both, backs[0][0]))
    backs[0] = (first, *backs[0][1:])
    text_part = z_sum(by_z(text_both), deep).astype(BF16)
    backs.append(self_pair(1))
    if pairs > 2:
        grad_heads, gate_up_part, second = lax.optimization_barrier((grad_heads, gate_up_part, backs[1][0]))
        backs[1] = (second, *backs[1][1:])
        backs += [self_pair(pair) for pair in range(2, pairs)]
    grad_gate_up_weight = z_sum(by_z(gate_up_part), deep)
    grad_text_slice = times_transposed(grad_text_columns, text_weight).astype(BF16)
    grad_text_normed = (
        exchange(
            grad_text_slice.reshape(image_count, narrow, caption_local, text_cols)
            .transpose(1, 0, 2, 3)
            .reshape(narrow, text_local, text_cols),
            "fsdp",
        )
        .transpose(1, 0, 2)
        .reshape(text_local, caption_width)
        .astype(F32)
    )
    text_state_unit = text_in * text_inverse
    grad_text_gain = jnp.sum(grad_text_normed * text_state_unit, axis=0)
    grad_text = (
        norm_pull(grad_text_normed * text_gain, text_state_unit, text_inverse)
        .astype(BF16)
        .reshape(image_count, caption_local, caption_width)
    )

    own_gate_grad = jnp.sum(gate_sums[:, 0, :].reshape(pairs * halves, head_dim), axis=1)[:heads_here]
    grad_head_gate = lax.dynamic_update_slice_in_dim(
        jnp.zeros((head_count,), F32), own_gate_grad, me * heads_here, 0
    ) * (1.0 - gate_tanh * gate_tanh)
    grad_projected_low, head_sums = heads_back(
        list(zip(*backs)), projected, stats_all, cosine, sine, head_gains, part,
        lambda value: fsdp_share(value, narrow, 4),
    )
    grad_projected_low, grad_gate_up_weight, text_part, out_part = lax.optimization_barrier(
        (grad_projected_low, grad_gate_up_weight, text_part, out_part)
    )
    everyone = ("z", "core", "fsdp")
    grad_text_weight = lax.ppermute(
        text_part,
        everyone,
        [
            ((z * 2 + c) * narrow + f, f * wide + c * deep + z)
            for z in range(deep) for c in range(2) for f in range(narrow)
        ],
    ).astype(F32)
    grad_out_weight = z_sum(by_z(out_part), deep)
    grad_normed = lax.psum_scatter(
        times_transposed(grad_projected_low, own_qkv).astype(BF16), "fsdp", scatter_dimension=0, tiled=True
    ).astype(F32)

    qkv_grad = outer_sum(normed_all, grad_projected_low).astype(BF16).reshape(deep, 2, model_width // wide, 3 * part_pad)
    own_grad, other_grad = by_core(qkv_grad[:, 0], qkv_grad[:, 1])
    own_grad = own_grad.astype(F32) + core_swap(other_grad).astype(F32)
    own_grad = z_sum(own_grad.astype(BF16), deep)
    grad_qkv_weight = (
        exchange(narrowed(own_grad.astype(BF16), 3).reshape(narrow, -1, 3 * part), "fsdp")
        .reshape(narrow, -1, 3, part)
        .transpose(1, 2, 0, 3)
        .reshape(-1, 3 * model_width)
        .astype(F32)
    )

    token_unit = token_in * token_inverse
    scale_attend = 1.0 + per_token(0)
    grad_normed_y = grad_normed * scale_attend
    grad_gain_zero = jnp.sum(grad_normed_y * token_unit, axis=0)
    grad_scale_attend = per_image(grad_normed * token_unit * norm_gains[0])
    grad_tokens = (
        grad_hidden + norm_pull(grad_normed_y * norm_gains[0], token_unit, token_inverse)
    ).astype(BF16)

    def placed_columns(value):
        return lax.dynamic_update_slice_in_dim(
            jnp.zeros((model_width,), F32), narrowed(value, 1), me * part, 0
        )

    grad_modulation = jnp.concatenate(
        [grad_scale_attend, grad_gate_attend, grad_scale_feed, grad_gate_feed], axis=1
    )
    group = lax.axis_index("z") * 2 + lax.axis_index("core")
    summed = jnp.concatenate(
        [
            grad_gain_zero,
            grad_gain_one,
            placed_columns(head_sums[0]),
            placed_columns(head_sums[2]),
            placed_columns(own_gain_four),
            grad_gain_five,
            grad_gain_six,
            placed_columns(head_sums[1]),
            placed_columns(head_sums[3]),
            grad_text_gain,
            grad_head_gate,
        ]
    )
    kept = jnp.concatenate(
        [grad_modulation.reshape(-1), jnp.where(me == 0, cond_low.astype(F32), 0.0).reshape(-1)]
    )
    summed, kept = finish(summed, kept, narrow, wide, 5)
    gain_count = norm_gains.size
    shift_end = gain_count + norm_shifts.size
    text_end = shift_end + text_gain.size
    grad_gains = summed[:gain_count].reshape(norm_gains.shape)
    grad_shifts = summed[gain_count:shift_end].reshape(norm_shifts.shape)
    grad_text_gain = summed[shift_end:text_end]
    grad_head_gate = summed[text_end:]
    every_image = wide * image_count
    slots = kept[:, : grad_modulation.size].reshape(every_image, grad_modulation.shape[1])
    cond_slots = kept[:, grad_modulation.size :].reshape(every_image, cond_low.shape[1])
    grad_ada_bias = jnp.sum(slots, axis=0)
    ada_rows = cond_rows // wide
    own_cond = lax.dynamic_slice_in_dim(cond_slots, (group * narrow + me) * ada_rows, ada_rows, 1)
    grad_ada_weight = exact_outer(own_cond, slots)
    return (
        result[None],
        grad_tokens[None],
        grad_text[None],
        grad_ada_weight,
        grad_qkv_weight,
        grad_out_weight,
        grad_text_weight,
        grad_gate_up_weight,
        grad_down_weight,
        grad_ada_bias,
        grad_gains,
        grad_shifts,
        grad_text_gain,
        grad_head_gate,
    )


def solution(mesh):
    wide, narrow = mesh.devices.shape
    fine = Mesh(mesh.devices.reshape(wide // 2, 2, narrow), ("z", "core", "fsdp"))
    groups = ("z", "core")
    every = ("z", "core", "fsdp")
    placed = (
        P(groups, "fsdp", None),
        P(groups, "fsdp", None),
        P(groups, None, "fsdp", None),
        P(groups, None, None),
        P(groups, None, None),
        P("fsdp", None),
        P(),
        P("fsdp", None),
        P("fsdp", None),
        P("fsdp", None),
        P("fsdp", None),
        P("fsdp", None),
        P(),
        P(),
        P(),
        P(),
    )
    return jax.shard_map(
        shards,
        mesh=fine,
        in_specs=placed,
        out_specs=(
            P(groups, "fsdp", None),
            P(groups, "fsdp", None),
            P(groups, None, "fsdp", None),
            P(every, None),
            P(every, None),
            P(every, None),
            P(every, None),
            P(every, None),
            P(every, None),
            P(),
            P(),
            P(),
            P(),
            P(),
        ),
        check_vma=False,
    )
```

```python
import functools

import jax
import jax.numpy as jnp
from jax import lax
from jax.experimental import pallas as pl
from jax.experimental.pallas import tpu as pltpu
from jax.sharding import Mesh
from jax.sharding import PartitionSpec as P

EPS = 1e-05
HIGHEST_PRECISION = lax.Precision.HIGHEST
MASKED = -1e30
LOG2E = 1.4426950408889634
FIRST_PATCHES = 16 * 12**2
FIRST_MOST = FIRST_PATCHES + 96
QBLOCK = 256
BF16 = jnp.bfloat16
F32 = jnp.float32
VMEM_LIMIT = 60 * 1024 * 1024


def round_up(value, step):
    return -(-value // step) * step


def low_product(left, right):
    return jnp.dot(left, right, preferred_element_type=F32)


def times_transposed(left, right):
    return lax.dot_general(left, right, (((1,), (1,)), ((), ())), preferred_element_type=F32)


def outer_sum(left, right):
    return lax.dot_general(left, right, (((0,), (0,)), ((), ())), preferred_element_type=F32)


def exact_outer(left, right):
    return lax.dot_general(
        left, right, (((0,), (0,)), ((), ())), precision=HIGHEST_PRECISION, preferred_element_type=F32
    )


def exact_transposed(left, right):
    return lax.dot_general(
        left, right, (((1,), (1,)), ((), ())), precision=HIGHEST_PRECISION, preferred_element_type=F32
    )


def row_mean(value):
    return jnp.mean(value, axis=-1, keepdims=True)


def inverse_rms(value):
    return lax.rsqrt(row_mean(value * value) + EPS)


def norm_pull(grad, unit, inverse):
    return (grad - unit * row_mean(grad * unit)) * inverse


def token_layout(image_sizes, position, image_count):
    start = jnp.int32(0)
    image_index = jnp.full(position.shape, image_count, jnp.int32)
    token_row = jnp.zeros(position.shape, jnp.int32)
    token_col = jnp.zeros(position.shape, jnp.int32)
    for i in range(image_count):
        width = image_sizes[i, 1] + 1
        end = start + image_sizes[i, 0] * width
        inside = (position >= start) & (position < end)
        offset = position - start
        image_index = jnp.where(inside, i, image_index)
        token_row = jnp.where(inside, offset // width, token_row)
        token_col = jnp.where(inside, offset % width, token_col)
        start = end
    return image_index, token_row, token_col


def rope_tables(token_row, token_col, head_dim):
    quarter = head_dim // 4
    pair = (jnp.arange(128, dtype=jnp.int32) % head_dim) // 2
    frequency = 10000.0 ** (-(pair % quarter).astype(F32) / quarter)
    place = jnp.where(
        (pair < quarter)[None, :], token_row.astype(F32)[:, None], token_col.astype(F32)[:, None]
    )
    angles = place * frequency[None, :]
    even = (jnp.arange(128, dtype=jnp.int32) % 2 == 0)[None, :]
    return jnp.cos(angles), jnp.where(even, -jnp.sin(angles), jnp.sin(angles))


def swap_pairs(value):
    width = value.shape[1]
    even = lax.broadcasted_iota(jnp.int32, value.shape, 1) % 2 == 0
    return jnp.where(even, pltpu.roll(value, width - 1, 1), pltpu.roll(value, 1, 1))


def wide_table(table, width):
    return jnp.concatenate([table] * (width // table.shape[1]), axis=1)


def pack_columns(columns):
    rows = columns[0].shape[0]
    lane = lax.broadcasted_iota(jnp.int32, (rows, 128), 1)
    packed = jnp.zeros((rows, 128), F32)
    for i, column in enumerate(columns):
        packed = jnp.where(lane == i, column, packed)
    return jnp.transpose(packed)[:8, :]


def as_columns(rows_list):
    width = rows_list[0].shape[1]
    stacked = jnp.concatenate(
        rows_list + [jnp.zeros((128 - len(rows_list), width), F32)], axis=0
    )
    return jnp.transpose(stacked)


def real_lanes(shape, part):
    return lax.broadcasted_iota(jnp.int32, shape, 1) < part


def own_stats(value, part):
    mean = jnp.sum(value, axis=1, keepdims=True) * (1.0 / part)
    centred = value - mean
    if value.shape[1] != part:
        centred = jnp.where(real_lanes(value.shape, part), centred, 0.0)
    return mean, jnp.sum(centred * centred, axis=1, keepdims=True)


def joined_stats(stats_ref, part, slot):
    narrow = stats_ref.shape[0]
    means = [stats_ref[i, 2 * slot : 2 * slot + 1, :] for i in range(narrow)]
    squares = [stats_ref[i, 2 * slot + 1 : 2 * slot + 2, :] for i in range(narrow)]
    mean = functools.reduce(jnp.add, means) * (1.0 / narrow)
    square = functools.reduce(jnp.add, squares)
    square = square + part * functools.reduce(jnp.add, [(m - mean) * (m - mean) for m in means])
    return mean, lax.rsqrt(square * (1.0 / (narrow * part)) + EPS)


def stats_kernel(part, slots, projected_ref, out_ref):
    padded = projected_ref.shape[1] // slots
    columns = []
    for slot in range(slots):
        columns += own_stats(projected_ref[:, slot * padded : (slot + 1) * padded], part)
    out_ref[...] = pack_columns(columns)


def column_stats(projected, part, padded, slots):
    rows = projected.shape[0]
    return pl.pallas_call(
        functools.partial(stats_kernel, part, slots),
        grid=(pl.cdiv(rows, QBLOCK),),
        in_specs=[pl.BlockSpec((QBLOCK, slots * padded), lambda i: (i, 0))],
        out_specs=pl.BlockSpec((8, QBLOCK), lambda i: (0, i)),
        out_shape=jax.ShapeDtypeStruct((8, rows), F32),
        compiler_params=pltpu.CompilerParams(vmem_limit_bytes=VMEM_LIMIT),
        cost_estimate=pl.CostEstimate(flops=10 * rows * slots * padded, bytes_accessed=4 * rows * slots * padded, transcendentals=0),
    )(projected)


def heads_kernel(part, query_scale, projected_ref, stats_ref, cos_ref, sin_ref, gains_ref, shifts_ref, out_ref):
    padded = projected_ref.shape[1] // 3
    cosine = wide_table(cos_ref[...], padded)
    sine = wide_table(sin_ref[...], padded)
    columns = as_columns([*joined_stats(stats_ref, part, 0), *joined_stats(stats_ref, part, 1)])
    for slot in range(3):
        place = slice(slot * padded, (slot + 1) * padded)
        value = projected_ref[:, place]
        if slot < 2:
            value = (value - columns[:, 2 * slot : 2 * slot + 1]) * columns[:, 2 * slot + 1 : 2 * slot + 2]
            value = value * gains_ref[slot : slot + 1, :] + shifts_ref[slot : slot + 1, :]
            value = value * cosine + swap_pairs(value) * sine
            if slot == 0:
                value = value * query_scale
        out_ref[:, place] = value.astype(BF16)


def make_heads(projected, stats, cosine, sine, gains, shifts, part, query_scale):
    rows, triple = projected.shape
    padded = triple // 3
    narrow = stats.shape[0]
    return pl.pallas_call(
        functools.partial(heads_kernel, part, query_scale),
        grid=(pl.cdiv(rows, QBLOCK),),
        in_specs=[
            pl.BlockSpec((QBLOCK, triple), lambda i: (i, 0)),
            pl.BlockSpec((narrow, 8, QBLOCK), lambda i: (0, 0, i)),
            pl.BlockSpec((QBLOCK, 128), lambda i: (i, 0)),
            pl.BlockSpec((QBLOCK, 128), lambda i: (i, 0)),
            pl.BlockSpec((2, padded), lambda i: (0, 0)),
            pl.BlockSpec((2, padded), lambda i: (0, 0)),
        ],
        out_specs=pl.BlockSpec((QBLOCK, triple), lambda i: (i, 0)),
        out_shape=jax.ShapeDtypeStruct((rows, triple), BF16),
        compiler_params=pltpu.CompilerParams(vmem_limit_bytes=VMEM_LIMIT),
        cost_estimate=pl.CostEstimate(flops=40 * rows * triple, bytes_accessed=6 * rows * triple, transcendentals=0),
    )(projected, stats, cosine, sine, gains, shifts)


def turned_back(refs, cosine, sine):
    grad = jnp.concatenate([ref[...].astype(F32) for ref in refs], axis=1)
    return grad * cosine - swap_pairs(grad) * sine


def grad_stats_kernel(rows, part, pairs, *refs):
    dq_refs, dk_refs = refs[:pairs], refs[pairs : 2 * pairs]
    projected_ref, stats_ref, cos_ref, sin_ref, gains_ref, out_ref, sums_ref = refs[2 * pairs :]
    step = pl.program_id(0)
    padded = 128 * pairs
    cosine = wide_table(cos_ref[...], padded)
    sine = wide_table(sin_ref[...], padded)
    height = cos_ref.shape[0]
    inside = step * height + lax.broadcasted_iota(jnp.int32, (height, 1), 0) < rows

    @pl.when(step == 0)
    def _():
        sums_ref[...] = jnp.zeros_like(sums_ref)

    columns = as_columns([*joined_stats(stats_ref, part, 0), *joined_stats(stats_ref, part, 1)])
    packed = []
    for slot, grads in enumerate((dq_refs, dk_refs)):
        grad = jnp.where(inside, turned_back(grads, cosine, sine), 0.0)
        unit = (projected_ref[:, slot * padded : (slot + 1) * padded] - columns[:, 2 * slot : 2 * slot + 1])
        unit = jnp.where(inside, unit * columns[:, 2 * slot + 1 : 2 * slot + 2], 0.0)
        both = grad * unit
        sums_ref[2 * slot : 2 * slot + 1, :] += jnp.sum(both, axis=0, keepdims=True)
        sums_ref[2 * slot + 1 : 2 * slot + 2, :] += jnp.sum(grad, axis=0, keepdims=True)
        gain = gains_ref[slot : slot + 1, :]
        packed.append(jnp.sum(grad * gain, axis=1, keepdims=True))
        packed.append(jnp.sum(both * gain, axis=1, keepdims=True))
    out_ref[...] = pack_columns(packed)


def heads_back_kernel(part, pairs, *refs):
    dq_refs, dk_refs, dv_refs = refs[:pairs], refs[pairs : 2 * pairs], refs[2 * pairs : 3 * pairs]
    projected_ref, stats_ref, totals_ref, cos_ref, sin_ref, gains_ref, out_ref = refs[3 * pairs :]
    padded = 128 * pairs
    narrow = stats_ref.shape[0]
    cosine = wide_table(cos_ref[...], padded)
    sine = wide_table(sin_ref[...], padded)
    means = [
        functools.reduce(jnp.add, [totals_ref[i, j : j + 1, :] for i in range(narrow)]) * (1.0 / (narrow * part))
        for j in range(4)
    ]
    columns = as_columns([*joined_stats(stats_ref, part, 0), *joined_stats(stats_ref, part, 1), *means])
    for slot, grads in enumerate((dq_refs, dk_refs)):
        grad = turned_back(grads, cosine, sine) * gains_ref[slot : slot + 1, :]
        inverse = columns[:, 2 * slot + 1 : 2 * slot + 2]
        unit = (projected_ref[:, slot * padded : (slot + 1) * padded] - columns[:, 2 * slot : 2 * slot + 1]) * inverse
        grad = grad - columns[:, 4 + 2 * slot : 5 + 2 * slot] - unit * columns[:, 5 + 2 * slot : 6 + 2 * slot]
        grad = grad * inverse
        if padded != part:
            grad = jnp.where(real_lanes(grad.shape, part), grad, 0.0)
        out_ref[:, slot * padded : (slot + 1) * padded] = grad.astype(BF16)
    for pair, ref in enumerate(dv_refs):
        out_ref[:, 2 * padded + 128 * pair : 2 * padded + 128 * (pair + 1)] = ref[...]


def heads_back(grads, projected, stats, cosine, sine, gains, part, share):
    rows, triple = projected.shape
    padded = triple // 3
    pairs = padded // 128
    narrow = stats.shape[0]
    pair_spec = pl.BlockSpec((QBLOCK, 128), lambda i: (i, 0))
    two_spec = pl.BlockSpec((QBLOCK, 2 * padded), lambda i: (i, 0))
    stat_spec = pl.BlockSpec((narrow, 8, QBLOCK), lambda i: (0, 0, i))
    gain_spec = pl.BlockSpec((2, padded), lambda i: (0, 0))
    own, sums = pl.pallas_call(
        functools.partial(grad_stats_kernel, rows, part, pairs),
        grid=(pl.cdiv(rows, QBLOCK),),
        in_specs=[pair_spec] * (2 * pairs) + [two_spec, stat_spec, pair_spec, pair_spec, gain_spec],
        out_specs=[
            pl.BlockSpec((8, QBLOCK), lambda i: (0, i)),
            pl.BlockSpec((8, padded), lambda i: (0, 0)),
        ],
        out_shape=[jax.ShapeDtypeStruct((8, rows), F32), jax.ShapeDtypeStruct((8, padded), F32)],
        compiler_params=pltpu.CompilerParams(vmem_limit_bytes=VMEM_LIMIT),
        cost_estimate=pl.CostEstimate(flops=40 * rows * triple, bytes_accessed=5 * rows * triple, transcendentals=0),
    )(*grads[0], *grads[1], projected, stats, cosine, sine, gains)
    totals = share(own)
    out = pl.pallas_call(
        functools.partial(heads_back_kernel, part, pairs),
        grid=(pl.cdiv(rows, QBLOCK),),
        in_specs=[pair_spec] * (3 * pairs) + [two_spec, stat_spec, stat_spec, pair_spec, pair_spec, gain_spec],
        out_specs=pl.BlockSpec((QBLOCK, triple), lambda i: (i, 0)),
        out_shape=jax.ShapeDtypeStruct((rows, triple), BF16),
        compiler_params=pltpu.CompilerParams(vmem_limit_bytes=VMEM_LIMIT),
        cost_estimate=pl.CostEstimate(flops=40 * rows * triple, bytes_accessed=7 * rows * triple, transcendentals=0),
    )(*grads[0], *grads[1], *grads[2], projected, stats, totals, cosine, sine, gains)
    return out, sums


def head_lanes(rows, half, head_dim):
    lane = lax.broadcasted_iota(jnp.int32, (rows, 128), 1)
    return (lane >= half * head_dim) & (lane < (half + 1) * head_dim)


def softmax_product(pieces):
    maximum = functools.reduce(jnp.maximum, [jnp.max(s, axis=1, keepdims=True) for s, _ in pieces])
    total, result = 0.0, 0.0
    for scores, values in pieces:
        weight = jnp.exp2(scores - maximum)
        total = total + jnp.sum(weight, axis=1, keepdims=True)
        result = result + low_product(weight.astype(BF16), values)
    return result * (1.0 / total), maximum + jnp.log2(total)


def attend_kernel(
    head_dim, first, most, caption, image_count,
    gate_ref, q_ref, k_ref, v_ref, tk_ref, tv_ref, column_ref, row_ref,
    mixed_ref, self_ref, cross_ref, stats_ref,
):
    count = q_ref.shape[0]
    halves = 128 // head_dim

    def emit(at, rows, outs):
        lanes = [head_lanes(rows, half, head_dim) for half in range(halves)]
        own, cross, gated = 0.0, 0.0, 0.0
        columns = []
        for half, (own_out, own_total, cross_out, cross_total) in enumerate(outs):
            gate = gate_ref[0, half]
            own = own + jnp.where(lanes[half], own_out, 0.0)
            cross = cross + jnp.where(lanes[half], cross_out, 0.0)
            gated = gated + jnp.where(lanes[half], gate * cross_out, 0.0)
            columns += [own_total, cross_total]
        self_ref[pl.ds(at, rows), :] = own
        cross_ref[pl.ds(at, rows), :] = cross
        mixed_ref[pl.ds(at, rows), :] = (own + gated).astype(BF16)
        lane = lax.broadcasted_iota(jnp.int32, (rows, 128), 1)
        packed = jnp.zeros((rows, 128), F32)
        for i, column in enumerate(columns):
            packed = jnp.where(lane == i, column, packed)
        stats_ref[:, pl.ds(at, rows)] = jnp.transpose(packed)[:8, :]

    def clean(block, carry):
        at = pl.multiple_of(block * QBLOCK, QBLOCK)
        queries = q_ref[pl.ds(at, QBLOCK), :]
        outs = []
        for half in range(halves):
            q = jnp.where(head_lanes(QBLOCK, half, head_dim), queries, jnp.zeros_like(queries))
            bias = jnp.where(row_ref[0:1, first:most] == 0, 0.0, MASKED)
            own_out, own_total = softmax_product([
                (times_transposed(q, k_ref[0:first, :]), v_ref[0:first, :]),
                (times_transposed(q, k_ref[first:most, :]) + bias, v_ref[first:most, :]),
            ])
            cross_out, cross_total = softmax_product(
                [(times_transposed(q, tk_ref[0:caption, :]), tv_ref[0:caption, :])]
            )
            outs.append((own_out, own_total, cross_out, cross_total))
        emit(at, QBLOCK, outs)
        return carry

    lax.fori_loop(0, first // QBLOCK, clean, 0)
    rest = count - first
    queries = q_ref[first:count, :]
    image = column_ref[first:count, :]
    outs = []
    for half in range(halves):
        q = jnp.where(head_lanes(rest, half, head_dim), queries, jnp.zeros_like(queries))
        own_out, own_total = softmax_product([
            (jnp.where(image == row_ref[0:1, :], times_transposed(q, k_ref[...]), MASKED), v_ref[...])
        ])
        scores = times_transposed(q, tk_ref[...])
        owner = lax.broadcasted_iota(jnp.int32, (1, scores.shape[1]), 1) // caption
        scores = jnp.where((image == owner) | (image == image_count), scores, MASKED)
        cross_out, cross_total = softmax_product([(scores, tv_ref[...])])
        outs.append((own_out, own_total, cross_out, cross_total))
    emit(first, rest, outs)


def attend(pair, gates, packed, text_packed, column, row, head_dim, image_count):
    count, texts = packed.shape[0], text_packed.shape[0]
    pairs = packed.shape[1] // 384
    halves = 128 // head_dim
    out = pl.BlockSpec((count, 128), lambda i: (0, 0))
    most = min(round_up(FIRST_MOST, 128), count)
    flops = 4 * count * (count + texts) * 128
    return pl.pallas_call(
        functools.partial(
            attend_kernel, head_dim, FIRST_PATCHES, most, texts // image_count, image_count
        ),
        grid=(1,),
        in_specs=[
            pl.BlockSpec((None, 1, halves), lambda i: (pair, 0, 0), memory_space=pltpu.SMEM),
            pl.BlockSpec((count, 128), lambda i: (0, pair)),
            pl.BlockSpec((count, 128), lambda i: (0, pairs + pair)),
            pl.BlockSpec((count, 128), lambda i: (0, 2 * pairs + pair)),
            pl.BlockSpec((texts, 128), lambda i: (0, pair)),
            pl.BlockSpec((texts, 128), lambda i: (0, pairs + pair)),
            pl.BlockSpec((count, 1), lambda i: (0, 0)),
            pl.BlockSpec((1, count), lambda i: (0, 0)),
        ],
        out_specs=[out, out, out, pl.BlockSpec((8, count), lambda i: (0, 0))],
        out_shape=[
            jax.ShapeDtypeStruct((count, 128), BF16),
            jax.ShapeDtypeStruct((count, 128), F32),
            jax.ShapeDtypeStruct((count, 128), F32),
            jax.ShapeDtypeStruct((8, count), F32),
        ],
        compiler_params=pltpu.CompilerParams(vmem_limit_bytes=VMEM_LIMIT),
        cost_estimate=pl.CostEstimate(flops=flops, bytes_accessed=20 * count * 128, transcendentals=2 * count * count),
    )(gates.reshape(pairs, 1, halves), packed, packed, packed, text_packed, text_packed, column, row)


def gate_lanes(gate_ref, head_dim):
    lane = lax.broadcasted_iota(jnp.int32, (1, 128), 1)
    gates = jnp.zeros((1, 128), F32)
    for half in range(128 // head_dim):
        gates = jnp.where(lane // head_dim == half, gate_ref[0, half], gates)
    return gates


def head_picks(head_dim):
    return (
        lax.broadcasted_iota(jnp.int32, (8, 128), 1) // head_dim
        == lax.broadcasted_iota(jnp.int32, (8, 128), 0)
    ).astype(F32)


def rows_back(head_dim, queries, outs, delta, stats, offset, keys, values, key_sum, value_sum, spans):
    rows = queries.shape[0]
    halves = 128 // head_dim
    zero = jnp.zeros((rows, 128), BF16)
    lanes = [head_lanes(rows, half, head_dim) for half in range(halves)]
    q_heads = [jnp.where(lane, queries, zero) for lane in lanes]
    out_heads = [jnp.where(lane, outs, zero) for lane in lanes]
    q_stack = jnp.concatenate(q_heads, axis=0)
    out_stack = jnp.concatenate(out_heads, axis=0)
    dq = [0.0] * halves
    for low, high, mask in spans:
        key_part = keys[low:high, :]
        value_part = values[low:high, :]
        probs, grads = [], []
        for half in range(halves):
            scores = mask(times_transposed(key_part, q_heads[half]))
            prob = jnp.exp2(scores - stats[2 * half + offset : 2 * half + offset + 1, :])
            dprob = times_transposed(value_part, out_heads[half])
            dscore = (prob * (dprob - delta[half : half + 1, :])).astype(BF16)
            probs.append(prob.astype(BF16))
            grads.append(dscore)
            dq[half] = dq[half] + outer_sum(dscore, key_part)
        value_sum[low:high, :] += low_product(jnp.concatenate(probs, axis=1), out_stack)
        key_sum[low:high, :] += low_product(jnp.concatenate(grads, axis=1), q_stack)
    total = 0.0
    for half in range(halves):
        total = total + jnp.where(lanes[half], dq[half], 0.0)
    return total


def cross_back_kernel(
    head_dim, first, caption, image_count, scale,
    gate_ref, q_ref, tk_ref, tv_ref, row_ref, grad_ref, cross_ref, stats_ref,
    dq_ref, dtk_ref, dtv_ref, gate_grad_ref, dtk_sum, dtv_sum,
):
    count = q_ref.shape[0]
    for total in (dtk_sum, dtv_sum, gate_grad_ref):
        total[...] = jnp.zeros_like(total)
    gates = gate_lanes(gate_ref, head_dim)
    picks = head_picks(head_dim)

    def part(at, rows, spans):
        wide = grad_ref[pl.ds(at, rows), :].astype(F32)
        cross = cross_ref[pl.ds(at, rows), :]
        gate_grad_ref[0:1, :] += jnp.sum(wide * cross, axis=0, keepdims=True)
        gated = (wide * gates).astype(BF16)
        delta = exact_transposed(picks, gated.astype(F32) * cross)
        dq = rows_back(
            head_dim, q_ref[pl.ds(at, rows), :], gated, delta, stats_ref[:, pl.ds(at, rows)], 1,
            tk_ref, tv_ref, dtk_sum, dtv_sum, spans,
        )
        dq_ref[pl.ds(at, rows), :] = (dq * scale).astype(BF16)

    def clean(block, carry):
        part(pl.multiple_of(block * QBLOCK, QBLOCK), QBLOCK, [(0, caption, lambda scores: scores)])
        return carry

    lax.fori_loop(0, first // QBLOCK, clean, 0)
    image = row_ref[0:1, first:count]
    owner = lax.broadcasted_iota(jnp.int32, (tk_ref.shape[0], 1), 0) // caption
    allowed = (owner == image) | (image == image_count)
    part(first, count - first, [(0, tk_ref.shape[0], lambda scores: jnp.where(allowed, scores, MASKED))])
    dtk_ref[...] = (dtk_sum[...] * (1.0 / LOG2E)).astype(BF16)
    dtv_ref[...] = dtv_sum[...].astype(BF16)


def cross_back(pair, gates, packed, text_packed, row, grad, cross, stats, head_dim, image_count, scale):
    count, texts = packed.shape[0], text_packed.shape[0]
    pairs = packed.shape[1] // 384
    halves = 128 // head_dim
    tokens = pl.BlockSpec((count, 128), lambda i: (0, pair))
    own_tokens = pl.BlockSpec((count, 128), lambda i: (0, 0))
    captions = pl.BlockSpec((texts, 128), lambda i: (0, 0))
    flops = 10 * count * texts * 128
    return pl.pallas_call(
        functools.partial(cross_back_kernel, head_dim, FIRST_PATCHES, texts // image_count, image_count, scale),
        grid=(1,),
        in_specs=[
            pl.BlockSpec((None, 1, halves), lambda i: (pair, 0, 0), memory_space=pltpu.SMEM),
            tokens,
            pl.BlockSpec((texts, 128), lambda i: (0, pair)),
            pl.BlockSpec((texts, 128), lambda i: (0, pairs + pair)),
            pl.BlockSpec((1, count), lambda i: (0, 0)),
            tokens,
            own_tokens,
            pl.BlockSpec((8, count), lambda i: (0, 0)),
        ],
        out_specs=[own_tokens, captions, captions, pl.BlockSpec((8, 128), lambda i: (0, 0))],
        out_shape=[
            jax.ShapeDtypeStruct((count, 128), BF16),
            jax.ShapeDtypeStruct((texts, 128), BF16),
            jax.ShapeDtypeStruct((texts, 128), BF16),
            jax.ShapeDtypeStruct((8, 128), F32),
        ],
        scratch_shapes=[pltpu.VMEM((texts, 128), F32), pltpu.VMEM((texts, 128), F32)],
        compiler_params=pltpu.CompilerParams(vmem_limit_bytes=VMEM_LIMIT),
        cost_estimate=pl.CostEstimate(flops=flops, bytes_accessed=12 * count * 128, transcendentals=count * texts),
    )(gates.reshape(pairs, 1, halves), packed, text_packed, text_packed, row, grad, cross, stats)


def self_back_kernel(
    head_dim, first, most, scale,
    q_ref, k_ref, v_ref, column_ref, row_ref, grad_ref, self_ref, stats_ref, more_ref,
    dq_ref, dk_ref, dv_ref, dk_sum, dv_sum,
):
    count = q_ref.shape[0]
    dk_sum[...] = jnp.zeros_like(dk_sum)
    dv_sum[...] = jnp.zeros_like(dv_sum)
    picks = head_picks(head_dim)

    def part(at, rows, spans):
        grad = grad_ref[pl.ds(at, rows), :]
        delta = exact_transposed(picks, grad.astype(F32) * self_ref[pl.ds(at, rows), :])
        dq = rows_back(
            head_dim, q_ref[pl.ds(at, rows), :], grad, delta, stats_ref[:, pl.ds(at, rows)], 0,
            k_ref, v_ref, dk_sum, dv_sum, spans,
        )
        dq_ref[pl.ds(at, rows), :] = (dq * scale + more_ref[pl.ds(at, rows), :].astype(F32)).astype(BF16)

    def clean(block, carry):
        bias = jnp.where(column_ref[first:most, :] == 0, 0.0, MASKED)
        part(
            pl.multiple_of(block * QBLOCK, QBLOCK), QBLOCK,
            [(0, first, lambda scores: scores), (first, most, lambda scores: scores + bias)],
        )
        return carry

    lax.fori_loop(0, first // QBLOCK, clean, 0)
    image = row_ref[0:1, first:count]
    part(first, count - first, [(0, count, lambda scores: jnp.where(column_ref[...] == image, scores, MASKED))])
    dk_ref[...] = (dk_sum[...] * (1.0 / LOG2E)).astype(BF16)
    dv_ref[...] = dv_sum[...].astype(BF16)


def self_back(pair, packed, column, row, grad, own, stats, more, head_dim, scale):
    count = packed.shape[0]
    pairs = packed.shape[1] // 384
    tokens = pl.BlockSpec((count, 128), lambda i: (0, pair))
    out = pl.BlockSpec((count, 128), lambda i: (0, 0))
    most = min(round_up(FIRST_MOST, 128), count)
    flops = 10 * count * count * 128
    return pl.pallas_call(
        functools.partial(self_back_kernel, head_dim, FIRST_PATCHES, most, scale),
        grid=(1,),
        in_specs=[
            tokens,
            pl.BlockSpec((count, 128), lambda i: (0, pairs + pair)),
            pl.BlockSpec((count, 128), lambda i: (0, 2 * pairs + pair)),
            pl.BlockSpec((count, 1), lambda i: (0, 0)),
            pl.BlockSpec((1, count), lambda i: (0, 0)),
            tokens,
            out,
            pl.BlockSpec((8, count), lambda i: (0, 0)),
            out,
        ],
        out_specs=[out, out, out],
        out_shape=[jax.ShapeDtypeStruct((count, 128), BF16)] * 3,
        scratch_shapes=[pltpu.VMEM((count, 128), F32), pltpu.VMEM((count, 128), F32)],
        compiler_params=pltpu.CompilerParams(vmem_limit_bytes=VMEM_LIMIT),
        cost_estimate=pl.CostEstimate(flops=flops, bytes_accessed=30 * count * 128, transcendentals=2 * count * count),
    )(packed, packed, packed, column, row, grad, own, stats, more)


def swiglu_kernel(core_ref, gate_ref, up_ref, out_ref, moved_ref):
    gate = gate_ref[...]
    half = 0.5 * gate
    value = ((half + half * jnp.tanh(half)) * up_ref[...]).astype(BF16)
    out_ref[...] = value
    moved_ref[...] = value


def swiglu(gate_up, core, deep, narrow):
    rows, double = gate_up.shape
    width = double // 2
    blocks = 2 * deep * narrow
    block = width // blocks

    def moved_place(i, core_ref):
        z, c, f = i // (2 * narrow), (i // narrow) % 2, i % narrow
        return (0, ((c + core_ref[0]) % 2) * (deep * narrow) + f * deep + z)

    return pl.pallas_call(
        swiglu_kernel,
        grid_spec=pltpu.PrefetchScalarGridSpec(
            num_scalar_prefetch=1,
            grid=(blocks,),
            in_specs=[
                pl.BlockSpec((rows, block), lambda i, core_ref: (0, i)),
                pl.BlockSpec((rows, block), lambda i, core_ref: (0, blocks + i)),
            ],
            out_specs=[
                pl.BlockSpec((rows, block), lambda i, core_ref: (0, i)),
                pl.BlockSpec((rows, block), moved_place),
            ],
        ),
        out_shape=[jax.ShapeDtypeStruct((rows, width), BF16)] * 2,
        compiler_params=pltpu.CompilerParams(vmem_limit_bytes=VMEM_LIMIT),
        cost_estimate=pl.CostEstimate(flops=6 * rows * width, bytes_accessed=12 * rows * width, transcendentals=rows * width),
    )(core.reshape(1), gate_up, gate_up)


def fsdp_share_kernel(narrow, x_ref, out_ref, send_sem, recv_sem):
    me = lax.axis_index("fsdp")
    barrier = pltpu.get_barrier_semaphore()
    for step in range(1, narrow):
        pl.semaphore_signal(
            barrier, inc=1, device_id={"fsdp": lax.rem(me + step, narrow)}, device_id_type=pl.DeviceIdType.MESH
        )
    pl.semaphore_wait(barrier, narrow - 1)
    copies = []
    for step in range(1, narrow):
        copy = pltpu.make_async_remote_copy(
            src_ref=x_ref,
            dst_ref=out_ref.at[me],
            send_sem=send_sem.at[step],
            recv_sem=recv_sem.at[step],
            device_id={"fsdp": lax.rem(me + step, narrow)},
            device_id_type=pl.DeviceIdType.MESH,
        )
        copy.start()
        copies.append(copy)
    out_ref[me] = x_ref[...]
    for copy in copies:
        copy.wait()


def fsdp_share(value, narrow, collective_id):
    return pl.pallas_call(
        functools.partial(fsdp_share_kernel, narrow),
        in_specs=[pl.BlockSpec(memory_space=pltpu.VMEM)],
        out_specs=pl.BlockSpec(memory_space=pltpu.VMEM),
        out_shape=jax.ShapeDtypeStruct((narrow,) + value.shape, value.dtype),
        scratch_shapes=[pltpu.SemaphoreType.DMA((narrow,)), pltpu.SemaphoreType.DMA((narrow,))],
        compiler_params=pltpu.CompilerParams(collective_id=collective_id, has_side_effects=True),
        cost_estimate=pl.CostEstimate(flops=0, bytes_accessed=8 * narrow * value.size, transcendentals=0),
    )(value)


def finish_kernel(narrow, wide, sum_rows, x_ref, out_ref, first_ref, second_ref, sends, recvs):
    me = lax.axis_index("fsdp")
    group = lax.axis_index("z") * 2 + lax.axis_index("core")
    rows = x_ref.shape[1]
    rest = rows - sum_rows
    barrier = pltpu.get_barrier_semaphore()
    places = [{"fsdp": lax.rem(me + step, narrow)} for step in range(1, narrow)]
    peers = [lax.rem(group + step, wide) for step in range(1, wide)]
    partners = [{"z": peer // 2, "core": peer % 2} for peer in peers]
    for place in places + partners:
        pl.semaphore_signal(barrier, inc=1, device_id=place, device_id_type=pl.DeviceIdType.MESH)
    pl.semaphore_wait(barrier, narrow + wide - 2)

    def send_all(targets, source, target, base):
        copies = []
        for i, place in enumerate(targets):
            copy = pltpu.make_async_remote_copy(
                src_ref=source(i),
                dst_ref=target,
                send_sem=sends.at[base + i],
                recv_sem=recvs.at[base + i],
                device_id=place,
                device_id_type=pl.DeviceIdType.MESH,
            )
            copy.start()
            copies.append(copy)
        return copies

    copies = send_all(places, lambda i: x_ref.at[lax.rem(me + i + 1, narrow)], first_ref.at[me], 0)
    first_ref[me] = x_ref[me]
    for copy in copies:
        copy.wait()
    total = first_ref[0]
    for i in range(1, narrow):
        total = total + first_ref[i]
    second_ref[group] = total
    copies = send_all(partners, lambda i: second_ref.at[group], second_ref.at[group], narrow)
    for copy in copies:
        copy.wait()
    total = second_ref[0, :sum_rows, :]
    for i in range(1, wide):
        total = total + second_ref[i, :sum_rows, :]
    out_ref[me, :sum_rows, :] = total
    for i in range(wide):
        out_ref[me, sum_rows + i * rest : sum_rows + (i + 1) * rest, :] = second_ref[i, sum_rows:, :]
    copies = send_all(places, lambda i: out_ref.at[me], out_ref.at[me], narrow + wide)
    for copy in copies:
        copy.wait()


def finish(summed, kept, narrow, wide, collective_id):
    sum_rows = round_up(-(-summed.size // (128 * narrow)), 8)
    kept_rows = round_up(-(-kept.size // (128 * narrow)), 8)

    def chunked(value, rows):
        return jnp.pad(value, (0, narrow * rows * 128 - value.size)).reshape(narrow, rows, 128)

    joined = jnp.concatenate([chunked(summed, sum_rows), chunked(kept, kept_rows)], axis=1)
    rows = sum_rows + kept_rows
    count = 2 * narrow + wide
    out = pl.pallas_call(
        functools.partial(finish_kernel, narrow, wide, sum_rows),
        in_specs=[pl.BlockSpec(memory_space=pltpu.VMEM)],
        out_specs=pl.BlockSpec(memory_space=pltpu.VMEM),
        out_shape=jax.ShapeDtypeStruct((narrow, sum_rows + wide * kept_rows, 128), F32),
        scratch_shapes=[
            pltpu.VMEM((narrow, rows, 128), F32),
            pltpu.VMEM((wide, rows, 128), F32),
            pltpu.SemaphoreType.DMA((count,)),
            pltpu.SemaphoreType.DMA((count,)),
        ],
        compiler_params=pltpu.CompilerParams(collective_id=collective_id, has_side_effects=True),
    )(joined)
    total = out[:, :sum_rows, :].reshape(-1)[: summed.size]
    groups = out[:, sum_rows:, :].reshape(narrow, wide, kept_rows * 128).transpose(1, 0, 2)
    return total, groups.reshape(wide, -1)[:, : kept.size]


def exchange(blocks, axis):
    return lax.all_to_all(blocks, axis, 0, 0, tiled=True)


def core_swap(value):
    return lax.ppermute(value, "core", [(0, 1), (1, 0)])


def by_core(low, high):
    first = lax.axis_index("core") == 0
    return jnp.where(first, low, high), jnp.where(first, high, low)


def in_core_order(own, other):
    first = lax.axis_index("core") == 0
    return jnp.where(first, own, other), jnp.where(first, other, own)


def chip_sum(own_left, other_left, right):
    came = core_swap(outer_sum(other_left, right).astype(BF16))
    return (outer_sum(own_left, right) + came.astype(F32)).astype(BF16)


def fsdp_sum(both):
    return lax.psum_scatter(both, "fsdp", scatter_dimension=0, tiled=True)


def z_pieces(blocks, deep):
    me = lax.axis_index("z")
    return [lax.dynamic_index_in_dim(blocks, me, 0, keepdims=False)] + [
        lax.ppermute(
            lax.dynamic_index_in_dim(blocks, me ^ step, 0, keepdims=False), "z", [(i, i ^ step) for i in range(deep)]
        )
        for step in range(1, deep)
    ]


def added(pieces):
    return functools.reduce(jnp.add, [piece.astype(F32) for piece in pieces])


def to_all(block, narrow):
    return [
        lax.ppermute(block, "fsdp", [(i, i ^ step) for i in range(narrow)]) for step in range(1, narrow)
    ]


def in_order(block, came):
    me = lax.axis_index("fsdp")
    narrow = len(came) + 1
    result = lax.dynamic_update_slice_in_dim(
        jnp.zeros((narrow,) + block.shape, block.dtype), block[None], me, 0
    )
    for step in range(1, narrow):
        result = lax.dynamic_update_slice_in_dim(result, came[step - 1][None], me ^ step, 0)
    return result


def device_columns(value, deep, narrow):
    rows, width = value.shape
    block = width // (2 * deep * narrow)
    core = lax.axis_index("core")
    target = jnp.arange(width, dtype=jnp.int32)
    c, f, z, r = (
        target // (narrow * deep * block), target // (deep * block) % narrow, target // block % deep, target % block,
    )
    c = (c + core) % 2
    source = ((z * 2 + c) * narrow + f) * block + r
    pick = (jnp.arange(width, dtype=jnp.int32)[:, None] == source[None, :]).astype(BF16)
    moved = low_product(value, pick).astype(BF16)
    return moved[:, : width // 2], moved[:, width // 2 :]


def whole_weight(shard):
    rows = shard.shape[0] // 2
    half = lax.dynamic_slice_in_dim(shard, lax.axis_index("core") * rows, rows, 0)
    return lax.all_gather(half, ("fsdp", "core"), axis=0, tiled=True)


def shards(
    tokens,
    cotangent,
    text_states,
    conditioning,
    image_sizes,
    ada_weight,
    ada_bias,
    qkv_weight,
    out_weight,
    text_weight,
    gate_up_weight,
    down_weight,
    norm_gains,
    norm_shifts,
    text_gain,
    head_gate,
):
    model_width = tokens.shape[2]
    head_count = head_gate.shape[0]
    head_dim = model_width // head_count
    image_count = text_states.shape[1]
    caption_local = text_states.shape[2]
    caption_width = text_states.shape[3]
    local_tok = tokens.shape[1]
    deep = lax.axis_size("z")
    narrow = lax.axis_size("fsdp")
    wide = 2 * deep
    me = lax.axis_index("fsdp")
    group_tok = local_tok * narrow
    caption_full = caption_local * narrow
    score_scale = head_dim ** (-0.5)
    text_total = image_count * caption_full
    text_local = image_count * caption_local
    part = model_width // narrow
    part_pad = round_up(part, 128)
    heads_here = head_count // narrow
    pairs = part_pad // 128
    halves = 128 // head_dim

    group_sizes = image_sizes[0]
    position = me * local_tok + jnp.arange(local_tok, dtype=jnp.int32)
    image_index = token_layout(group_sizes, position, image_count)[0]
    key_image, key_row, key_col = token_layout(
        group_sizes, jnp.arange(group_tok, dtype=jnp.int32), image_count
    )
    member = [(image_index == i).astype(F32)[:, None] for i in range(image_count)]
    cosine, sine = rope_tables(key_row, key_col, head_dim)

    cond_low = jax.nn.silu(conditioning[0].astype(F32)).astype(BF16)
    cond_rows = ada_weight.shape[0]
    cond_part = lax.dynamic_slice_in_dim(cond_low, me * cond_rows, cond_rows, 1)
    modulation_part = low_product(cond_part, ada_weight)
    modulation = (
        jnp.sum(fsdp_share(modulation_part.reshape(-1, 128), narrow, 0), axis=0).reshape(modulation_part.shape)
        + ada_bias
    )

    def per_token(index):
        rows = modulation[:, index * model_width : (index + 1) * model_width]
        return functools.reduce(
            jnp.add, [member[i] * rows[i : i + 1, :] for i in range(image_count)]
        )

    def per_image(value):
        return jnp.stack([jnp.sum(member[i] * value, axis=0) for i in range(image_count)])

    token_in = tokens[0].astype(F32)
    token_inverse = inverse_rms(token_in)
    tokens_all = lax.all_gather(tokens[0], "fsdp", axis=0, tiled=True)
    def widened(value, slots):
        if part == part_pad:
            return value
        lead = value.shape[:-1]
        value = value.reshape(*lead, slots, part)
        pads = [(0, 0)] * (len(lead) + 1) + [(0, part_pad - part)]
        return jnp.pad(value, pads).reshape(*lead, slots * part_pad)

    def narrowed(value, slots):
        if part == part_pad:
            return value
        lead = value.shape[:-1]
        return value.reshape(*lead, slots, part_pad)[..., :part].reshape(*lead, slots * part)

    def own_columns(value):
        return widened(lax.dynamic_slice_in_dim(value, me * part, part, value.ndim - 1), 1)

    qkv_rows = qkv_weight.shape[0] // 2
    qkv_half = lax.dynamic_slice_in_dim(qkv_weight, lax.axis_index("core") * qkv_rows, qkv_rows, 0)
    qkv_half = exchange(
        qkv_half.reshape(qkv_rows, 3, narrow, part).transpose(2, 0, 1, 3).reshape(narrow, qkv_rows, 3 * part), "fsdp"
    )
    own_qkv = widened(
        jnp.concatenate(in_core_order(qkv_half, core_swap(qkv_half)), axis=1).reshape(model_width, 3 * part), 3
    )

    full_out = whole_weight(out_weight)
    full_gate_up = whole_weight(gate_up_weight)
    full_down = whole_weight(down_weight)

    text_in = text_states[0].astype(F32).reshape(text_local, caption_width)
    text_inverse = inverse_rms(text_in)
    text_low = (text_in * text_inverse * text_gain).astype(BF16)
    text_cols = caption_width // narrow
    text_slice = (
        exchange(text_low.reshape(text_local, narrow, text_cols).transpose(1, 0, 2), "fsdp")
        .reshape(narrow, image_count, caption_local, text_cols)
        .transpose(1, 0, 2, 3)
        .reshape(text_total, text_cols)
    )
    own_text_weight = (
        text_weight.reshape(text_cols, 2, narrow, part).transpose(2, 0, 1, 3).reshape(narrow, text_cols, 2 * part)
    )
    text_partial = jnp.stack([low_product(text_slice, own_text_weight[i]).astype(BF16) for i in range(narrow)])
    text_partial, tokens_all = lax.optimization_barrier((text_partial, tokens_all))
    text_projected = widened(jnp.sum(exchange(text_partial, "fsdp").astype(F32), axis=0), 2)
    text_parts = fsdp_share(column_stats(text_projected, part, part_pad, 1), narrow, 1)
    text_means = text_parts[:, 0, :]
    text_mean = jnp.mean(text_means, axis=0)
    text_square = jnp.sum(text_parts[:, 1, :], axis=0) + part * jnp.sum((text_means - text_mean) ** 2, axis=0)
    text_key_inverse = lax.rsqrt(text_square / model_width + EPS)[:, None]
    text_unit = (text_projected[:, :part_pad] - text_mean[:, None]) * text_key_inverse
    text_gains = own_columns(norm_gains[4])
    text_packed = jnp.concatenate(
        [(text_unit * text_gains).astype(BF16), text_projected[:, part_pad:].astype(BF16)], axis=1
    )

    wide_tokens = tokens_all.astype(F32)
    wide_scale = functools.reduce(
        jnp.add,
        [(key_image == i).astype(F32)[:, None] * modulation[i : i + 1, :model_width] for i in range(image_count)],
    )
    normed_all = (wide_tokens * inverse_rms(wide_tokens) * norm_gains[0] * (1.0 + wide_scale)).astype(BF16)

    projected = low_product(normed_all, own_qkv)
    stats_all = fsdp_share(column_stats(projected, part, part_pad, 2), narrow, 2)
    head_gains = own_columns(norm_gains[2:4])
    packed = make_heads(
        projected, stats_all, cosine, sine, head_gains, own_columns(norm_shifts), part, score_scale * LOG2E
    )
    gate_tanh = jnp.tanh(head_gate)
    own_gates = lax.dynamic_slice_in_dim(gate_tanh, me * heads_here, heads_here, 0)
    own_gates = jnp.concatenate([own_gates, jnp.ones((pairs * halves - heads_here,), F32)])
    column = key_image[:, None]
    row = key_image[None, :]
    attended = [
        attend(pair, own_gates, packed, text_packed, column, row, head_dim, image_count) for pair in range(pairs)
    ]
    mixed_pairs = [exchange(one[0].reshape(narrow, local_tok, 128), "fsdp") for one in attended]
    self_outs = [one[1] for one in attended]
    cross_outs = [one[2] for one in attended]
    stats = [one[3] for one in attended]
    mixed_low = (
        narrowed(jnp.concatenate(mixed_pairs, axis=2), 1).transpose(1, 0, 2).reshape(local_tok, model_width)
    )

    branch = low_product(mixed_low, full_out)
    branch_inverse = inverse_rms(branch)
    branch_unit = branch * branch_inverse
    gate_attend = jnp.tanh(per_token(1))
    hidden = token_in + gate_attend * (branch_unit * norm_gains[1])
    hidden_inverse = inverse_rms(hidden)
    hidden_unit = hidden * hidden_inverse
    scale_feed = 1.0 + per_token(2)
    normed_feed_low = (hidden_unit * norm_gains[5] * scale_feed).astype(BF16)
    gate_up = low_product(normed_feed_low, full_gate_up)
    hidden_units = gate_up.shape[1] // 2
    gate_half = gate_up[:, :hidden_units]
    up_half = gate_up[:, hidden_units:]
    sigmoid = jax.nn.sigmoid(gate_half)
    if hidden_units // (wide * narrow) % 128 == 0:
        activated_low, moved = swiglu(gate_up, lax.axis_index("core"), deep, narrow)
        down_columns = (moved[:, : hidden_units // 2], moved[:, hidden_units // 2 :])
    else:
        activated_low = (gate_half * sigmoid * up_half).astype(BF16)
        down_columns = device_columns(activated_low, deep, narrow)
    down_out = low_product(activated_low, full_down)
    down_inverse = inverse_rms(down_out)
    down_unit = down_out * down_inverse
    gate_feed = jnp.tanh(per_token(3))
    down_normed = down_unit * norm_gains[6]
    result = (hidden + gate_feed * down_normed).astype(BF16)

    grad_result = cotangent[0].astype(F32)
    grad_down_y = grad_result * gate_feed
    grad_gain_six = jnp.sum(grad_down_y * down_unit, axis=0)
    grad_gate_feed = per_image(grad_result * down_normed * (1.0 - gate_feed * gate_feed))
    grad_down_low = norm_pull(grad_down_y * norm_gains[6], down_unit, down_inverse).astype(BF16)
    grad_activated = times_transposed(grad_down_low, full_down)
    grad_gate_up_low = jnp.concatenate(
        [
            (grad_activated * up_half * sigmoid * (1.0 + gate_half * (1.0 - sigmoid))).astype(BF16),
            (grad_activated * gate_half * sigmoid).astype(BF16),
        ],
        axis=1,
    )
    grad_normed_feed = times_transposed(grad_gate_up_low, full_gate_up)
    grad_feed_y = grad_normed_feed * scale_feed
    grad_gain_five = jnp.sum(grad_feed_y * hidden_unit, axis=0)
    grad_scale_feed = per_image(grad_normed_feed * hidden_unit * norm_gains[5])
    grad_hidden = grad_result + norm_pull(grad_feed_y * norm_gains[5], hidden_unit, hidden_inverse)
    grad_branch_y = grad_hidden * gate_attend
    grad_gain_one = jnp.sum(grad_branch_y * branch_unit, axis=0)
    grad_gate_attend = per_image(
        grad_hidden * branch_unit * norm_gains[1] * (1.0 - gate_attend * gate_attend)
    )
    grad_branch_low = norm_pull(grad_branch_y * norm_gains[1], branch_unit, branch_inverse).astype(BF16)
    grad_mixed = times_transposed(grad_branch_low, full_out).astype(BF16)
    grad_blocks = widened(grad_mixed.reshape(local_tok, narrow, part).transpose(1, 0, 2), 1)
    grad_heads = exchange(grad_blocks, "fsdp").reshape(group_tok, part_pad)
    def by_z(value):
        return value.reshape(deep, -1, value.shape[1])

    down_both = chip_sum(*down_columns, grad_down_low)
    gate_up_both = chip_sum(*device_columns(normed_feed_low, deep, narrow), grad_gate_up_low)
    out_both = chip_sum(*device_columns(mixed_low, deep, narrow), grad_branch_low)
    down_part = fsdp_sum(down_both)
    grad_heads, gate_up_both, out_both, down_part = lax.optimization_barrier(
        (grad_heads, gate_up_both, out_both, down_part)
    )
    came_downs = exchange(by_z(down_part), "z")
    gate_up_part = fsdp_sum(gate_up_both)
    out_part = fsdp_sum(out_both)
    crossed = [
        cross_back(
            pair, own_gates, packed, text_packed, row, grad_heads, cross_outs[pair], stats[pair],
            head_dim, image_count, score_scale,
        )
        for pair in range(pairs)
    ]
    dtk = jnp.concatenate([one[1] for one in crossed], axis=1)
    dtv = jnp.concatenate([one[2] for one in crossed], axis=1)
    gate_sums = jnp.stack([one[3] for one in crossed])

    grad_text_keys = dtk.astype(F32)
    own_gain_four = jnp.sum(grad_text_keys * text_unit, axis=0)
    grad_text_unit = grad_text_keys * text_gains
    text_sums = jnp.stack([jnp.sum(grad_text_unit, axis=1), jnp.sum(grad_text_unit * text_unit, axis=1)])
    text_sums = jnp.sum(
        fsdp_share(jnp.pad(text_sums, ((0, 6), (0, 0))), narrow, 3), axis=0
    ) * (1.0 / model_width)
    grad_text_key_in = (grad_text_unit - text_sums[0][:, None] - text_unit * text_sums[1][:, None]) * text_key_inverse
    grad_text_own = jnp.concatenate(
        [narrowed(grad_text_key_in.astype(BF16), 1), narrowed(dtv, 1)], axis=1
    )
    def self_pair(pair):
        return self_back(
            pair, packed, column, row, grad_heads, self_outs[pair], stats[pair], crossed[pair][0], head_dim, score_scale
        )

    came_texts = to_all(grad_text_own, narrow)
    backs = [self_pair(0)]
    first, came_downs, *came_texts = lax.optimization_barrier((backs[0][0], came_downs, *came_texts))
    grad_down_weight = jnp.sum(came_downs.astype(F32), axis=0)
    backs[0] = (first, *backs[0][1:])
    grad_text_all = in_order(grad_text_own, came_texts)
    grad_text_columns = (
        grad_text_all.reshape(narrow, text_total, 2, part).transpose(1, 2, 0, 3).reshape(text_total, 2 * model_width)
    )
    text_half = text_cols // 2
    own_text, other_text = by_core(text_slice[:, :text_half], text_slice[:, text_half:])
    came_text = core_swap(outer_sum(other_text, grad_text_columns).astype(BF16))
    text_both = (outer_sum(own_text, grad_text_columns) + came_text.astype(F32)).astype(BF16)
    grad_heads, text_both, first = lax.optimization_barrier((grad_heads, text_both, backs[0][0]))
    backs[0] = (first, *backs[0][1:])
    came_text_z = exchange(by_z(text_both), "z")
    backs.append(self_pair(1))
    if pairs > 2:
        grad_heads, gate_up_part, out_part, second = lax.optimization_barrier(
            (grad_heads, gate_up_part, out_part, backs[1][0])
        )
        backs[1] = (second, *backs[1][1:])
        backs += [self_pair(pair) for pair in range(2, pairs)]
    grad_gate_up_weight = added(z_pieces(by_z(gate_up_part), deep))
    last, came_text_z = lax.optimization_barrier((backs[-1][0], came_text_z))
    backs[-1] = (last, *backs[-1][1:])
    text_part = jnp.sum(came_text_z.astype(F32), axis=0).astype(BF16)
    came_out_z = exchange(by_z(out_part), "z")
    own_gate_grad = jnp.sum(gate_sums[:, 0, :].reshape(pairs * halves, head_dim), axis=1)[:heads_here]
    grad_head_gate = lax.dynamic_update_slice_in_dim(
        jnp.zeros((head_count,), F32), own_gate_grad, me * heads_here, 0
    ) * (1.0 - gate_tanh * gate_tanh)
    grad_projected_low, head_sums = heads_back(
        list(zip(*backs)), projected, stats_all, cosine, sine, head_gains, part,
        lambda value: fsdp_share(value, narrow, 4),
    )
    grad_projected_low, grad_gate_up_weight, came_out_z = lax.optimization_barrier(
        (grad_projected_low, grad_gate_up_weight, came_out_z)
    )
    everyone = ("z", "core", "fsdp")
    grad_text_weight = lax.ppermute(
        text_part,
        everyone,
        [
            ((z * 2 + c) * narrow + f, f * wide + c * deep + z)
            for z in range(deep) for c in range(2) for f in range(narrow)
        ],
    )
    grad_out_weight = jnp.sum(came_out_z.astype(F32), axis=0)
    grad_normed = lax.psum_scatter(
        times_transposed(grad_projected_low, own_qkv).astype(BF16), "fsdp", scatter_dimension=0, tiled=True
    )

    qkv_grad = outer_sum(normed_all, grad_projected_low).astype(BF16).reshape(deep, 2, model_width // wide, 3 * part_pad)
    own_grad, other_grad = by_core(qkv_grad[:, 0], qkv_grad[:, 1])
    own_grad = (own_grad.astype(F32) + core_swap(other_grad).astype(F32)).astype(BF16)
    own_grad, grad_text_columns = lax.optimization_barrier((own_grad, grad_text_columns))
    own_pieces = z_pieces(own_grad, deep)
    grad_text_slice = times_transposed(grad_text_columns, text_weight).astype(BF16)
    came_text = exchange(
            grad_text_slice.reshape(image_count, narrow, caption_local, text_cols)
            .transpose(1, 0, 2, 3)
            .reshape(narrow, text_local, text_cols),
            "fsdp",
        )

    def placed_columns(value):
        return lax.dynamic_update_slice_in_dim(
            jnp.zeros((model_width,), F32), narrowed(value, 1), me * part, 0
        )

    group = lax.axis_index("z") * 2 + lax.axis_index("core")
    later_modulation = jnp.concatenate([grad_gate_attend, grad_scale_feed, grad_gate_feed], axis=1)
    summed = jnp.concatenate(
        [
            grad_gain_one,
            placed_columns(head_sums[0]),
            placed_columns(head_sums[2]),
            placed_columns(own_gain_four),
            grad_gain_five,
            grad_gain_six,
            placed_columns(head_sums[1]),
            placed_columns(head_sums[3]),
            grad_head_gate,
        ]
    )
    kept = jnp.concatenate(
        [later_modulation.reshape(-1), jnp.where(me == 0, cond_low.astype(F32), 0.0).reshape(-1)]
    )
    summed, kept = finish(summed, kept, narrow, wide, 5)
    summed, kept, came_text, grad_text_weight, *own_pieces = lax.optimization_barrier(
        (summed, kept, came_text, grad_text_weight, *own_pieces)
    )
    grad_text_weight = grad_text_weight.astype(F32)
    own_grad = added(own_pieces)
    grad_qkv_weight = (
        exchange(narrowed(own_grad.astype(BF16), 3).reshape(narrow, -1, 3 * part), "fsdp")
        .reshape(narrow, -1, 3, part)
        .transpose(1, 2, 0, 3)
        .reshape(-1, 3 * model_width)
        .astype(F32)
    )

    grad_text_normed = (
        came_text
        .transpose(1, 0, 2)
        .reshape(text_local, caption_width)
        .astype(F32)
    )
    text_state_unit = text_in * text_inverse
    grad_text_gain = jnp.sum(grad_text_normed * text_state_unit, axis=0)
    grad_text = (
        norm_pull(grad_text_normed * text_gain, text_state_unit, text_inverse)
        .astype(BF16)
        .reshape(image_count, caption_local, caption_width)
    )

    every_image = wide * image_count
    ada_rows = cond_rows // wide
    slots = kept[:, : later_modulation.size].reshape(every_image, later_modulation.shape[1])
    cond_slots = kept[:, later_modulation.size :].reshape(every_image, cond_low.shape[1])
    own_cond = lax.dynamic_slice_in_dim(cond_slots, (group * narrow + me) * ada_rows, ada_rows, 1)
    ada_later = exact_outer(own_cond, slots)
    grad_normed, ada_later, own_cond = lax.optimization_barrier((grad_normed, ada_later, own_cond))
    grad_normed = grad_normed.astype(F32)

    token_unit = token_in * token_inverse
    scale_attend = 1.0 + per_token(0)
    grad_normed_y = grad_normed * scale_attend
    grad_gain_zero = jnp.sum(grad_normed_y * token_unit, axis=0)
    grad_scale_attend = per_image(grad_normed * token_unit * norm_gains[0])
    grad_tokens = (
        grad_hidden + norm_pull(grad_normed_y * norm_gains[0], token_unit, token_inverse)
    ).astype(BF16)
    last_sums, first_slots = finish(
        jnp.concatenate([grad_gain_zero, grad_text_gain]), grad_scale_attend.reshape(-1), narrow, wide, 6
    )
    grad_text_gain = last_sums[model_width:]
    first_slots = first_slots.reshape(every_image, model_width)
    grad_ada_weight = jnp.concatenate([exact_outer(own_cond, first_slots), ada_later], axis=1)
    grad_ada_bias = jnp.concatenate([jnp.sum(first_slots, axis=0), jnp.sum(slots, axis=0)])
    gain_count = norm_gains.size - model_width
    shift_end = gain_count + norm_shifts.size
    grad_gains = jnp.concatenate([last_sums[:model_width], summed[:gain_count]]).reshape(norm_gains.shape)
    grad_shifts = summed[gain_count:shift_end].reshape(norm_shifts.shape)
    grad_head_gate = summed[shift_end:]
    return (
        result[None],
        grad_tokens[None],
        grad_text[None],
        grad_ada_weight,
        grad_qkv_weight,
        grad_out_weight,
        grad_text_weight,
        grad_gate_up_weight,
        grad_down_weight,
        grad_ada_bias,
        grad_gains,
        grad_shifts,
        grad_text_gain,
        grad_head_gate,
    )


def solution(mesh):
    wide, narrow = mesh.devices.shape
    fine = Mesh(mesh.devices.reshape(wide // 2, 2, narrow), ("z", "core", "fsdp"))
    groups = ("z", "core")
    every = ("z", "core", "fsdp")
    placed = (
        P(groups, "fsdp", None),
        P(groups, "fsdp", None),
        P(groups, None, "fsdp", None),
        P(groups, None, None),
        P(groups, None, None),
        P("fsdp", None),
        P(),
        P("fsdp", None),
        P("fsdp", None),
        P("fsdp", None),
        P("fsdp", None),
        P("fsdp", None),
        P(),
        P(),
        P(),
        P(),
    )
    return jax.shard_map(
        shards,
        mesh=fine,
        in_specs=placed,
        out_specs=(
            P(groups, "fsdp", None),
            P(groups, "fsdp", None),
            P(groups, None, "fsdp", None),
            P(every, None),
            P(every, None),
            P(every, None),
            P(every, None),
            P(every, None),
            P(every, None),
            P(),
            P(),
            P(),
            P(),
            P(),
        ),
        check_vma=False,
    )
```

```python
import functools

import jax
import jax.numpy as jnp
from jax import lax
from jax.experimental import pallas as pl
from jax.experimental.pallas import tpu as pltpu
from jax.sharding import Mesh
from jax.sharding import PartitionSpec as P

EPS = 1e-05
HIGHEST_PRECISION = lax.Precision.HIGHEST
MASKED = -1e30
LOG2E = 1.4426950408889634
FIRST_PATCHES = 16 * 12**2
FIRST_MOST = FIRST_PATCHES + 96
QBLOCK = 256
BF16 = jnp.bfloat16
F32 = jnp.float32
VMEM_LIMIT = 60 * 1024 * 1024


def round_up(value, step):
    return -(-value // step) * step


def low_product(left, right):
    return jnp.dot(left, right, preferred_element_type=F32)


def times_transposed(left, right):
    return lax.dot_general(left, right, (((1,), (1,)), ((), ())), preferred_element_type=F32)


def outer_sum(left, right):
    return lax.dot_general(left, right, (((0,), (0,)), ((), ())), preferred_element_type=F32)


def exact_outer(left, right):
    return lax.dot_general(
        left, right, (((0,), (0,)), ((), ())), precision=HIGHEST_PRECISION, preferred_element_type=F32
    )


def exact_transposed(left, right):
    return lax.dot_general(
        left, right, (((1,), (1,)), ((), ())), precision=HIGHEST_PRECISION, preferred_element_type=F32
    )


def row_mean(value):
    return jnp.mean(value, axis=-1, keepdims=True)


def inverse_rms(value):
    return lax.rsqrt(row_mean(value * value) + EPS)


def norm_pull(grad, unit, inverse):
    return (grad - unit * row_mean(grad * unit)) * inverse


def token_layout(image_sizes, position, image_count):
    start = jnp.int32(0)
    image_index = jnp.full(position.shape, image_count, jnp.int32)
    token_row = jnp.zeros(position.shape, jnp.int32)
    token_col = jnp.zeros(position.shape, jnp.int32)
    for i in range(image_count):
        width = image_sizes[i, 1] + 1
        end = start + image_sizes[i, 0] * width
        inside = (position >= start) & (position < end)
        offset = position - start
        image_index = jnp.where(inside, i, image_index)
        token_row = jnp.where(inside, offset // width, token_row)
        token_col = jnp.where(inside, offset % width, token_col)
        start = end
    return image_index, token_row, token_col


def rope_tables(token_row, token_col, head_dim):
    quarter = head_dim // 4
    pair = (jnp.arange(128, dtype=jnp.int32) % head_dim) // 2
    frequency = 10000.0 ** (-(pair % quarter).astype(F32) / quarter)
    place = jnp.where(
        (pair < quarter)[None, :], token_row.astype(F32)[:, None], token_col.astype(F32)[:, None]
    )
    angles = place * frequency[None, :]
    even = (jnp.arange(128, dtype=jnp.int32) % 2 == 0)[None, :]
    return jnp.cos(angles), jnp.where(even, -jnp.sin(angles), jnp.sin(angles))


def swap_pairs(value):
    width = value.shape[1]
    even = lax.broadcasted_iota(jnp.int32, value.shape, 1) % 2 == 0
    return jnp.where(even, pltpu.roll(value, width - 1, 1), pltpu.roll(value, 1, 1))


def wide_table(table, width):
    return jnp.concatenate([table] * (width // table.shape[1]), axis=1)


def pack_columns(columns):
    rows = columns[0].shape[0]
    lane = lax.broadcasted_iota(jnp.int32, (rows, 128), 1)
    packed = jnp.zeros((rows, 128), F32)
    for i, column in enumerate(columns):
        packed = jnp.where(lane == i, column, packed)
    return jnp.transpose(packed)[:8, :]


def as_columns(rows_list):
    width = rows_list[0].shape[1]
    stacked = jnp.concatenate(
        rows_list + [jnp.zeros((128 - len(rows_list), width), F32)], axis=0
    )
    return jnp.transpose(stacked)


def real_lanes(shape, part):
    return lax.broadcasted_iota(jnp.int32, shape, 1) < part


def own_stats(value, part):
    mean = jnp.sum(value, axis=1, keepdims=True) * (1.0 / part)
    centred = value - mean
    if value.shape[1] != part:
        centred = jnp.where(real_lanes(value.shape, part), centred, 0.0)
    return mean, jnp.sum(centred * centred, axis=1, keepdims=True)


def joined_stats(stats_ref, part, slot):
    narrow = stats_ref.shape[0]
    means = [stats_ref[i, 2 * slot : 2 * slot + 1, :] for i in range(narrow)]
    squares = [stats_ref[i, 2 * slot + 1 : 2 * slot + 2, :] for i in range(narrow)]
    mean = functools.reduce(jnp.add, means) * (1.0 / narrow)
    square = functools.reduce(jnp.add, squares)
    square = square + part * functools.reduce(jnp.add, [(m - mean) * (m - mean) for m in means])
    return mean, lax.rsqrt(square * (1.0 / (narrow * part)) + EPS)


def stats_kernel(part, slots, projected_ref, out_ref):
    padded = projected_ref.shape[1] // slots
    columns = []
    for slot in range(slots):
        columns += own_stats(projected_ref[:, slot * padded : (slot + 1) * padded], part)
    out_ref[...] = pack_columns(columns)


def column_stats(projected, part, padded, slots):
    rows = projected.shape[0]
    return pl.pallas_call(
        functools.partial(stats_kernel, part, slots),
        grid=(pl.cdiv(rows, QBLOCK),),
        in_specs=[pl.BlockSpec((QBLOCK, slots * padded), lambda i: (i, 0))],
        out_specs=pl.BlockSpec((8, QBLOCK), lambda i: (0, i)),
        out_shape=jax.ShapeDtypeStruct((8, rows), F32),
        compiler_params=pltpu.CompilerParams(vmem_limit_bytes=VMEM_LIMIT),
        cost_estimate=pl.CostEstimate(flops=10 * rows * slots * padded, bytes_accessed=4 * rows * slots * padded, transcendentals=0),
    )(projected)


def heads_kernel(part, query_scale, projected_ref, stats_ref, cos_ref, sin_ref, gains_ref, shifts_ref, out_ref):
    padded = projected_ref.shape[1] // 3
    cosine = wide_table(cos_ref[...], padded)
    sine = wide_table(sin_ref[...], padded)
    columns = as_columns([*joined_stats(stats_ref, part, 0), *joined_stats(stats_ref, part, 1)])
    for slot in range(3):
        place = slice(slot * padded, (slot + 1) * padded)
        value = projected_ref[:, place]
        if slot < 2:
            value = (value - columns[:, 2 * slot : 2 * slot + 1]) * columns[:, 2 * slot + 1 : 2 * slot + 2]
            value = value * gains_ref[slot : slot + 1, :] + shifts_ref[slot : slot + 1, :]
            value = value * cosine + swap_pairs(value) * sine
            if slot == 0:
                value = value * query_scale
        out_ref[:, place] = value.astype(BF16)


def make_heads(projected, stats, cosine, sine, gains, shifts, part, query_scale):
    rows, triple = projected.shape
    padded = triple // 3
    narrow = stats.shape[0]
    return pl.pallas_call(
        functools.partial(heads_kernel, part, query_scale),
        grid=(pl.cdiv(rows, QBLOCK),),
        in_specs=[
            pl.BlockSpec((QBLOCK, triple), lambda i: (i, 0)),
            pl.BlockSpec((narrow, 8, QBLOCK), lambda i: (0, 0, i)),
            pl.BlockSpec((QBLOCK, 128), lambda i: (i, 0)),
            pl.BlockSpec((QBLOCK, 128), lambda i: (i, 0)),
            pl.BlockSpec((2, padded), lambda i: (0, 0)),
            pl.BlockSpec((2, padded), lambda i: (0, 0)),
        ],
        out_specs=pl.BlockSpec((QBLOCK, triple), lambda i: (i, 0)),
        out_shape=jax.ShapeDtypeStruct((rows, triple), BF16),
        compiler_params=pltpu.CompilerParams(vmem_limit_bytes=VMEM_LIMIT),
        cost_estimate=pl.CostEstimate(flops=40 * rows * triple, bytes_accessed=6 * rows * triple, transcendentals=0),
    )(projected, stats, cosine, sine, gains, shifts)


def turned_back(refs, cosine, sine):
    grad = jnp.concatenate([ref[...].astype(F32) for ref in refs], axis=1)
    return grad * cosine - swap_pairs(grad) * sine


def grad_stats_kernel(rows, part, pairs, *refs):
    dq_refs, dk_refs = refs[:pairs], refs[pairs : 2 * pairs]
    projected_ref, stats_ref, cos_ref, sin_ref, gains_ref, out_ref, sums_ref = refs[2 * pairs :]
    step = pl.program_id(0)
    padded = 128 * pairs
    cosine = wide_table(cos_ref[...], padded)
    sine = wide_table(sin_ref[...], padded)
    height = cos_ref.shape[0]
    inside = step * height + lax.broadcasted_iota(jnp.int32, (height, 1), 0) < rows

    @pl.when(step == 0)
    def _():
        sums_ref[...] = jnp.zeros_like(sums_ref)

    columns = as_columns([*joined_stats(stats_ref, part, 0), *joined_stats(stats_ref, part, 1)])
    packed = []
    for slot, grads in enumerate((dq_refs, dk_refs)):
        grad = jnp.where(inside, turned_back(grads, cosine, sine), 0.0)
        unit = (projected_ref[:, slot * padded : (slot + 1) * padded] - columns[:, 2 * slot : 2 * slot + 1])
        unit = jnp.where(inside, unit * columns[:, 2 * slot + 1 : 2 * slot + 2], 0.0)
        both = grad * unit
        sums_ref[2 * slot : 2 * slot + 1, :] += jnp.sum(both, axis=0, keepdims=True)
        sums_ref[2 * slot + 1 : 2 * slot + 2, :] += jnp.sum(grad, axis=0, keepdims=True)
        gain = gains_ref[slot : slot + 1, :]
        packed.append(jnp.sum(grad * gain, axis=1, keepdims=True))
        packed.append(jnp.sum(both * gain, axis=1, keepdims=True))
    out_ref[...] = pack_columns(packed)


def heads_back_kernel(part, pairs, *refs):
    dq_refs, dk_refs, dv_refs = refs[:pairs], refs[pairs : 2 * pairs], refs[2 * pairs : 3 * pairs]
    projected_ref, stats_ref, totals_ref, cos_ref, sin_ref, gains_ref, out_ref = refs[3 * pairs :]
    padded = 128 * pairs
    narrow = stats_ref.shape[0]
    cosine = wide_table(cos_ref[...], padded)
    sine = wide_table(sin_ref[...], padded)
    means = [
        functools.reduce(jnp.add, [totals_ref[i, j : j + 1, :] for i in range(narrow)]) * (1.0 / (narrow * part))
        for j in range(4)
    ]
    columns = as_columns([*joined_stats(stats_ref, part, 0), *joined_stats(stats_ref, part, 1), *means])
    for slot, grads in enumerate((dq_refs, dk_refs)):
        grad = turned_back(grads, cosine, sine) * gains_ref[slot : slot + 1, :]
        inverse = columns[:, 2 * slot + 1 : 2 * slot + 2]
        unit = (projected_ref[:, slot * padded : (slot + 1) * padded] - columns[:, 2 * slot : 2 * slot + 1]) * inverse
        grad = grad - columns[:, 4 + 2 * slot : 5 + 2 * slot] - unit * columns[:, 5 + 2 * slot : 6 + 2 * slot]
        grad = grad * inverse
        if padded != part:
            grad = jnp.where(real_lanes(grad.shape, part), grad, 0.0)
        out_ref[:, slot * padded : (slot + 1) * padded] = grad.astype(BF16)
    for pair, ref in enumerate(dv_refs):
        out_ref[:, 2 * padded + 128 * pair : 2 * padded + 128 * (pair + 1)] = ref[...]


def heads_back(grads, projected, stats, cosine, sine, gains, part, share):
    rows, triple = projected.shape
    padded = triple // 3
    pairs = padded // 128
    narrow = stats.shape[0]
    pair_spec = pl.BlockSpec((QBLOCK, 128), lambda i: (i, 0))
    two_spec = pl.BlockSpec((QBLOCK, 2 * padded), lambda i: (i, 0))
    stat_spec = pl.BlockSpec((narrow, 8, QBLOCK), lambda i: (0, 0, i))
    gain_spec = pl.BlockSpec((2, padded), lambda i: (0, 0))
    own, sums = pl.pallas_call(
        functools.partial(grad_stats_kernel, rows, part, pairs),
        grid=(pl.cdiv(rows, QBLOCK),),
        in_specs=[pair_spec] * (2 * pairs) + [two_spec, stat_spec, pair_spec, pair_spec, gain_spec],
        out_specs=[
            pl.BlockSpec((8, QBLOCK), lambda i: (0, i)),
            pl.BlockSpec((8, padded), lambda i: (0, 0)),
        ],
        out_shape=[jax.ShapeDtypeStruct((8, rows), F32), jax.ShapeDtypeStruct((8, padded), F32)],
        compiler_params=pltpu.CompilerParams(vmem_limit_bytes=VMEM_LIMIT),
        cost_estimate=pl.CostEstimate(flops=40 * rows * triple, bytes_accessed=5 * rows * triple, transcendentals=0),
    )(*grads[0], *grads[1], projected, stats, cosine, sine, gains)
    totals = share(own)
    out = pl.pallas_call(
        functools.partial(heads_back_kernel, part, pairs),
        grid=(pl.cdiv(rows, QBLOCK),),
        in_specs=[pair_spec] * (3 * pairs) + [two_spec, stat_spec, stat_spec, pair_spec, pair_spec, gain_spec],
        out_specs=pl.BlockSpec((QBLOCK, triple), lambda i: (i, 0)),
        out_shape=jax.ShapeDtypeStruct((rows, triple), BF16),
        compiler_params=pltpu.CompilerParams(vmem_limit_bytes=VMEM_LIMIT),
        cost_estimate=pl.CostEstimate(flops=40 * rows * triple, bytes_accessed=7 * rows * triple, transcendentals=0),
    )(*grads[0], *grads[1], *grads[2], projected, stats, totals, cosine, sine, gains)
    return out, sums


def head_lanes(rows, half, head_dim):
    lane = lax.broadcasted_iota(jnp.int32, (rows, 128), 1)
    return (lane >= half * head_dim) & (lane < (half + 1) * head_dim)


def softmax_product(pieces):
    maximum = functools.reduce(jnp.maximum, [jnp.max(s, axis=1, keepdims=True) for s, _ in pieces])
    total, result = 0.0, 0.0
    for scores, values in pieces:
        weight = jnp.exp2(scores - maximum)
        total = total + jnp.sum(weight, axis=1, keepdims=True)
        result = result + low_product(weight.astype(BF16), values)
    return result * (1.0 / total), maximum + jnp.log2(total)


def attend_kernel(
    head_dim, first, most, caption, image_count,
    gate_ref, q_ref, k_ref, v_ref, tk_ref, tv_ref, column_ref, row_ref,
    mixed_ref, self_ref, cross_ref, stats_ref,
):
    count = q_ref.shape[0]
    halves = 128 // head_dim

    def emit(at, rows, outs):
        lanes = [head_lanes(rows, half, head_dim) for half in range(halves)]
        own, cross, gated = 0.0, 0.0, 0.0
        columns = []
        for half, (own_out, own_total, cross_out, cross_total) in enumerate(outs):
            gate = gate_ref[0, half]
            own = own + jnp.where(lanes[half], own_out, 0.0)
            cross = cross + jnp.where(lanes[half], cross_out, 0.0)
            gated = gated + jnp.where(lanes[half], gate * cross_out, 0.0)
            columns += [own_total, cross_total]
        self_ref[pl.ds(at, rows), :] = own
        cross_ref[pl.ds(at, rows), :] = cross
        mixed_ref[pl.ds(at, rows), :] = (own + gated).astype(BF16)
        lane = lax.broadcasted_iota(jnp.int32, (rows, 128), 1)
        packed = jnp.zeros((rows, 128), F32)
        for i, column in enumerate(columns):
            packed = jnp.where(lane == i, column, packed)
        stats_ref[:, pl.ds(at, rows)] = jnp.transpose(packed)[:8, :]

    def clean(block, carry):
        at = pl.multiple_of(block * QBLOCK, QBLOCK)
        queries = q_ref[pl.ds(at, QBLOCK), :]
        outs = []
        for half in range(halves):
            q = jnp.where(head_lanes(QBLOCK, half, head_dim), queries, jnp.zeros_like(queries))
            bias = jnp.where(row_ref[0:1, first:most] == 0, 0.0, MASKED)
            own_out, own_total = softmax_product([
                (times_transposed(q, k_ref[0:first, :]), v_ref[0:first, :]),
                (times_transposed(q, k_ref[first:most, :]) + bias, v_ref[first:most, :]),
            ])
            cross_out, cross_total = softmax_product(
                [(times_transposed(q, tk_ref[0:caption, :]), tv_ref[0:caption, :])]
            )
            outs.append((own_out, own_total, cross_out, cross_total))
        emit(at, QBLOCK, outs)
        return carry

    lax.fori_loop(0, first // QBLOCK, clean, 0)
    rest = count - first
    queries = q_ref[first:count, :]
    image = column_ref[first:count, :]
    outs = []
    for half in range(halves):
        q = jnp.where(head_lanes(rest, half, head_dim), queries, jnp.zeros_like(queries))
        own_out, own_total = softmax_product([
            (jnp.where(image == row_ref[0:1, :], times_transposed(q, k_ref[...]), MASKED), v_ref[...])
        ])
        scores = times_transposed(q, tk_ref[...])
        owner = lax.broadcasted_iota(jnp.int32, (1, scores.shape[1]), 1) // caption
        scores = jnp.where((image == owner) | (image == image_count), scores, MASKED)
        cross_out, cross_total = softmax_product([(scores, tv_ref[...])])
        outs.append((own_out, own_total, cross_out, cross_total))
    emit(first, rest, outs)


def attend(pair, gates, packed, text_packed, column, row, head_dim, image_count):
    count, texts = packed.shape[0], text_packed.shape[0]
    pairs = packed.shape[1] // 384
    halves = 128 // head_dim
    out = pl.BlockSpec((count, 128), lambda i: (0, 0))
    most = min(round_up(FIRST_MOST, 128), count)
    flops = 4 * count * (count + texts) * 128
    return pl.pallas_call(
        functools.partial(
            attend_kernel, head_dim, FIRST_PATCHES, most, texts // image_count, image_count
        ),
        grid=(1,),
        in_specs=[
            pl.BlockSpec((None, 1, halves), lambda i: (pair, 0, 0), memory_space=pltpu.SMEM),
            pl.BlockSpec((count, 128), lambda i: (0, pair)),
            pl.BlockSpec((count, 128), lambda i: (0, pairs + pair)),
            pl.BlockSpec((count, 128), lambda i: (0, 2 * pairs + pair)),
            pl.BlockSpec((texts, 128), lambda i: (0, pair)),
            pl.BlockSpec((texts, 128), lambda i: (0, pairs + pair)),
            pl.BlockSpec((count, 1), lambda i: (0, 0)),
            pl.BlockSpec((1, count), lambda i: (0, 0)),
        ],
        out_specs=[out, out, out, pl.BlockSpec((8, count), lambda i: (0, 0))],
        out_shape=[
            jax.ShapeDtypeStruct((count, 128), BF16),
            jax.ShapeDtypeStruct((count, 128), F32),
            jax.ShapeDtypeStruct((count, 128), F32),
            jax.ShapeDtypeStruct((8, count), F32),
        ],
        compiler_params=pltpu.CompilerParams(vmem_limit_bytes=VMEM_LIMIT),
        cost_estimate=pl.CostEstimate(flops=flops, bytes_accessed=20 * count * 128, transcendentals=2 * count * count),
    )(gates.reshape(pairs, 1, halves), packed, packed, packed, text_packed, text_packed, column, row)


def gate_lanes(gate_ref, head_dim):
    lane = lax.broadcasted_iota(jnp.int32, (1, 128), 1)
    gates = jnp.zeros((1, 128), F32)
    for half in range(128 // head_dim):
        gates = jnp.where(lane // head_dim == half, gate_ref[0, half], gates)
    return gates


def head_picks(head_dim):
    return (
        lax.broadcasted_iota(jnp.int32, (8, 128), 1) // head_dim
        == lax.broadcasted_iota(jnp.int32, (8, 128), 0)
    ).astype(F32)


def rows_back(head_dim, queries, outs, delta, stats, offset, keys, values, key_sum, value_sum, spans):
    rows = queries.shape[0]
    halves = 128 // head_dim
    zero = jnp.zeros((rows, 128), BF16)
    lanes = [head_lanes(rows, half, head_dim) for half in range(halves)]
    q_heads = [jnp.where(lane, queries, zero) for lane in lanes]
    out_heads = [jnp.where(lane, outs, zero) for lane in lanes]
    q_stack = jnp.concatenate(q_heads, axis=0)
    out_stack = jnp.concatenate(out_heads, axis=0)
    dq = [0.0] * halves
    for low, high, mask in spans:
        key_part = keys[low:high, :]
        value_part = values[low:high, :]
        probs, grads = [], []
        for half in range(halves):
            scores = mask(times_transposed(key_part, q_heads[half]))
            prob = jnp.exp2(scores - stats[2 * half + offset : 2 * half + offset + 1, :])
            dprob = times_transposed(value_part, out_heads[half])
            dscore = (prob * (dprob - delta[half : half + 1, :])).astype(BF16)
            probs.append(prob.astype(BF16))
            grads.append(dscore)
            dq[half] = dq[half] + outer_sum(dscore, key_part)
        value_sum[low:high, :] += low_product(jnp.concatenate(probs, axis=1), out_stack)
        key_sum[low:high, :] += low_product(jnp.concatenate(grads, axis=1), q_stack)
    total = 0.0
    for half in range(halves):
        total = total + jnp.where(lanes[half], dq[half], 0.0)
    return total


def cross_back_kernel(
    head_dim, first, caption, image_count, scale,
    gate_ref, q_ref, tk_ref, tv_ref, row_ref, grad_ref, cross_ref, stats_ref,
    dq_ref, dtk_ref, dtv_ref, gate_grad_ref, dtk_sum, dtv_sum,
):
    count = q_ref.shape[0]
    for total in (dtk_sum, dtv_sum, gate_grad_ref):
        total[...] = jnp.zeros_like(total)
    gates = gate_lanes(gate_ref, head_dim)
    picks = head_picks(head_dim)

    def part(at, rows, spans):
        wide = grad_ref[pl.ds(at, rows), :].astype(F32)
        cross = cross_ref[pl.ds(at, rows), :]
        gate_grad_ref[0:1, :] += jnp.sum(wide * cross, axis=0, keepdims=True)
        gated = (wide * gates).astype(BF16)
        delta = exact_transposed(picks, gated.astype(F32) * cross)
        dq = rows_back(
            head_dim, q_ref[pl.ds(at, rows), :], gated, delta, stats_ref[:, pl.ds(at, rows)], 1,
            tk_ref, tv_ref, dtk_sum, dtv_sum, spans,
        )
        dq_ref[pl.ds(at, rows), :] = (dq * scale).astype(BF16)

    def clean(block, carry):
        part(pl.multiple_of(block * QBLOCK, QBLOCK), QBLOCK, [(0, caption, lambda scores: scores)])
        return carry

    lax.fori_loop(0, first // QBLOCK, clean, 0)
    image = row_ref[0:1, first:count]
    owner = lax.broadcasted_iota(jnp.int32, (tk_ref.shape[0], 1), 0) // caption
    allowed = (owner == image) | (image == image_count)
    part(first, count - first, [(0, tk_ref.shape[0], lambda scores: jnp.where(allowed, scores, MASKED))])
    dtk_ref[...] = (dtk_sum[...] * (1.0 / LOG2E)).astype(BF16)
    dtv_ref[...] = dtv_sum[...].astype(BF16)


def cross_back(pair, gates, packed, text_packed, row, grad, cross, stats, head_dim, image_count, scale):
    count, texts = packed.shape[0], text_packed.shape[0]
    pairs = packed.shape[1] // 384
    halves = 128 // head_dim
    tokens = pl.BlockSpec((count, 128), lambda i: (0, pair))
    own_tokens = pl.BlockSpec((count, 128), lambda i: (0, 0))
    captions = pl.BlockSpec((texts, 128), lambda i: (0, 0))
    flops = 10 * count * texts * 128
    return pl.pallas_call(
        functools.partial(cross_back_kernel, head_dim, FIRST_PATCHES, texts // image_count, image_count, scale),
        grid=(1,),
        in_specs=[
            pl.BlockSpec((None, 1, halves), lambda i: (pair, 0, 0), memory_space=pltpu.SMEM),
            tokens,
            pl.BlockSpec((texts, 128), lambda i: (0, pair)),
            pl.BlockSpec((texts, 128), lambda i: (0, pairs + pair)),
            pl.BlockSpec((1, count), lambda i: (0, 0)),
            tokens,
            own_tokens,
            pl.BlockSpec((8, count), lambda i: (0, 0)),
        ],
        out_specs=[own_tokens, captions, captions, pl.BlockSpec((8, 128), lambda i: (0, 0))],
        out_shape=[
            jax.ShapeDtypeStruct((count, 128), BF16),
            jax.ShapeDtypeStruct((texts, 128), BF16),
            jax.ShapeDtypeStruct((texts, 128), BF16),
            jax.ShapeDtypeStruct((8, 128), F32),
        ],
        scratch_shapes=[pltpu.VMEM((texts, 128), F32), pltpu.VMEM((texts, 128), F32)],
        compiler_params=pltpu.CompilerParams(vmem_limit_bytes=VMEM_LIMIT),
        cost_estimate=pl.CostEstimate(flops=flops, bytes_accessed=12 * count * 128, transcendentals=count * texts),
    )(gates.reshape(pairs, 1, halves), packed, text_packed, text_packed, row, grad, cross, stats)


def self_back_kernel(
    head_dim, first, most, scale,
    q_ref, k_ref, v_ref, column_ref, row_ref, grad_ref, self_ref, stats_ref, more_ref,
    dq_ref, dk_ref, dv_ref, dk_sum, dv_sum,
):
    count = q_ref.shape[0]
    dk_sum[...] = jnp.zeros_like(dk_sum)
    dv_sum[...] = jnp.zeros_like(dv_sum)
    picks = head_picks(head_dim)

    def part(at, rows, spans):
        grad = grad_ref[pl.ds(at, rows), :]
        delta = exact_transposed(picks, grad.astype(F32) * self_ref[pl.ds(at, rows), :])
        dq = rows_back(
            head_dim, q_ref[pl.ds(at, rows), :], grad, delta, stats_ref[:, pl.ds(at, rows)], 0,
            k_ref, v_ref, dk_sum, dv_sum, spans,
        )
        dq_ref[pl.ds(at, rows), :] = (dq * scale + more_ref[pl.ds(at, rows), :].astype(F32)).astype(BF16)

    def clean(block, carry):
        bias = jnp.where(column_ref[first:most, :] == 0, 0.0, MASKED)
        part(
            pl.multiple_of(block * QBLOCK, QBLOCK), QBLOCK,
            [(0, first, lambda scores: scores), (first, most, lambda scores: scores + bias)],
        )
        return carry

    lax.fori_loop(0, first // QBLOCK, clean, 0)
    image = row_ref[0:1, first:count]
    part(first, count - first, [(0, count, lambda scores: jnp.where(column_ref[...] == image, scores, MASKED))])
    dk_ref[...] = (dk_sum[...] * (1.0 / LOG2E)).astype(BF16)
    dv_ref[...] = dv_sum[...].astype(BF16)


def self_back(pair, packed, column, row, grad, own, stats, more, head_dim, scale):
    count = packed.shape[0]
    pairs = packed.shape[1] // 384
    tokens = pl.BlockSpec((count, 128), lambda i: (0, pair))
    out = pl.BlockSpec((count, 128), lambda i: (0, 0))
    most = min(round_up(FIRST_MOST, 128), count)
    flops = 10 * count * count * 128
    return pl.pallas_call(
        functools.partial(self_back_kernel, head_dim, FIRST_PATCHES, most, scale),
        grid=(1,),
        in_specs=[
            tokens,
            pl.BlockSpec((count, 128), lambda i: (0, pairs + pair)),
            pl.BlockSpec((count, 128), lambda i: (0, 2 * pairs + pair)),
            pl.BlockSpec((count, 1), lambda i: (0, 0)),
            pl.BlockSpec((1, count), lambda i: (0, 0)),
            tokens,
            out,
            pl.BlockSpec((8, count), lambda i: (0, 0)),
            out,
        ],
        out_specs=[out, out, out],
        out_shape=[jax.ShapeDtypeStruct((count, 128), BF16)] * 3,
        scratch_shapes=[pltpu.VMEM((count, 128), F32), pltpu.VMEM((count, 128), F32)],
        compiler_params=pltpu.CompilerParams(vmem_limit_bytes=VMEM_LIMIT),
        cost_estimate=pl.CostEstimate(flops=flops, bytes_accessed=30 * count * 128, transcendentals=2 * count * count),
    )(packed, packed, packed, column, row, grad, own, stats, more)


def swiglu_kernel(core_ref, gate_ref, up_ref, out_ref, moved_ref):
    gate = gate_ref[...]
    half = 0.5 * gate
    value = ((half + half * jnp.tanh(half)) * up_ref[...]).astype(BF16)
    out_ref[...] = value
    moved_ref[...] = value


def swiglu(gate_up, core, deep, narrow):
    rows, double = gate_up.shape
    width = double // 2
    blocks = 2 * deep * narrow
    block = width // blocks

    def moved_place(i, core_ref):
        z, c, f = i // (2 * narrow), (i // narrow) % 2, i % narrow
        return (0, ((c + core_ref[0]) % 2) * (deep * narrow) + f * deep + z)

    return pl.pallas_call(
        swiglu_kernel,
        grid_spec=pltpu.PrefetchScalarGridSpec(
            num_scalar_prefetch=1,
            grid=(blocks,),
            in_specs=[
                pl.BlockSpec((rows, block), lambda i, core_ref: (0, i)),
                pl.BlockSpec((rows, block), lambda i, core_ref: (0, blocks + i)),
            ],
            out_specs=[
                pl.BlockSpec((rows, block), lambda i, core_ref: (0, i)),
                pl.BlockSpec((rows, block), moved_place),
            ],
        ),
        out_shape=[jax.ShapeDtypeStruct((rows, width), BF16)] * 2,
        compiler_params=pltpu.CompilerParams(vmem_limit_bytes=VMEM_LIMIT),
        cost_estimate=pl.CostEstimate(flops=6 * rows * width, bytes_accessed=12 * rows * width, transcendentals=rows * width),
    )(core.reshape(1), gate_up, gate_up)


def fsdp_share_kernel(narrow, x_ref, out_ref, send_sem, recv_sem):
    me = lax.axis_index("fsdp")
    barrier = pltpu.get_barrier_semaphore()
    for step in range(1, narrow):
        pl.semaphore_signal(
            barrier, inc=1, device_id={"fsdp": lax.rem(me + step, narrow)}, device_id_type=pl.DeviceIdType.MESH
        )
    pl.semaphore_wait(barrier, narrow - 1)
    copies = []
    for step in range(1, narrow):
        copy = pltpu.make_async_remote_copy(
            src_ref=x_ref,
            dst_ref=out_ref.at[me],
            send_sem=send_sem.at[step],
            recv_sem=recv_sem.at[step],
            device_id={"fsdp": lax.rem(me + step, narrow)},
            device_id_type=pl.DeviceIdType.MESH,
        )
        copy.start()
        copies.append(copy)
    out_ref[me] = x_ref[...]
    for copy in copies:
        copy.wait()


def fsdp_share(value, narrow, collective_id):
    return pl.pallas_call(
        functools.partial(fsdp_share_kernel, narrow),
        in_specs=[pl.BlockSpec(memory_space=pltpu.VMEM)],
        out_specs=pl.BlockSpec(memory_space=pltpu.VMEM),
        out_shape=jax.ShapeDtypeStruct((narrow,) + value.shape, value.dtype),
        scratch_shapes=[pltpu.SemaphoreType.DMA((narrow,)), pltpu.SemaphoreType.DMA((narrow,))],
        compiler_params=pltpu.CompilerParams(collective_id=collective_id, has_side_effects=True),
        cost_estimate=pl.CostEstimate(flops=0, bytes_accessed=8 * narrow * value.size, transcendentals=0),
    )(value)


def place_rows(items, x_ref, chunk, base):
    rows = [(ref, row) for ref in items for row in range(ref.shape[0])]
    at = 0
    while at < len(rows):
        ref, row = rows[at]
        off = at % chunk
        take = min(ref.shape[0] - row, chunk - off)
        x_ref[at // chunk, base + off : base + off + take, :] = ref[row : row + take, :]
        at += take
    while at < x_ref.shape[0] * chunk:
        off = at % chunk
        x_ref[at // chunk, base + off : base + chunk, :] = jnp.zeros((chunk - off, 128), F32)
        at += chunk - off


def finish_kernel(narrow, wide, sum_rows, sum_count, *refs):
    items, (out_ref, x_ref, first_ref, second_ref, sends, recvs) = refs[:-6], refs[-6:]
    place_rows(items[:sum_count], x_ref, sum_rows, 0)
    place_rows(items[sum_count:], x_ref, x_ref.shape[1] - sum_rows, sum_rows)
    me = lax.axis_index("fsdp")
    group = lax.axis_index("z") * 2 + lax.axis_index("core")
    rows = x_ref.shape[1]
    rest = rows - sum_rows
    barrier = pltpu.get_barrier_semaphore()
    places = [{"fsdp": lax.rem(me + step, narrow)} for step in range(1, narrow)]
    peers = [lax.rem(group + step, wide) for step in range(1, wide)]
    partners = [{"z": peer // 2, "core": peer % 2} for peer in peers]
    for place in places + partners:
        pl.semaphore_signal(barrier, inc=1, device_id=place, device_id_type=pl.DeviceIdType.MESH)
    pl.semaphore_wait(barrier, narrow + wide - 2)

    def send_all(targets, source, target, base):
        copies = []
        for i, place in enumerate(targets):
            copy = pltpu.make_async_remote_copy(
                src_ref=source(i),
                dst_ref=target,
                send_sem=sends.at[base + i],
                recv_sem=recvs.at[base + i],
                device_id=place,
                device_id_type=pl.DeviceIdType.MESH,
            )
            copy.start()
            copies.append(copy)
        return copies

    copies = send_all(places, lambda i: x_ref.at[lax.rem(me + i + 1, narrow)], first_ref.at[me], 0)
    first_ref[me] = x_ref[me]
    for copy in copies:
        copy.wait()
    total = first_ref[0]
    for i in range(1, narrow):
        total = total + first_ref[i]
    second_ref[group] = total
    copies = send_all(partners, lambda i: second_ref.at[group], second_ref.at[group], narrow)
    for copy in copies:
        copy.wait()
    total = second_ref[0, :sum_rows, :]
    for i in range(1, wide):
        total = total + second_ref[i, :sum_rows, :]
    out_ref[me, :sum_rows, :] = total
    for i in range(wide):
        out_ref[me, sum_rows + i * rest : sum_rows + (i + 1) * rest, :] = second_ref[i, sum_rows:, :]
    copies = send_all(places, lambda i: out_ref.at[me], out_ref.at[me], narrow + wide)
    for copy in copies:
        copy.wait()


def finish(summed, kept, narrow, wide, collective_id):
    sum_total = sum(item.shape[0] for item in summed)
    kept_total = sum(item.shape[0] for item in kept)
    sum_rows = round_up(-(-sum_total // narrow), 8)
    kept_rows = round_up(-(-kept_total // narrow), 8)
    rows = sum_rows + kept_rows
    count = 2 * narrow + wide
    out = pl.pallas_call(
        functools.partial(finish_kernel, narrow, wide, sum_rows, len(summed)),
        in_specs=[pl.BlockSpec(memory_space=pltpu.VMEM)] * (len(summed) + len(kept)),
        out_specs=pl.BlockSpec(memory_space=pltpu.VMEM),
        out_shape=jax.ShapeDtypeStruct((narrow, sum_rows + wide * kept_rows, 128), F32),
        scratch_shapes=[
            pltpu.VMEM((narrow, rows, 128), F32),
            pltpu.VMEM((narrow, rows, 128), F32),
            pltpu.VMEM((wide, rows, 128), F32),
            pltpu.SemaphoreType.DMA((count,)),
            pltpu.SemaphoreType.DMA((count,)),
        ],
        compiler_params=pltpu.CompilerParams(collective_id=collective_id, has_side_effects=True),
    )(*summed, *kept)
    total = out[:, :sum_rows, :].reshape(narrow * sum_rows, 128)[:sum_total]
    groups = out[:, sum_rows:, :].reshape(narrow, wide, kept_rows, 128).transpose(1, 0, 2, 3)
    return total, groups.reshape(wide, narrow * kept_rows, 128)[:, :kept_total]


def exchange(blocks, axis):
    return lax.all_to_all(blocks, axis, 0, 0, tiled=True)


def core_swap(value):
    return lax.ppermute(value, "core", [(0, 1), (1, 0)])


def by_core(low, high):
    first = lax.axis_index("core") == 0
    return jnp.where(first, low, high), jnp.where(first, high, low)


def in_core_order(own, other):
    first = lax.axis_index("core") == 0
    return jnp.where(first, own, other), jnp.where(first, other, own)


def chip_sum(own_left, other_left, right):
    came = core_swap(outer_sum(other_left, right).astype(BF16))
    return (outer_sum(own_left, right) + came.astype(F32)).astype(BF16)


def fsdp_sum(both):
    return lax.psum_scatter(both, "fsdp", scatter_dimension=0, tiled=True)


def z_pieces(blocks, deep):
    me = lax.axis_index("z")
    return [lax.dynamic_index_in_dim(blocks, me, 0, keepdims=False)] + [
        lax.ppermute(
            lax.dynamic_index_in_dim(blocks, me ^ step, 0, keepdims=False), "z", [(i, i ^ step) for i in range(deep)]
        )
        for step in range(1, deep)
    ]


def added(pieces):
    return functools.reduce(jnp.add, [piece.astype(F32) for piece in pieces])


def to_all(block, narrow):
    return [
        lax.ppermute(block, "fsdp", [(i, i ^ step) for i in range(narrow)]) for step in range(1, narrow)
    ]


def in_order(block, came):
    me = lax.axis_index("fsdp")
    narrow = len(came) + 1
    result = lax.dynamic_update_slice_in_dim(
        jnp.zeros((narrow,) + block.shape, block.dtype), block[None], me, 0
    )
    for step in range(1, narrow):
        result = lax.dynamic_update_slice_in_dim(result, came[step - 1][None], me ^ step, 0)
    return result


def device_columns(value, deep, narrow):
    rows, width = value.shape
    block = width // (2 * deep * narrow)
    core = lax.axis_index("core")
    target = jnp.arange(width, dtype=jnp.int32)
    c, f, z, r = (
        target // (narrow * deep * block), target // (deep * block) % narrow, target // block % deep, target % block,
    )
    c = (c + core) % 2
    source = ((z * 2 + c) * narrow + f) * block + r
    pick = (jnp.arange(width, dtype=jnp.int32)[:, None] == source[None, :]).astype(BF16)
    moved = low_product(value, pick).astype(BF16)
    return moved[:, : width // 2], moved[:, width // 2 :]


def whole_weight(shard):
    rows = shard.shape[0] // 2
    half = lax.dynamic_slice_in_dim(shard, lax.axis_index("core") * rows, rows, 0)
    return lax.all_gather(half, ("fsdp", "core"), axis=0, tiled=True)


def shards(
    tokens,
    cotangent,
    text_states,
    conditioning,
    image_sizes,
    ada_weight,
    ada_bias,
    qkv_weight,
    out_weight,
    text_weight,
    gate_up_weight,
    down_weight,
    norm_gains,
    norm_shifts,
    text_gain,
    head_gate,
):
    model_width = tokens.shape[2]
    head_count = head_gate.shape[0]
    head_dim = model_width // head_count
    image_count = text_states.shape[1]
    caption_local = text_states.shape[2]
    caption_width = text_states.shape[3]
    local_tok = tokens.shape[1]
    deep = lax.axis_size("z")
    narrow = lax.axis_size("fsdp")
    wide = 2 * deep
    me = lax.axis_index("fsdp")
    group_tok = local_tok * narrow
    caption_full = caption_local * narrow
    score_scale = head_dim ** (-0.5)
    text_total = image_count * caption_full
    text_local = image_count * caption_local
    part = model_width // narrow
    part_pad = round_up(part, 128)
    heads_here = head_count // narrow
    pairs = part_pad // 128
    halves = 128 // head_dim

    group_sizes = image_sizes[0]
    position = me * local_tok + jnp.arange(local_tok, dtype=jnp.int32)
    image_index = token_layout(group_sizes, position, image_count)[0]
    key_image, key_row, key_col = token_layout(
        group_sizes, jnp.arange(group_tok, dtype=jnp.int32), image_count
    )
    member = [(image_index == i).astype(F32)[:, None] for i in range(image_count)]
    cosine, sine = rope_tables(key_row, key_col, head_dim)

    cond_low = jax.nn.silu(conditioning[0].astype(F32)).astype(BF16)
    cond_rows = ada_weight.shape[0]
    cond_part = lax.dynamic_slice_in_dim(cond_low, me * cond_rows, cond_rows, 1)
    modulation_part = low_product(cond_part, ada_weight)
    modulation = (
        jnp.sum(fsdp_share(modulation_part.reshape(-1, 128), narrow, 0), axis=0).reshape(modulation_part.shape)
        + ada_bias
    )

    def per_token(index):
        rows = modulation[:, index * model_width : (index + 1) * model_width]
        return functools.reduce(
            jnp.add, [member[i] * rows[i : i + 1, :] for i in range(image_count)]
        )

    def per_image(value):
        return [jnp.sum(member[i] * value, axis=0).reshape(-1, 128) for i in range(image_count)]

    token_in = tokens[0].astype(F32)
    token_inverse = inverse_rms(token_in)
    tokens_all = lax.all_gather(tokens[0], "fsdp", axis=0, tiled=True)
    def widened(value, slots):
        if part == part_pad:
            return value
        lead = value.shape[:-1]
        value = value.reshape(*lead, slots, part)
        pads = [(0, 0)] * (len(lead) + 1) + [(0, part_pad - part)]
        return jnp.pad(value, pads).reshape(*lead, slots * part_pad)

    def narrowed(value, slots):
        if part == part_pad:
            return value
        lead = value.shape[:-1]
        return value.reshape(*lead, slots, part_pad)[..., :part].reshape(*lead, slots * part)

    def own_columns(value):
        return widened(lax.dynamic_slice_in_dim(value, me * part, part, value.ndim - 1), 1)

    qkv_rows = qkv_weight.shape[0] // 2
    qkv_half = lax.dynamic_slice_in_dim(qkv_weight, lax.axis_index("core") * qkv_rows, qkv_rows, 0)
    qkv_half = exchange(
        qkv_half.reshape(qkv_rows, 3, narrow, part).transpose(2, 0, 1, 3).reshape(narrow, qkv_rows, 3 * part), "fsdp"
    )
    own_qkv = widened(
        jnp.concatenate(in_core_order(qkv_half, core_swap(qkv_half)), axis=1).reshape(model_width, 3 * part), 3
    )

    full_out = whole_weight(out_weight)
    full_gate_up = whole_weight(gate_up_weight)
    full_down = whole_weight(down_weight)

    text_in = text_states[0].astype(F32).reshape(text_local, caption_width)
    text_inverse = inverse_rms(text_in)
    text_low = (text_in * text_inverse * text_gain).astype(BF16)
    text_cols = caption_width // narrow
    text_slice = (
        exchange(text_low.reshape(text_local, narrow, text_cols).transpose(1, 0, 2), "fsdp")
        .reshape(narrow, image_count, caption_local, text_cols)
        .transpose(1, 0, 2, 3)
        .reshape(text_total, text_cols)
    )
    own_text_weight = (
        text_weight.reshape(text_cols, 2, narrow, part).transpose(2, 0, 1, 3).reshape(narrow, text_cols, 2 * part)
    )
    text_partial = jnp.stack([low_product(text_slice, own_text_weight[i]).astype(BF16) for i in range(narrow)])
    text_partial, tokens_all = lax.optimization_barrier((text_partial, tokens_all))
    text_projected = widened(jnp.sum(exchange(text_partial, "fsdp").astype(F32), axis=0), 2)
    text_parts = fsdp_share(column_stats(text_projected, part, part_pad, 1), narrow, 1)
    text_means = text_parts[:, 0, :]
    text_mean = jnp.mean(text_means, axis=0)
    text_square = jnp.sum(text_parts[:, 1, :], axis=0) + part * jnp.sum((text_means - text_mean) ** 2, axis=0)
    text_key_inverse = lax.rsqrt(text_square / model_width + EPS)[:, None]
    text_unit = (text_projected[:, :part_pad] - text_mean[:, None]) * text_key_inverse
    text_gains = own_columns(norm_gains[4])
    text_packed = jnp.concatenate(
        [(text_unit * text_gains).astype(BF16), text_projected[:, part_pad:].astype(BF16)], axis=1
    )

    wide_tokens = tokens_all.astype(F32)
    wide_scale = functools.reduce(
        jnp.add,
        [(key_image == i).astype(F32)[:, None] * modulation[i : i + 1, :model_width] for i in range(image_count)],
    )
    normed_all = (wide_tokens * inverse_rms(wide_tokens) * norm_gains[0] * (1.0 + wide_scale)).astype(BF16)

    projected = low_product(normed_all, own_qkv)
    stats_all = fsdp_share(column_stats(projected, part, part_pad, 2), narrow, 2)
    head_gains = own_columns(norm_gains[2:4])
    packed = make_heads(
        projected, stats_all, cosine, sine, head_gains, own_columns(norm_shifts), part, score_scale * LOG2E
    )
    gate_tanh = jnp.tanh(head_gate)
    own_gates = lax.dynamic_slice_in_dim(gate_tanh, me * heads_here, heads_here, 0)
    own_gates = jnp.concatenate([own_gates, jnp.ones((pairs * halves - heads_here,), F32)])
    column = key_image[:, None]
    row = key_image[None, :]
    attended = [
        attend(pair, own_gates, packed, text_packed, column, row, head_dim, image_count) for pair in range(pairs)
    ]
    mixed_pairs = [exchange(one[0].reshape(narrow, local_tok, 128), "fsdp") for one in attended]
    self_outs = [one[1] for one in attended]
    cross_outs = [one[2] for one in attended]
    stats = [one[3] for one in attended]
    mixed_low = (
        narrowed(jnp.concatenate(mixed_pairs, axis=2), 1).transpose(1, 0, 2).reshape(local_tok, model_width)
    )

    branch = low_product(mixed_low, full_out)
    branch_inverse = inverse_rms(branch)
    branch_unit = branch * branch_inverse
    gate_attend = jnp.tanh(per_token(1))
    hidden = token_in + gate_attend * (branch_unit * norm_gains[1])
    hidden_inverse = inverse_rms(hidden)
    hidden_unit = hidden * hidden_inverse
    scale_feed = 1.0 + per_token(2)
    normed_feed_low = (hidden_unit * norm_gains[5] * scale_feed).astype(BF16)
    gate_up = low_product(normed_feed_low, full_gate_up)
    hidden_units = gate_up.shape[1] // 2
    gate_half = gate_up[:, :hidden_units]
    up_half = gate_up[:, hidden_units:]
    sigmoid = jax.nn.sigmoid(gate_half)
    if hidden_units // (wide * narrow) % 128 == 0:
        activated_low, moved = swiglu(gate_up, lax.axis_index("core"), deep, narrow)
        down_columns = (moved[:, : hidden_units // 2], moved[:, hidden_units // 2 :])
    else:
        activated_low = (gate_half * sigmoid * up_half).astype(BF16)
        down_columns = device_columns(activated_low, deep, narrow)
    down_out = low_product(activated_low, full_down)
    down_inverse = inverse_rms(down_out)
    down_unit = down_out * down_inverse
    gate_feed = jnp.tanh(per_token(3))
    down_normed = down_unit * norm_gains[6]
    result = (hidden + gate_feed * down_normed).astype(BF16)

    grad_result = cotangent[0].astype(F32)
    grad_down_y = grad_result * gate_feed
    grad_gain_six = jnp.sum(grad_down_y * down_unit, axis=0)
    grad_gate_feed = per_image(grad_result * down_normed * (1.0 - gate_feed * gate_feed))
    grad_down_low = norm_pull(grad_down_y * norm_gains[6], down_unit, down_inverse).astype(BF16)
    grad_activated = times_transposed(grad_down_low, full_down)
    grad_gate_up_low = jnp.concatenate(
        [
            (grad_activated * up_half * sigmoid * (1.0 + gate_half * (1.0 - sigmoid))).astype(BF16),
            (grad_activated * gate_half * sigmoid).astype(BF16),
        ],
        axis=1,
    )
    grad_normed_feed = times_transposed(grad_gate_up_low, full_gate_up)
    grad_feed_y = grad_normed_feed * scale_feed
    grad_gain_five = jnp.sum(grad_feed_y * hidden_unit, axis=0)
    grad_scale_feed = per_image(grad_normed_feed * hidden_unit * norm_gains[5])
    grad_hidden = grad_result + norm_pull(grad_feed_y * norm_gains[5], hidden_unit, hidden_inverse)
    grad_branch_y = grad_hidden * gate_attend
    grad_gain_one = jnp.sum(grad_branch_y * branch_unit, axis=0)
    grad_gate_attend = per_image(
        grad_hidden * branch_unit * norm_gains[1] * (1.0 - gate_attend * gate_attend)
    )
    grad_branch_low = norm_pull(grad_branch_y * norm_gains[1], branch_unit, branch_inverse).astype(BF16)
    grad_mixed = times_transposed(grad_branch_low, full_out).astype(BF16)
    grad_blocks = widened(grad_mixed.reshape(local_tok, narrow, part).transpose(1, 0, 2), 1)
    grad_heads = exchange(grad_blocks, "fsdp").reshape(group_tok, part_pad)
    def by_z(value):
        return value.reshape(deep, -1, value.shape[1])

    down_both = chip_sum(*down_columns, grad_down_low)
    gate_up_both = chip_sum(*device_columns(normed_feed_low, deep, narrow), grad_gate_up_low)
    out_both = chip_sum(*device_columns(mixed_low, deep, narrow), grad_branch_low)
    down_part = fsdp_sum(down_both)
    grad_heads, gate_up_both, out_both, down_part = lax.optimization_barrier(
        (grad_heads, gate_up_both, out_both, down_part)
    )
    came_downs = exchange(by_z(down_part), "z")
    gate_up_part = fsdp_sum(gate_up_both)
    out_part = fsdp_sum(out_both)
    crossed = [
        cross_back(
            pair, own_gates, packed, text_packed, row, grad_heads, cross_outs[pair], stats[pair],
            head_dim, image_count, score_scale,
        )
        for pair in range(pairs)
    ]
    dtk = jnp.concatenate([one[1] for one in crossed], axis=1)
    dtv = jnp.concatenate([one[2] for one in crossed], axis=1)
    gate_sums = jnp.stack([one[3] for one in crossed])

    grad_text_keys = dtk.astype(F32)
    own_gain_four = jnp.sum(grad_text_keys * text_unit, axis=0)
    grad_text_unit = grad_text_keys * text_gains
    text_sums = jnp.stack([jnp.sum(grad_text_unit, axis=1), jnp.sum(grad_text_unit * text_unit, axis=1)])
    text_sums = jnp.sum(
        fsdp_share(jnp.pad(text_sums, ((0, 6), (0, 0))), narrow, 3), axis=0
    ) * (1.0 / model_width)
    grad_text_key_in = (grad_text_unit - text_sums[0][:, None] - text_unit * text_sums[1][:, None]) * text_key_inverse
    grad_text_own = jnp.concatenate(
        [narrowed(grad_text_key_in.astype(BF16), 1), narrowed(dtv, 1)], axis=1
    )
    def self_pair(pair):
        return self_back(
            pair, packed, column, row, grad_heads, self_outs[pair], stats[pair], crossed[pair][0], head_dim, score_scale
        )

    came_texts = to_all(grad_text_own, narrow)
    backs = [self_pair(0)]
    first, came_downs, *came_texts = lax.optimization_barrier((backs[0][0], came_downs, *came_texts))
    grad_down_weight = jnp.sum(came_downs.astype(F32), axis=0)
    backs[0] = (first, *backs[0][1:])
    grad_text_all = in_order(grad_text_own, came_texts)
    grad_text_columns = (
        grad_text_all.reshape(narrow, text_total, 2, part).transpose(1, 2, 0, 3).reshape(text_total, 2 * model_width)
    )
    text_half = text_cols // 2
    own_text, other_text = by_core(text_slice[:, :text_half], text_slice[:, text_half:])
    came_text = core_swap(outer_sum(other_text, grad_text_columns).astype(BF16))
    text_both = (outer_sum(own_text, grad_text_columns) + came_text.astype(F32)).astype(BF16)
    grad_heads, text_both, first = lax.optimization_barrier((grad_heads, text_both, backs[0][0]))
    backs[0] = (first, *backs[0][1:])
    came_text_z = exchange(by_z(text_both), "z")
    backs.append(self_pair(1))
    if pairs > 2:
        grad_heads, gate_up_part, out_part, second = lax.optimization_barrier(
            (grad_heads, gate_up_part, out_part, backs[1][0])
        )
        backs[1] = (second, *backs[1][1:])
        backs += [self_pair(pair) for pair in range(2, pairs)]
    grad_gate_up_weight = added(z_pieces(by_z(gate_up_part), deep))
    last, came_text_z = lax.optimization_barrier((backs[-1][0], came_text_z))
    backs[-1] = (last, *backs[-1][1:])
    text_part = jnp.sum(came_text_z.astype(F32), axis=0).astype(BF16)
    came_out_z = exchange(by_z(out_part), "z")
    own_gate_grad = jnp.sum(gate_sums[:, 0, :].reshape(pairs * halves, head_dim), axis=1)[:heads_here]
    grad_head_gate = lax.dynamic_update_slice_in_dim(
        jnp.zeros((head_count,), F32), own_gate_grad, me * heads_here, 0
    ) * (1.0 - gate_tanh * gate_tanh)
    grad_projected_low, head_sums = heads_back(
        list(zip(*backs)), projected, stats_all, cosine, sine, head_gains, part,
        lambda value: fsdp_share(value, narrow, 4),
    )
    everyone = ("z", "core", "fsdp")
    grad_text_weight = lax.ppermute(
        text_part,
        everyone,
        [
            ((z * 2 + c) * narrow + f, f * wide + c * deep + z)
            for z in range(deep) for c in range(2) for f in range(narrow)
        ],
    )
    grad_projected_low, grad_gate_up_weight, came_out_z, grad_text_weight = lax.optimization_barrier(
        (grad_projected_low, grad_gate_up_weight, came_out_z, grad_text_weight)
    )
    grad_text_weight = grad_text_weight.astype(F32)
    grad_out_weight = jnp.sum(came_out_z.astype(F32), axis=0)
    grad_normed = lax.psum_scatter(
        times_transposed(grad_projected_low, own_qkv).astype(BF16), "fsdp", scatter_dimension=0, tiled=True
    )

    def lane_rows(value):
        return value.reshape(-1, 128)

    group = lax.axis_index("z") * 2 + lax.axis_index("core")
    columns_here = jnp.stack(
        [narrowed(value, 1) for value in (head_sums[0], head_sums[2], own_gain_four, head_sums[1], head_sums[3])]
    )
    here = (jnp.arange(narrow, dtype=jnp.int32) == me)[None, :, None]
    placed = lane_rows(jnp.where(here, columns_here[:, None, :], 0.0))
    cond_rows_here = lane_rows(jnp.where(me == 0, cond_low.astype(F32), 0.0))
    gate_row = jnp.pad(grad_head_gate, (0, 128 - head_count)).reshape(1, 128)
    ready = [lane_rows(grad_gain_one), lane_rows(grad_gain_five), lane_rows(grad_gain_six), placed, gate_row]
    summed, kept = finish(
        ready, [*grad_gate_attend, *grad_scale_feed, *grad_gate_feed, cond_rows_here], narrow, wide, 5
    )
    projected_again, summed, kept = lax.optimization_barrier((grad_projected_low, summed, kept))
    qkv_grad = outer_sum(normed_all, projected_again).astype(BF16).reshape(deep, 2, model_width // wide, 3 * part_pad)
    own_grad, other_grad = by_core(qkv_grad[:, 0], qkv_grad[:, 1])
    own_grad = (own_grad.astype(F32) + core_swap(other_grad).astype(F32)).astype(BF16)
    own_grad, grad_text_columns = lax.optimization_barrier((own_grad, grad_text_columns))
    own_pieces = z_pieces(own_grad, deep)
    grad_text_slice = times_transposed(grad_text_columns, text_weight).astype(BF16)
    came_text = exchange(
        grad_text_slice.reshape(image_count, narrow, caption_local, text_cols)
        .transpose(1, 0, 2, 3)
        .reshape(narrow, text_local, text_cols),
        "fsdp",
    )

    grad_text_normed = (
        came_text
        .transpose(1, 0, 2)
        .reshape(text_local, caption_width)
        .astype(F32)
    )
    text_state_unit = text_in * text_inverse
    grad_text_gain = jnp.sum(grad_text_normed * text_state_unit, axis=0)
    grad_text = (
        norm_pull(grad_text_normed * text_gain, text_state_unit, text_inverse)
        .astype(BF16)
        .reshape(image_count, caption_local, caption_width)
    )

    grad_text, grad_text_gain, *own_pieces = lax.optimization_barrier((grad_text, grad_text_gain, *own_pieces))
    own_grad = added(own_pieces)
    grad_qkv_weight = (
        exchange(narrowed(own_grad.astype(BF16), 3).reshape(narrow, -1, 3 * part), "fsdp")
        .reshape(narrow, -1, 3, part)
        .transpose(1, 2, 0, 3)
        .reshape(-1, 3 * model_width)
        .astype(F32)
    )

    every_image = wide * image_count
    ada_rows = cond_rows // wide
    lanes_of_row = model_width // 128

    def image_rows(value, width):
        return value.reshape(every_image, width)

    per_part = image_count * lanes_of_row
    slots = jnp.concatenate(
        [image_rows(kept[:, i * per_part : (i + 1) * per_part], model_width) for i in range(3)], axis=1
    )
    cond_slots = image_rows(kept[:, 3 * per_part :], cond_low.shape[1])
    own_cond = lax.dynamic_slice_in_dim(cond_slots, (group * narrow + me) * ada_rows, ada_rows, 1)
    ada_later = exact_outer(own_cond, slots)
    later_bias = jnp.sum(slots, axis=0)
    grad_normed, ada_later, own_cond, later_bias = lax.optimization_barrier(
        (grad_normed, ada_later, own_cond, later_bias)
    )
    grad_normed = grad_normed.astype(F32)

    token_unit = token_in * token_inverse
    scale_attend = 1.0 + per_token(0)
    grad_normed_y = grad_normed * scale_attend
    grad_gain_zero = jnp.sum(grad_normed_y * token_unit, axis=0)
    grad_scale_attend = per_image(grad_normed * token_unit * norm_gains[0])
    grad_tokens = (
        grad_hidden + norm_pull(grad_normed_y * norm_gains[0], token_unit, token_inverse)
    ).astype(BF16)
    last_sums, first_slots = finish(
        [lane_rows(grad_gain_zero), lane_rows(grad_text_gain)], grad_scale_attend, narrow, wide, 6
    )
    grad_text_gain = last_sums[lanes_of_row:].reshape(-1)
    first_slots = image_rows(first_slots, model_width)
    grad_ada_weight = jnp.concatenate([exact_outer(own_cond, first_slots), ada_later], axis=1)
    grad_ada_bias = jnp.concatenate([jnp.sum(first_slots, axis=0), later_bias])
    first, two, three, four = (summed[i * lanes_of_row : (i + 1) * lanes_of_row] for i in (0, 3, 4, 5))
    five, six = (summed[i * lanes_of_row : (i + 1) * lanes_of_row] for i in (1, 2))
    grad_gains = jnp.concatenate(
        [last_sums[:lanes_of_row], first, two, three, four, five, six]
    ).reshape(norm_gains.shape)
    grad_shifts = summed[6 * lanes_of_row : 8 * lanes_of_row].reshape(norm_shifts.shape)
    grad_head_gate = summed[8 * lanes_of_row, :head_count]
    return (
        result[None],
        grad_tokens[None],
        grad_text[None],
        grad_ada_weight,
        grad_qkv_weight,
        grad_out_weight,
        grad_text_weight,
        grad_gate_up_weight,
        grad_down_weight,
        grad_ada_bias,
        grad_gains,
        grad_shifts,
        grad_text_gain,
        grad_head_gate,
    )


def solution(mesh):
    wide, narrow = mesh.devices.shape
    fine = Mesh(mesh.devices.reshape(wide // 2, 2, narrow), ("z", "core", "fsdp"))
    groups = ("z", "core")
    every = ("z", "core", "fsdp")
    placed = (
        P(groups, "fsdp", None),
        P(groups, "fsdp", None),
        P(groups, None, "fsdp", None),
        P(groups, None, None),
        P(groups, None, None),
        P("fsdp", None),
        P(),
        P("fsdp", None),
        P("fsdp", None),
        P("fsdp", None),
        P("fsdp", None),
        P("fsdp", None),
        P(),
        P(),
        P(),
        P(),
    )
    return jax.shard_map(
        shards,
        mesh=fine,
        in_specs=placed,
        out_specs=(
            P(groups, "fsdp", None),
            P(groups, "fsdp", None),
            P(groups, None, "fsdp", None),
            P(every, None),
            P(every, None),
            P(every, None),
            P(every, None),
            P(every, None),
            P(every, None),
            P(),
            P(),
            P(),
            P(),
            P(),
        ),
        check_vma=False,
    )
```

```python
import functools

import jax
import jax.numpy as jnp
from jax import lax
from jax.experimental import pallas as pl
from jax.experimental.pallas import tpu as pltpu
from jax.sharding import Mesh
from jax.sharding import PartitionSpec as P

EPS = 1e-05
HIGHEST_PRECISION = lax.Precision.HIGHEST
MASKED = -1e30
LOG2E = 1.4426950408889634
FIRST_PATCHES = 16 * 12**2
FIRST_MOST = FIRST_PATCHES + 96
QBLOCK = 256
BF16 = jnp.bfloat16
F32 = jnp.float32
VMEM_LIMIT = 60 * 1024 * 1024


def round_up(value, step):
    return -(-value // step) * step


def low_product(left, right):
    return jnp.dot(left, right, preferred_element_type=F32)


def times_transposed(left, right):
    return lax.dot_general(left, right, (((1,), (1,)), ((), ())), preferred_element_type=F32)


def outer_sum(left, right):
    return lax.dot_general(left, right, (((0,), (0,)), ((), ())), preferred_element_type=F32)


def exact_outer(left, right):
    return lax.dot_general(
        left, right, (((0,), (0,)), ((), ())), precision=HIGHEST_PRECISION, preferred_element_type=F32
    )


def exact_transposed(left, right):
    return lax.dot_general(
        left, right, (((1,), (1,)), ((), ())), precision=HIGHEST_PRECISION, preferred_element_type=F32
    )


def row_mean(value):
    return jnp.mean(value, axis=-1, keepdims=True)


def inverse_rms(value):
    return lax.rsqrt(row_mean(value * value) + EPS)


def norm_pull(grad, unit, inverse):
    return (grad - unit * row_mean(grad * unit)) * inverse


def token_layout(image_sizes, position, image_count):
    start = jnp.int32(0)
    image_index = jnp.full(position.shape, image_count, jnp.int32)
    token_row = jnp.zeros(position.shape, jnp.int32)
    token_col = jnp.zeros(position.shape, jnp.int32)
    for i in range(image_count):
        width = image_sizes[i, 1] + 1
        end = start + image_sizes[i, 0] * width
        inside = (position >= start) & (position < end)
        offset = position - start
        image_index = jnp.where(inside, i, image_index)
        token_row = jnp.where(inside, offset // width, token_row)
        token_col = jnp.where(inside, offset % width, token_col)
        start = end
    return image_index, token_row, token_col


def rope_tables(token_row, token_col, head_dim):
    quarter = head_dim // 4
    pair = (jnp.arange(128, dtype=jnp.int32) % head_dim) // 2
    frequency = 10000.0 ** (-(pair % quarter).astype(F32) / quarter)
    place = jnp.where(
        (pair < quarter)[None, :], token_row.astype(F32)[:, None], token_col.astype(F32)[:, None]
    )
    angles = place * frequency[None, :]
    even = (jnp.arange(128, dtype=jnp.int32) % 2 == 0)[None, :]
    return jnp.cos(angles), jnp.where(even, -jnp.sin(angles), jnp.sin(angles))


def swap_pairs(value):
    width = value.shape[1]
    even = lax.broadcasted_iota(jnp.int32, value.shape, 1) % 2 == 0
    return jnp.where(even, pltpu.roll(value, width - 1, 1), pltpu.roll(value, 1, 1))


def wide_table(table, width):
    return jnp.concatenate([table] * (width // table.shape[1]), axis=1)


def pack_columns(columns):
    rows = columns[0].shape[0]
    lane = lax.broadcasted_iota(jnp.int32, (rows, 128), 1)
    packed = jnp.zeros((rows, 128), F32)
    for i, column in enumerate(columns):
        packed = jnp.where(lane == i, column, packed)
    return jnp.transpose(packed)[:8, :]


def as_columns(rows_list):
    width = rows_list[0].shape[1]
    stacked = jnp.concatenate(
        rows_list + [jnp.zeros((128 - len(rows_list), width), F32)], axis=0
    )
    return jnp.transpose(stacked)


def real_lanes(shape, part):
    return lax.broadcasted_iota(jnp.int32, shape, 1) < part


def own_stats(value, part):
    mean = jnp.sum(value, axis=1, keepdims=True) * (1.0 / part)
    centred = value - mean
    if value.shape[1] != part:
        centred = jnp.where(real_lanes(value.shape, part), centred, 0.0)
    return mean, jnp.sum(centred * centred, axis=1, keepdims=True)


def joined_stats(stats_ref, part, slot):
    narrow = stats_ref.shape[0]
    means = [stats_ref[i, 2 * slot : 2 * slot + 1, :] for i in range(narrow)]
    squares = [stats_ref[i, 2 * slot + 1 : 2 * slot + 2, :] for i in range(narrow)]
    mean = functools.reduce(jnp.add, means) * (1.0 / narrow)
    square = functools.reduce(jnp.add, squares)
    square = square + part * functools.reduce(jnp.add, [(m - mean) * (m - mean) for m in means])
    return mean, lax.rsqrt(square * (1.0 / (narrow * part)) + EPS)


def stats_kernel(part, slots, projected_ref, out_ref):
    padded = projected_ref.shape[1] // slots
    columns = []
    for slot in range(slots):
        columns += own_stats(projected_ref[:, slot * padded : (slot + 1) * padded], part)
    out_ref[...] = pack_columns(columns)


def column_stats(projected, part, padded, slots):
    rows = projected.shape[0]
    return pl.pallas_call(
        functools.partial(stats_kernel, part, slots),
        grid=(pl.cdiv(rows, QBLOCK),),
        in_specs=[pl.BlockSpec((QBLOCK, slots * padded), lambda i: (i, 0))],
        out_specs=pl.BlockSpec((8, QBLOCK), lambda i: (0, i)),
        out_shape=jax.ShapeDtypeStruct((8, rows), F32),
        compiler_params=pltpu.CompilerParams(vmem_limit_bytes=VMEM_LIMIT),
        cost_estimate=pl.CostEstimate(flops=10 * rows * slots * padded, bytes_accessed=4 * rows * slots * padded, transcendentals=0),
    )(projected)


def heads_kernel(part, query_scale, projected_ref, stats_ref, cos_ref, sin_ref, gains_ref, shifts_ref, out_ref):
    padded = projected_ref.shape[1] // 3
    cosine = wide_table(cos_ref[...], padded)
    sine = wide_table(sin_ref[...], padded)
    columns = as_columns([*joined_stats(stats_ref, part, 0), *joined_stats(stats_ref, part, 1)])
    for slot in range(3):
        place = slice(slot * padded, (slot + 1) * padded)
        value = projected_ref[:, place]
        if slot < 2:
            value = (value - columns[:, 2 * slot : 2 * slot + 1]) * columns[:, 2 * slot + 1 : 2 * slot + 2]
            value = value * gains_ref[slot : slot + 1, :] + shifts_ref[slot : slot + 1, :]
            value = value * cosine + swap_pairs(value) * sine
            if slot == 0:
                value = value * query_scale
        out_ref[:, place] = value.astype(BF16)


def make_heads(projected, stats, cosine, sine, gains, shifts, part, query_scale):
    rows, triple = projected.shape
    padded = triple // 3
    narrow = stats.shape[0]
    return pl.pallas_call(
        functools.partial(heads_kernel, part, query_scale),
        grid=(pl.cdiv(rows, QBLOCK),),
        in_specs=[
            pl.BlockSpec((QBLOCK, triple), lambda i: (i, 0)),
            pl.BlockSpec((narrow, 8, QBLOCK), lambda i: (0, 0, i)),
            pl.BlockSpec((QBLOCK, 128), lambda i: (i, 0)),
            pl.BlockSpec((QBLOCK, 128), lambda i: (i, 0)),
            pl.BlockSpec((2, padded), lambda i: (0, 0)),
            pl.BlockSpec((2, padded), lambda i: (0, 0)),
        ],
        out_specs=pl.BlockSpec((QBLOCK, triple), lambda i: (i, 0)),
        out_shape=jax.ShapeDtypeStruct((rows, triple), BF16),
        compiler_params=pltpu.CompilerParams(vmem_limit_bytes=VMEM_LIMIT),
        cost_estimate=pl.CostEstimate(flops=40 * rows * triple, bytes_accessed=6 * rows * triple, transcendentals=0),
    )(projected, stats, cosine, sine, gains, shifts)


def turned_back(refs, cosine, sine):
    grad = jnp.concatenate([ref[...].astype(F32) for ref in refs], axis=1)
    return grad * cosine - swap_pairs(grad) * sine


def grad_stats_kernel(rows, part, pairs, *refs):
    dq_refs, dk_refs = refs[:pairs], refs[pairs : 2 * pairs]
    projected_ref, stats_ref, cos_ref, sin_ref, gains_ref, out_ref, sums_ref = refs[2 * pairs :]
    step = pl.program_id(0)
    padded = 128 * pairs
    cosine = wide_table(cos_ref[...], padded)
    sine = wide_table(sin_ref[...], padded)
    height = cos_ref.shape[0]
    inside = step * height + lax.broadcasted_iota(jnp.int32, (height, 1), 0) < rows

    @pl.when(step == 0)
    def _():
        sums_ref[...] = jnp.zeros_like(sums_ref)

    columns = as_columns([*joined_stats(stats_ref, part, 0), *joined_stats(stats_ref, part, 1)])
    packed = []
    for slot, grads in enumerate((dq_refs, dk_refs)):
        grad = jnp.where(inside, turned_back(grads, cosine, sine), 0.0)
        unit = (projected_ref[:, slot * padded : (slot + 1) * padded] - columns[:, 2 * slot : 2 * slot + 1])
        unit = jnp.where(inside, unit * columns[:, 2 * slot + 1 : 2 * slot + 2], 0.0)
        both = grad * unit
        sums_ref[2 * slot : 2 * slot + 1, :] += jnp.sum(both, axis=0, keepdims=True)
        sums_ref[2 * slot + 1 : 2 * slot + 2, :] += jnp.sum(grad, axis=0, keepdims=True)
        gain = gains_ref[slot : slot + 1, :]
        packed.append(jnp.sum(grad * gain, axis=1, keepdims=True))
        packed.append(jnp.sum(both * gain, axis=1, keepdims=True))
    out_ref[...] = pack_columns(packed)


def heads_back_kernel(part, pairs, *refs):
    dq_refs, dk_refs, dv_refs = refs[:pairs], refs[pairs : 2 * pairs], refs[2 * pairs : 3 * pairs]
    projected_ref, stats_ref, totals_ref, cos_ref, sin_ref, gains_ref, out_ref = refs[3 * pairs :]
    padded = 128 * pairs
    narrow = stats_ref.shape[0]
    cosine = wide_table(cos_ref[...], padded)
    sine = wide_table(sin_ref[...], padded)
    means = [
        functools.reduce(jnp.add, [totals_ref[i, j : j + 1, :] for i in range(narrow)]) * (1.0 / (narrow * part))
        for j in range(4)
    ]
    columns = as_columns([*joined_stats(stats_ref, part, 0), *joined_stats(stats_ref, part, 1), *means])
    for slot, grads in enumerate((dq_refs, dk_refs)):
        grad = turned_back(grads, cosine, sine) * gains_ref[slot : slot + 1, :]
        inverse = columns[:, 2 * slot + 1 : 2 * slot + 2]
        unit = (projected_ref[:, slot * padded : (slot + 1) * padded] - columns[:, 2 * slot : 2 * slot + 1]) * inverse
        grad = grad - columns[:, 4 + 2 * slot : 5 + 2 * slot] - unit * columns[:, 5 + 2 * slot : 6 + 2 * slot]
        grad = grad * inverse
        if padded != part:
            grad = jnp.where(real_lanes(grad.shape, part), grad, 0.0)
        out_ref[:, slot * padded : (slot + 1) * padded] = grad.astype(BF16)
    for pair, ref in enumerate(dv_refs):
        out_ref[:, 2 * padded + 128 * pair : 2 * padded + 128 * (pair + 1)] = ref[...]


def heads_back(grads, projected, stats, cosine, sine, gains, part, share):
    rows, triple = projected.shape
    padded = triple // 3
    pairs = padded // 128
    narrow = stats.shape[0]
    pair_spec = pl.BlockSpec((QBLOCK, 128), lambda i: (i, 0))
    two_spec = pl.BlockSpec((QBLOCK, 2 * padded), lambda i: (i, 0))
    stat_spec = pl.BlockSpec((narrow, 8, QBLOCK), lambda i: (0, 0, i))
    gain_spec = pl.BlockSpec((2, padded), lambda i: (0, 0))
    own, sums = pl.pallas_call(
        functools.partial(grad_stats_kernel, rows, part, pairs),
        grid=(pl.cdiv(rows, QBLOCK),),
        in_specs=[pair_spec] * (2 * pairs) + [two_spec, stat_spec, pair_spec, pair_spec, gain_spec],
        out_specs=[
            pl.BlockSpec((8, QBLOCK), lambda i: (0, i)),
            pl.BlockSpec((8, padded), lambda i: (0, 0)),
        ],
        out_shape=[jax.ShapeDtypeStruct((8, rows), F32), jax.ShapeDtypeStruct((8, padded), F32)],
        compiler_params=pltpu.CompilerParams(vmem_limit_bytes=VMEM_LIMIT),
        cost_estimate=pl.CostEstimate(flops=40 * rows * triple, bytes_accessed=5 * rows * triple, transcendentals=0),
    )(*grads[0], *grads[1], projected, stats, cosine, sine, gains)
    totals = share(own)
    out = pl.pallas_call(
        functools.partial(heads_back_kernel, part, pairs),
        grid=(pl.cdiv(rows, QBLOCK),),
        in_specs=[pair_spec] * (3 * pairs) + [two_spec, stat_spec, stat_spec, pair_spec, pair_spec, gain_spec],
        out_specs=pl.BlockSpec((QBLOCK, triple), lambda i: (i, 0)),
        out_shape=jax.ShapeDtypeStruct((rows, triple), BF16),
        compiler_params=pltpu.CompilerParams(vmem_limit_bytes=VMEM_LIMIT),
        cost_estimate=pl.CostEstimate(flops=40 * rows * triple, bytes_accessed=7 * rows * triple, transcendentals=0),
    )(*grads[0], *grads[1], *grads[2], projected, stats, totals, cosine, sine, gains)
    return out, sums


def head_lanes(rows, half, head_dim):
    lane = lax.broadcasted_iota(jnp.int32, (rows, 128), 1)
    return (lane >= half * head_dim) & (lane < (half + 1) * head_dim)


def softmax_product(pieces):
    maximum = functools.reduce(jnp.maximum, [jnp.max(s, axis=1, keepdims=True) for s, _ in pieces])
    total, result = 0.0, 0.0
    for scores, values in pieces:
        weight = jnp.exp2(scores - maximum)
        total = total + jnp.sum(weight, axis=1, keepdims=True)
        result = result + low_product(weight.astype(BF16), values)
    return result * (1.0 / total), maximum + jnp.log2(total)


def attend_kernel(
    head_dim, first, most, caption, image_count,
    gate_ref, q_ref, k_ref, v_ref, tk_ref, tv_ref, column_ref, row_ref,
    mixed_ref, self_ref, cross_ref, stats_ref,
):
    count = q_ref.shape[0]
    halves = 128 // head_dim

    def emit(at, rows, outs):
        lanes = [head_lanes(rows, half, head_dim) for half in range(halves)]
        own, cross, gated = 0.0, 0.0, 0.0
        columns = []
        for half, (own_out, own_total, cross_out, cross_total) in enumerate(outs):
            gate = gate_ref[0, half]
            own = own + jnp.where(lanes[half], own_out, 0.0)
            cross = cross + jnp.where(lanes[half], cross_out, 0.0)
            gated = gated + jnp.where(lanes[half], gate * cross_out, 0.0)
            columns += [own_total, cross_total]
        self_ref[pl.ds(at, rows), :] = own
        cross_ref[pl.ds(at, rows), :] = cross
        mixed_ref[pl.ds(at, rows), :] = (own + gated).astype(BF16)
        lane = lax.broadcasted_iota(jnp.int32, (rows, 128), 1)
        packed = jnp.zeros((rows, 128), F32)
        for i, column in enumerate(columns):
            packed = jnp.where(lane == i, column, packed)
        stats_ref[:, pl.ds(at, rows)] = jnp.transpose(packed)[:8, :]

    def clean(block, carry):
        at = pl.multiple_of(block * QBLOCK, QBLOCK)
        queries = q_ref[pl.ds(at, QBLOCK), :]
        outs = []
        for half in range(halves):
            q = jnp.where(head_lanes(QBLOCK, half, head_dim), queries, jnp.zeros_like(queries))
            bias = jnp.where(row_ref[0:1, first:most] == 0, 0.0, MASKED)
            own_out, own_total = softmax_product([
                (times_transposed(q, k_ref[0:first, :]), v_ref[0:first, :]),
                (times_transposed(q, k_ref[first:most, :]) + bias, v_ref[first:most, :]),
            ])
            cross_out, cross_total = softmax_product(
                [(times_transposed(q, tk_ref[0:caption, :]), tv_ref[0:caption, :])]
            )
            outs.append((own_out, own_total, cross_out, cross_total))
        emit(at, QBLOCK, outs)
        return carry

    lax.fori_loop(0, first // QBLOCK, clean, 0)
    rest = count - first
    queries = q_ref[first:count, :]
    image = column_ref[first:count, :]
    outs = []
    for half in range(halves):
        q = jnp.where(head_lanes(rest, half, head_dim), queries, jnp.zeros_like(queries))
        own_out, own_total = softmax_product([
            (jnp.where(image == row_ref[0:1, :], times_transposed(q, k_ref[...]), MASKED), v_ref[...])
        ])
        scores = times_transposed(q, tk_ref[...])
        owner = lax.broadcasted_iota(jnp.int32, (1, scores.shape[1]), 1) // caption
        scores = jnp.where((image == owner) | (image == image_count), scores, MASKED)
        cross_out, cross_total = softmax_product([(scores, tv_ref[...])])
        outs.append((own_out, own_total, cross_out, cross_total))
    emit(first, rest, outs)


def attend(pair, gates, packed, text_packed, column, row, head_dim, image_count):
    count, texts = packed.shape[0], text_packed.shape[0]
    pairs = packed.shape[1] // 384
    halves = 128 // head_dim
    out = pl.BlockSpec((count, 128), lambda i: (0, 0))
    most = min(round_up(FIRST_MOST, 128), count)
    flops = 4 * count * (count + texts) * 128
    return pl.pallas_call(
        functools.partial(
            attend_kernel, head_dim, FIRST_PATCHES, most, texts // image_count, image_count
        ),
        grid=(1,),
        in_specs=[
            pl.BlockSpec((None, 1, halves), lambda i: (pair, 0, 0), memory_space=pltpu.SMEM),
            pl.BlockSpec((count, 128), lambda i: (0, pair)),
            pl.BlockSpec((count, 128), lambda i: (0, pairs + pair)),
            pl.BlockSpec((count, 128), lambda i: (0, 2 * pairs + pair)),
            pl.BlockSpec((texts, 128), lambda i: (0, pair)),
            pl.BlockSpec((texts, 128), lambda i: (0, pairs + pair)),
            pl.BlockSpec((count, 1), lambda i: (0, 0)),
            pl.BlockSpec((1, count), lambda i: (0, 0)),
        ],
        out_specs=[out, out, out, pl.BlockSpec((8, count), lambda i: (0, 0))],
        out_shape=[
            jax.ShapeDtypeStruct((count, 128), BF16),
            jax.ShapeDtypeStruct((count, 128), F32),
            jax.ShapeDtypeStruct((count, 128), F32),
            jax.ShapeDtypeStruct((8, count), F32),
        ],
        compiler_params=pltpu.CompilerParams(vmem_limit_bytes=VMEM_LIMIT),
        cost_estimate=pl.CostEstimate(flops=flops, bytes_accessed=20 * count * 128, transcendentals=2 * count * count),
    )(gates.reshape(pairs, 1, halves), packed, packed, packed, text_packed, text_packed, column, row)


def gate_lanes(gate_ref, head_dim):
    lane = lax.broadcasted_iota(jnp.int32, (1, 128), 1)
    gates = jnp.zeros((1, 128), F32)
    for half in range(128 // head_dim):
        gates = jnp.where(lane // head_dim == half, gate_ref[0, half], gates)
    return gates


def head_picks(head_dim):
    return (
        lax.broadcasted_iota(jnp.int32, (8, 128), 1) // head_dim
        == lax.broadcasted_iota(jnp.int32, (8, 128), 0)
    ).astype(F32)


def rows_back(head_dim, queries, outs, delta, stats, offset, keys, values, key_sum, value_sum, spans):
    rows = queries.shape[0]
    halves = 128 // head_dim
    zero = jnp.zeros((rows, 128), BF16)
    lanes = [head_lanes(rows, half, head_dim) for half in range(halves)]
    q_heads = [jnp.where(lane, queries, zero) for lane in lanes]
    out_heads = [jnp.where(lane, outs, zero) for lane in lanes]
    q_stack = jnp.concatenate(q_heads, axis=0)
    out_stack = jnp.concatenate(out_heads, axis=0)
    dq = [0.0] * halves
    for low, high, mask in spans:
        key_part = keys[low:high, :]
        value_part = values[low:high, :]
        probs, grads = [], []
        for half in range(halves):
            scores = mask(times_transposed(key_part, q_heads[half]))
            prob = jnp.exp2(scores - stats[2 * half + offset : 2 * half + offset + 1, :])
            dprob = times_transposed(value_part, out_heads[half])
            dscore = (prob * (dprob - delta[half : half + 1, :])).astype(BF16)
            probs.append(prob.astype(BF16))
            grads.append(dscore)
            dq[half] = dq[half] + outer_sum(dscore, key_part)
        value_sum[low:high, :] += low_product(jnp.concatenate(probs, axis=1), out_stack)
        key_sum[low:high, :] += low_product(jnp.concatenate(grads, axis=1), q_stack)
    total = 0.0
    for half in range(halves):
        total = total + jnp.where(lanes[half], dq[half], 0.0)
    return total


def cross_back_kernel(
    head_dim, first, caption, image_count, scale,
    gate_ref, q_ref, tk_ref, tv_ref, row_ref, grad_ref, cross_ref, stats_ref,
    dq_ref, dtk_ref, dtv_ref, gate_grad_ref, dtk_sum, dtv_sum,
):
    count = q_ref.shape[0]
    for total in (dtk_sum, dtv_sum, gate_grad_ref):
        total[...] = jnp.zeros_like(total)
    gates = gate_lanes(gate_ref, head_dim)
    picks = head_picks(head_dim)

    def part(at, rows, spans):
        wide = grad_ref[pl.ds(at, rows), :].astype(F32)
        cross = cross_ref[pl.ds(at, rows), :]
        gate_grad_ref[0:1, :] += jnp.sum(wide * cross, axis=0, keepdims=True)
        gated = (wide * gates).astype(BF16)
        delta = exact_transposed(picks, gated.astype(F32) * cross)
        dq = rows_back(
            head_dim, q_ref[pl.ds(at, rows), :], gated, delta, stats_ref[:, pl.ds(at, rows)], 1,
            tk_ref, tv_ref, dtk_sum, dtv_sum, spans,
        )
        dq_ref[pl.ds(at, rows), :] = (dq * scale).astype(BF16)

    def clean(block, carry):
        part(pl.multiple_of(block * QBLOCK, QBLOCK), QBLOCK, [(0, caption, lambda scores: scores)])
        return carry

    lax.fori_loop(0, first // QBLOCK, clean, 0)
    image = row_ref[0:1, first:count]
    owner = lax.broadcasted_iota(jnp.int32, (tk_ref.shape[0], 1), 0) // caption
    allowed = (owner == image) | (image == image_count)
    part(first, count - first, [(0, tk_ref.shape[0], lambda scores: jnp.where(allowed, scores, MASKED))])
    dtk_ref[...] = (dtk_sum[...] * (1.0 / LOG2E)).astype(BF16)
    dtv_ref[...] = dtv_sum[...].astype(BF16)


def cross_back(pair, gates, packed, text_packed, row, grad, cross, stats, head_dim, image_count, scale):
    count, texts = packed.shape[0], text_packed.shape[0]
    pairs = packed.shape[1] // 384
    halves = 128 // head_dim
    tokens = pl.BlockSpec((count, 128), lambda i: (0, pair))
    own_tokens = pl.BlockSpec((count, 128), lambda i: (0, 0))
    captions = pl.BlockSpec((texts, 128), lambda i: (0, 0))
    flops = 10 * count * texts * 128
    return pl.pallas_call(
        functools.partial(cross_back_kernel, head_dim, FIRST_PATCHES, texts // image_count, image_count, scale),
        grid=(1,),
        in_specs=[
            pl.BlockSpec((None, 1, halves), lambda i: (pair, 0, 0), memory_space=pltpu.SMEM),
            tokens,
            pl.BlockSpec((texts, 128), lambda i: (0, pair)),
            pl.BlockSpec((texts, 128), lambda i: (0, pairs + pair)),
            pl.BlockSpec((1, count), lambda i: (0, 0)),
            tokens,
            own_tokens,
            pl.BlockSpec((8, count), lambda i: (0, 0)),
        ],
        out_specs=[own_tokens, captions, captions, pl.BlockSpec((8, 128), lambda i: (0, 0))],
        out_shape=[
            jax.ShapeDtypeStruct((count, 128), BF16),
            jax.ShapeDtypeStruct((texts, 128), BF16),
            jax.ShapeDtypeStruct((texts, 128), BF16),
            jax.ShapeDtypeStruct((8, 128), F32),
        ],
        scratch_shapes=[pltpu.VMEM((texts, 128), F32), pltpu.VMEM((texts, 128), F32)],
        compiler_params=pltpu.CompilerParams(vmem_limit_bytes=VMEM_LIMIT),
        cost_estimate=pl.CostEstimate(flops=flops, bytes_accessed=12 * count * 128, transcendentals=count * texts),
    )(gates.reshape(pairs, 1, halves), packed, text_packed, text_packed, row, grad, cross, stats)


def self_back_kernel(
    head_dim, first, most, scale,
    q_ref, k_ref, v_ref, column_ref, row_ref, grad_ref, self_ref, stats_ref, more_ref,
    dq_ref, dk_ref, dv_ref, dk_sum, dv_sum,
):
    count = q_ref.shape[0]
    dk_sum[...] = jnp.zeros_like(dk_sum)
    dv_sum[...] = jnp.zeros_like(dv_sum)
    picks = head_picks(head_dim)

    def part(at, rows, spans):
        grad = grad_ref[pl.ds(at, rows), :]
        delta = exact_transposed(picks, grad.astype(F32) * self_ref[pl.ds(at, rows), :])
        dq = rows_back(
            head_dim, q_ref[pl.ds(at, rows), :], grad, delta, stats_ref[:, pl.ds(at, rows)], 0,
            k_ref, v_ref, dk_sum, dv_sum, spans,
        )
        dq_ref[pl.ds(at, rows), :] = (dq * scale + more_ref[pl.ds(at, rows), :].astype(F32)).astype(BF16)

    def clean(block, carry):
        bias = jnp.where(column_ref[first:most, :] == 0, 0.0, MASKED)
        part(
            pl.multiple_of(block * QBLOCK, QBLOCK), QBLOCK,
            [(0, first, lambda scores: scores), (first, most, lambda scores: scores + bias)],
        )
        return carry

    lax.fori_loop(0, first // QBLOCK, clean, 0)
    image = row_ref[0:1, first:count]
    part(first, count - first, [(0, count, lambda scores: jnp.where(column_ref[...] == image, scores, MASKED))])
    dk_ref[...] = (dk_sum[...] * (1.0 / LOG2E)).astype(BF16)
    dv_ref[...] = dv_sum[...].astype(BF16)


def self_back(pair, packed, column, row, grad, own, stats, more, head_dim, scale):
    count = packed.shape[0]
    pairs = packed.shape[1] // 384
    tokens = pl.BlockSpec((count, 128), lambda i: (0, pair))
    out = pl.BlockSpec((count, 128), lambda i: (0, 0))
    most = min(round_up(FIRST_MOST, 128), count)
    flops = 10 * count * count * 128
    return pl.pallas_call(
        functools.partial(self_back_kernel, head_dim, FIRST_PATCHES, most, scale),
        grid=(1,),
        in_specs=[
            tokens,
            pl.BlockSpec((count, 128), lambda i: (0, pairs + pair)),
            pl.BlockSpec((count, 128), lambda i: (0, 2 * pairs + pair)),
            pl.BlockSpec((count, 1), lambda i: (0, 0)),
            pl.BlockSpec((1, count), lambda i: (0, 0)),
            tokens,
            out,
            pl.BlockSpec((8, count), lambda i: (0, 0)),
            out,
        ],
        out_specs=[out, out, out],
        out_shape=[jax.ShapeDtypeStruct((count, 128), BF16)] * 3,
        scratch_shapes=[pltpu.VMEM((count, 128), F32), pltpu.VMEM((count, 128), F32)],
        compiler_params=pltpu.CompilerParams(vmem_limit_bytes=VMEM_LIMIT),
        cost_estimate=pl.CostEstimate(flops=flops, bytes_accessed=30 * count * 128, transcendentals=2 * count * count),
    )(packed, packed, packed, column, row, grad, own, stats, more)


def swiglu_kernel(core_ref, gate_ref, up_ref, out_ref, moved_ref):
    gate = gate_ref[...]
    half = 0.5 * gate
    value = ((half + half * jnp.tanh(half)) * up_ref[...]).astype(BF16)
    out_ref[...] = value
    moved_ref[...] = value


def swiglu(gate_up, core, deep, narrow):
    rows, double = gate_up.shape
    width = double // 2
    blocks = 2 * deep * narrow
    block = width // blocks

    def moved_place(i, core_ref):
        z, c, f = i // (2 * narrow), (i // narrow) % 2, i % narrow
        return (0, ((c + core_ref[0]) % 2) * (deep * narrow) + f * deep + z)

    return pl.pallas_call(
        swiglu_kernel,
        grid_spec=pltpu.PrefetchScalarGridSpec(
            num_scalar_prefetch=1,
            grid=(blocks,),
            in_specs=[
                pl.BlockSpec((rows, block), lambda i, core_ref: (0, i)),
                pl.BlockSpec((rows, block), lambda i, core_ref: (0, blocks + i)),
            ],
            out_specs=[
                pl.BlockSpec((rows, block), lambda i, core_ref: (0, i)),
                pl.BlockSpec((rows, block), moved_place),
            ],
        ),
        out_shape=[jax.ShapeDtypeStruct((rows, width), BF16)] * 2,
        compiler_params=pltpu.CompilerParams(vmem_limit_bytes=VMEM_LIMIT),
        cost_estimate=pl.CostEstimate(flops=6 * rows * width, bytes_accessed=12 * rows * width, transcendentals=rows * width),
    )(core.reshape(1), gate_up, gate_up)


def fsdp_share_kernel(narrow, x_ref, out_ref, send_sem, recv_sem):
    me = lax.axis_index("fsdp")
    barrier = pltpu.get_barrier_semaphore()
    for step in range(1, narrow):
        pl.semaphore_signal(
            barrier, inc=1, device_id={"fsdp": lax.rem(me + step, narrow)}, device_id_type=pl.DeviceIdType.MESH
        )
    pl.semaphore_wait(barrier, narrow - 1)
    copies = []
    for step in range(1, narrow):
        copy = pltpu.make_async_remote_copy(
            src_ref=x_ref,
            dst_ref=out_ref.at[me],
            send_sem=send_sem.at[step],
            recv_sem=recv_sem.at[step],
            device_id={"fsdp": lax.rem(me + step, narrow)},
            device_id_type=pl.DeviceIdType.MESH,
        )
        copy.start()
        copies.append(copy)
    out_ref[me] = x_ref[...]
    for copy in copies:
        copy.wait()


def fsdp_share(value, narrow, collective_id):
    return pl.pallas_call(
        functools.partial(fsdp_share_kernel, narrow),
        in_specs=[pl.BlockSpec(memory_space=pltpu.VMEM)],
        out_specs=pl.BlockSpec(memory_space=pltpu.VMEM),
        out_shape=jax.ShapeDtypeStruct((narrow,) + value.shape, value.dtype),
        scratch_shapes=[pltpu.SemaphoreType.DMA((narrow,)), pltpu.SemaphoreType.DMA((narrow,))],
        compiler_params=pltpu.CompilerParams(collective_id=collective_id, has_side_effects=True),
        cost_estimate=pl.CostEstimate(flops=0, bytes_accessed=8 * narrow * value.size, transcendentals=0),
    )(value)


def place_rows(items, x_ref, chunk, base):
    rows = [(ref, row) for ref in items for row in range(ref.shape[0])]
    at = 0
    while at < len(rows):
        ref, row = rows[at]
        off = at % chunk
        take = min(ref.shape[0] - row, chunk - off)
        x_ref[at // chunk, base + off : base + off + take, :] = ref[row : row + take, :]
        at += take
    while at < x_ref.shape[0] * chunk:
        off = at % chunk
        x_ref[at // chunk, base + off : base + chunk, :] = jnp.zeros((chunk - off, 128), F32)
        at += chunk - off


def finish_kernel(narrow, wide, sum_rows, sum_count, *refs):
    items, (out_ref, x_ref, first_ref, second_ref, sends, recvs) = refs[:-6], refs[-6:]
    place_rows(items[:sum_count], x_ref, sum_rows, 0)
    place_rows(items[sum_count:], x_ref, x_ref.shape[1] - sum_rows, sum_rows)
    me = lax.axis_index("fsdp")
    group = lax.axis_index("z") * 2 + lax.axis_index("core")
    rows = x_ref.shape[1]
    rest = rows - sum_rows
    barrier = pltpu.get_barrier_semaphore()
    places = [{"fsdp": lax.rem(me + step, narrow)} for step in range(1, narrow)]
    peers = [lax.rem(group + step, wide) for step in range(1, wide)]
    partners = [{"z": peer // 2, "core": peer % 2} for peer in peers]
    for place in places + partners:
        pl.semaphore_signal(barrier, inc=1, device_id=place, device_id_type=pl.DeviceIdType.MESH)
    pl.semaphore_wait(barrier, narrow + wide - 2)

    def send_all(targets, source, target, base):
        copies = []
        for i, place in enumerate(targets):
            copy = pltpu.make_async_remote_copy(
                src_ref=source(i),
                dst_ref=target,
                send_sem=sends.at[base + i],
                recv_sem=recvs.at[base + i],
                device_id=place,
                device_id_type=pl.DeviceIdType.MESH,
            )
            copy.start()
            copies.append(copy)
        return copies

    copies = send_all(places, lambda i: x_ref.at[lax.rem(me + i + 1, narrow)], first_ref.at[me], 0)
    first_ref[me] = x_ref[me]
    for copy in copies:
        copy.wait()
    total = first_ref[0]
    for i in range(1, narrow):
        total = total + first_ref[i]
    second_ref[group] = total
    copies = send_all(partners, lambda i: second_ref.at[group], second_ref.at[group], narrow)
    for copy in copies:
        copy.wait()
    total = second_ref[0, :sum_rows, :]
    for i in range(1, wide):
        total = total + second_ref[i, :sum_rows, :]
    out_ref[me, :sum_rows, :] = total
    for i in range(wide):
        out_ref[me, sum_rows + i * rest : sum_rows + (i + 1) * rest, :] = second_ref[i, sum_rows:, :]
    copies = send_all(places, lambda i: out_ref.at[me], out_ref.at[me], narrow + wide)
    for copy in copies:
        copy.wait()


def finish(summed, kept, narrow, wide, collective_id):
    sum_total = sum(item.shape[0] for item in summed)
    kept_total = sum(item.shape[0] for item in kept)
    sum_rows = round_up(-(-sum_total // narrow), 8)
    kept_rows = round_up(-(-kept_total // narrow), 8)
    rows = sum_rows + kept_rows
    count = 2 * narrow + wide
    out = pl.pallas_call(
        functools.partial(finish_kernel, narrow, wide, sum_rows, len(summed)),
        in_specs=[pl.BlockSpec(memory_space=pltpu.VMEM)] * (len(summed) + len(kept)),
        out_specs=pl.BlockSpec(memory_space=pltpu.VMEM),
        out_shape=jax.ShapeDtypeStruct((narrow, sum_rows + wide * kept_rows, 128), F32),
        scratch_shapes=[
            pltpu.VMEM((narrow, rows, 128), F32),
            pltpu.VMEM((narrow, rows, 128), F32),
            pltpu.VMEM((wide, rows, 128), F32),
            pltpu.SemaphoreType.DMA((count,)),
            pltpu.SemaphoreType.DMA((count,)),
        ],
        compiler_params=pltpu.CompilerParams(collective_id=collective_id, has_side_effects=True),
    )(*summed, *kept)
    total = out[:, :sum_rows, :].reshape(narrow * sum_rows, 128)[:sum_total]
    groups = out[:, sum_rows:, :].reshape(narrow, wide, kept_rows, 128).transpose(1, 0, 2, 3)
    return total, groups.reshape(wide, narrow * kept_rows, 128)[:, :kept_total]


def exchange(blocks, axis):
    return lax.all_to_all(blocks, axis, 0, 0, tiled=True)


def core_swap(value):
    return lax.ppermute(value, "core", [(0, 1), (1, 0)])


def by_core(low, high):
    first = lax.axis_index("core") == 0
    return jnp.where(first, low, high), jnp.where(first, high, low)


def in_core_order(own, other):
    first = lax.axis_index("core") == 0
    return jnp.where(first, own, other), jnp.where(first, other, own)


def chip_sum(own_left, other_left, right):
    came = core_swap(outer_sum(other_left, right).astype(BF16))
    return (outer_sum(own_left, right) + came.astype(F32)).astype(BF16)


def fsdp_sum(both):
    return lax.psum_scatter(both, "fsdp", scatter_dimension=0, tiled=True)


def z_pieces(blocks, deep):
    me = lax.axis_index("z")
    return [lax.dynamic_index_in_dim(blocks, me, 0, keepdims=False)] + [
        lax.ppermute(
            lax.dynamic_index_in_dim(blocks, me ^ step, 0, keepdims=False), "z", [(i, i ^ step) for i in range(deep)]
        )
        for step in range(1, deep)
    ]


def added(pieces):
    return functools.reduce(jnp.add, [piece.astype(F32) for piece in pieces])


def to_all(block, narrow):
    return [
        lax.ppermute(block, "fsdp", [(i, i ^ step) for i in range(narrow)]) for step in range(1, narrow)
    ]


def in_order(block, came):
    me = lax.axis_index("fsdp")
    narrow = len(came) + 1
    result = lax.dynamic_update_slice_in_dim(
        jnp.zeros((narrow,) + block.shape, block.dtype), block[None], me, 0
    )
    for step in range(1, narrow):
        result = lax.dynamic_update_slice_in_dim(result, came[step - 1][None], me ^ step, 0)
    return result


def device_columns(value, deep, narrow):
    rows, width = value.shape
    block = width // (2 * deep * narrow)
    core = lax.axis_index("core")
    target = jnp.arange(width, dtype=jnp.int32)
    c, f, z, r = (
        target // (narrow * deep * block), target // (deep * block) % narrow, target // block % deep, target % block,
    )
    c = (c + core) % 2
    source = ((z * 2 + c) * narrow + f) * block + r
    pick = (jnp.arange(width, dtype=jnp.int32)[:, None] == source[None, :]).astype(BF16)
    moved = low_product(value, pick).astype(BF16)
    return moved[:, : width // 2], moved[:, width // 2 :]


def whole_weight(shard):
    rows = shard.shape[0] // 2
    half = lax.dynamic_slice_in_dim(shard, lax.axis_index("core") * rows, rows, 0)
    return lax.all_gather(half, ("fsdp", "core"), axis=0, tiled=True)


def shards(
    tokens,
    cotangent,
    text_states,
    conditioning,
    image_sizes,
    ada_weight,
    ada_bias,
    qkv_weight,
    out_weight,
    text_weight,
    gate_up_weight,
    down_weight,
    norm_gains,
    norm_shifts,
    text_gain,
    head_gate,
):
    model_width = tokens.shape[2]
    head_count = head_gate.shape[0]
    head_dim = model_width // head_count
    image_count = text_states.shape[1]
    caption_local = text_states.shape[2]
    caption_width = text_states.shape[3]
    local_tok = tokens.shape[1]
    deep = lax.axis_size("z")
    narrow = lax.axis_size("fsdp")
    wide = 2 * deep
    me = lax.axis_index("fsdp")
    group_tok = local_tok * narrow
    caption_full = caption_local * narrow
    score_scale = head_dim ** (-0.5)
    text_total = image_count * caption_full
    text_local = image_count * caption_local
    part = model_width // narrow
    part_pad = round_up(part, 128)
    heads_here = head_count // narrow
    pairs = part_pad // 128
    halves = 128 // head_dim

    group_sizes = image_sizes[0]
    position = me * local_tok + jnp.arange(local_tok, dtype=jnp.int32)
    image_index = token_layout(group_sizes, position, image_count)[0]
    key_image, key_row, key_col = token_layout(
        group_sizes, jnp.arange(group_tok, dtype=jnp.int32), image_count
    )
    member = [(image_index == i).astype(F32)[:, None] for i in range(image_count)]
    cosine, sine = rope_tables(key_row, key_col, head_dim)

    cond_low = jax.nn.silu(conditioning[0].astype(F32)).astype(BF16)
    cond_rows = ada_weight.shape[0]
    cond_part = lax.dynamic_slice_in_dim(cond_low, me * cond_rows, cond_rows, 1)
    modulation_part = low_product(cond_part, ada_weight)
    modulation = (
        jnp.sum(fsdp_share(modulation_part.reshape(-1, 128), narrow, 0), axis=0).reshape(modulation_part.shape)
        + ada_bias
    )

    def per_token(index):
        rows = modulation[:, index * model_width : (index + 1) * model_width]
        return functools.reduce(
            jnp.add, [member[i] * rows[i : i + 1, :] for i in range(image_count)]
        )

    def per_image(value):
        return [jnp.sum(member[i] * value, axis=0).reshape(-1, 128) for i in range(image_count)]

    token_in = tokens[0].astype(F32)
    token_inverse = inverse_rms(token_in)
    tokens_all = lax.all_gather(tokens[0], "fsdp", axis=0, tiled=True)
    def widened(value, slots):
        if part == part_pad:
            return value
        lead = value.shape[:-1]
        value = value.reshape(*lead, slots, part)
        pads = [(0, 0)] * (len(lead) + 1) + [(0, part_pad - part)]
        return jnp.pad(value, pads).reshape(*lead, slots * part_pad)

    def narrowed(value, slots):
        if part == part_pad:
            return value
        lead = value.shape[:-1]
        return value.reshape(*lead, slots, part_pad)[..., :part].reshape(*lead, slots * part)

    def own_columns(value):
        return widened(lax.dynamic_slice_in_dim(value, me * part, part, value.ndim - 1), 1)

    qkv_rows = qkv_weight.shape[0] // 2
    qkv_half = lax.dynamic_slice_in_dim(qkv_weight, lax.axis_index("core") * qkv_rows, qkv_rows, 0)
    qkv_half = exchange(
        qkv_half.reshape(qkv_rows, 3, narrow, part).transpose(2, 0, 1, 3).reshape(narrow, qkv_rows, 3 * part), "fsdp"
    )
    own_qkv = widened(
        jnp.concatenate(in_core_order(qkv_half, core_swap(qkv_half)), axis=1).reshape(model_width, 3 * part), 3
    )

    full_out = whole_weight(out_weight)
    full_gate_up = whole_weight(gate_up_weight)
    full_down = whole_weight(down_weight)

    text_in = text_states[0].astype(F32).reshape(text_local, caption_width)
    text_inverse = inverse_rms(text_in)
    text_low = (text_in * text_inverse * text_gain).astype(BF16)
    text_cols = caption_width // narrow
    text_slice = (
        exchange(text_low.reshape(text_local, narrow, text_cols).transpose(1, 0, 2), "fsdp")
        .reshape(narrow, image_count, caption_local, text_cols)
        .transpose(1, 0, 2, 3)
        .reshape(text_total, text_cols)
    )
    own_text_weight = (
        text_weight.reshape(text_cols, 2, narrow, part).transpose(2, 0, 1, 3).reshape(narrow, text_cols, 2 * part)
    )
    text_partial = jnp.stack([low_product(text_slice, own_text_weight[i]).astype(BF16) for i in range(narrow)])
    text_partial, tokens_all = lax.optimization_barrier((text_partial, tokens_all))
    text_projected = widened(jnp.sum(exchange(text_partial, "fsdp").astype(F32), axis=0), 2)
    text_parts = fsdp_share(column_stats(text_projected, part, part_pad, 1), narrow, 1)
    text_means = text_parts[:, 0, :]
    text_mean = jnp.mean(text_means, axis=0)
    text_square = jnp.sum(text_parts[:, 1, :], axis=0) + part * jnp.sum((text_means - text_mean) ** 2, axis=0)
    text_key_inverse = lax.rsqrt(text_square / model_width + EPS)[:, None]
    text_unit = (text_projected[:, :part_pad] - text_mean[:, None]) * text_key_inverse
    text_gains = own_columns(norm_gains[4])
    text_packed = jnp.concatenate(
        [(text_unit * text_gains).astype(BF16), text_projected[:, part_pad:].astype(BF16)], axis=1
    )

    wide_tokens = tokens_all.astype(F32)
    wide_scale = functools.reduce(
        jnp.add,
        [(key_image == i).astype(F32)[:, None] * modulation[i : i + 1, :model_width] for i in range(image_count)],
    )
    normed_all = (wide_tokens * inverse_rms(wide_tokens) * norm_gains[0] * (1.0 + wide_scale)).astype(BF16)

    projected = low_product(normed_all, own_qkv)
    stats_all = fsdp_share(column_stats(projected, part, part_pad, 2), narrow, 2)
    head_gains = own_columns(norm_gains[2:4])
    packed = make_heads(
        projected, stats_all, cosine, sine, head_gains, own_columns(norm_shifts), part, score_scale * LOG2E
    )
    gate_tanh = jnp.tanh(head_gate)
    own_gates = lax.dynamic_slice_in_dim(gate_tanh, me * heads_here, heads_here, 0)
    own_gates = jnp.concatenate([own_gates, jnp.ones((pairs * halves - heads_here,), F32)])
    column = key_image[:, None]
    row = key_image[None, :]
    attended = [
        attend(pair, own_gates, packed, text_packed, column, row, head_dim, image_count) for pair in range(pairs)
    ]
    mixed_pairs = [exchange(one[0].reshape(narrow, local_tok, 128), "fsdp") for one in attended]
    self_outs = [one[1] for one in attended]
    cross_outs = [one[2] for one in attended]
    stats = [one[3] for one in attended]
    mixed_low = (
        narrowed(jnp.concatenate(mixed_pairs, axis=2), 1).transpose(1, 0, 2).reshape(local_tok, model_width)
    )

    branch = low_product(mixed_low, full_out)
    branch_inverse = inverse_rms(branch)
    branch_unit = branch * branch_inverse
    gate_attend = jnp.tanh(per_token(1))
    hidden = token_in + gate_attend * (branch_unit * norm_gains[1])
    hidden_inverse = inverse_rms(hidden)
    hidden_unit = hidden * hidden_inverse
    scale_feed = 1.0 + per_token(2)
    normed_feed_low = (hidden_unit * norm_gains[5] * scale_feed).astype(BF16)
    gate_up = low_product(normed_feed_low, full_gate_up)
    hidden_units = gate_up.shape[1] // 2
    gate_half = gate_up[:, :hidden_units]
    up_half = gate_up[:, hidden_units:]
    sigmoid = jax.nn.sigmoid(gate_half)
    if hidden_units // (wide * narrow) % 128 == 0:
        activated_low, moved = swiglu(gate_up, lax.axis_index("core"), deep, narrow)
        down_columns = (moved[:, : hidden_units // 2], moved[:, hidden_units // 2 :])
    else:
        activated_low = (gate_half * sigmoid * up_half).astype(BF16)
        down_columns = device_columns(activated_low, deep, narrow)
    down_out = low_product(activated_low, full_down)
    down_inverse = inverse_rms(down_out)
    down_unit = down_out * down_inverse
    gate_feed = jnp.tanh(per_token(3))
    down_normed = down_unit * norm_gains[6]
    result = (hidden + gate_feed * down_normed).astype(BF16)

    grad_result = cotangent[0].astype(F32)
    grad_down_y = grad_result * gate_feed
    grad_gain_six = jnp.sum(grad_down_y * down_unit, axis=0)
    grad_gate_feed = per_image(grad_result * down_normed * (1.0 - gate_feed * gate_feed))
    grad_down_low = norm_pull(grad_down_y * norm_gains[6], down_unit, down_inverse).astype(BF16)
    grad_activated = times_transposed(grad_down_low, full_down)
    grad_gate_up_low = jnp.concatenate(
        [
            (grad_activated * up_half * sigmoid * (1.0 + gate_half * (1.0 - sigmoid))).astype(BF16),
            (grad_activated * gate_half * sigmoid).astype(BF16),
        ],
        axis=1,
    )
    grad_normed_feed = times_transposed(grad_gate_up_low, full_gate_up)
    grad_feed_y = grad_normed_feed * scale_feed
    grad_gain_five = jnp.sum(grad_feed_y * hidden_unit, axis=0)
    grad_scale_feed = per_image(grad_normed_feed * hidden_unit * norm_gains[5])
    grad_hidden = grad_result + norm_pull(grad_feed_y * norm_gains[5], hidden_unit, hidden_inverse)
    grad_branch_y = grad_hidden * gate_attend
    grad_gain_one = jnp.sum(grad_branch_y * branch_unit, axis=0)
    grad_gate_attend = per_image(
        grad_hidden * branch_unit * norm_gains[1] * (1.0 - gate_attend * gate_attend)
    )
    grad_branch_low = norm_pull(grad_branch_y * norm_gains[1], branch_unit, branch_inverse).astype(BF16)
    grad_mixed = times_transposed(grad_branch_low, full_out).astype(BF16)
    grad_blocks = widened(grad_mixed.reshape(local_tok, narrow, part).transpose(1, 0, 2), 1)
    grad_heads = exchange(grad_blocks, "fsdp").reshape(group_tok, part_pad)
    def by_z(value):
        return value.reshape(deep, -1, value.shape[1])

    down_both = chip_sum(*down_columns, grad_down_low)
    gate_up_both = chip_sum(*device_columns(normed_feed_low, deep, narrow), grad_gate_up_low)
    out_both = chip_sum(*device_columns(mixed_low, deep, narrow), grad_branch_low)
    down_part = fsdp_sum(down_both)
    grad_heads, gate_up_both, out_both, down_part = lax.optimization_barrier(
        (grad_heads, gate_up_both, out_both, down_part)
    )
    came_downs = exchange(by_z(down_part), "z")
    gate_up_part = fsdp_sum(gate_up_both)
    out_part = fsdp_sum(out_both)
    crossed = [
        cross_back(
            pair, own_gates, packed, text_packed, row, grad_heads, cross_outs[pair], stats[pair],
            head_dim, image_count, score_scale,
        )
        for pair in range(pairs)
    ]
    dtk = jnp.concatenate([one[1] for one in crossed], axis=1)
    dtv = jnp.concatenate([one[2] for one in crossed], axis=1)
    gate_sums = jnp.stack([one[3] for one in crossed])

    grad_text_keys = dtk.astype(F32)
    own_gain_four = jnp.sum(grad_text_keys * text_unit, axis=0)
    grad_text_unit = grad_text_keys * text_gains
    text_sums = jnp.stack([jnp.sum(grad_text_unit, axis=1), jnp.sum(grad_text_unit * text_unit, axis=1)])
    text_sums = jnp.sum(
        fsdp_share(jnp.pad(text_sums, ((0, 6), (0, 0))), narrow, 3), axis=0
    ) * (1.0 / model_width)
    grad_text_key_in = (grad_text_unit - text_sums[0][:, None] - text_unit * text_sums[1][:, None]) * text_key_inverse
    grad_text_own = jnp.concatenate(
        [narrowed(grad_text_key_in.astype(BF16), 1), narrowed(dtv, 1)], axis=1
    )
    def self_pair(pair):
        return self_back(
            pair, packed, column, row, grad_heads, self_outs[pair], stats[pair], crossed[pair][0], head_dim, score_scale
        )

    came_texts = to_all(grad_text_own, narrow)
    backs = [self_pair(0)]
    first, came_downs, *came_texts = lax.optimization_barrier((backs[0][0], came_downs, *came_texts))
    grad_down_weight = jnp.sum(came_downs.astype(F32), axis=0)
    backs[0] = (first, *backs[0][1:])
    grad_text_all = in_order(grad_text_own, came_texts)
    grad_text_columns = (
        grad_text_all.reshape(narrow, text_total, 2, part).transpose(1, 2, 0, 3).reshape(text_total, 2 * model_width)
    )
    text_half = text_cols // 2
    own_text, other_text = by_core(text_slice[:, :text_half], text_slice[:, text_half:])
    came_text = core_swap(outer_sum(other_text, grad_text_columns).astype(BF16))
    text_both = (outer_sum(own_text, grad_text_columns) + came_text.astype(F32)).astype(BF16)
    grad_heads, text_both, first = lax.optimization_barrier((grad_heads, text_both, backs[0][0]))
    backs[0] = (first, *backs[0][1:])
    text_part = lax.psum_scatter(text_both, "z", scatter_dimension=0, tiled=True)
    backs.append(self_pair(1))
    if pairs > 2:
        grad_heads, gate_up_part, out_part, second = lax.optimization_barrier(
            (grad_heads, gate_up_part, out_part, backs[1][0])
        )
        backs[1] = (second, *backs[1][1:])
        backs += [self_pair(pair) for pair in range(2, pairs)]
    grad_gate_up_weight = added(z_pieces(by_z(gate_up_part), deep))
    last, text_part = lax.optimization_barrier((backs[-1][0], text_part))
    backs[-1] = (last, *backs[-1][1:])
    came_out_z = exchange(by_z(out_part), "z")
    own_gate_grad = jnp.sum(gate_sums[:, 0, :].reshape(pairs * halves, head_dim), axis=1)[:heads_here]
    grad_head_gate = lax.dynamic_update_slice_in_dim(
        jnp.zeros((head_count,), F32), own_gate_grad, me * heads_here, 0
    ) * (1.0 - gate_tanh * gate_tanh)
    grad_projected_low, head_sums = heads_back(
        list(zip(*backs)), projected, stats_all, cosine, sine, head_gains, part,
        lambda value: fsdp_share(value, narrow, 4),
    )
    everyone = ("z", "core", "fsdp")
    grad_text_weight = lax.ppermute(
        text_part,
        everyone,
        [
            ((z * 2 + c) * narrow + f, f * wide + c * deep + z)
            for z in range(deep) for c in range(2) for f in range(narrow)
        ],
    )
    grad_projected_low, grad_gate_up_weight = lax.optimization_barrier((grad_projected_low, grad_gate_up_weight))
    grad_normed = lax.psum_scatter(
        times_transposed(grad_projected_low, own_qkv).astype(BF16), "fsdp", scatter_dimension=0, tiled=True
    )

    def lane_rows(value):
        return value.reshape(-1, 128)

    group = lax.axis_index("z") * 2 + lax.axis_index("core")
    columns_here = jnp.stack(
        [narrowed(value, 1) for value in (head_sums[0], head_sums[2], own_gain_four, head_sums[1], head_sums[3])]
    )
    here = (jnp.arange(narrow, dtype=jnp.int32) == me)[None, :, None]
    placed = lane_rows(jnp.where(here, columns_here[:, None, :], 0.0))
    cond_rows_here = lane_rows(jnp.where(me == 0, cond_low.astype(F32), 0.0))
    gate_row = jnp.pad(grad_head_gate, (0, 128 - head_count)).reshape(1, 128)
    ready = [lane_rows(grad_gain_one), lane_rows(grad_gain_five), lane_rows(grad_gain_six), placed, gate_row]
    later = [*grad_gate_attend, *grad_scale_feed, *grad_gate_feed, cond_rows_here]
    ready = lax.optimization_barrier(tuple(ready))
    qkv_grad = outer_sum(normed_all, grad_projected_low).astype(BF16).reshape(deep, 2, model_width // wide, 3 * part_pad)
    qkv_grad, came_out_z, grad_text_weight = lax.optimization_barrier((qkv_grad, came_out_z, grad_text_weight))
    grad_text_weight = grad_text_weight.astype(F32)
    grad_out_weight = jnp.sum(came_out_z.astype(F32), axis=0)
    own_grad, other_grad = by_core(qkv_grad[:, 0], qkv_grad[:, 1])
    own_grad = (own_grad.astype(F32) + core_swap(other_grad).astype(F32)).astype(BF16)
    own_grad, grad_text_columns = lax.optimization_barrier((own_grad, grad_text_columns))
    own_pieces = z_pieces(own_grad, deep)
    grad_text_slice = times_transposed(grad_text_columns, text_weight).astype(BF16)
    came_text = exchange(
        grad_text_slice.reshape(image_count, narrow, caption_local, text_cols)
        .transpose(1, 0, 2, 3)
        .reshape(narrow, text_local, text_cols),
        "fsdp",
    )

    grad_text_normed = (
        came_text
        .transpose(1, 0, 2)
        .reshape(text_local, caption_width)
        .astype(F32)
    )
    text_state_unit = text_in * text_inverse
    grad_text_gain = jnp.sum(grad_text_normed * text_state_unit, axis=0)
    grad_text = (
        norm_pull(grad_text_normed * text_gain, text_state_unit, text_inverse)
        .astype(BF16)
        .reshape(image_count, caption_local, caption_width)
    )

    grad_text, grad_text_gain, *own_pieces = lax.optimization_barrier((grad_text, grad_text_gain, *own_pieces))
    own_grad = added(own_pieces)
    grad_qkv_weight = (
        exchange(narrowed(own_grad.astype(BF16), 3).reshape(narrow, -1, 3 * part), "fsdp")
        .reshape(narrow, -1, 3, part)
        .transpose(1, 2, 0, 3)
        .reshape(-1, 3 * model_width)
        .astype(F32)
    )

    grad_normed = grad_normed.astype(F32)

    token_unit = token_in * token_inverse
    scale_attend = 1.0 + per_token(0)
    grad_normed_y = grad_normed * scale_attend
    grad_gain_zero = jnp.sum(grad_normed_y * token_unit, axis=0)
    grad_scale_attend = per_image(grad_normed * token_unit * norm_gains[0])
    grad_tokens = (
        grad_hidden + norm_pull(grad_normed_y * norm_gains[0], token_unit, token_inverse)
    ).astype(BF16)
    lanes_of_row = model_width // 128
    summed, kept = finish(
        [lane_rows(grad_gain_zero), *ready, lane_rows(grad_text_gain)], [*grad_scale_attend, *later], narrow, wide, 5
    )
    every_image = wide * image_count
    per_part = image_count * lanes_of_row
    slots = jnp.concatenate(
        [kept[:, i * per_part : (i + 1) * per_part].reshape(every_image, model_width) for i in range(4)], axis=1
    )
    cond_slots = kept[:, 4 * per_part :].reshape(every_image, cond_low.shape[1])
    ada_rows = cond_rows // wide
    own_cond = lax.dynamic_slice_in_dim(cond_slots, (group * narrow + me) * ada_rows, ada_rows, 1)
    grad_ada_weight = exact_outer(own_cond, slots)
    grad_ada_bias = jnp.sum(slots, axis=0)

    def rows_of(first, count):
        return summed[first * lanes_of_row : (first + count) * lanes_of_row]

    grad_gains = jnp.concatenate([rows_of(0, 2), rows_of(4, 3), rows_of(2, 2)]).reshape(norm_gains.shape)
    grad_shifts = rows_of(7, 2).reshape(norm_shifts.shape)
    grad_head_gate = summed[9 * lanes_of_row, :head_count]
    grad_text_gain = summed[9 * lanes_of_row + 1 :].reshape(-1)
    return (
        result[None],
        grad_tokens[None],
        grad_text[None],
        grad_ada_weight,
        grad_qkv_weight,
        grad_out_weight,
        grad_text_weight,
        grad_gate_up_weight,
        grad_down_weight,
        grad_ada_bias,
        grad_gains,
        grad_shifts,
        grad_text_gain,
        grad_head_gate,
    )


def solution(mesh):
    wide, narrow = mesh.devices.shape
    fine = Mesh(mesh.devices.reshape(wide // 2, 2, narrow), ("z", "core", "fsdp"))
    groups = ("z", "core")
    every = ("z", "core", "fsdp")
    placed = (
        P(groups, "fsdp", None),
        P(groups, "fsdp", None),
        P(groups, None, "fsdp", None),
        P(groups, None, None),
        P(groups, None, None),
        P("fsdp", None),
        P(),
        P("fsdp", None),
        P("fsdp", None),
        P("fsdp", None),
        P("fsdp", None),
        P("fsdp", None),
        P(),
        P(),
        P(),
        P(),
    )
    return jax.shard_map(
        shards,
        mesh=fine,
        in_specs=placed,
        out_specs=(
            P(groups, "fsdp", None),
            P(groups, "fsdp", None),
            P(groups, None, "fsdp", None),
            P(every, None),
            P(every, None),
            P(every, None),
            P(every, None),
            P(every, None),
            P(every, None),
            P(),
            P(),
            P(),
            P(),
            P(),
        ),
        check_vma=False,
    )
```

```python
import functools

import jax
import jax.numpy as jnp
from jax import lax
from jax.experimental import pallas as pl
from jax.experimental.pallas import tpu as pltpu
from jax.sharding import Mesh
from jax.sharding import PartitionSpec as P

EPS = 1e-05
HIGHEST_PRECISION = lax.Precision.HIGHEST
MASKED = -1e30
LOG2E = 1.4426950408889634
FIRST_PATCHES = 16 * 12**2
FIRST_MOST = FIRST_PATCHES + 96
QBLOCK = 256
BF16 = jnp.bfloat16
F32 = jnp.float32
VMEM_LIMIT = 60 * 1024 * 1024


def round_up(value, step):
    return -(-value // step) * step


def low_product(left, right):
    return jnp.dot(left, right, preferred_element_type=F32)


def times_transposed(left, right):
    return lax.dot_general(left, right, (((1,), (1,)), ((), ())), preferred_element_type=F32)


def outer_sum(left, right):
    return lax.dot_general(left, right, (((0,), (0,)), ((), ())), preferred_element_type=F32)


def exact_outer(left, right):
    return lax.dot_general(
        left, right, (((0,), (0,)), ((), ())), precision=HIGHEST_PRECISION, preferred_element_type=F32
    )


def exact_transposed(left, right):
    return lax.dot_general(
        left, right, (((1,), (1,)), ((), ())), precision=HIGHEST_PRECISION, preferred_element_type=F32
    )


def row_mean(value):
    return jnp.mean(value, axis=-1, keepdims=True)


def inverse_rms(value):
    return lax.rsqrt(row_mean(value * value) + EPS)


def norm_pull(grad, unit, inverse):
    return (grad - unit * row_mean(grad * unit)) * inverse


def token_layout(image_sizes, position, image_count):
    start = jnp.int32(0)
    image_index = jnp.full(position.shape, image_count, jnp.int32)
    token_row = jnp.zeros(position.shape, jnp.int32)
    token_col = jnp.zeros(position.shape, jnp.int32)
    for i in range(image_count):
        width = image_sizes[i, 1] + 1
        end = start + image_sizes[i, 0] * width
        inside = (position >= start) & (position < end)
        offset = position - start
        image_index = jnp.where(inside, i, image_index)
        token_row = jnp.where(inside, offset // width, token_row)
        token_col = jnp.where(inside, offset % width, token_col)
        start = end
    return image_index, token_row, token_col


def rope_tables(token_row, token_col, head_dim):
    quarter = head_dim // 4
    pair = (jnp.arange(128, dtype=jnp.int32) % head_dim) // 2
    frequency = 10000.0 ** (-(pair % quarter).astype(F32) / quarter)
    place = jnp.where(
        (pair < quarter)[None, :], token_row.astype(F32)[:, None], token_col.astype(F32)[:, None]
    )
    angles = place * frequency[None, :]
    even = (jnp.arange(128, dtype=jnp.int32) % 2 == 0)[None, :]
    return jnp.cos(angles), jnp.where(even, -jnp.sin(angles), jnp.sin(angles))


def swap_pairs(value):
    width = value.shape[1]
    even = lax.broadcasted_iota(jnp.int32, value.shape, 1) % 2 == 0
    return jnp.where(even, pltpu.roll(value, width - 1, 1), pltpu.roll(value, 1, 1))


def wide_table(table, width):
    return jnp.concatenate([table] * (width // table.shape[1]), axis=1)


def pack_columns(columns):
    rows = columns[0].shape[0]
    lane = lax.broadcasted_iota(jnp.int32, (rows, 128), 1)
    packed = jnp.zeros((rows, 128), F32)
    for i, column in enumerate(columns):
        packed = jnp.where(lane == i, column, packed)
    return jnp.transpose(packed)[:8, :]


def as_columns(rows_list):
    width = rows_list[0].shape[1]
    stacked = jnp.concatenate(
        rows_list + [jnp.zeros((128 - len(rows_list), width), F32)], axis=0
    )
    return jnp.transpose(stacked)


def real_lanes(shape, part):
    return lax.broadcasted_iota(jnp.int32, shape, 1) < part


def own_stats(value, part):
    mean = jnp.sum(value, axis=1, keepdims=True) * (1.0 / part)
    centred = value - mean
    if value.shape[1] != part:
        centred = jnp.where(real_lanes(value.shape, part), centred, 0.0)
    return mean, jnp.sum(centred * centred, axis=1, keepdims=True)


def joined_stats(stats_ref, part, slot):
    narrow = stats_ref.shape[0]
    means = [stats_ref[i, 2 * slot : 2 * slot + 1, :] for i in range(narrow)]
    squares = [stats_ref[i, 2 * slot + 1 : 2 * slot + 2, :] for i in range(narrow)]
    mean = functools.reduce(jnp.add, means) * (1.0 / narrow)
    square = functools.reduce(jnp.add, squares)
    square = square + part * functools.reduce(jnp.add, [(m - mean) * (m - mean) for m in means])
    return mean, lax.rsqrt(square * (1.0 / (narrow * part)) + EPS)


def stats_kernel(part, slots, projected_ref, out_ref):
    padded = projected_ref.shape[1] // slots
    columns = []
    for slot in range(slots):
        columns += own_stats(projected_ref[:, slot * padded : (slot + 1) * padded], part)
    out_ref[...] = pack_columns(columns)


def column_stats(projected, part, padded, slots):
    rows = projected.shape[0]
    return pl.pallas_call(
        functools.partial(stats_kernel, part, slots),
        grid=(pl.cdiv(rows, QBLOCK),),
        in_specs=[pl.BlockSpec((QBLOCK, slots * padded), lambda i: (i, 0))],
        out_specs=pl.BlockSpec((8, QBLOCK), lambda i: (0, i)),
        out_shape=jax.ShapeDtypeStruct((8, rows), F32),
        compiler_params=pltpu.CompilerParams(vmem_limit_bytes=VMEM_LIMIT),
        cost_estimate=pl.CostEstimate(flops=10 * rows * slots * padded, bytes_accessed=4 * rows * slots * padded, transcendentals=0),
    )(projected)


def heads_kernel(part, query_scale, projected_ref, stats_ref, cos_ref, sin_ref, gains_ref, shifts_ref, out_ref):
    padded = projected_ref.shape[1] // 3
    cosine = wide_table(cos_ref[...], padded)
    sine = wide_table(sin_ref[...], padded)
    columns = as_columns([*joined_stats(stats_ref, part, 0), *joined_stats(stats_ref, part, 1)])
    for slot in range(3):
        place = slice(slot * padded, (slot + 1) * padded)
        value = projected_ref[:, place]
        if slot < 2:
            value = (value - columns[:, 2 * slot : 2 * slot + 1]) * columns[:, 2 * slot + 1 : 2 * slot + 2]
            value = value * gains_ref[slot : slot + 1, :] + shifts_ref[slot : slot + 1, :]
            value = value * cosine + swap_pairs(value) * sine
            if slot == 0:
                value = value * query_scale
        out_ref[:, place] = value.astype(BF16)


def make_heads(projected, stats, cosine, sine, gains, shifts, part, query_scale):
    rows, triple = projected.shape
    padded = triple // 3
    narrow = stats.shape[0]
    return pl.pallas_call(
        functools.partial(heads_kernel, part, query_scale),
        grid=(pl.cdiv(rows, QBLOCK),),
        in_specs=[
            pl.BlockSpec((QBLOCK, triple), lambda i: (i, 0)),
            pl.BlockSpec((narrow, 8, QBLOCK), lambda i: (0, 0, i)),
            pl.BlockSpec((QBLOCK, 128), lambda i: (i, 0)),
            pl.BlockSpec((QBLOCK, 128), lambda i: (i, 0)),
            pl.BlockSpec((2, padded), lambda i: (0, 0)),
            pl.BlockSpec((2, padded), lambda i: (0, 0)),
        ],
        out_specs=pl.BlockSpec((QBLOCK, triple), lambda i: (i, 0)),
        out_shape=jax.ShapeDtypeStruct((rows, triple), BF16),
        compiler_params=pltpu.CompilerParams(vmem_limit_bytes=VMEM_LIMIT),
        cost_estimate=pl.CostEstimate(flops=40 * rows * triple, bytes_accessed=6 * rows * triple, transcendentals=0),
    )(projected, stats, cosine, sine, gains, shifts)


def turned_back(refs, cosine, sine):
    grad = jnp.concatenate([ref[...].astype(F32) for ref in refs], axis=1)
    return grad * cosine - swap_pairs(grad) * sine


def grad_stats_kernel(rows, part, pairs, *refs):
    dq_refs, dk_refs = refs[:pairs], refs[pairs : 2 * pairs]
    projected_ref, stats_ref, cos_ref, sin_ref, gains_ref, out_ref, sums_ref = refs[2 * pairs :]
    step = pl.program_id(0)
    padded = 128 * pairs
    cosine = wide_table(cos_ref[...], padded)
    sine = wide_table(sin_ref[...], padded)
    height = cos_ref.shape[0]
    inside = step * height + lax.broadcasted_iota(jnp.int32, (height, 1), 0) < rows

    @pl.when(step == 0)
    def _():
        sums_ref[...] = jnp.zeros_like(sums_ref)

    columns = as_columns([*joined_stats(stats_ref, part, 0), *joined_stats(stats_ref, part, 1)])
    packed = []
    for slot, grads in enumerate((dq_refs, dk_refs)):
        grad = jnp.where(inside, turned_back(grads, cosine, sine), 0.0)
        unit = (projected_ref[:, slot * padded : (slot + 1) * padded] - columns[:, 2 * slot : 2 * slot + 1])
        unit = jnp.where(inside, unit * columns[:, 2 * slot + 1 : 2 * slot + 2], 0.0)
        both = grad * unit
        sums_ref[2 * slot : 2 * slot + 1, :] += jnp.sum(both, axis=0, keepdims=True)
        sums_ref[2 * slot + 1 : 2 * slot + 2, :] += jnp.sum(grad, axis=0, keepdims=True)
        gain = gains_ref[slot : slot + 1, :]
        packed.append(jnp.sum(grad * gain, axis=1, keepdims=True))
        packed.append(jnp.sum(both * gain, axis=1, keepdims=True))
    out_ref[...] = pack_columns(packed)


def heads_back_kernel(part, pairs, *refs):
    dq_refs, dk_refs, dv_refs = refs[:pairs], refs[pairs : 2 * pairs], refs[2 * pairs : 3 * pairs]
    projected_ref, stats_ref, totals_ref, cos_ref, sin_ref, gains_ref, out_ref = refs[3 * pairs :]
    padded = 128 * pairs
    narrow = stats_ref.shape[0]
    cosine = wide_table(cos_ref[...], padded)
    sine = wide_table(sin_ref[...], padded)
    means = [
        functools.reduce(jnp.add, [totals_ref[i, j : j + 1, :] for i in range(narrow)]) * (1.0 / (narrow * part))
        for j in range(4)
    ]
    columns = as_columns([*joined_stats(stats_ref, part, 0), *joined_stats(stats_ref, part, 1), *means])
    for slot, grads in enumerate((dq_refs, dk_refs)):
        grad = turned_back(grads, cosine, sine) * gains_ref[slot : slot + 1, :]
        inverse = columns[:, 2 * slot + 1 : 2 * slot + 2]
        unit = (projected_ref[:, slot * padded : (slot + 1) * padded] - columns[:, 2 * slot : 2 * slot + 1]) * inverse
        grad = grad - columns[:, 4 + 2 * slot : 5 + 2 * slot] - unit * columns[:, 5 + 2 * slot : 6 + 2 * slot]
        grad = grad * inverse
        if padded != part:
            grad = jnp.where(real_lanes(grad.shape, part), grad, 0.0)
        out_ref[:, slot * padded : (slot + 1) * padded] = grad.astype(BF16)
    for pair, ref in enumerate(dv_refs):
        out_ref[:, 2 * padded + 128 * pair : 2 * padded + 128 * (pair + 1)] = ref[...]


def heads_back(grads, projected, stats, cosine, sine, gains, part, share):
    rows, triple = projected.shape
    padded = triple // 3
    pairs = padded // 128
    narrow = stats.shape[0]
    pair_spec = pl.BlockSpec((QBLOCK, 128), lambda i: (i, 0))
    two_spec = pl.BlockSpec((QBLOCK, 2 * padded), lambda i: (i, 0))
    stat_spec = pl.BlockSpec((narrow, 8, QBLOCK), lambda i: (0, 0, i))
    gain_spec = pl.BlockSpec((2, padded), lambda i: (0, 0))
    own, sums = pl.pallas_call(
        functools.partial(grad_stats_kernel, rows, part, pairs),
        grid=(pl.cdiv(rows, QBLOCK),),
        in_specs=[pair_spec] * (2 * pairs) + [two_spec, stat_spec, pair_spec, pair_spec, gain_spec],
        out_specs=[
            pl.BlockSpec((8, QBLOCK), lambda i: (0, i)),
            pl.BlockSpec((8, padded), lambda i: (0, 0)),
        ],
        out_shape=[jax.ShapeDtypeStruct((8, rows), F32), jax.ShapeDtypeStruct((8, padded), F32)],
        compiler_params=pltpu.CompilerParams(vmem_limit_bytes=VMEM_LIMIT),
        cost_estimate=pl.CostEstimate(flops=40 * rows * triple, bytes_accessed=5 * rows * triple, transcendentals=0),
    )(*grads[0], *grads[1], projected, stats, cosine, sine, gains)
    totals = share(own)
    out = pl.pallas_call(
        functools.partial(heads_back_kernel, part, pairs),
        grid=(pl.cdiv(rows, QBLOCK),),
        in_specs=[pair_spec] * (3 * pairs) + [two_spec, stat_spec, stat_spec, pair_spec, pair_spec, gain_spec],
        out_specs=pl.BlockSpec((QBLOCK, triple), lambda i: (i, 0)),
        out_shape=jax.ShapeDtypeStruct((rows, triple), BF16),
        compiler_params=pltpu.CompilerParams(vmem_limit_bytes=VMEM_LIMIT),
        cost_estimate=pl.CostEstimate(flops=40 * rows * triple, bytes_accessed=7 * rows * triple, transcendentals=0),
    )(*grads[0], *grads[1], *grads[2], projected, stats, totals, cosine, sine, gains)
    return out, sums


def head_lanes(rows, half, head_dim):
    lane = lax.broadcasted_iota(jnp.int32, (rows, 128), 1)
    return (lane >= half * head_dim) & (lane < (half + 1) * head_dim)


def softmax_product(pieces):
    maximum = functools.reduce(jnp.maximum, [jnp.max(s, axis=1, keepdims=True) for s, _ in pieces])
    total, result = 0.0, 0.0
    for scores, values in pieces:
        weight = jnp.exp2(scores - maximum)
        total = total + jnp.sum(weight, axis=1, keepdims=True)
        result = result + low_product(weight.astype(BF16), values)
    return result * (1.0 / total), maximum + jnp.log2(total)


def attend_kernel(
    head_dim, first, most, caption, image_count,
    gate_ref, q_ref, k_ref, v_ref, tk_ref, tv_ref, column_ref, row_ref,
    mixed_ref, self_ref, cross_ref, stats_ref,
):
    count = q_ref.shape[0]
    halves = 128 // head_dim

    def emit(at, rows, outs):
        lanes = [head_lanes(rows, half, head_dim) for half in range(halves)]
        own, cross, gated = 0.0, 0.0, 0.0
        columns = []
        for half, (own_out, own_total, cross_out, cross_total) in enumerate(outs):
            gate = gate_ref[0, half]
            own = own + jnp.where(lanes[half], own_out, 0.0)
            cross = cross + jnp.where(lanes[half], cross_out, 0.0)
            gated = gated + jnp.where(lanes[half], gate * cross_out, 0.0)
            columns += [own_total, cross_total]
        self_ref[pl.ds(at, rows), :] = own
        cross_ref[pl.ds(at, rows), :] = cross
        mixed_ref[pl.ds(at, rows), :] = (own + gated).astype(BF16)
        lane = lax.broadcasted_iota(jnp.int32, (rows, 128), 1)
        packed = jnp.zeros((rows, 128), F32)
        for i, column in enumerate(columns):
            packed = jnp.where(lane == i, column, packed)
        stats_ref[:, pl.ds(at, rows)] = jnp.transpose(packed)[:8, :]

    def clean(block, carry):
        at = pl.multiple_of(block * QBLOCK, QBLOCK)
        queries = q_ref[pl.ds(at, QBLOCK), :]
        outs = []
        for half in range(halves):
            q = jnp.where(head_lanes(QBLOCK, half, head_dim), queries, jnp.zeros_like(queries))
            bias = jnp.where(row_ref[0:1, first:most] == 0, 0.0, MASKED)
            own_out, own_total = softmax_product([
                (times_transposed(q, k_ref[0:first, :]), v_ref[0:first, :]),
                (times_transposed(q, k_ref[first:most, :]) + bias, v_ref[first:most, :]),
            ])
            cross_out, cross_total = softmax_product(
                [(times_transposed(q, tk_ref[0:caption, :]), tv_ref[0:caption, :])]
            )
            outs.append((own_out, own_total, cross_out, cross_total))
        emit(at, QBLOCK, outs)
        return carry

    lax.fori_loop(0, first // QBLOCK, clean, 0)
    rest = count - first
    queries = q_ref[first:count, :]
    image = column_ref[first:count, :]
    outs = []
    for half in range(halves):
        q = jnp.where(head_lanes(rest, half, head_dim), queries, jnp.zeros_like(queries))
        own_out, own_total = softmax_product([
            (jnp.where(image == row_ref[0:1, :], times_transposed(q, k_ref[...]), MASKED), v_ref[...])
        ])
        scores = times_transposed(q, tk_ref[...])
        owner = lax.broadcasted_iota(jnp.int32, (1, scores.shape[1]), 1) // caption
        scores = jnp.where((image == owner) | (image == image_count), scores, MASKED)
        cross_out, cross_total = softmax_product([(scores, tv_ref[...])])
        outs.append((own_out, own_total, cross_out, cross_total))
    emit(first, rest, outs)


def attend(pair, gates, packed, text_packed, column, row, head_dim, image_count):
    count, texts = packed.shape[0], text_packed.shape[0]
    pairs = packed.shape[1] // 384
    halves = 128 // head_dim
    out = pl.BlockSpec((count, 128), lambda i: (0, 0))
    most = min(round_up(FIRST_MOST, 128), count)
    flops = 4 * count * (count + texts) * 128
    return pl.pallas_call(
        functools.partial(
            attend_kernel, head_dim, FIRST_PATCHES, most, texts // image_count, image_count
        ),
        grid=(1,),
        in_specs=[
            pl.BlockSpec((None, 1, halves), lambda i: (pair, 0, 0), memory_space=pltpu.SMEM),
            pl.BlockSpec((count, 128), lambda i: (0, pair)),
            pl.BlockSpec((count, 128), lambda i: (0, pairs + pair)),
            pl.BlockSpec((count, 128), lambda i: (0, 2 * pairs + pair)),
            pl.BlockSpec((texts, 128), lambda i: (0, pair)),
            pl.BlockSpec((texts, 128), lambda i: (0, pairs + pair)),
            pl.BlockSpec((count, 1), lambda i: (0, 0)),
            pl.BlockSpec((1, count), lambda i: (0, 0)),
        ],
        out_specs=[out, out, out, pl.BlockSpec((8, count), lambda i: (0, 0))],
        out_shape=[
            jax.ShapeDtypeStruct((count, 128), BF16),
            jax.ShapeDtypeStruct((count, 128), F32),
            jax.ShapeDtypeStruct((count, 128), F32),
            jax.ShapeDtypeStruct((8, count), F32),
        ],
        compiler_params=pltpu.CompilerParams(vmem_limit_bytes=VMEM_LIMIT),
        cost_estimate=pl.CostEstimate(flops=flops, bytes_accessed=20 * count * 128, transcendentals=2 * count * count),
    )(gates.reshape(pairs, 1, halves), packed, packed, packed, text_packed, text_packed, column, row)


def gate_lanes(gate_ref, head_dim):
    lane = lax.broadcasted_iota(jnp.int32, (1, 128), 1)
    gates = jnp.zeros((1, 128), F32)
    for half in range(128 // head_dim):
        gates = jnp.where(lane // head_dim == half, gate_ref[0, half], gates)
    return gates


def head_picks(head_dim):
    return (
        lax.broadcasted_iota(jnp.int32, (8, 128), 1) // head_dim
        == lax.broadcasted_iota(jnp.int32, (8, 128), 0)
    ).astype(F32)


def rows_back(head_dim, queries, outs, delta, stats, offset, keys, values, key_sum, value_sum, spans):
    rows = queries.shape[0]
    halves = 128 // head_dim
    zero = jnp.zeros((rows, 128), BF16)
    lanes = [head_lanes(rows, half, head_dim) for half in range(halves)]
    q_heads = [jnp.where(lane, queries, zero) for lane in lanes]
    out_heads = [jnp.where(lane, outs, zero) for lane in lanes]
    q_stack = jnp.concatenate(q_heads, axis=0)
    out_stack = jnp.concatenate(out_heads, axis=0)
    dq = [0.0] * halves
    for low, high, mask in spans:
        key_part = keys[low:high, :]
        value_part = values[low:high, :]
        probs, grads = [], []
        for half in range(halves):
            scores = mask(times_transposed(key_part, q_heads[half]))
            prob = jnp.exp2(scores - stats[2 * half + offset : 2 * half + offset + 1, :])
            dprob = times_transposed(value_part, out_heads[half])
            dscore = (prob * (dprob - delta[half : half + 1, :])).astype(BF16)
            probs.append(prob.astype(BF16))
            grads.append(dscore)
            dq[half] = dq[half] + outer_sum(dscore, key_part)
        value_sum[low:high, :] += low_product(jnp.concatenate(probs, axis=1), out_stack)
        key_sum[low:high, :] += low_product(jnp.concatenate(grads, axis=1), q_stack)
    total = 0.0
    for half in range(halves):
        total = total + jnp.where(lanes[half], dq[half], 0.0)
    return total


def cross_back_kernel(
    head_dim, first, caption, image_count, scale,
    gate_ref, q_ref, tk_ref, tv_ref, row_ref, grad_ref, cross_ref, stats_ref,
    dq_ref, dtk_ref, dtv_ref, gate_grad_ref, dtk_sum, dtv_sum,
):
    count = q_ref.shape[0]
    for total in (dtk_sum, dtv_sum, gate_grad_ref):
        total[...] = jnp.zeros_like(total)
    gates = gate_lanes(gate_ref, head_dim)
    picks = head_picks(head_dim)

    def part(at, rows, spans):
        wide = grad_ref[pl.ds(at, rows), :].astype(F32)
        cross = cross_ref[pl.ds(at, rows), :]
        gate_grad_ref[0:1, :] += jnp.sum(wide * cross, axis=0, keepdims=True)
        gated = (wide * gates).astype(BF16)
        delta = exact_transposed(picks, gated.astype(F32) * cross)
        dq = rows_back(
            head_dim, q_ref[pl.ds(at, rows), :], gated, delta, stats_ref[:, pl.ds(at, rows)], 1,
            tk_ref, tv_ref, dtk_sum, dtv_sum, spans,
        )
        dq_ref[pl.ds(at, rows), :] = (dq * scale).astype(BF16)

    def clean(block, carry):
        part(pl.multiple_of(block * QBLOCK, QBLOCK), QBLOCK, [(0, caption, lambda scores: scores)])
        return carry

    lax.fori_loop(0, first // QBLOCK, clean, 0)
    image = row_ref[0:1, first:count]
    owner = lax.broadcasted_iota(jnp.int32, (tk_ref.shape[0], 1), 0) // caption
    allowed = (owner == image) | (image == image_count)
    part(first, count - first, [(0, tk_ref.shape[0], lambda scores: jnp.where(allowed, scores, MASKED))])
    dtk_ref[...] = (dtk_sum[...] * (1.0 / LOG2E)).astype(BF16)
    dtv_ref[...] = dtv_sum[...].astype(BF16)


def cross_back(pair, gates, packed, text_packed, row, grad, cross, stats, head_dim, image_count, scale):
    count, texts = packed.shape[0], text_packed.shape[0]
    pairs = packed.shape[1] // 384
    halves = 128 // head_dim
    tokens = pl.BlockSpec((count, 128), lambda i: (0, pair))
    own_tokens = pl.BlockSpec((count, 128), lambda i: (0, 0))
    captions = pl.BlockSpec((texts, 128), lambda i: (0, 0))
    flops = 10 * count * texts * 128
    return pl.pallas_call(
        functools.partial(cross_back_kernel, head_dim, FIRST_PATCHES, texts // image_count, image_count, scale),
        grid=(1,),
        in_specs=[
            pl.BlockSpec((None, 1, halves), lambda i: (pair, 0, 0), memory_space=pltpu.SMEM),
            tokens,
            pl.BlockSpec((texts, 128), lambda i: (0, pair)),
            pl.BlockSpec((texts, 128), lambda i: (0, pairs + pair)),
            pl.BlockSpec((1, count), lambda i: (0, 0)),
            tokens,
            own_tokens,
            pl.BlockSpec((8, count), lambda i: (0, 0)),
        ],
        out_specs=[own_tokens, captions, captions, pl.BlockSpec((8, 128), lambda i: (0, 0))],
        out_shape=[
            jax.ShapeDtypeStruct((count, 128), BF16),
            jax.ShapeDtypeStruct((texts, 128), BF16),
            jax.ShapeDtypeStruct((texts, 128), BF16),
            jax.ShapeDtypeStruct((8, 128), F32),
        ],
        scratch_shapes=[pltpu.VMEM((texts, 128), F32), pltpu.VMEM((texts, 128), F32)],
        compiler_params=pltpu.CompilerParams(vmem_limit_bytes=VMEM_LIMIT),
        cost_estimate=pl.CostEstimate(flops=flops, bytes_accessed=12 * count * 128, transcendentals=count * texts),
    )(gates.reshape(pairs, 1, halves), packed, text_packed, text_packed, row, grad, cross, stats)


def self_back_kernel(
    head_dim, first, most, scale,
    q_ref, k_ref, v_ref, column_ref, row_ref, grad_ref, self_ref, stats_ref, more_ref,
    dq_ref, dk_ref, dv_ref, dk_sum, dv_sum,
):
    count = q_ref.shape[0]
    dk_sum[...] = jnp.zeros_like(dk_sum)
    dv_sum[...] = jnp.zeros_like(dv_sum)
    picks = head_picks(head_dim)

    def part(at, rows, spans):
        grad = grad_ref[pl.ds(at, rows), :]
        delta = exact_transposed(picks, grad.astype(F32) * self_ref[pl.ds(at, rows), :])
        dq = rows_back(
            head_dim, q_ref[pl.ds(at, rows), :], grad, delta, stats_ref[:, pl.ds(at, rows)], 0,
            k_ref, v_ref, dk_sum, dv_sum, spans,
        )
        dq_ref[pl.ds(at, rows), :] = (dq * scale + more_ref[pl.ds(at, rows), :].astype(F32)).astype(BF16)

    def clean(block, carry):
        bias = jnp.where(column_ref[first:most, :] == 0, 0.0, MASKED)
        part(
            pl.multiple_of(block * QBLOCK, QBLOCK), QBLOCK,
            [(0, first, lambda scores: scores), (first, most, lambda scores: scores + bias)],
        )
        return carry

    lax.fori_loop(0, first // QBLOCK, clean, 0)
    image = row_ref[0:1, first:count]
    part(first, count - first, [(0, count, lambda scores: jnp.where(column_ref[...] == image, scores, MASKED))])
    dk_ref[...] = (dk_sum[...] * (1.0 / LOG2E)).astype(BF16)
    dv_ref[...] = dv_sum[...].astype(BF16)


def self_back(pair, packed, column, row, grad, own, stats, more, head_dim, scale):
    count = packed.shape[0]
    pairs = packed.shape[1] // 384
    tokens = pl.BlockSpec((count, 128), lambda i: (0, pair))
    out = pl.BlockSpec((count, 128), lambda i: (0, 0))
    most = min(round_up(FIRST_MOST, 128), count)
    flops = 10 * count * count * 128
    return pl.pallas_call(
        functools.partial(self_back_kernel, head_dim, FIRST_PATCHES, most, scale),
        grid=(1,),
        in_specs=[
            tokens,
            pl.BlockSpec((count, 128), lambda i: (0, pairs + pair)),
            pl.BlockSpec((count, 128), lambda i: (0, 2 * pairs + pair)),
            pl.BlockSpec((count, 1), lambda i: (0, 0)),
            pl.BlockSpec((1, count), lambda i: (0, 0)),
            tokens,
            out,
            pl.BlockSpec((8, count), lambda i: (0, 0)),
            out,
        ],
        out_specs=[out, out, out],
        out_shape=[jax.ShapeDtypeStruct((count, 128), BF16)] * 3,
        scratch_shapes=[pltpu.VMEM((count, 128), F32), pltpu.VMEM((count, 128), F32)],
        compiler_params=pltpu.CompilerParams(vmem_limit_bytes=VMEM_LIMIT),
        cost_estimate=pl.CostEstimate(flops=flops, bytes_accessed=30 * count * 128, transcendentals=2 * count * count),
    )(packed, packed, packed, column, row, grad, own, stats, more)


def swiglu_kernel(core_ref, gate_ref, up_ref, out_ref, moved_ref):
    gate = gate_ref[...]
    half = 0.5 * gate
    value = ((half + half * jnp.tanh(half)) * up_ref[...]).astype(BF16)
    out_ref[...] = value
    moved_ref[...] = value


def swiglu(gate_up, core, deep, narrow):
    rows, double = gate_up.shape
    width = double // 2
    blocks = 2 * deep * narrow
    block = width // blocks

    def moved_place(i, core_ref):
        z, c, f = i // (2 * narrow), (i // narrow) % 2, i % narrow
        return (0, ((c + core_ref[0]) % 2) * (deep * narrow) + f * deep + z)

    return pl.pallas_call(
        swiglu_kernel,
        grid_spec=pltpu.PrefetchScalarGridSpec(
            num_scalar_prefetch=1,
            grid=(blocks,),
            in_specs=[
                pl.BlockSpec((rows, block), lambda i, core_ref: (0, i)),
                pl.BlockSpec((rows, block), lambda i, core_ref: (0, blocks + i)),
            ],
            out_specs=[
                pl.BlockSpec((rows, block), lambda i, core_ref: (0, i)),
                pl.BlockSpec((rows, block), moved_place),
            ],
        ),
        out_shape=[jax.ShapeDtypeStruct((rows, width), BF16)] * 2,
        compiler_params=pltpu.CompilerParams(vmem_limit_bytes=VMEM_LIMIT),
        cost_estimate=pl.CostEstimate(flops=6 * rows * width, bytes_accessed=12 * rows * width, transcendentals=rows * width),
    )(core.reshape(1), gate_up, gate_up)


def fsdp_share_kernel(narrow, x_ref, out_ref, send_sem, recv_sem):
    me = lax.axis_index("fsdp")
    barrier = pltpu.get_barrier_semaphore()
    for step in range(1, narrow):
        pl.semaphore_signal(
            barrier, inc=1, device_id={"fsdp": lax.rem(me + step, narrow)}, device_id_type=pl.DeviceIdType.MESH
        )
    pl.semaphore_wait(barrier, narrow - 1)
    copies = []
    for step in range(1, narrow):
        copy = pltpu.make_async_remote_copy(
            src_ref=x_ref,
            dst_ref=out_ref.at[me],
            send_sem=send_sem.at[step],
            recv_sem=recv_sem.at[step],
            device_id={"fsdp": lax.rem(me + step, narrow)},
            device_id_type=pl.DeviceIdType.MESH,
        )
        copy.start()
        copies.append(copy)
    out_ref[me] = x_ref[...]
    for copy in copies:
        copy.wait()


def fsdp_share(value, narrow, collective_id):
    return pl.pallas_call(
        functools.partial(fsdp_share_kernel, narrow),
        in_specs=[pl.BlockSpec(memory_space=pltpu.VMEM)],
        out_specs=pl.BlockSpec(memory_space=pltpu.VMEM),
        out_shape=jax.ShapeDtypeStruct((narrow,) + value.shape, value.dtype),
        scratch_shapes=[pltpu.SemaphoreType.DMA((narrow,)), pltpu.SemaphoreType.DMA((narrow,))],
        compiler_params=pltpu.CompilerParams(collective_id=collective_id, has_side_effects=True),
        cost_estimate=pl.CostEstimate(flops=0, bytes_accessed=8 * narrow * value.size, transcendentals=0),
    )(value)


def place_rows(items, x_ref, chunk, base):
    rows = [(ref, row) for ref in items for row in range(ref.shape[0])]
    at = 0
    while at < len(rows):
        ref, row = rows[at]
        off = at % chunk
        take = min(ref.shape[0] - row, chunk - off)
        x_ref[at // chunk, base + off : base + off + take, :] = ref[row : row + take, :]
        at += take
    while at < x_ref.shape[0] * chunk:
        off = at % chunk
        x_ref[at // chunk, base + off : base + chunk, :] = jnp.zeros((chunk - off, 128), F32)
        at += chunk - off


def finish_kernel(narrow, wide, sum_rows, sum_count, *refs):
    items, (out_ref, x_ref, first_ref, second_ref, sends, recvs) = refs[:-6], refs[-6:]
    place_rows(items[:sum_count], x_ref, sum_rows, 0)
    place_rows(items[sum_count:], x_ref, x_ref.shape[1] - sum_rows, sum_rows)
    me = lax.axis_index("fsdp")
    group = lax.axis_index("z") * 2 + lax.axis_index("core")
    rows = x_ref.shape[1]
    rest = rows - sum_rows
    barrier = pltpu.get_barrier_semaphore()
    places = [{"fsdp": lax.rem(me + step, narrow)} for step in range(1, narrow)]
    peers = [lax.rem(group + step, wide) for step in range(1, wide)]
    partners = [{"z": peer // 2, "core": peer % 2} for peer in peers]
    for place in places + partners:
        pl.semaphore_signal(barrier, inc=1, device_id=place, device_id_type=pl.DeviceIdType.MESH)
    pl.semaphore_wait(barrier, narrow + wide - 2)

    def send_all(targets, source, target, base):
        copies = []
        for i, place in enumerate(targets):
            copy = pltpu.make_async_remote_copy(
                src_ref=source(i),
                dst_ref=target,
                send_sem=sends.at[base + i],
                recv_sem=recvs.at[base + i],
                device_id=place,
                device_id_type=pl.DeviceIdType.MESH,
            )
            copy.start()
            copies.append(copy)
        return copies

    copies = send_all(places, lambda i: x_ref.at[lax.rem(me + i + 1, narrow)], first_ref.at[me], 0)
    first_ref[me] = x_ref[me]
    for copy in copies:
        copy.wait()
    total = first_ref[0]
    for i in range(1, narrow):
        total = total + first_ref[i]
    second_ref[group] = total
    copies = send_all(partners, lambda i: second_ref.at[group], second_ref.at[group], narrow)
    for copy in copies:
        copy.wait()
    total = second_ref[0, :sum_rows, :]
    for i in range(1, wide):
        total = total + second_ref[i, :sum_rows, :]
    out_ref[me, :sum_rows, :] = total
    for i in range(wide):
        out_ref[me, sum_rows + i * rest : sum_rows + (i + 1) * rest, :] = second_ref[i, sum_rows:, :]
    copies = send_all(places, lambda i: out_ref.at[me], out_ref.at[me], narrow + wide)
    for copy in copies:
        copy.wait()


def finish(summed, kept, narrow, wide, collective_id):
    sum_total = sum(item.shape[0] for item in summed)
    kept_total = sum(item.shape[0] for item in kept)
    sum_rows = round_up(-(-sum_total // narrow), 8)
    kept_rows = round_up(-(-kept_total // narrow), 8)
    rows = sum_rows + kept_rows
    count = 2 * narrow + wide
    out = pl.pallas_call(
        functools.partial(finish_kernel, narrow, wide, sum_rows, len(summed)),
        in_specs=[pl.BlockSpec(memory_space=pltpu.VMEM)] * (len(summed) + len(kept)),
        out_specs=pl.BlockSpec(memory_space=pltpu.VMEM),
        out_shape=jax.ShapeDtypeStruct((narrow, sum_rows + wide * kept_rows, 128), F32),
        scratch_shapes=[
            pltpu.VMEM((narrow, rows, 128), F32),
            pltpu.VMEM((narrow, rows, 128), F32),
            pltpu.VMEM((wide, rows, 128), F32),
            pltpu.SemaphoreType.DMA((count,)),
            pltpu.SemaphoreType.DMA((count,)),
        ],
        compiler_params=pltpu.CompilerParams(collective_id=collective_id, has_side_effects=True),
    )(*summed, *kept)
    total = out[:, :sum_rows, :].reshape(narrow * sum_rows, 128)[:sum_total]
    groups = out[:, sum_rows:, :].reshape(narrow, wide, kept_rows, 128).transpose(1, 0, 2, 3)
    return total, groups.reshape(wide, narrow * kept_rows, 128)[:, :kept_total]


def exchange(blocks, axis):
    return lax.all_to_all(blocks, axis, 0, 0, tiled=True)


def core_swap(value):
    return lax.ppermute(value, "core", [(0, 1), (1, 0)])


def by_core(low, high):
    first = lax.axis_index("core") == 0
    return jnp.where(first, low, high), jnp.where(first, high, low)


def in_core_order(own, other):
    first = lax.axis_index("core") == 0
    return jnp.where(first, own, other), jnp.where(first, other, own)


def chip_sum(own_left, other_left, right):
    came = core_swap(outer_sum(other_left, right).astype(BF16))
    return (outer_sum(own_left, right) + came.astype(F32)).astype(BF16)


def fsdp_sum(both):
    return lax.psum_scatter(both, "fsdp", scatter_dimension=0, tiled=True)


def z_pieces(blocks, deep):
    me = lax.axis_index("z")
    return [lax.dynamic_index_in_dim(blocks, me, 0, keepdims=False)] + [
        lax.ppermute(
            lax.dynamic_index_in_dim(blocks, me ^ step, 0, keepdims=False), "z", [(i, i ^ step) for i in range(deep)]
        )
        for step in range(1, deep)
    ]


def added(pieces):
    return functools.reduce(jnp.add, [piece.astype(F32) for piece in pieces])


def to_all(block, narrow):
    return [
        lax.ppermute(block, "fsdp", [(i, i ^ step) for i in range(narrow)]) for step in range(1, narrow)
    ]


def in_order(block, came):
    me = lax.axis_index("fsdp")
    narrow = len(came) + 1
    result = lax.dynamic_update_slice_in_dim(
        jnp.zeros((narrow,) + block.shape, block.dtype), block[None], me, 0
    )
    for step in range(1, narrow):
        result = lax.dynamic_update_slice_in_dim(result, came[step - 1][None], me ^ step, 0)
    return result


def device_columns(value, deep, narrow):
    rows, width = value.shape
    block = width // (2 * deep * narrow)
    core = lax.axis_index("core")
    target = jnp.arange(width, dtype=jnp.int32)
    c, f, z, r = (
        target // (narrow * deep * block), target // (deep * block) % narrow, target // block % deep, target % block,
    )
    c = (c + core) % 2
    source = ((z * 2 + c) * narrow + f) * block + r
    pick = (jnp.arange(width, dtype=jnp.int32)[:, None] == source[None, :]).astype(BF16)
    moved = low_product(value, pick).astype(BF16)
    return moved[:, : width // 2], moved[:, width // 2 :]


def whole_weight(shard):
    rows = shard.shape[0] // 2
    half = lax.dynamic_slice_in_dim(shard, lax.axis_index("core") * rows, rows, 0)
    return lax.all_gather(half, ("fsdp", "core"), axis=0, tiled=True)


def shards(
    tokens,
    cotangent,
    text_states,
    conditioning,
    image_sizes,
    ada_weight,
    ada_bias,
    qkv_weight,
    out_weight,
    text_weight,
    gate_up_weight,
    down_weight,
    norm_gains,
    norm_shifts,
    text_gain,
    head_gate,
):
    model_width = tokens.shape[2]
    head_count = head_gate.shape[0]
    head_dim = model_width // head_count
    image_count = text_states.shape[1]
    caption_local = text_states.shape[2]
    caption_width = text_states.shape[3]
    local_tok = tokens.shape[1]
    deep = lax.axis_size("z")
    narrow = lax.axis_size("fsdp")
    wide = 2 * deep
    me = lax.axis_index("fsdp")
    group_tok = local_tok * narrow
    caption_full = caption_local * narrow
    score_scale = head_dim ** (-0.5)
    text_total = image_count * caption_full
    text_local = image_count * caption_local
    part = model_width // narrow
    part_pad = round_up(part, 128)
    heads_here = head_count // narrow
    pairs = part_pad // 128
    halves = 128 // head_dim

    group_sizes = image_sizes[0]
    position = me * local_tok + jnp.arange(local_tok, dtype=jnp.int32)
    image_index = token_layout(group_sizes, position, image_count)[0]
    key_image, key_row, key_col = token_layout(
        group_sizes, jnp.arange(group_tok, dtype=jnp.int32), image_count
    )
    member = [(image_index == i).astype(F32)[:, None] for i in range(image_count)]
    cosine, sine = rope_tables(key_row, key_col, head_dim)

    cond_low = jax.nn.silu(conditioning[0].astype(F32)).astype(BF16)
    cond_rows = ada_weight.shape[0]
    cond_part = lax.dynamic_slice_in_dim(cond_low, me * cond_rows, cond_rows, 1)
    modulation_part = low_product(cond_part, ada_weight)
    modulation = (
        jnp.sum(fsdp_share(modulation_part.reshape(-1, 128), narrow, 0), axis=0).reshape(modulation_part.shape)
        + ada_bias
    )

    def per_token(index):
        rows = modulation[:, index * model_width : (index + 1) * model_width]
        return functools.reduce(
            jnp.add, [member[i] * rows[i : i + 1, :] for i in range(image_count)]
        )

    def per_image(value):
        return [jnp.sum(member[i] * value, axis=0).reshape(-1, 128) for i in range(image_count)]

    token_in = tokens[0].astype(F32)
    token_inverse = inverse_rms(token_in)
    tokens_all = lax.all_gather(tokens[0], "fsdp", axis=0, tiled=True)
    def widened(value, slots):
        if part == part_pad:
            return value
        lead = value.shape[:-1]
        value = value.reshape(*lead, slots, part)
        pads = [(0, 0)] * (len(lead) + 1) + [(0, part_pad - part)]
        return jnp.pad(value, pads).reshape(*lead, slots * part_pad)

    def narrowed(value, slots):
        if part == part_pad:
            return value
        lead = value.shape[:-1]
        return value.reshape(*lead, slots, part_pad)[..., :part].reshape(*lead, slots * part)

    def own_columns(value):
        return widened(lax.dynamic_slice_in_dim(value, me * part, part, value.ndim - 1), 1)

    qkv_rows = qkv_weight.shape[0] // 2
    qkv_half = lax.dynamic_slice_in_dim(qkv_weight, lax.axis_index("core") * qkv_rows, qkv_rows, 0)
    qkv_half = exchange(
        qkv_half.reshape(qkv_rows, 3, narrow, part).transpose(2, 0, 1, 3).reshape(narrow, qkv_rows, 3 * part), "fsdp"
    )
    own_qkv = widened(
        jnp.concatenate(in_core_order(qkv_half, core_swap(qkv_half)), axis=1).reshape(model_width, 3 * part), 3
    )

    full_out = whole_weight(out_weight)
    full_gate_up = whole_weight(gate_up_weight)
    full_down = whole_weight(down_weight)

    text_in = text_states[0].astype(F32).reshape(text_local, caption_width)
    text_inverse = inverse_rms(text_in)
    text_low = (text_in * text_inverse * text_gain).astype(BF16)
    text_cols = caption_width // narrow
    text_slice = (
        exchange(text_low.reshape(text_local, narrow, text_cols).transpose(1, 0, 2), "fsdp")
        .reshape(narrow, image_count, caption_local, text_cols)
        .transpose(1, 0, 2, 3)
        .reshape(text_total, text_cols)
    )
    own_text_weight = (
        text_weight.reshape(text_cols, 2, narrow, part).transpose(2, 0, 1, 3).reshape(narrow, text_cols, 2 * part)
    )
    text_partial = jnp.stack([low_product(text_slice, own_text_weight[i]).astype(BF16) for i in range(narrow)])
    text_partial, tokens_all = lax.optimization_barrier((text_partial, tokens_all))
    text_projected = widened(jnp.sum(exchange(text_partial, "fsdp").astype(F32), axis=0), 2)
    text_parts = fsdp_share(column_stats(text_projected, part, part_pad, 1), narrow, 1)
    text_means = text_parts[:, 0, :]
    text_mean = jnp.mean(text_means, axis=0)
    text_square = jnp.sum(text_parts[:, 1, :], axis=0) + part * jnp.sum((text_means - text_mean) ** 2, axis=0)
    text_key_inverse = lax.rsqrt(text_square / model_width + EPS)[:, None]
    text_unit = (text_projected[:, :part_pad] - text_mean[:, None]) * text_key_inverse
    text_gains = own_columns(norm_gains[4])
    text_packed = jnp.concatenate(
        [(text_unit * text_gains).astype(BF16), text_projected[:, part_pad:].astype(BF16)], axis=1
    )

    wide_tokens = tokens_all.astype(F32)
    wide_scale = functools.reduce(
        jnp.add,
        [(key_image == i).astype(F32)[:, None] * modulation[i : i + 1, :model_width] for i in range(image_count)],
    )
    normed_all = (wide_tokens * inverse_rms(wide_tokens) * norm_gains[0] * (1.0 + wide_scale)).astype(BF16)

    projected = low_product(normed_all, own_qkv)
    stats_all = fsdp_share(column_stats(projected, part, part_pad, 2), narrow, 2)
    head_gains = own_columns(norm_gains[2:4])
    packed = make_heads(
        projected, stats_all, cosine, sine, head_gains, own_columns(norm_shifts), part, score_scale * LOG2E
    )
    gate_tanh = jnp.tanh(head_gate)
    own_gates = lax.dynamic_slice_in_dim(gate_tanh, me * heads_here, heads_here, 0)
    own_gates = jnp.concatenate([own_gates, jnp.ones((pairs * halves - heads_here,), F32)])
    column = key_image[:, None]
    row = key_image[None, :]
    attended = [
        attend(pair, own_gates, packed, text_packed, column, row, head_dim, image_count) for pair in range(pairs)
    ]
    mixed_pairs = [exchange(one[0].reshape(narrow, local_tok, 128), "fsdp") for one in attended]
    self_outs = [one[1] for one in attended]
    cross_outs = [one[2] for one in attended]
    stats = [one[3] for one in attended]
    mixed_low = (
        narrowed(jnp.concatenate(mixed_pairs, axis=2), 1).transpose(1, 0, 2).reshape(local_tok, model_width)
    )

    branch = low_product(mixed_low, full_out)
    branch_inverse = inverse_rms(branch)
    branch_unit = branch * branch_inverse
    gate_attend = jnp.tanh(per_token(1))
    hidden = token_in + gate_attend * (branch_unit * norm_gains[1])
    hidden_inverse = inverse_rms(hidden)
    hidden_unit = hidden * hidden_inverse
    scale_feed = 1.0 + per_token(2)
    normed_feed_low = (hidden_unit * norm_gains[5] * scale_feed).astype(BF16)
    gate_up = low_product(normed_feed_low, full_gate_up)
    hidden_units = gate_up.shape[1] // 2
    gate_half = gate_up[:, :hidden_units]
    up_half = gate_up[:, hidden_units:]
    sigmoid = jax.nn.sigmoid(gate_half)
    if hidden_units // (wide * narrow) % 128 == 0:
        activated_low, moved = swiglu(gate_up, lax.axis_index("core"), deep, narrow)
        down_columns = (moved[:, : hidden_units // 2], moved[:, hidden_units // 2 :])
    else:
        activated_low = (gate_half * sigmoid * up_half).astype(BF16)
        down_columns = device_columns(activated_low, deep, narrow)
    down_out = low_product(activated_low, full_down)
    down_inverse = inverse_rms(down_out)
    down_unit = down_out * down_inverse
    gate_feed = jnp.tanh(per_token(3))
    down_normed = down_unit * norm_gains[6]
    result = (hidden + gate_feed * down_normed).astype(BF16)

    grad_result = cotangent[0].astype(F32)
    grad_down_y = grad_result * gate_feed
    grad_gain_six = jnp.sum(grad_down_y * down_unit, axis=0)
    grad_gate_feed = per_image(grad_result * down_normed * (1.0 - gate_feed * gate_feed))
    grad_down_low = norm_pull(grad_down_y * norm_gains[6], down_unit, down_inverse).astype(BF16)
    grad_activated = times_transposed(grad_down_low, full_down)
    grad_gate_low = (grad_activated * up_half * sigmoid * (1.0 + gate_half * (1.0 - sigmoid))).astype(BF16)
    grad_up_low = (grad_activated * gate_half * sigmoid).astype(BF16)
    grad_gate_up_low = jnp.concatenate([grad_gate_low, grad_up_low], axis=1)
    grad_normed_feed = times_transposed(grad_gate_up_low, full_gate_up)
    grad_feed_y = grad_normed_feed * scale_feed
    grad_gain_five = jnp.sum(grad_feed_y * hidden_unit, axis=0)
    grad_scale_feed = per_image(grad_normed_feed * hidden_unit * norm_gains[5])
    grad_hidden = grad_result + norm_pull(grad_feed_y * norm_gains[5], hidden_unit, hidden_inverse)
    grad_branch_y = grad_hidden * gate_attend
    grad_gain_one = jnp.sum(grad_branch_y * branch_unit, axis=0)
    grad_gate_attend = per_image(
        grad_hidden * branch_unit * norm_gains[1] * (1.0 - gate_attend * gate_attend)
    )
    grad_branch_low = norm_pull(grad_branch_y * norm_gains[1], branch_unit, branch_inverse).astype(BF16)
    grad_mixed = times_transposed(grad_branch_low, full_out).astype(BF16)
    grad_blocks = widened(grad_mixed.reshape(local_tok, narrow, part).transpose(1, 0, 2), 1)
    grad_heads = exchange(grad_blocks, "fsdp").reshape(group_tok, part_pad)
    def by_z(value):
        return value.reshape(deep, -1, value.shape[1])

    down_both = chip_sum(*down_columns, grad_down_low)
    feed_columns = device_columns(normed_feed_low, deep, narrow)
    gate_both = chip_sum(*feed_columns, grad_gate_low)
    up_both = chip_sum(*feed_columns, grad_up_low)
    out_both = chip_sum(*device_columns(mixed_low, deep, narrow), grad_branch_low)
    down_part = fsdp_sum(down_both)
    grad_heads, gate_both, up_both, out_both, down_part = lax.optimization_barrier(
        (grad_heads, gate_both, up_both, out_both, down_part)
    )
    gate_part = fsdp_sum(gate_both)
    out_part = fsdp_sum(out_both)
    up_part = fsdp_sum(up_both)
    came_downs = exchange(by_z(down_part), "z")
    crossed = [
        cross_back(
            pair, own_gates, packed, text_packed, row, grad_heads, cross_outs[pair], stats[pair],
            head_dim, image_count, score_scale,
        )
        for pair in range(pairs)
    ]
    dtk = jnp.concatenate([one[1] for one in crossed], axis=1)
    dtv = jnp.concatenate([one[2] for one in crossed], axis=1)
    gate_sums = jnp.stack([one[3] for one in crossed])

    grad_text_keys = dtk.astype(F32)
    own_gain_four = jnp.sum(grad_text_keys * text_unit, axis=0)
    grad_text_unit = grad_text_keys * text_gains
    text_sums = jnp.stack([jnp.sum(grad_text_unit, axis=1), jnp.sum(grad_text_unit * text_unit, axis=1)])
    text_sums = jnp.sum(
        fsdp_share(jnp.pad(text_sums, ((0, 6), (0, 0))), narrow, 3), axis=0
    ) * (1.0 / model_width)
    grad_text_key_in = (grad_text_unit - text_sums[0][:, None] - text_unit * text_sums[1][:, None]) * text_key_inverse
    grad_text_own = jnp.concatenate(
        [narrowed(grad_text_key_in.astype(BF16), 1), narrowed(dtv, 1)], axis=1
    )
    def self_pair(pair):
        return self_back(
            pair, packed, column, row, grad_heads, self_outs[pair], stats[pair], crossed[pair][0], head_dim, score_scale
        )

    came_texts = to_all(grad_text_own, narrow)
    backs = [self_pair(0)]
    first, came_downs, gate_part, *came_texts = lax.optimization_barrier(
        (backs[0][0], came_downs, gate_part, *came_texts)
    )
    gate_pieces = z_pieces(by_z(gate_part), deep)
    grad_down_weight = jnp.sum(came_downs.astype(F32), axis=0)
    backs[0] = (first, *backs[0][1:])
    grad_text_all = in_order(grad_text_own, came_texts)
    grad_text_columns = (
        grad_text_all.reshape(narrow, text_total, 2, part).transpose(1, 2, 0, 3).reshape(text_total, 2 * model_width)
    )
    text_half = text_cols // 2
    own_text, other_text = by_core(text_slice[:, :text_half], text_slice[:, text_half:])
    came_text = core_swap(outer_sum(other_text, grad_text_columns).astype(BF16))
    text_both = (outer_sum(own_text, grad_text_columns) + came_text.astype(F32)).astype(BF16)
    grad_heads, text_both, first = lax.optimization_barrier((grad_heads, text_both, backs[0][0]))
    backs[0] = (first, *backs[0][1:])
    came_text_z = exchange(by_z(text_both), "z")
    backs.append(self_pair(1))
    if pairs > 2:
        grad_heads, up_part, out_part, second = lax.optimization_barrier(
            (grad_heads, up_part, out_part, backs[1][0])
        )
        backs[1] = (second, *backs[1][1:])
        backs += [self_pair(pair) for pair in range(2, pairs)]
    up_pieces = z_pieces(by_z(up_part), deep)
    last, came_text_z = lax.optimization_barrier((backs[-1][0], came_text_z))
    backs[-1] = (last, *backs[-1][1:])
    text_part = jnp.sum(came_text_z.astype(F32), axis=0).astype(BF16)
    last, grad_text_columns = lax.optimization_barrier((backs[-1][0], grad_text_columns))
    backs[-1] = (last, *backs[-1][1:])
    grad_text_slice = times_transposed(grad_text_columns, text_weight).astype(BF16)
    came_text = exchange(
        grad_text_slice.reshape(image_count, narrow, caption_local, text_cols)
        .transpose(1, 0, 2, 3)
        .reshape(narrow, text_local, text_cols),
        "fsdp",
    )
    came_out_z = exchange(by_z(out_part), "z")
    own_gate_grad = jnp.sum(gate_sums[:, 0, :].reshape(pairs * halves, head_dim), axis=1)[:heads_here]
    grad_head_gate = lax.dynamic_update_slice_in_dim(
        jnp.zeros((head_count,), F32), own_gate_grad, me * heads_here, 0
    ) * (1.0 - gate_tanh * gate_tanh)
    grad_projected_low, head_sums = heads_back(
        list(zip(*backs)), projected, stats_all, cosine, sine, head_gains, part,
        lambda value: fsdp_share(value, narrow, 4),
    )
    everyone = ("z", "core", "fsdp")
    grad_text_weight = lax.ppermute(
        text_part,
        everyone,
        [
            ((z * 2 + c) * narrow + f, f * wide + c * deep + z)
            for z in range(deep) for c in range(2) for f in range(narrow)
        ],
    )
    grad_projected_low, came_text, *pieces = lax.optimization_barrier(
        (grad_projected_low, came_text, *gate_pieces, *up_pieces)
    )
    grad_gate_up_weight = jnp.concatenate([added(pieces[:deep]), added(pieces[deep:])], axis=1)
    grad_normed = lax.psum_scatter(
        times_transposed(grad_projected_low, own_qkv).astype(BF16), "fsdp", scatter_dimension=0, tiled=True
    )

    def lane_rows(value):
        return value.reshape(-1, 128)

    group = lax.axis_index("z") * 2 + lax.axis_index("core")
    columns_here = jnp.stack(
        [narrowed(value, 1) for value in (head_sums[0], head_sums[2], own_gain_four, head_sums[1], head_sums[3])]
    )
    here = (jnp.arange(narrow, dtype=jnp.int32) == me)[None, :, None]
    placed = lane_rows(jnp.where(here, columns_here[:, None, :], 0.0))
    cond_rows_here = lane_rows(jnp.where(me == 0, cond_low.astype(F32), 0.0))
    gate_row = jnp.pad(grad_head_gate, (0, 128 - head_count)).reshape(1, 128)
    ready = [lane_rows(grad_gain_one), lane_rows(grad_gain_five), lane_rows(grad_gain_six), placed, gate_row]
    later = [*grad_gate_attend, *grad_scale_feed, *grad_gate_feed, cond_rows_here]
    ready = lax.optimization_barrier(tuple(ready))
    qkv_grad = outer_sum(normed_all, grad_projected_low).astype(BF16).reshape(deep, 2, model_width // wide, 3 * part_pad)
    qkv_grad, came_out_z, grad_text_weight = lax.optimization_barrier((qkv_grad, came_out_z, grad_text_weight))
    grad_text_weight = grad_text_weight.astype(F32)
    grad_out_weight = jnp.sum(came_out_z.astype(F32), axis=0)
    own_grad, other_grad = by_core(qkv_grad[:, 0], qkv_grad[:, 1])
    own_grad = (own_grad.astype(F32) + core_swap(other_grad).astype(F32)).astype(BF16)
    own_pieces = z_pieces(own_grad, deep)
    grad_text_normed = (
        came_text
        .transpose(1, 0, 2)
        .reshape(text_local, caption_width)
        .astype(F32)
    )
    text_state_unit = text_in * text_inverse
    grad_text_gain = jnp.sum(grad_text_normed * text_state_unit, axis=0)
    grad_text = (
        norm_pull(grad_text_normed * text_gain, text_state_unit, text_inverse)
        .astype(BF16)
        .reshape(image_count, caption_local, caption_width)
    )

    grad_text, grad_text_gain, *own_pieces = lax.optimization_barrier((grad_text, grad_text_gain, *own_pieces))
    grad_normed = grad_normed.astype(F32)

    token_unit = token_in * token_inverse
    scale_attend = 1.0 + per_token(0)
    grad_normed_y = grad_normed * scale_attend
    grad_gain_zero = jnp.sum(grad_normed_y * token_unit, axis=0)
    grad_scale_attend = per_image(grad_normed * token_unit * norm_gains[0])
    grad_tokens = (
        grad_hidden + norm_pull(grad_normed_y * norm_gains[0], token_unit, token_inverse)
    ).astype(BF16)
    lanes_of_row = model_width // 128
    summed, kept = finish(
        [lane_rows(grad_gain_zero), *ready, lane_rows(grad_text_gain)], [*grad_scale_attend, *later], narrow, wide, 5
    )
    summed, kept, *own_pieces = lax.optimization_barrier((summed, kept, *own_pieces))
    own_grad = added(own_pieces)
    grad_qkv_weight = (
        exchange(narrowed(own_grad.astype(BF16), 3).reshape(narrow, -1, 3 * part), "fsdp")
        .reshape(narrow, -1, 3, part)
        .transpose(1, 2, 0, 3)
        .reshape(-1, 3 * model_width)
        .astype(F32)
    )
    every_image = wide * image_count
    per_part = image_count * lanes_of_row
    slots = jnp.concatenate(
        [kept[:, i * per_part : (i + 1) * per_part].reshape(every_image, model_width) for i in range(4)], axis=1
    )
    cond_slots = kept[:, 4 * per_part :].reshape(every_image, cond_low.shape[1])
    ada_rows = cond_rows // wide
    own_cond = lax.dynamic_slice_in_dim(cond_slots, (group * narrow + me) * ada_rows, ada_rows, 1)
    grad_ada_weight = exact_outer(own_cond, slots)
    grad_ada_bias = jnp.sum(slots, axis=0)

    def rows_of(first, count):
        return summed[first * lanes_of_row : (first + count) * lanes_of_row]

    grad_gains = jnp.concatenate([rows_of(0, 2), rows_of(4, 3), rows_of(2, 2)]).reshape(norm_gains.shape)
    grad_shifts = rows_of(7, 2).reshape(norm_shifts.shape)
    grad_head_gate = summed[9 * lanes_of_row, :head_count]
    grad_text_gain = summed[9 * lanes_of_row + 1 :].reshape(-1)
    return (
        result[None],
        grad_tokens[None],
        grad_text[None],
        grad_ada_weight,
        grad_qkv_weight,
        grad_out_weight,
        grad_text_weight,
        grad_gate_up_weight,
        grad_down_weight,
        grad_ada_bias,
        grad_gains,
        grad_shifts,
        grad_text_gain,
        grad_head_gate,
    )


def solution(mesh):
    wide, narrow = mesh.devices.shape
    fine = Mesh(mesh.devices.reshape(wide // 2, 2, narrow), ("z", "core", "fsdp"))
    groups = ("z", "core")
    every = ("z", "core", "fsdp")
    placed = (
        P(groups, "fsdp", None),
        P(groups, "fsdp", None),
        P(groups, None, "fsdp", None),
        P(groups, None, None),
        P(groups, None, None),
        P("fsdp", None),
        P(),
        P("fsdp", None),
        P("fsdp", None),
        P("fsdp", None),
        P("fsdp", None),
        P("fsdp", None),
        P(),
        P(),
        P(),
        P(),
    )
    return jax.shard_map(
        shards,
        mesh=fine,
        in_specs=placed,
        out_specs=(
            P(groups, "fsdp", None),
            P(groups, "fsdp", None),
            P(groups, None, "fsdp", None),
            P(every, None),
            P(every, None),
            P(every, None),
            P(every, None),
            P(every, None),
            P(every, None),
            P(),
            P(),
            P(),
            P(),
            P(),
        ),
        check_vma=False,
    )
```

```python
import functools

import jax
import jax.numpy as jnp
from jax import lax
from jax.experimental import pallas as pl
from jax.experimental.pallas import tpu as pltpu
from jax.sharding import Mesh
from jax.sharding import PartitionSpec as P

EPS = 1e-05
HIGHEST_PRECISION = lax.Precision.HIGHEST
MASKED = -1e30
LOG2E = 1.4426950408889634
FIRST_PATCHES = 16 * 12**2
FIRST_MOST = FIRST_PATCHES + 96
QBLOCK = 256
BF16 = jnp.bfloat16
F32 = jnp.float32
VMEM_LIMIT = 60 * 1024 * 1024


def round_up(value, step):
    return -(-value // step) * step


def low_product(left, right):
    return jnp.dot(left, right, preferred_element_type=F32)


def times_transposed(left, right):
    return lax.dot_general(left, right, (((1,), (1,)), ((), ())), preferred_element_type=F32)


def outer_sum(left, right):
    return lax.dot_general(left, right, (((0,), (0,)), ((), ())), preferred_element_type=F32)


def exact_outer(left, right):
    return lax.dot_general(
        left, right, (((0,), (0,)), ((), ())), precision=HIGHEST_PRECISION, preferred_element_type=F32
    )


def exact_transposed(left, right):
    return lax.dot_general(
        left, right, (((1,), (1,)), ((), ())), precision=HIGHEST_PRECISION, preferred_element_type=F32
    )


def row_mean(value):
    return jnp.mean(value, axis=-1, keepdims=True)


def inverse_rms(value):
    return lax.rsqrt(row_mean(value * value) + EPS)


def norm_pull(grad, unit, inverse):
    return (grad - unit * row_mean(grad * unit)) * inverse


def token_layout(image_sizes, position, image_count):
    start = jnp.int32(0)
    image_index = jnp.full(position.shape, image_count, jnp.int32)
    token_row = jnp.zeros(position.shape, jnp.int32)
    token_col = jnp.zeros(position.shape, jnp.int32)
    for i in range(image_count):
        width = image_sizes[i, 1] + 1
        end = start + image_sizes[i, 0] * width
        inside = (position >= start) & (position < end)
        offset = position - start
        image_index = jnp.where(inside, i, image_index)
        token_row = jnp.where(inside, offset // width, token_row)
        token_col = jnp.where(inside, offset % width, token_col)
        start = end
    return image_index, token_row, token_col


def rope_tables(token_row, token_col, head_dim):
    quarter = head_dim // 4
    pair = (jnp.arange(128, dtype=jnp.int32) % head_dim) // 2
    frequency = 10000.0 ** (-(pair % quarter).astype(F32) / quarter)
    place = jnp.where(
        (pair < quarter)[None, :], token_row.astype(F32)[:, None], token_col.astype(F32)[:, None]
    )
    angles = place * frequency[None, :]
    even = (jnp.arange(128, dtype=jnp.int32) % 2 == 0)[None, :]
    return jnp.cos(angles), jnp.where(even, -jnp.sin(angles), jnp.sin(angles))


def swap_pairs(value):
    width = value.shape[1]
    even = lax.broadcasted_iota(jnp.int32, value.shape, 1) % 2 == 0
    return jnp.where(even, pltpu.roll(value, width - 1, 1), pltpu.roll(value, 1, 1))


def wide_table(table, width):
    return jnp.concatenate([table] * (width // table.shape[1]), axis=1)


def pack_columns(columns):
    rows = columns[0].shape[0]
    lane = lax.broadcasted_iota(jnp.int32, (rows, 128), 1)
    packed = jnp.zeros((rows, 128), F32)
    for i, column in enumerate(columns):
        packed = jnp.where(lane == i, column, packed)
    return jnp.transpose(packed)[:8, :]


def as_columns(rows_list):
    width = rows_list[0].shape[1]
    stacked = jnp.concatenate(
        rows_list + [jnp.zeros((128 - len(rows_list), width), F32)], axis=0
    )
    return jnp.transpose(stacked)


def real_lanes(shape, part):
    return lax.broadcasted_iota(jnp.int32, shape, 1) < part


def own_stats(value, part):
    mean = jnp.sum(value, axis=1, keepdims=True) * (1.0 / part)
    centred = value - mean
    if value.shape[1] != part:
        centred = jnp.where(real_lanes(value.shape, part), centred, 0.0)
    return mean, jnp.sum(centred * centred, axis=1, keepdims=True)


def joined_stats(stats_ref, part, slot):
    narrow = stats_ref.shape[0]
    means = [stats_ref[i, 2 * slot : 2 * slot + 1, :] for i in range(narrow)]
    squares = [stats_ref[i, 2 * slot + 1 : 2 * slot + 2, :] for i in range(narrow)]
    mean = functools.reduce(jnp.add, means) * (1.0 / narrow)
    square = functools.reduce(jnp.add, squares)
    square = square + part * functools.reduce(jnp.add, [(m - mean) * (m - mean) for m in means])
    return mean, lax.rsqrt(square * (1.0 / (narrow * part)) + EPS)


def stats_kernel(part, slots, projected_ref, out_ref):
    padded = projected_ref.shape[1] // slots
    columns = []
    for slot in range(slots):
        columns += own_stats(projected_ref[:, slot * padded : (slot + 1) * padded], part)
    out_ref[...] = pack_columns(columns)


def column_stats(projected, part, padded, slots):
    rows = projected.shape[0]
    return pl.pallas_call(
        functools.partial(stats_kernel, part, slots),
        grid=(pl.cdiv(rows, QBLOCK),),
        in_specs=[pl.BlockSpec((QBLOCK, slots * padded), lambda i: (i, 0))],
        out_specs=pl.BlockSpec((8, QBLOCK), lambda i: (0, i)),
        out_shape=jax.ShapeDtypeStruct((8, rows), F32),
        compiler_params=pltpu.CompilerParams(vmem_limit_bytes=VMEM_LIMIT),
        cost_estimate=pl.CostEstimate(flops=10 * rows * slots * padded, bytes_accessed=4 * rows * slots * padded, transcendentals=0),
    )(projected)


def heads_kernel(part, query_scale, projected_ref, stats_ref, cos_ref, sin_ref, gains_ref, shifts_ref, out_ref):
    padded = projected_ref.shape[1] // 3
    cosine = wide_table(cos_ref[...], padded)
    sine = wide_table(sin_ref[...], padded)
    columns = as_columns([*joined_stats(stats_ref, part, 0), *joined_stats(stats_ref, part, 1)])
    for slot in range(3):
        place = slice(slot * padded, (slot + 1) * padded)
        value = projected_ref[:, place]
        if slot < 2:
            value = (value - columns[:, 2 * slot : 2 * slot + 1]) * columns[:, 2 * slot + 1 : 2 * slot + 2]
            value = value * gains_ref[slot : slot + 1, :] + shifts_ref[slot : slot + 1, :]
            value = value * cosine + swap_pairs(value) * sine
            if slot == 0:
                value = value * query_scale
        out_ref[:, place] = value.astype(BF16)


def make_heads(projected, stats, cosine, sine, gains, shifts, part, query_scale):
    rows, triple = projected.shape
    padded = triple // 3
    narrow = stats.shape[0]
    return pl.pallas_call(
        functools.partial(heads_kernel, part, query_scale),
        grid=(pl.cdiv(rows, QBLOCK),),
        in_specs=[
            pl.BlockSpec((QBLOCK, triple), lambda i: (i, 0)),
            pl.BlockSpec((narrow, 8, QBLOCK), lambda i: (0, 0, i)),
            pl.BlockSpec((QBLOCK, 128), lambda i: (i, 0)),
            pl.BlockSpec((QBLOCK, 128), lambda i: (i, 0)),
            pl.BlockSpec((2, padded), lambda i: (0, 0)),
            pl.BlockSpec((2, padded), lambda i: (0, 0)),
        ],
        out_specs=pl.BlockSpec((QBLOCK, triple), lambda i: (i, 0)),
        out_shape=jax.ShapeDtypeStruct((rows, triple), BF16),
        compiler_params=pltpu.CompilerParams(vmem_limit_bytes=VMEM_LIMIT),
        cost_estimate=pl.CostEstimate(flops=40 * rows * triple, bytes_accessed=6 * rows * triple, transcendentals=0),
    )(projected, stats, cosine, sine, gains, shifts)


def turned_back(refs, cosine, sine):
    grad = jnp.concatenate([ref[...].astype(F32) for ref in refs], axis=1)
    return grad * cosine - swap_pairs(grad) * sine


def grad_stats_kernel(rows, part, pairs, *refs):
    dq_refs, dk_refs = refs[:pairs], refs[pairs : 2 * pairs]
    projected_ref, stats_ref, cos_ref, sin_ref, gains_ref, out_ref, sums_ref = refs[2 * pairs :]
    step = pl.program_id(0)
    padded = 128 * pairs
    cosine = wide_table(cos_ref[...], padded)
    sine = wide_table(sin_ref[...], padded)
    height = cos_ref.shape[0]
    inside = step * height + lax.broadcasted_iota(jnp.int32, (height, 1), 0) < rows

    @pl.when(step == 0)
    def _():
        sums_ref[...] = jnp.zeros_like(sums_ref)

    columns = as_columns([*joined_stats(stats_ref, part, 0), *joined_stats(stats_ref, part, 1)])
    packed = []
    for slot, grads in enumerate((dq_refs, dk_refs)):
        grad = jnp.where(inside, turned_back(grads, cosine, sine), 0.0)
        unit = (projected_ref[:, slot * padded : (slot + 1) * padded] - columns[:, 2 * slot : 2 * slot + 1])
        unit = jnp.where(inside, unit * columns[:, 2 * slot + 1 : 2 * slot + 2], 0.0)
        both = grad * unit
        sums_ref[2 * slot : 2 * slot + 1, :] += jnp.sum(both, axis=0, keepdims=True)
        sums_ref[2 * slot + 1 : 2 * slot + 2, :] += jnp.sum(grad, axis=0, keepdims=True)
        gain = gains_ref[slot : slot + 1, :]
        packed.append(jnp.sum(grad * gain, axis=1, keepdims=True))
        packed.append(jnp.sum(both * gain, axis=1, keepdims=True))
    out_ref[...] = pack_columns(packed)


def heads_back_kernel(part, pairs, *refs):
    dq_refs, dk_refs, dv_refs = refs[:pairs], refs[pairs : 2 * pairs], refs[2 * pairs : 3 * pairs]
    projected_ref, stats_ref, totals_ref, cos_ref, sin_ref, gains_ref, out_ref = refs[3 * pairs :]
    padded = 128 * pairs
    narrow = stats_ref.shape[0]
    cosine = wide_table(cos_ref[...], padded)
    sine = wide_table(sin_ref[...], padded)
    means = [
        functools.reduce(jnp.add, [totals_ref[i, j : j + 1, :] for i in range(narrow)]) * (1.0 / (narrow * part))
        for j in range(4)
    ]
    columns = as_columns([*joined_stats(stats_ref, part, 0), *joined_stats(stats_ref, part, 1), *means])
    for slot, grads in enumerate((dq_refs, dk_refs)):
        grad = turned_back(grads, cosine, sine) * gains_ref[slot : slot + 1, :]
        inverse = columns[:, 2 * slot + 1 : 2 * slot + 2]
        unit = (projected_ref[:, slot * padded : (slot + 1) * padded] - columns[:, 2 * slot : 2 * slot + 1]) * inverse
        grad = grad - columns[:, 4 + 2 * slot : 5 + 2 * slot] - unit * columns[:, 5 + 2 * slot : 6 + 2 * slot]
        grad = grad * inverse
        if padded != part:
            grad = jnp.where(real_lanes(grad.shape, part), grad, 0.0)
        out_ref[:, slot * padded : (slot + 1) * padded] = grad.astype(BF16)
    for pair, ref in enumerate(dv_refs):
        out_ref[:, 2 * padded + 128 * pair : 2 * padded + 128 * (pair + 1)] = ref[...]


def heads_back(grads, projected, stats, cosine, sine, gains, part, share):
    rows, triple = projected.shape
    padded = triple // 3
    pairs = padded // 128
    narrow = stats.shape[0]
    pair_spec = pl.BlockSpec((QBLOCK, 128), lambda i: (i, 0))
    two_spec = pl.BlockSpec((QBLOCK, 2 * padded), lambda i: (i, 0))
    stat_spec = pl.BlockSpec((narrow, 8, QBLOCK), lambda i: (0, 0, i))
    gain_spec = pl.BlockSpec((2, padded), lambda i: (0, 0))
    own, sums = pl.pallas_call(
        functools.partial(grad_stats_kernel, rows, part, pairs),
        grid=(pl.cdiv(rows, QBLOCK),),
        in_specs=[pair_spec] * (2 * pairs) + [two_spec, stat_spec, pair_spec, pair_spec, gain_spec],
        out_specs=[
            pl.BlockSpec((8, QBLOCK), lambda i: (0, i)),
            pl.BlockSpec((8, padded), lambda i: (0, 0)),
        ],
        out_shape=[jax.ShapeDtypeStruct((8, rows), F32), jax.ShapeDtypeStruct((8, padded), F32)],
        compiler_params=pltpu.CompilerParams(vmem_limit_bytes=VMEM_LIMIT),
        cost_estimate=pl.CostEstimate(flops=4 * rows * triple, bytes_accessed=rows * triple // 16, transcendentals=0),
    )(*grads[0], *grads[1], projected, stats, cosine, sine, gains)
    totals = share(own)
    out = pl.pallas_call(
        functools.partial(heads_back_kernel, part, pairs),
        grid=(pl.cdiv(rows, QBLOCK),),
        in_specs=[pair_spec] * (3 * pairs) + [two_spec, stat_spec, stat_spec, pair_spec, pair_spec, gain_spec],
        out_specs=pl.BlockSpec((QBLOCK, triple), lambda i: (i, 0)),
        out_shape=jax.ShapeDtypeStruct((rows, triple), BF16),
        compiler_params=pltpu.CompilerParams(vmem_limit_bytes=VMEM_LIMIT),
        cost_estimate=pl.CostEstimate(flops=4 * rows * triple, bytes_accessed=rows * triple // 16, transcendentals=0),
    )(*grads[0], *grads[1], *grads[2], projected, stats, totals, cosine, sine, gains)
    return out, sums


def head_lanes(rows, half, head_dim):
    lane = lax.broadcasted_iota(jnp.int32, (rows, 128), 1)
    return (lane >= half * head_dim) & (lane < (half + 1) * head_dim)


def softmax_product(pieces):
    maximum = functools.reduce(jnp.maximum, [jnp.max(s, axis=1, keepdims=True) for s, _ in pieces])
    total, result = 0.0, 0.0
    for scores, values in pieces:
        weight = jnp.exp2(scores - maximum)
        total = total + jnp.sum(weight, axis=1, keepdims=True)
        result = result + low_product(weight.astype(BF16), values)
    return result * (1.0 / total), maximum + jnp.log2(total)


def attend_kernel(
    head_dim, first, most, caption, image_count,
    gate_ref, q_ref, k_ref, v_ref, tk_ref, tv_ref, column_ref, row_ref,
    mixed_ref, self_ref, cross_ref, stats_ref,
):
    count = q_ref.shape[0]
    halves = 128 // head_dim

    def emit(at, rows, outs):
        lanes = [head_lanes(rows, half, head_dim) for half in range(halves)]
        own, cross, gated = 0.0, 0.0, 0.0
        columns = []
        for half, (own_out, own_total, cross_out, cross_total) in enumerate(outs):
            gate = gate_ref[0, half]
            own = own + jnp.where(lanes[half], own_out, 0.0)
            cross = cross + jnp.where(lanes[half], cross_out, 0.0)
            gated = gated + jnp.where(lanes[half], gate * cross_out, 0.0)
            columns += [own_total, cross_total]
        self_ref[pl.ds(at, rows), :] = own
        cross_ref[pl.ds(at, rows), :] = cross
        mixed_ref[pl.ds(at, rows), :] = (own + gated).astype(BF16)
        lane = lax.broadcasted_iota(jnp.int32, (rows, 128), 1)
        packed = jnp.zeros((rows, 128), F32)
        for i, column in enumerate(columns):
            packed = jnp.where(lane == i, column, packed)
        stats_ref[:, pl.ds(at, rows)] = jnp.transpose(packed)[:8, :]

    def clean(block, carry):
        at = pl.multiple_of(block * QBLOCK, QBLOCK)
        queries = q_ref[pl.ds(at, QBLOCK), :]
        outs = []
        for half in range(halves):
            q = jnp.where(head_lanes(QBLOCK, half, head_dim), queries, jnp.zeros_like(queries))
            bias = jnp.where(row_ref[0:1, first:most] == 0, 0.0, MASKED)
            own_out, own_total = softmax_product([
                (times_transposed(q, k_ref[0:first, :]), v_ref[0:first, :]),
                (times_transposed(q, k_ref[first:most, :]) + bias, v_ref[first:most, :]),
            ])
            cross_out, cross_total = softmax_product(
                [(times_transposed(q, tk_ref[0:caption, :]), tv_ref[0:caption, :])]
            )
            outs.append((own_out, own_total, cross_out, cross_total))
        emit(at, QBLOCK, outs)
        return carry

    lax.fori_loop(0, first // QBLOCK, clean, 0)
    rest = count - first
    queries = q_ref[first:count, :]
    image = column_ref[first:count, :]
    outs = []
    for half in range(halves):
        q = jnp.where(head_lanes(rest, half, head_dim), queries, jnp.zeros_like(queries))
        own_out, own_total = softmax_product([
            (jnp.where(image == row_ref[0:1, :], times_transposed(q, k_ref[...]), MASKED), v_ref[...])
        ])
        scores = times_transposed(q, tk_ref[...])
        owner = lax.broadcasted_iota(jnp.int32, (1, scores.shape[1]), 1) // caption
        scores = jnp.where((image == owner) | (image == image_count), scores, MASKED)
        cross_out, cross_total = softmax_product([(scores, tv_ref[...])])
        outs.append((own_out, own_total, cross_out, cross_total))
    emit(first, rest, outs)


def attend(pair, gates, packed, text_packed, column, row, head_dim, image_count):
    count, texts = packed.shape[0], text_packed.shape[0]
    pairs = packed.shape[1] // 384
    halves = 128 // head_dim
    out = pl.BlockSpec((count, 128), lambda i: (0, 0))
    most = min(round_up(FIRST_MOST, 128), count)
    flops = 4 * count * (count + texts) * 128
    return pl.pallas_call(
        functools.partial(
            attend_kernel, head_dim, FIRST_PATCHES, most, texts // image_count, image_count
        ),
        grid=(1,),
        in_specs=[
            pl.BlockSpec((None, 1, halves), lambda i: (pair, 0, 0), memory_space=pltpu.SMEM),
            pl.BlockSpec((count, 128), lambda i: (0, pair)),
            pl.BlockSpec((count, 128), lambda i: (0, pairs + pair)),
            pl.BlockSpec((count, 128), lambda i: (0, 2 * pairs + pair)),
            pl.BlockSpec((texts, 128), lambda i: (0, pair)),
            pl.BlockSpec((texts, 128), lambda i: (0, pairs + pair)),
            pl.BlockSpec((count, 1), lambda i: (0, 0)),
            pl.BlockSpec((1, count), lambda i: (0, 0)),
        ],
        out_specs=[out, out, out, pl.BlockSpec((8, count), lambda i: (0, 0))],
        out_shape=[
            jax.ShapeDtypeStruct((count, 128), BF16),
            jax.ShapeDtypeStruct((count, 128), F32),
            jax.ShapeDtypeStruct((count, 128), F32),
            jax.ShapeDtypeStruct((8, count), F32),
        ],
        compiler_params=pltpu.CompilerParams(vmem_limit_bytes=VMEM_LIMIT),
        cost_estimate=pl.CostEstimate(flops=flops, bytes_accessed=20 * count * 128, transcendentals=2 * count * count),
    )(gates.reshape(pairs, 1, halves), packed, packed, packed, text_packed, text_packed, column, row)


def gate_lanes(gate_ref, head_dim):
    lane = lax.broadcasted_iota(jnp.int32, (1, 128), 1)
    gates = jnp.zeros((1, 128), F32)
    for half in range(128 // head_dim):
        gates = jnp.where(lane // head_dim == half, gate_ref[0, half], gates)
    return gates


def head_picks(head_dim):
    return (
        lax.broadcasted_iota(jnp.int32, (8, 128), 1) // head_dim
        == lax.broadcasted_iota(jnp.int32, (8, 128), 0)
    ).astype(F32)


def rows_back(head_dim, queries, outs, delta, stats, offset, keys, values, key_sum, value_sum, spans):
    rows = queries.shape[0]
    halves = 128 // head_dim
    zero = jnp.zeros((rows, 128), BF16)
    lanes = [head_lanes(rows, half, head_dim) for half in range(halves)]
    q_heads = [jnp.where(lane, queries, zero) for lane in lanes]
    out_heads = [jnp.where(lane, outs, zero) for lane in lanes]
    q_stack = jnp.concatenate(q_heads, axis=0)
    out_stack = jnp.concatenate(out_heads, axis=0)
    dq = [0.0] * halves
    for low, high, mask in spans:
        key_part = keys[low:high, :]
        value_part = values[low:high, :]
        probs, grads = [], []
        for half in range(halves):
            scores = mask(times_transposed(key_part, q_heads[half]))
            prob = jnp.exp2(scores - stats[2 * half + offset : 2 * half + offset + 1, :])
            dprob = times_transposed(value_part, out_heads[half])
            dscore = (prob * (dprob - delta[half : half + 1, :])).astype(BF16)
            probs.append(prob.astype(BF16))
            grads.append(dscore)
            dq[half] = dq[half] + outer_sum(dscore, key_part)
        value_sum[low:high, :] += low_product(jnp.concatenate(probs, axis=1), out_stack)
        key_sum[low:high, :] += low_product(jnp.concatenate(grads, axis=1), q_stack)
    total = 0.0
    for half in range(halves):
        total = total + jnp.where(lanes[half], dq[half], 0.0)
    return total


def cross_back_kernel(
    head_dim, first, caption, image_count, scale,
    gate_ref, q_ref, tk_ref, tv_ref, row_ref, grad_ref, cross_ref, stats_ref,
    dq_ref, dtk_ref, dtv_ref, gate_grad_ref, dtk_sum, dtv_sum,
):
    count = q_ref.shape[0]
    for total in (dtk_sum, dtv_sum, gate_grad_ref):
        total[...] = jnp.zeros_like(total)
    gates = gate_lanes(gate_ref, head_dim)
    picks = head_picks(head_dim)

    def part(at, rows, spans):
        wide = grad_ref[pl.ds(at, rows), :].astype(F32)
        cross = cross_ref[pl.ds(at, rows), :]
        gate_grad_ref[0:1, :] += jnp.sum(wide * cross, axis=0, keepdims=True)
        gated = (wide * gates).astype(BF16)
        delta = exact_transposed(picks, gated.astype(F32) * cross)
        dq = rows_back(
            head_dim, q_ref[pl.ds(at, rows), :], gated, delta, stats_ref[:, pl.ds(at, rows)], 1,
            tk_ref, tv_ref, dtk_sum, dtv_sum, spans,
        )
        dq_ref[pl.ds(at, rows), :] = (dq * scale).astype(BF16)

    def clean(block, carry):
        part(pl.multiple_of(block * QBLOCK, QBLOCK), QBLOCK, [(0, caption, lambda scores: scores)])
        return carry

    lax.fori_loop(0, first // QBLOCK, clean, 0)
    image = row_ref[0:1, first:count]
    owner = lax.broadcasted_iota(jnp.int32, (tk_ref.shape[0], 1), 0) // caption
    allowed = (owner == image) | (image == image_count)
    part(first, count - first, [(0, tk_ref.shape[0], lambda scores: jnp.where(allowed, scores, MASKED))])
    dtk_ref[...] = (dtk_sum[...] * (1.0 / LOG2E)).astype(BF16)
    dtv_ref[...] = dtv_sum[...].astype(BF16)


def cross_back(pair, gates, packed, text_packed, row, grad, cross, stats, head_dim, image_count, scale):
    count, texts = packed.shape[0], text_packed.shape[0]
    pairs = packed.shape[1] // 384
    halves = 128 // head_dim
    tokens = pl.BlockSpec((count, 128), lambda i: (0, pair))
    own_tokens = pl.BlockSpec((count, 128), lambda i: (0, 0))
    captions = pl.BlockSpec((texts, 128), lambda i: (0, 0))
    flops = 10 * count * texts * 128
    return pl.pallas_call(
        functools.partial(cross_back_kernel, head_dim, FIRST_PATCHES, texts // image_count, image_count, scale),
        grid=(1,),
        in_specs=[
            pl.BlockSpec((None, 1, halves), lambda i: (pair, 0, 0), memory_space=pltpu.SMEM),
            tokens,
            pl.BlockSpec((texts, 128), lambda i: (0, pair)),
            pl.BlockSpec((texts, 128), lambda i: (0, pairs + pair)),
            pl.BlockSpec((1, count), lambda i: (0, 0)),
            tokens,
            own_tokens,
            pl.BlockSpec((8, count), lambda i: (0, 0)),
        ],
        out_specs=[own_tokens, captions, captions, pl.BlockSpec((8, 128), lambda i: (0, 0))],
        out_shape=[
            jax.ShapeDtypeStruct((count, 128), BF16),
            jax.ShapeDtypeStruct((texts, 128), BF16),
            jax.ShapeDtypeStruct((texts, 128), BF16),
            jax.ShapeDtypeStruct((8, 128), F32),
        ],
        scratch_shapes=[pltpu.VMEM((texts, 128), F32), pltpu.VMEM((texts, 128), F32)],
        compiler_params=pltpu.CompilerParams(vmem_limit_bytes=VMEM_LIMIT),
        cost_estimate=pl.CostEstimate(flops=flops, bytes_accessed=12 * count * 128, transcendentals=count * texts),
    )(gates.reshape(pairs, 1, halves), packed, text_packed, text_packed, row, grad, cross, stats)


def self_back_kernel(
    head_dim, first, most, scale,
    q_ref, k_ref, v_ref, column_ref, row_ref, grad_ref, self_ref, stats_ref, more_ref,
    dq_ref, dk_ref, dv_ref, dk_sum, dv_sum,
):
    count = q_ref.shape[0]
    dk_sum[...] = jnp.zeros_like(dk_sum)
    dv_sum[...] = jnp.zeros_like(dv_sum)
    picks = head_picks(head_dim)

    def part(at, rows, spans):
        grad = grad_ref[pl.ds(at, rows), :]
        delta = exact_transposed(picks, grad.astype(F32) * self_ref[pl.ds(at, rows), :])
        dq = rows_back(
            head_dim, q_ref[pl.ds(at, rows), :], grad, delta, stats_ref[:, pl.ds(at, rows)], 0,
            k_ref, v_ref, dk_sum, dv_sum, spans,
        )
        dq_ref[pl.ds(at, rows), :] = (dq * scale + more_ref[pl.ds(at, rows), :].astype(F32)).astype(BF16)

    def clean(block, carry):
        bias = jnp.where(column_ref[first:most, :] == 0, 0.0, MASKED)
        part(
            pl.multiple_of(block * QBLOCK, QBLOCK), QBLOCK,
            [(0, first, lambda scores: scores), (first, most, lambda scores: scores + bias)],
        )
        return carry

    lax.fori_loop(0, first // QBLOCK, clean, 0)
    image = row_ref[0:1, first:count]
    part(first, count - first, [(0, count, lambda scores: jnp.where(column_ref[...] == image, scores, MASKED))])
    dk_ref[...] = (dk_sum[...] * (1.0 / LOG2E)).astype(BF16)
    dv_ref[...] = dv_sum[...].astype(BF16)


def self_back(pair, packed, column, row, grad, own, stats, more, head_dim, scale):
    count = packed.shape[0]
    pairs = packed.shape[1] // 384
    tokens = pl.BlockSpec((count, 128), lambda i: (0, pair))
    out = pl.BlockSpec((count, 128), lambda i: (0, 0))
    most = min(round_up(FIRST_MOST, 128), count)
    flops = 10 * count * count * 128
    return pl.pallas_call(
        functools.partial(self_back_kernel, head_dim, FIRST_PATCHES, most, scale),
        grid=(1,),
        in_specs=[
            tokens,
            pl.BlockSpec((count, 128), lambda i: (0, pairs + pair)),
            pl.BlockSpec((count, 128), lambda i: (0, 2 * pairs + pair)),
            pl.BlockSpec((count, 1), lambda i: (0, 0)),
            pl.BlockSpec((1, count), lambda i: (0, 0)),
            tokens,
            out,
            pl.BlockSpec((8, count), lambda i: (0, 0)),
            out,
        ],
        out_specs=[out, out, out],
        out_shape=[jax.ShapeDtypeStruct((count, 128), BF16)] * 3,
        scratch_shapes=[pltpu.VMEM((count, 128), F32), pltpu.VMEM((count, 128), F32)],
        compiler_params=pltpu.CompilerParams(vmem_limit_bytes=VMEM_LIMIT),
        cost_estimate=pl.CostEstimate(flops=flops, bytes_accessed=30 * count * 128, transcendentals=2 * count * count),
    )(packed, packed, packed, column, row, grad, own, stats, more)


def swiglu_kernel(core_ref, gate_ref, up_ref, out_ref, moved_ref):
    gate = gate_ref[...]
    half = 0.5 * gate
    value = ((half + half * jnp.tanh(half)) * up_ref[...]).astype(BF16)
    out_ref[...] = value
    moved_ref[...] = value


def swiglu(gate_up, core, deep, narrow):
    rows, double = gate_up.shape
    width = double // 2
    blocks = 2 * deep * narrow
    block = width // blocks

    def moved_place(i, core_ref):
        z, c, f = i // (2 * narrow), (i // narrow) % 2, i % narrow
        return (0, ((c + core_ref[0]) % 2) * (deep * narrow) + f * deep + z)

    return pl.pallas_call(
        swiglu_kernel,
        grid_spec=pltpu.PrefetchScalarGridSpec(
            num_scalar_prefetch=1,
            grid=(blocks,),
            in_specs=[
                pl.BlockSpec((rows, block), lambda i, core_ref: (0, i)),
                pl.BlockSpec((rows, block), lambda i, core_ref: (0, blocks + i)),
            ],
            out_specs=[
                pl.BlockSpec((rows, block), lambda i, core_ref: (0, i)),
                pl.BlockSpec((rows, block), moved_place),
            ],
        ),
        out_shape=[jax.ShapeDtypeStruct((rows, width), BF16)] * 2,
        compiler_params=pltpu.CompilerParams(vmem_limit_bytes=VMEM_LIMIT),
        cost_estimate=pl.CostEstimate(flops=6 * rows * width, bytes_accessed=12 * rows * width, transcendentals=rows * width),
    )(core.reshape(1), gate_up, gate_up)


def fsdp_share_kernel(narrow, x_ref, out_ref, send_sem, recv_sem):
    me = lax.axis_index("fsdp")
    barrier = pltpu.get_barrier_semaphore()
    for step in range(1, narrow):
        pl.semaphore_signal(
            barrier, inc=1, device_id={"fsdp": lax.rem(me + step, narrow)}, device_id_type=pl.DeviceIdType.MESH
        )
    pl.semaphore_wait(barrier, narrow - 1)
    copies = []
    for step in range(1, narrow):
        copy = pltpu.make_async_remote_copy(
            src_ref=x_ref,
            dst_ref=out_ref.at[me],
            send_sem=send_sem.at[step],
            recv_sem=recv_sem.at[step],
            device_id={"fsdp": lax.rem(me + step, narrow)},
            device_id_type=pl.DeviceIdType.MESH,
        )
        copy.start()
        copies.append(copy)
    out_ref[me] = x_ref[...]
    for copy in copies:
        copy.wait()


def fsdp_share(value, narrow, collective_id):
    return pl.pallas_call(
        functools.partial(fsdp_share_kernel, narrow),
        in_specs=[pl.BlockSpec(memory_space=pltpu.VMEM)],
        out_specs=pl.BlockSpec(memory_space=pltpu.VMEM),
        out_shape=jax.ShapeDtypeStruct((narrow,) + value.shape, value.dtype),
        scratch_shapes=[pltpu.SemaphoreType.DMA((narrow,)), pltpu.SemaphoreType.DMA((narrow,))],
        compiler_params=pltpu.CompilerParams(collective_id=collective_id, has_side_effects=True),
        cost_estimate=pl.CostEstimate(flops=0, bytes_accessed=8 * narrow * value.size, transcendentals=0),
    )(value)


def place_rows(items, x_ref, chunk, base):
    rows = [(ref, row) for ref in items for row in range(ref.shape[0])]
    at = 0
    while at < len(rows):
        ref, row = rows[at]
        off = at % chunk
        take = min(ref.shape[0] - row, chunk - off)
        x_ref[at // chunk, base + off : base + off + take, :] = ref[row : row + take, :]
        at += take
    while at < x_ref.shape[0] * chunk:
        off = at % chunk
        x_ref[at // chunk, base + off : base + chunk, :] = jnp.zeros((chunk - off, 128), F32)
        at += chunk - off


def finish_kernel(narrow, wide, sum_rows, sum_count, *refs):
    items, (out_ref, x_ref, first_ref, second_ref, sends, recvs) = refs[:-6], refs[-6:]
    place_rows(items[:sum_count], x_ref, sum_rows, 0)
    place_rows(items[sum_count:], x_ref, x_ref.shape[1] - sum_rows, sum_rows)
    me = lax.axis_index("fsdp")
    group = lax.axis_index("z") * 2 + lax.axis_index("core")
    rows = x_ref.shape[1]
    rest = rows - sum_rows
    barrier = pltpu.get_barrier_semaphore()
    places = [{"fsdp": lax.rem(me + step, narrow)} for step in range(1, narrow)]
    peers = [lax.rem(group + step, wide) for step in range(1, wide)]
    partners = [{"z": peer // 2, "core": peer % 2} for peer in peers]
    for place in places + partners:
        pl.semaphore_signal(barrier, inc=1, device_id=place, device_id_type=pl.DeviceIdType.MESH)
    pl.semaphore_wait(barrier, narrow + wide - 2)

    def send_all(targets, source, target, base):
        copies = []
        for i, place in enumerate(targets):
            copy = pltpu.make_async_remote_copy(
                src_ref=source(i),
                dst_ref=target,
                send_sem=sends.at[base + i],
                recv_sem=recvs.at[base + i],
                device_id=place,
                device_id_type=pl.DeviceIdType.MESH,
            )
            copy.start()
            copies.append(copy)
        return copies

    copies = send_all(places, lambda i: x_ref.at[lax.rem(me + i + 1, narrow)], first_ref.at[me], 0)
    first_ref[me] = x_ref[me]
    for copy in copies:
        copy.wait()
    total = first_ref[0]
    for i in range(1, narrow):
        total = total + first_ref[i]
    second_ref[group] = total
    copies = send_all(partners, lambda i: second_ref.at[group], second_ref.at[group], narrow)
    for copy in copies:
        copy.wait()
    total = second_ref[0, :sum_rows, :]
    for i in range(1, wide):
        total = total + second_ref[i, :sum_rows, :]
    out_ref[me, :sum_rows, :] = total
    for i in range(wide):
        out_ref[me, sum_rows + i * rest : sum_rows + (i + 1) * rest, :] = second_ref[i, sum_rows:, :]
    copies = send_all(places, lambda i: out_ref.at[me], out_ref.at[me], narrow + wide)
    for copy in copies:
        copy.wait()


def finish(summed, kept, narrow, wide, collective_id):
    sum_total = sum(item.shape[0] for item in summed)
    kept_total = sum(item.shape[0] for item in kept)
    sum_rows = round_up(-(-sum_total // narrow), 8)
    kept_rows = round_up(-(-kept_total // narrow), 8)
    rows = sum_rows + kept_rows
    count = 2 * narrow + wide
    out = pl.pallas_call(
        functools.partial(finish_kernel, narrow, wide, sum_rows, len(summed)),
        in_specs=[pl.BlockSpec(memory_space=pltpu.VMEM)] * (len(summed) + len(kept)),
        out_specs=pl.BlockSpec(memory_space=pltpu.VMEM),
        out_shape=jax.ShapeDtypeStruct((narrow, sum_rows + wide * kept_rows, 128), F32),
        scratch_shapes=[
            pltpu.VMEM((narrow, rows, 128), F32),
            pltpu.VMEM((narrow, rows, 128), F32),
            pltpu.VMEM((wide, rows, 128), F32),
            pltpu.SemaphoreType.DMA((count,)),
            pltpu.SemaphoreType.DMA((count,)),
        ],
        compiler_params=pltpu.CompilerParams(collective_id=collective_id, has_side_effects=True),
    )(*summed, *kept)
    total = out[:, :sum_rows, :].reshape(narrow * sum_rows, 128)[:sum_total]
    groups = out[:, sum_rows:, :].reshape(narrow, wide, kept_rows, 128).transpose(1, 0, 2, 3)
    return total, groups.reshape(wide, narrow * kept_rows, 128)[:, :kept_total]


def exchange(blocks, axis):
    return lax.all_to_all(blocks, axis, 0, 0, tiled=True)


def core_swap(value):
    return lax.ppermute(value, "core", [(0, 1), (1, 0)])


def by_core(low, high):
    first = lax.axis_index("core") == 0
    return jnp.where(first, low, high), jnp.where(first, high, low)


def in_core_order(own, other):
    first = lax.axis_index("core") == 0
    return jnp.where(first, own, other), jnp.where(first, other, own)


def chip_sum(own_left, other_left, right):
    came = core_swap(outer_sum(other_left, right).astype(BF16))
    return (outer_sum(own_left, right) + came.astype(F32)).astype(BF16)


def fsdp_sum(both):
    return lax.psum_scatter(both, "fsdp", scatter_dimension=0, tiled=True)


def z_pieces(blocks, deep):
    me = lax.axis_index("z")
    return [lax.dynamic_index_in_dim(blocks, me, 0, keepdims=False)] + [
        lax.ppermute(
            lax.dynamic_index_in_dim(blocks, me ^ step, 0, keepdims=False), "z", [(i, i ^ step) for i in range(deep)]
        )
        for step in range(1, deep)
    ]


def added(pieces):
    return functools.reduce(jnp.add, [piece.astype(F32) for piece in pieces])


def to_all(block, narrow):
    return [
        lax.ppermute(block, "fsdp", [(i, i ^ step) for i in range(narrow)]) for step in range(1, narrow)
    ]


def relative(blocks, me, axis):
    return jnp.concatenate(
        [lax.dynamic_slice_in_dim(blocks, me ^ step, 1, axis) for step in range(blocks.shape[axis])], axis=axis
    )


def device_columns(value, deep, narrow):
    rows, width = value.shape
    block = width // (2 * deep * narrow)
    core = lax.axis_index("core")
    target = jnp.arange(width, dtype=jnp.int32)
    c, f, z, r = (
        target // (narrow * deep * block), target // (deep * block) % narrow, target // block % deep, target % block,
    )
    c = (c + core) % 2
    source = ((z * 2 + c) * narrow + f) * block + r
    pick = (jnp.arange(width, dtype=jnp.int32)[:, None] == source[None, :]).astype(BF16)
    moved = low_product(value, pick).astype(BF16)
    return moved[:, : width // 2], moved[:, width // 2 :]


def whole_weight(shard):
    rows = shard.shape[0] // 2
    half = lax.dynamic_slice_in_dim(shard, lax.axis_index("core") * rows, rows, 0)
    return lax.all_gather(half, ("fsdp", "core"), axis=0, tiled=True)


def shards(
    tokens,
    cotangent,
    text_states,
    conditioning,
    image_sizes,
    ada_weight,
    ada_bias,
    qkv_weight,
    out_weight,
    text_weight,
    gate_up_weight,
    down_weight,
    norm_gains,
    norm_shifts,
    text_gain,
    head_gate,
):
    model_width = tokens.shape[2]
    head_count = head_gate.shape[0]
    head_dim = model_width // head_count
    image_count = text_states.shape[1]
    caption_local = text_states.shape[2]
    caption_width = text_states.shape[3]
    local_tok = tokens.shape[1]
    deep = lax.axis_size("z")
    narrow = lax.axis_size("fsdp")
    wide = 2 * deep
    me = lax.axis_index("fsdp")
    group_tok = local_tok * narrow
    caption_full = caption_local * narrow
    score_scale = head_dim ** (-0.5)
    text_total = image_count * caption_full
    text_local = image_count * caption_local
    part = model_width // narrow
    part_pad = round_up(part, 128)
    heads_here = head_count // narrow
    pairs = part_pad // 128
    halves = 128 // head_dim

    group_sizes = image_sizes[0]
    position = me * local_tok + jnp.arange(local_tok, dtype=jnp.int32)
    image_index = token_layout(group_sizes, position, image_count)[0]
    key_image, key_row, key_col = token_layout(
        group_sizes, jnp.arange(group_tok, dtype=jnp.int32), image_count
    )
    member = [(image_index == i).astype(F32)[:, None] for i in range(image_count)]
    cosine, sine = rope_tables(key_row, key_col, head_dim)

    cond_low = jax.nn.silu(conditioning[0].astype(F32)).astype(BF16)
    cond_rows = ada_weight.shape[0]
    cond_part = lax.dynamic_slice_in_dim(cond_low, me * cond_rows, cond_rows, 1)
    modulation_part = low_product(cond_part, ada_weight)
    modulation = (
        jnp.sum(fsdp_share(modulation_part.reshape(-1, 128), narrow, 0), axis=0).reshape(modulation_part.shape)
        + ada_bias
    )

    def per_token(index):
        rows = modulation[:, index * model_width : (index + 1) * model_width]
        return functools.reduce(
            jnp.add, [member[i] * rows[i : i + 1, :] for i in range(image_count)]
        )

    def per_image(value):
        return [jnp.sum(member[i] * value, axis=0).reshape(-1, 128) for i in range(image_count)]

    token_in = tokens[0].astype(F32)
    token_inverse = inverse_rms(token_in)
    tokens_all = lax.all_gather(tokens[0], "fsdp", axis=0, tiled=True)
    def widened(value, slots):
        if part == part_pad:
            return value
        lead = value.shape[:-1]
        value = value.reshape(*lead, slots, part)
        pads = [(0, 0)] * (len(lead) + 1) + [(0, part_pad - part)]
        return jnp.pad(value, pads).reshape(*lead, slots * part_pad)

    def narrowed(value, slots):
        if part == part_pad:
            return value
        lead = value.shape[:-1]
        return value.reshape(*lead, slots, part_pad)[..., :part].reshape(*lead, slots * part)

    def own_columns(value):
        return widened(lax.dynamic_slice_in_dim(value, me * part, part, value.ndim - 1), 1)

    qkv_rows = qkv_weight.shape[0] // 2
    qkv_half = lax.dynamic_slice_in_dim(qkv_weight, lax.axis_index("core") * qkv_rows, qkv_rows, 0)
    qkv_half = exchange(
        qkv_half.reshape(qkv_rows, 3, narrow, part).transpose(2, 0, 1, 3).reshape(narrow, qkv_rows, 3 * part), "fsdp"
    )
    own_qkv = widened(
        jnp.concatenate(in_core_order(qkv_half, core_swap(qkv_half)), axis=1).reshape(model_width, 3 * part), 3
    )

    full_out = whole_weight(out_weight)
    full_gate_up = whole_weight(gate_up_weight)
    full_down = whole_weight(down_weight)

    text_in = text_states[0].astype(F32).reshape(text_local, caption_width)
    text_inverse = inverse_rms(text_in)
    text_low = (text_in * text_inverse * text_gain).astype(BF16)
    text_cols = caption_width // narrow
    text_slice = (
        exchange(text_low.reshape(text_local, narrow, text_cols).transpose(1, 0, 2), "fsdp")
        .reshape(narrow, image_count, caption_local, text_cols)
        .transpose(1, 0, 2, 3)
        .reshape(text_total, text_cols)
    )
    own_text_weight = (
        text_weight.reshape(text_cols, 2, narrow, part).transpose(2, 0, 1, 3).reshape(narrow, text_cols, 2 * part)
    )
    relative_text_weight = (
        relative(own_text_weight, me, 0).transpose(1, 0, 2).reshape(text_cols, 2 * model_width)
    )
    text_partial = jnp.stack([low_product(text_slice, own_text_weight[i]).astype(BF16) for i in range(narrow)])
    text_partial, tokens_all = lax.optimization_barrier((text_partial, tokens_all))
    text_projected = widened(jnp.sum(exchange(text_partial, "fsdp").astype(F32), axis=0), 2)
    text_parts = fsdp_share(column_stats(text_projected, part, part_pad, 1), narrow, 1)
    text_means = text_parts[:, 0, :]
    text_mean = jnp.mean(text_means, axis=0)
    text_square = jnp.sum(text_parts[:, 1, :], axis=0) + part * jnp.sum((text_means - text_mean) ** 2, axis=0)
    text_key_inverse = lax.rsqrt(text_square / model_width + EPS)[:, None]
    text_unit = (text_projected[:, :part_pad] - text_mean[:, None]) * text_key_inverse
    text_gains = own_columns(norm_gains[4])
    text_packed = jnp.concatenate(
        [(text_unit * text_gains).astype(BF16), text_projected[:, part_pad:].astype(BF16)], axis=1
    )

    wide_tokens = tokens_all.astype(F32)
    wide_scale = functools.reduce(
        jnp.add,
        [(key_image == i).astype(F32)[:, None] * modulation[i : i + 1, :model_width] for i in range(image_count)],
    )
    normed_all = (wide_tokens * inverse_rms(wide_tokens) * norm_gains[0] * (1.0 + wide_scale)).astype(BF16)

    projected = low_product(normed_all, own_qkv)
    stats_all = fsdp_share(column_stats(projected, part, part_pad, 2), narrow, 2)
    head_gains = own_columns(norm_gains[2:4])
    packed = make_heads(
        projected, stats_all, cosine, sine, head_gains, own_columns(norm_shifts), part, score_scale * LOG2E
    )
    gate_tanh = jnp.tanh(head_gate)
    own_gates = lax.dynamic_slice_in_dim(gate_tanh, me * heads_here, heads_here, 0)
    own_gates = jnp.concatenate([own_gates, jnp.ones((pairs * halves - heads_here,), F32)])
    column = key_image[:, None]
    row = key_image[None, :]
    attended = [
        attend(pair, own_gates, packed, text_packed, column, row, head_dim, image_count) for pair in range(pairs)
    ]
    mixed_pairs = [exchange(one[0].reshape(narrow, local_tok, 128), "fsdp") for one in attended]
    self_outs = [one[1] for one in attended]
    cross_outs = [one[2] for one in attended]
    stats = [one[3] for one in attended]
    mixed_low = (
        narrowed(jnp.concatenate(mixed_pairs, axis=2), 1).transpose(1, 0, 2).reshape(local_tok, model_width)
    )

    branch = low_product(mixed_low, full_out)
    branch_inverse = inverse_rms(branch)
    branch_unit = branch * branch_inverse
    gate_attend = jnp.tanh(per_token(1))
    hidden = token_in + gate_attend * (branch_unit * norm_gains[1])
    hidden_inverse = inverse_rms(hidden)
    hidden_unit = hidden * hidden_inverse
    scale_feed = 1.0 + per_token(2)
    normed_feed_low = (hidden_unit * norm_gains[5] * scale_feed).astype(BF16)
    gate_up = low_product(normed_feed_low, full_gate_up)
    hidden_units = gate_up.shape[1] // 2
    gate_half = gate_up[:, :hidden_units]
    up_half = gate_up[:, hidden_units:]
    sigmoid = jax.nn.sigmoid(gate_half)
    if hidden_units // (wide * narrow) % 128 == 0:
        activated_low, moved = swiglu(gate_up, lax.axis_index("core"), deep, narrow)
        down_columns = (moved[:, : hidden_units // 2], moved[:, hidden_units // 2 :])
    else:
        activated_low = (gate_half * sigmoid * up_half).astype(BF16)
        down_columns = device_columns(activated_low, deep, narrow)
    down_out = low_product(activated_low, full_down)
    down_inverse = inverse_rms(down_out)
    down_unit = down_out * down_inverse
    gate_feed = jnp.tanh(per_token(3))
    down_normed = down_unit * norm_gains[6]
    result = (hidden + gate_feed * down_normed).astype(BF16)

    grad_result = cotangent[0].astype(F32)
    grad_down_y = grad_result * gate_feed
    grad_gain_six = jnp.sum(grad_down_y * down_unit, axis=0)
    grad_gate_feed = per_image(grad_result * down_normed * (1.0 - gate_feed * gate_feed))
    grad_down_low = norm_pull(grad_down_y * norm_gains[6], down_unit, down_inverse).astype(BF16)
    grad_activated = times_transposed(grad_down_low, full_down)
    grad_gate_low = (grad_activated * up_half * sigmoid * (1.0 + gate_half * (1.0 - sigmoid))).astype(BF16)
    grad_up_low = (grad_activated * gate_half * sigmoid).astype(BF16)
    grad_gate_up_low = jnp.concatenate([grad_gate_low, grad_up_low], axis=1)
    grad_normed_feed = times_transposed(grad_gate_up_low, full_gate_up)
    grad_feed_y = grad_normed_feed * scale_feed
    grad_gain_five = jnp.sum(grad_feed_y * hidden_unit, axis=0)
    grad_scale_feed = per_image(grad_normed_feed * hidden_unit * norm_gains[5])
    grad_hidden = grad_result + norm_pull(grad_feed_y * norm_gains[5], hidden_unit, hidden_inverse)
    grad_branch_y = grad_hidden * gate_attend
    grad_gain_one = jnp.sum(grad_branch_y * branch_unit, axis=0)
    grad_gate_attend = per_image(
        grad_hidden * branch_unit * norm_gains[1] * (1.0 - gate_attend * gate_attend)
    )
    grad_branch_low = norm_pull(grad_branch_y * norm_gains[1], branch_unit, branch_inverse).astype(BF16)
    grad_mixed = times_transposed(grad_branch_low, full_out).astype(BF16)
    grad_blocks = widened(grad_mixed.reshape(local_tok, narrow, part).transpose(1, 0, 2), 1)
    grad_heads = exchange(grad_blocks, "fsdp").reshape(group_tok, part_pad)
    def by_z(value):
        return value.reshape(deep, -1, value.shape[1])

    down_both = chip_sum(*down_columns, grad_down_low)
    feed_columns = device_columns(normed_feed_low, deep, narrow)
    gate_both = chip_sum(*feed_columns, grad_gate_low)
    up_both = chip_sum(*feed_columns, grad_up_low)
    out_both = chip_sum(*device_columns(mixed_low, deep, narrow), grad_branch_low)
    down_part = fsdp_sum(down_both)
    grad_heads, gate_both, up_both, out_both, down_part = lax.optimization_barrier(
        (grad_heads, gate_both, up_both, out_both, down_part)
    )
    gate_part = fsdp_sum(gate_both)
    out_part = fsdp_sum(out_both)
    up_part = fsdp_sum(up_both)
    came_downs = exchange(by_z(down_part), "z")
    crossed = [
        cross_back(
            pair, own_gates, packed, text_packed, row, grad_heads, cross_outs[pair], stats[pair],
            head_dim, image_count, score_scale,
        )
        for pair in range(pairs)
    ]
    dtk = jnp.concatenate([one[1] for one in crossed], axis=1)
    dtv = jnp.concatenate([one[2] for one in crossed], axis=1)
    gate_sums = jnp.stack([one[3] for one in crossed])

    grad_text_keys = dtk.astype(F32)
    own_gain_four = jnp.sum(grad_text_keys * text_unit, axis=0)
    grad_text_unit = grad_text_keys * text_gains
    text_sums = jnp.stack([jnp.sum(grad_text_unit, axis=1), jnp.sum(grad_text_unit * text_unit, axis=1)])
    text_sums = jnp.sum(
        fsdp_share(jnp.pad(text_sums, ((0, 6), (0, 0))), narrow, 3), axis=0
    ) * (1.0 / model_width)
    grad_text_key_in = (grad_text_unit - text_sums[0][:, None] - text_unit * text_sums[1][:, None]) * text_key_inverse
    grad_text_own = jnp.concatenate(
        [narrowed(grad_text_key_in.astype(BF16), 1), narrowed(dtv, 1)], axis=1
    )
    def self_pair(pair):
        return self_back(
            pair, packed, column, row, grad_heads, self_outs[pair], stats[pair], crossed[pair][0], head_dim, score_scale
        )

    came_texts = to_all(grad_text_own, narrow)
    backs = [self_pair(0)]
    first, came_downs, *came_texts = lax.optimization_barrier((backs[0][0], came_downs, *came_texts))
    grad_down_weight = jnp.sum(came_downs.astype(F32), axis=0)
    backs[0] = (first, *backs[0][1:])
    grad_text_columns = jnp.concatenate([grad_text_own, *came_texts], axis=1)
    text_half = text_cols // 2
    own_text, other_text = by_core(text_slice[:, :text_half], text_slice[:, text_half:])
    came_text = core_swap(outer_sum(other_text, grad_text_columns).astype(BF16))
    text_both = (outer_sum(own_text, grad_text_columns) + came_text.astype(F32)).astype(BF16)
    grad_heads, text_both, first = lax.optimization_barrier((grad_heads, text_both, backs[0][0]))
    backs[0] = (first, *backs[0][1:])
    came_text_z = exchange(by_z(text_both), "z")
    backs.append(self_pair(1))
    if pairs > 2:
        grad_heads, gate_part, up_part, second = lax.optimization_barrier(
            (grad_heads, gate_part, up_part, backs[1][0])
        )
        backs[1] = (second, *backs[1][1:])
        backs += [self_pair(pair) for pair in range(2, pairs)]
    gate_pieces = z_pieces(by_z(gate_part), deep)
    last, came_text_z, up_part, *gate_pieces = lax.optimization_barrier(
        (backs[-1][0], came_text_z, up_part, *gate_pieces)
    )
    up_pieces = z_pieces(by_z(up_part), deep)
    backs[-1] = (last, *backs[-1][1:])
    text_part = jnp.sum(came_text_z.astype(F32), axis=0).astype(BF16)
    everyone = ("z", "core", "fsdp")
    grad_text_weight = lax.ppermute(
        text_part,
        everyone,
        [
            ((z * 2 + c) * narrow + f, f * wide + c * deep + z)
            for z in range(deep) for c in range(2) for f in range(narrow)
        ],
    )
    last, grad_text_columns = lax.optimization_barrier((backs[-1][0], grad_text_columns))
    backs[-1] = (last, *backs[-1][1:])
    grad_text_slice = times_transposed(grad_text_columns, relative_text_weight).astype(BF16)
    came_text = exchange(
        grad_text_slice.reshape(image_count, narrow, caption_local, text_cols)
        .transpose(1, 0, 2, 3)
        .reshape(narrow, text_local, text_cols),
        "fsdp",
    )
    came_out_z = exchange(by_z(out_part), "z")
    own_gate_grad = jnp.sum(gate_sums[:, 0, :].reshape(pairs * halves, head_dim), axis=1)[:heads_here]
    grad_head_gate = lax.dynamic_update_slice_in_dim(
        jnp.zeros((head_count,), F32), own_gate_grad, me * heads_here, 0
    ) * (1.0 - gate_tanh * gate_tanh)
    grad_projected_low, head_sums = heads_back(
        list(zip(*backs)), projected, stats_all, cosine, sine, head_gains, part,
        lambda value: fsdp_share(value, narrow, 4),
    )
    grad_projected_low, came_text, *up_pieces = lax.optimization_barrier(
        (grad_projected_low, came_text, *up_pieces)
    )
    grad_gate_up_weight = jnp.concatenate([added(gate_pieces), added(up_pieces)], axis=1)
    partial_normed, grad_text_weight = lax.optimization_barrier(
        (times_transposed(grad_projected_low, own_qkv).astype(BF16), grad_text_weight)
    )
    grad_normed = lax.psum_scatter(partial_normed, "fsdp", scatter_dimension=0, tiled=True)

    def lane_rows(value):
        return value.reshape(-1, 128)

    group = lax.axis_index("z") * 2 + lax.axis_index("core")
    columns_here = jnp.stack(
        [narrowed(value, 1) for value in (head_sums[0], head_sums[2], own_gain_four, head_sums[1], head_sums[3])]
    )
    here = (jnp.arange(narrow, dtype=jnp.int32) == me)[None, :, None]
    placed = lane_rows(jnp.where(here, columns_here[:, None, :], 0.0))
    cond_rows_here = lane_rows(jnp.where(me == 0, cond_low.astype(F32), 0.0))
    gate_row = jnp.pad(grad_head_gate, (0, 128 - head_count)).reshape(1, 128)
    ready = [lane_rows(grad_gain_one), lane_rows(grad_gain_five), lane_rows(grad_gain_six), placed, gate_row]
    later = [*grad_gate_attend, *grad_scale_feed, *grad_gate_feed, cond_rows_here]
    ready = lax.optimization_barrier(tuple(ready))
    qkv_grad = outer_sum(normed_all, grad_projected_low).astype(BF16).reshape(deep, 2, model_width // wide, 3 * part_pad)
    qkv_grad, came_out_z = lax.optimization_barrier((qkv_grad, came_out_z))
    place = (lax.axis_index("z") * 2 + lax.axis_index("core")) * narrow + me
    grad_text_weight = (
        relative(grad_text_weight.reshape(-1, narrow, 2 * part), place // wide, 1)
        .reshape(-1, narrow, 2, part)
        .transpose(0, 2, 1, 3)
        .reshape(-1, 2 * model_width)
        .astype(F32)
    )
    grad_out_weight = jnp.sum(came_out_z.astype(F32), axis=0)
    own_grad, other_grad = by_core(qkv_grad[:, 0], qkv_grad[:, 1])
    own_grad = (own_grad.astype(F32) + core_swap(other_grad).astype(F32)).astype(BF16)
    own_pieces = z_pieces(own_grad, deep)
    grad_text_normed = (
        came_text
        .transpose(1, 0, 2)
        .reshape(text_local, caption_width)
        .astype(F32)
    )
    text_state_unit = text_in * text_inverse
    grad_text_gain = jnp.sum(grad_text_normed * text_state_unit, axis=0)
    grad_text = (
        norm_pull(grad_text_normed * text_gain, text_state_unit, text_inverse)
        .astype(BF16)
        .reshape(image_count, caption_local, caption_width)
    )

    grad_text, grad_text_gain, *own_pieces = lax.optimization_barrier((grad_text, grad_text_gain, *own_pieces))
    own_grad = added(own_pieces)
    grad_qkv_weight = (
        exchange(narrowed(own_grad.astype(BF16), 3).reshape(narrow, -1, 3 * part), "fsdp")
        .reshape(narrow, -1, 3, part)
        .transpose(1, 2, 0, 3)
        .reshape(-1, 3 * model_width)
        .astype(F32)
    )
    grad_normed, grad_qkv_weight = lax.optimization_barrier((grad_normed, grad_qkv_weight))
    grad_normed = grad_normed.astype(F32)

    token_unit = token_in * token_inverse
    scale_attend = 1.0 + per_token(0)
    grad_normed_y = grad_normed * scale_attend
    grad_gain_zero = jnp.sum(grad_normed_y * token_unit, axis=0)
    grad_scale_attend = per_image(grad_normed * token_unit * norm_gains[0])
    grad_tokens = (
        grad_hidden + norm_pull(grad_normed_y * norm_gains[0], token_unit, token_inverse)
    ).astype(BF16)
    lanes_of_row = model_width // 128
    summed, kept = finish(
        [lane_rows(grad_gain_zero), *ready, lane_rows(grad_text_gain)], [*grad_scale_attend, *later], narrow, wide, 5
    )
    every_image = wide * image_count
    per_part = image_count * lanes_of_row
    slots = jnp.concatenate(
        [kept[:, i * per_part : (i + 1) * per_part].reshape(every_image, model_width) for i in range(4)], axis=1
    )
    cond_slots = kept[:, 4 * per_part :].reshape(every_image, cond_low.shape[1])
    ada_rows = cond_rows // wide
    own_cond = lax.dynamic_slice_in_dim(cond_slots, (group * narrow + me) * ada_rows, ada_rows, 1)
    grad_ada_weight = exact_outer(own_cond, slots)
    grad_ada_bias = jnp.sum(slots, axis=0)

    def rows_of(first, count):
        return summed[first * lanes_of_row : (first + count) * lanes_of_row]

    grad_gains = jnp.concatenate([rows_of(0, 2), rows_of(4, 3), rows_of(2, 2)]).reshape(norm_gains.shape)
    grad_shifts = rows_of(7, 2).reshape(norm_shifts.shape)
    grad_head_gate = summed[9 * lanes_of_row, :head_count]
    grad_text_gain = summed[9 * lanes_of_row + 1 :].reshape(-1)
    return (
        result[None],
        grad_tokens[None],
        grad_text[None],
        grad_ada_weight,
        grad_qkv_weight,
        grad_out_weight,
        grad_text_weight,
        grad_gate_up_weight,
        grad_down_weight,
        grad_ada_bias,
        grad_gains,
        grad_shifts,
        grad_text_gain,
        grad_head_gate,
    )


def solution(mesh):
    wide, narrow = mesh.devices.shape
    fine = Mesh(mesh.devices.reshape(wide // 2, 2, narrow), ("z", "core", "fsdp"))
    groups = ("z", "core")
    every = ("z", "core", "fsdp")
    placed = (
        P(groups, "fsdp", None),
        P(groups, "fsdp", None),
        P(groups, None, "fsdp", None),
        P(groups, None, None),
        P(groups, None, None),
        P("fsdp", None),
        P(),
        P("fsdp", None),
        P("fsdp", None),
        P("fsdp", None),
        P("fsdp", None),
        P("fsdp", None),
        P(),
        P(),
        P(),
        P(),
    )
    return jax.shard_map(
        shards,
        mesh=fine,
        in_specs=placed,
        out_specs=(
            P(groups, "fsdp", None),
            P(groups, "fsdp", None),
            P(groups, None, "fsdp", None),
            P(every, None),
            P(every, None),
            P(every, None),
            P(every, None),
            P(every, None),
            P(every, None),
            P(),
            P(),
            P(),
            P(),
            P(),
        ),
        check_vma=False,
    )
```

```python
import functools

import jax
import jax.numpy as jnp
from jax import lax
from jax.experimental import pallas as pl
from jax.experimental.pallas import tpu as pltpu
from jax.sharding import Mesh
from jax.sharding import PartitionSpec as P

EPS = 1e-05
HIGHEST_PRECISION = lax.Precision.HIGHEST
MASKED = -1e30
LOG2E = 1.4426950408889634
FIRST_PATCHES = 16 * 12**2
FIRST_MOST = FIRST_PATCHES + 96
QBLOCK = 256
BF16 = jnp.bfloat16
F32 = jnp.float32
VMEM_LIMIT = 60 * 1024 * 1024


def round_up(value, step):
    return -(-value // step) * step


def low_product(left, right):
    return jnp.dot(left, right, preferred_element_type=F32)


def times_transposed(left, right):
    return lax.dot_general(left, right, (((1,), (1,)), ((), ())), preferred_element_type=F32)


def outer_sum(left, right):
    return lax.dot_general(left, right, (((0,), (0,)), ((), ())), preferred_element_type=F32)


def exact_outer(left, right):
    return lax.dot_general(
        left, right, (((0,), (0,)), ((), ())), precision=HIGHEST_PRECISION, preferred_element_type=F32
    )


def exact_transposed(left, right):
    return lax.dot_general(
        left, right, (((1,), (1,)), ((), ())), precision=HIGHEST_PRECISION, preferred_element_type=F32
    )


def row_mean(value):
    return jnp.mean(value, axis=-1, keepdims=True)


def inverse_rms(value):
    return lax.rsqrt(row_mean(value * value) + EPS)


def norm_pull(grad, unit, inverse):
    return (grad - unit * row_mean(grad * unit)) * inverse


def token_layout(image_sizes, position, image_count):
    start = jnp.int32(0)
    image_index = jnp.full(position.shape, image_count, jnp.int32)
    token_row = jnp.zeros(position.shape, jnp.int32)
    token_col = jnp.zeros(position.shape, jnp.int32)
    for i in range(image_count):
        width = image_sizes[i, 1] + 1
        end = start + image_sizes[i, 0] * width
        inside = (position >= start) & (position < end)
        offset = position - start
        image_index = jnp.where(inside, i, image_index)
        token_row = jnp.where(inside, offset // width, token_row)
        token_col = jnp.where(inside, offset % width, token_col)
        start = end
    return image_index, token_row, token_col


def rope_tables(token_row, token_col, head_dim):
    quarter = head_dim // 4
    pair = (jnp.arange(128, dtype=jnp.int32) % head_dim) // 2
    frequency = 10000.0 ** (-(pair % quarter).astype(F32) / quarter)
    place = jnp.where(
        (pair < quarter)[None, :], token_row.astype(F32)[:, None], token_col.astype(F32)[:, None]
    )
    angles = place * frequency[None, :]
    even = (jnp.arange(128, dtype=jnp.int32) % 2 == 0)[None, :]
    return jnp.cos(angles), jnp.where(even, -jnp.sin(angles), jnp.sin(angles))


def swap_pairs(value):
    width = value.shape[1]
    even = lax.broadcasted_iota(jnp.int32, value.shape, 1) % 2 == 0
    return jnp.where(even, pltpu.roll(value, width - 1, 1), pltpu.roll(value, 1, 1))


def wide_table(table, width):
    return jnp.concatenate([table] * (width // table.shape[1]), axis=1)


def pack_columns(columns):
    rows = columns[0].shape[0]
    lane = lax.broadcasted_iota(jnp.int32, (rows, 128), 1)
    packed = jnp.zeros((rows, 128), F32)
    for i, column in enumerate(columns):
        packed = jnp.where(lane == i, column, packed)
    return jnp.transpose(packed)[:8, :]


def as_columns(rows_list):
    width = rows_list[0].shape[1]
    stacked = jnp.concatenate(
        rows_list + [jnp.zeros((128 - len(rows_list), width), F32)], axis=0
    )
    return jnp.transpose(stacked)


def real_lanes(shape, part):
    return lax.broadcasted_iota(jnp.int32, shape, 1) < part


def own_stats(value, part):
    mean = jnp.sum(value, axis=1, keepdims=True) * (1.0 / part)
    centred = value - mean
    if value.shape[1] != part:
        centred = jnp.where(real_lanes(value.shape, part), centred, 0.0)
    return mean, jnp.sum(centred * centred, axis=1, keepdims=True)


def joined_stats(stats_ref, part, slot):
    narrow = stats_ref.shape[0]
    means = [stats_ref[i, 2 * slot : 2 * slot + 1, :] for i in range(narrow)]
    squares = [stats_ref[i, 2 * slot + 1 : 2 * slot + 2, :] for i in range(narrow)]
    mean = functools.reduce(jnp.add, means) * (1.0 / narrow)
    square = functools.reduce(jnp.add, squares)
    square = square + part * functools.reduce(jnp.add, [(m - mean) * (m - mean) for m in means])
    return mean, lax.rsqrt(square * (1.0 / (narrow * part)) + EPS)


def stats_kernel(part, slots, projected_ref, out_ref):
    padded = projected_ref.shape[1] // slots
    columns = []
    for slot in range(slots):
        columns += own_stats(projected_ref[:, slot * padded : (slot + 1) * padded], part)
    out_ref[...] = pack_columns(columns)


def column_stats(projected, part, padded, slots):
    rows = projected.shape[0]
    return pl.pallas_call(
        functools.partial(stats_kernel, part, slots),
        grid=(pl.cdiv(rows, QBLOCK),),
        in_specs=[pl.BlockSpec((QBLOCK, slots * padded), lambda i: (i, 0))],
        out_specs=pl.BlockSpec((8, QBLOCK), lambda i: (0, i)),
        out_shape=jax.ShapeDtypeStruct((8, rows), F32),
        compiler_params=pltpu.CompilerParams(vmem_limit_bytes=VMEM_LIMIT),
        cost_estimate=pl.CostEstimate(flops=10 * rows * slots * padded, bytes_accessed=4 * rows * slots * padded, transcendentals=0),
    )(projected)


def heads_kernel(part, query_scale, projected_ref, stats_ref, cos_ref, sin_ref, gains_ref, shifts_ref, out_ref):
    padded = projected_ref.shape[1] // 3
    cosine = wide_table(cos_ref[...], padded)
    sine = wide_table(sin_ref[...], padded)
    columns = as_columns([*joined_stats(stats_ref, part, 0), *joined_stats(stats_ref, part, 1)])
    for slot in range(3):
        place = slice(slot * padded, (slot + 1) * padded)
        value = projected_ref[:, place]
        if slot < 2:
            value = (value - columns[:, 2 * slot : 2 * slot + 1]) * columns[:, 2 * slot + 1 : 2 * slot + 2]
            value = value * gains_ref[slot : slot + 1, :] + shifts_ref[slot : slot + 1, :]
            value = value * cosine + swap_pairs(value) * sine
            if slot == 0:
                value = value * query_scale
        out_ref[:, place] = value.astype(BF16)


def make_heads(projected, stats, cosine, sine, gains, shifts, part, query_scale):
    rows, triple = projected.shape
    padded = triple // 3
    narrow = stats.shape[0]
    return pl.pallas_call(
        functools.partial(heads_kernel, part, query_scale),
        grid=(pl.cdiv(rows, QBLOCK),),
        in_specs=[
            pl.BlockSpec((QBLOCK, triple), lambda i: (i, 0)),
            pl.BlockSpec((narrow, 8, QBLOCK), lambda i: (0, 0, i)),
            pl.BlockSpec((QBLOCK, 128), lambda i: (i, 0)),
            pl.BlockSpec((QBLOCK, 128), lambda i: (i, 0)),
            pl.BlockSpec((2, padded), lambda i: (0, 0)),
            pl.BlockSpec((2, padded), lambda i: (0, 0)),
        ],
        out_specs=pl.BlockSpec((QBLOCK, triple), lambda i: (i, 0)),
        out_shape=jax.ShapeDtypeStruct((rows, triple), BF16),
        compiler_params=pltpu.CompilerParams(vmem_limit_bytes=VMEM_LIMIT),
        cost_estimate=pl.CostEstimate(flops=40 * rows * triple, bytes_accessed=6 * rows * triple, transcendentals=0),
    )(projected, stats, cosine, sine, gains, shifts)


def turned_back(refs, cosine, sine):
    grad = jnp.concatenate([ref[...].astype(F32) for ref in refs], axis=1)
    return grad * cosine - swap_pairs(grad) * sine


def grad_stats_kernel(rows, part, pairs, *refs):
    dq_refs, dk_refs = refs[:pairs], refs[pairs : 2 * pairs]
    projected_ref, stats_ref, cos_ref, sin_ref, gains_ref, out_ref, sums_ref = refs[2 * pairs :]
    step = pl.program_id(0)
    padded = 128 * pairs
    cosine = wide_table(cos_ref[...], padded)
    sine = wide_table(sin_ref[...], padded)
    height = cos_ref.shape[0]
    inside = step * height + lax.broadcasted_iota(jnp.int32, (height, 1), 0) < rows

    @pl.when(step == 0)
    def _():
        sums_ref[...] = jnp.zeros_like(sums_ref)

    columns = as_columns([*joined_stats(stats_ref, part, 0), *joined_stats(stats_ref, part, 1)])
    packed = []
    for slot, grads in enumerate((dq_refs, dk_refs)):
        grad = jnp.where(inside, turned_back(grads, cosine, sine), 0.0)
        unit = (projected_ref[:, slot * padded : (slot + 1) * padded] - columns[:, 2 * slot : 2 * slot + 1])
        unit = jnp.where(inside, unit * columns[:, 2 * slot + 1 : 2 * slot + 2], 0.0)
        both = grad * unit
        sums_ref[2 * slot : 2 * slot + 1, :] += jnp.sum(both, axis=0, keepdims=True)
        sums_ref[2 * slot + 1 : 2 * slot + 2, :] += jnp.sum(grad, axis=0, keepdims=True)
        gain = gains_ref[slot : slot + 1, :]
        packed.append(jnp.sum(grad * gain, axis=1, keepdims=True))
        packed.append(jnp.sum(both * gain, axis=1, keepdims=True))
    out_ref[...] = pack_columns(packed)


def heads_back_kernel(part, pairs, *refs):
    dq_refs, dk_refs, dv_refs = refs[:pairs], refs[pairs : 2 * pairs], refs[2 * pairs : 3 * pairs]
    projected_ref, stats_ref, totals_ref, cos_ref, sin_ref, gains_ref, out_ref = refs[3 * pairs :]
    padded = 128 * pairs
    narrow = stats_ref.shape[0]
    cosine = wide_table(cos_ref[...], padded)
    sine = wide_table(sin_ref[...], padded)
    means = [
        functools.reduce(jnp.add, [totals_ref[i, j : j + 1, :] for i in range(narrow)]) * (1.0 / (narrow * part))
        for j in range(4)
    ]
    columns = as_columns([*joined_stats(stats_ref, part, 0), *joined_stats(stats_ref, part, 1), *means])
    for slot, grads in enumerate((dq_refs, dk_refs)):
        grad = turned_back(grads, cosine, sine) * gains_ref[slot : slot + 1, :]
        inverse = columns[:, 2 * slot + 1 : 2 * slot + 2]
        unit = (projected_ref[:, slot * padded : (slot + 1) * padded] - columns[:, 2 * slot : 2 * slot + 1]) * inverse
        grad = grad - columns[:, 4 + 2 * slot : 5 + 2 * slot] - unit * columns[:, 5 + 2 * slot : 6 + 2 * slot]
        grad = grad * inverse
        if padded != part:
            grad = jnp.where(real_lanes(grad.shape, part), grad, 0.0)
        out_ref[:, slot * padded : (slot + 1) * padded] = grad.astype(BF16)
    for pair, ref in enumerate(dv_refs):
        out_ref[:, 2 * padded + 128 * pair : 2 * padded + 128 * (pair + 1)] = ref[...]


def heads_back(grads, projected, stats, cosine, sine, gains, part, share):
    rows, triple = projected.shape
    padded = triple // 3
    pairs = padded // 128
    narrow = stats.shape[0]
    pair_spec = pl.BlockSpec((QBLOCK, 128), lambda i: (i, 0))
    two_spec = pl.BlockSpec((QBLOCK, 2 * padded), lambda i: (i, 0))
    stat_spec = pl.BlockSpec((narrow, 8, QBLOCK), lambda i: (0, 0, i))
    gain_spec = pl.BlockSpec((2, padded), lambda i: (0, 0))
    own, sums = pl.pallas_call(
        functools.partial(grad_stats_kernel, rows, part, pairs),
        grid=(pl.cdiv(rows, QBLOCK),),
        in_specs=[pair_spec] * (2 * pairs) + [two_spec, stat_spec, pair_spec, pair_spec, gain_spec],
        out_specs=[
            pl.BlockSpec((8, QBLOCK), lambda i: (0, i)),
            pl.BlockSpec((8, padded), lambda i: (0, 0)),
        ],
        out_shape=[jax.ShapeDtypeStruct((8, rows), F32), jax.ShapeDtypeStruct((8, padded), F32)],
        compiler_params=pltpu.CompilerParams(vmem_limit_bytes=VMEM_LIMIT),
        cost_estimate=pl.CostEstimate(flops=4 * rows * triple, bytes_accessed=rows * triple // 16, transcendentals=0),
    )(*grads[0], *grads[1], projected, stats, cosine, sine, gains)
    totals = share(own)
    out = pl.pallas_call(
        functools.partial(heads_back_kernel, part, pairs),
        grid=(pl.cdiv(rows, QBLOCK),),
        in_specs=[pair_spec] * (3 * pairs) + [two_spec, stat_spec, stat_spec, pair_spec, pair_spec, gain_spec],
        out_specs=pl.BlockSpec((QBLOCK, triple), lambda i: (i, 0)),
        out_shape=jax.ShapeDtypeStruct((rows, triple), BF16),
        compiler_params=pltpu.CompilerParams(vmem_limit_bytes=VMEM_LIMIT),
        cost_estimate=pl.CostEstimate(flops=4 * rows * triple, bytes_accessed=rows * triple // 16, transcendentals=0),
    )(*grads[0], *grads[1], *grads[2], projected, stats, totals, cosine, sine, gains)
    return out, sums


def head_lanes(rows, half, head_dim):
    lane = lax.broadcasted_iota(jnp.int32, (rows, 128), 1)
    return (lane >= half * head_dim) & (lane < (half + 1) * head_dim)


def softmax_product(pieces):
    maximum = functools.reduce(jnp.maximum, [jnp.max(s, axis=1, keepdims=True) for s, _ in pieces])
    total, result = 0.0, 0.0
    for scores, values in pieces:
        weight = jnp.exp2(scores - maximum)
        total = total + jnp.sum(weight, axis=1, keepdims=True)
        result = result + low_product(weight.astype(BF16), values)
    return result * (1.0 / total), maximum + jnp.log2(total)


def attend_kernel(
    head_dim, first, most, caption, image_count,
    gate_ref, q_ref, k_ref, v_ref, tk_ref, tv_ref, column_ref, row_ref,
    mixed_ref, self_ref, cross_ref, stats_ref,
):
    count = q_ref.shape[0]
    halves = 128 // head_dim

    def emit(at, rows, outs):
        lanes = [head_lanes(rows, half, head_dim) for half in range(halves)]
        own, cross, gated = 0.0, 0.0, 0.0
        columns = []
        for half, (own_out, own_total, cross_out, cross_total) in enumerate(outs):
            gate = gate_ref[0, half]
            own = own + jnp.where(lanes[half], own_out, 0.0)
            cross = cross + jnp.where(lanes[half], cross_out, 0.0)
            gated = gated + jnp.where(lanes[half], gate * cross_out, 0.0)
            columns += [own_total, cross_total]
        self_ref[pl.ds(at, rows), :] = own
        cross_ref[pl.ds(at, rows), :] = cross
        mixed_ref[pl.ds(at, rows), :] = (own + gated).astype(BF16)
        lane = lax.broadcasted_iota(jnp.int32, (rows, 128), 1)
        packed = jnp.zeros((rows, 128), F32)
        for i, column in enumerate(columns):
            packed = jnp.where(lane == i, column, packed)
        stats_ref[:, pl.ds(at, rows)] = jnp.transpose(packed)[:8, :]

    def clean(block, carry):
        at = pl.multiple_of(block * QBLOCK, QBLOCK)
        queries = q_ref[pl.ds(at, QBLOCK), :]
        outs = []
        for half in range(halves):
            q = jnp.where(head_lanes(QBLOCK, half, head_dim), queries, jnp.zeros_like(queries))
            bias = jnp.where(row_ref[0:1, first:most] == 0, 0.0, MASKED)
            own_out, own_total = softmax_product([
                (times_transposed(q, k_ref[0:first, :]), v_ref[0:first, :]),
                (times_transposed(q, k_ref[first:most, :]) + bias, v_ref[first:most, :]),
            ])
            cross_out, cross_total = softmax_product(
                [(times_transposed(q, tk_ref[0:caption, :]), tv_ref[0:caption, :])]
            )
            outs.append((own_out, own_total, cross_out, cross_total))
        emit(at, QBLOCK, outs)
        return carry

    lax.fori_loop(0, first // QBLOCK, clean, 0)
    rest = count - first
    queries = q_ref[first:count, :]
    image = column_ref[first:count, :]
    outs = []
    for half in range(halves):
        q = jnp.where(head_lanes(rest, half, head_dim), queries, jnp.zeros_like(queries))
        own_out, own_total = softmax_product([
            (jnp.where(image == row_ref[0:1, :], times_transposed(q, k_ref[...]), MASKED), v_ref[...])
        ])
        scores = times_transposed(q, tk_ref[...])
        owner = lax.broadcasted_iota(jnp.int32, (1, scores.shape[1]), 1) // caption
        scores = jnp.where((image == owner) | (image == image_count), scores, MASKED)
        cross_out, cross_total = softmax_product([(scores, tv_ref[...])])
        outs.append((own_out, own_total, cross_out, cross_total))
    emit(first, rest, outs)


def attend(pair, gates, packed, text_packed, column, row, head_dim, image_count):
    count, texts = packed.shape[0], text_packed.shape[0]
    pairs = packed.shape[1] // 384
    halves = 128 // head_dim
    out = pl.BlockSpec((count, 128), lambda i: (0, 0))
    most = min(round_up(FIRST_MOST, 128), count)
    flops = 4 * count * (count + texts) * 128
    return pl.pallas_call(
        functools.partial(
            attend_kernel, head_dim, FIRST_PATCHES, most, texts // image_count, image_count
        ),
        grid=(1,),
        in_specs=[
            pl.BlockSpec((None, 1, halves), lambda i: (pair, 0, 0), memory_space=pltpu.SMEM),
            pl.BlockSpec((count, 128), lambda i: (0, pair)),
            pl.BlockSpec((count, 128), lambda i: (0, pairs + pair)),
            pl.BlockSpec((count, 128), lambda i: (0, 2 * pairs + pair)),
            pl.BlockSpec((texts, 128), lambda i: (0, pair)),
            pl.BlockSpec((texts, 128), lambda i: (0, pairs + pair)),
            pl.BlockSpec((count, 1), lambda i: (0, 0)),
            pl.BlockSpec((1, count), lambda i: (0, 0)),
        ],
        out_specs=[out, out, out, pl.BlockSpec((8, count), lambda i: (0, 0))],
        out_shape=[
            jax.ShapeDtypeStruct((count, 128), BF16),
            jax.ShapeDtypeStruct((count, 128), F32),
            jax.ShapeDtypeStruct((count, 128), F32),
            jax.ShapeDtypeStruct((8, count), F32),
        ],
        compiler_params=pltpu.CompilerParams(vmem_limit_bytes=VMEM_LIMIT),
        cost_estimate=pl.CostEstimate(flops=flops, bytes_accessed=20 * count * 128, transcendentals=2 * count * count),
    )(gates.reshape(pairs, 1, halves), packed, packed, packed, text_packed, text_packed, column, row)


def gate_lanes(gate_ref, head_dim):
    lane = lax.broadcasted_iota(jnp.int32, (1, 128), 1)
    gates = jnp.zeros((1, 128), F32)
    for half in range(128 // head_dim):
        gates = jnp.where(lane // head_dim == half, gate_ref[0, half], gates)
    return gates


def head_picks(head_dim):
    return (
        lax.broadcasted_iota(jnp.int32, (8, 128), 1) // head_dim
        == lax.broadcasted_iota(jnp.int32, (8, 128), 0)
    ).astype(F32)


def rows_back(head_dim, queries, outs, delta, stats, offset, keys, values, key_sum, value_sum, spans):
    rows = queries.shape[0]
    halves = 128 // head_dim
    zero = jnp.zeros((rows, 128), BF16)
    lanes = [head_lanes(rows, half, head_dim) for half in range(halves)]
    q_heads = [jnp.where(lane, queries, zero) for lane in lanes]
    out_heads = [jnp.where(lane, outs, zero) for lane in lanes]
    q_stack = jnp.concatenate(q_heads, axis=0)
    out_stack = jnp.concatenate(out_heads, axis=0)
    dq = [0.0] * halves
    for low, high, mask in spans:
        key_part = keys[low:high, :]
        value_part = values[low:high, :]
        probs, grads = [], []
        for half in range(halves):
            scores = mask(times_transposed(key_part, q_heads[half]))
            prob = jnp.exp2(scores - stats[2 * half + offset : 2 * half + offset + 1, :])
            dprob = times_transposed(value_part, out_heads[half])
            dscore = (prob * (dprob - delta[half : half + 1, :])).astype(BF16)
            probs.append(prob.astype(BF16))
            grads.append(dscore)
            dq[half] = dq[half] + outer_sum(dscore, key_part)
        value_sum[low:high, :] += low_product(jnp.concatenate(probs, axis=1), out_stack)
        key_sum[low:high, :] += low_product(jnp.concatenate(grads, axis=1), q_stack)
    total = 0.0
    for half in range(halves):
        total = total + jnp.where(lanes[half], dq[half], 0.0)
    return total


def cross_back_kernel(
    head_dim, first, caption, image_count, scale,
    gate_ref, q_ref, tk_ref, tv_ref, row_ref, grad_ref, cross_ref, stats_ref,
    dq_ref, dtk_ref, dtv_ref, gate_grad_ref, dtk_sum, dtv_sum,
):
    count = q_ref.shape[0]
    for total in (dtk_sum, dtv_sum, gate_grad_ref):
        total[...] = jnp.zeros_like(total)
    gates = gate_lanes(gate_ref, head_dim)
    picks = head_picks(head_dim)

    def part(at, rows, spans):
        wide = grad_ref[pl.ds(at, rows), :].astype(F32)
        cross = cross_ref[pl.ds(at, rows), :]
        gate_grad_ref[0:1, :] += jnp.sum(wide * cross, axis=0, keepdims=True)
        gated = (wide * gates).astype(BF16)
        delta = exact_transposed(picks, gated.astype(F32) * cross)
        dq = rows_back(
            head_dim, q_ref[pl.ds(at, rows), :], gated, delta, stats_ref[:, pl.ds(at, rows)], 1,
            tk_ref, tv_ref, dtk_sum, dtv_sum, spans,
        )
        dq_ref[pl.ds(at, rows), :] = (dq * scale).astype(BF16)

    def clean(block, carry):
        part(pl.multiple_of(block * QBLOCK, QBLOCK), QBLOCK, [(0, caption, lambda scores: scores)])
        return carry

    lax.fori_loop(0, first // QBLOCK, clean, 0)
    image = row_ref[0:1, first:count]
    owner = lax.broadcasted_iota(jnp.int32, (tk_ref.shape[0], 1), 0) // caption
    allowed = (owner == image) | (image == image_count)
    part(first, count - first, [(0, tk_ref.shape[0], lambda scores: jnp.where(allowed, scores, MASKED))])
    dtk_ref[...] = (dtk_sum[...] * (1.0 / LOG2E)).astype(BF16)
    dtv_ref[...] = dtv_sum[...].astype(BF16)


def cross_back(pair, gates, packed, text_packed, row, grad, cross, stats, head_dim, image_count, scale):
    count, texts = packed.shape[0], text_packed.shape[0]
    pairs = packed.shape[1] // 384
    halves = 128 // head_dim
    tokens = pl.BlockSpec((count, 128), lambda i: (0, pair))
    own_tokens = pl.BlockSpec((count, 128), lambda i: (0, 0))
    captions = pl.BlockSpec((texts, 128), lambda i: (0, 0))
    flops = 10 * count * texts * 128
    return pl.pallas_call(
        functools.partial(cross_back_kernel, head_dim, FIRST_PATCHES, texts // image_count, image_count, scale),
        grid=(1,),
        in_specs=[
            pl.BlockSpec((None, 1, halves), lambda i: (pair, 0, 0), memory_space=pltpu.SMEM),
            tokens,
            pl.BlockSpec((texts, 128), lambda i: (0, pair)),
            pl.BlockSpec((texts, 128), lambda i: (0, pairs + pair)),
            pl.BlockSpec((1, count), lambda i: (0, 0)),
            tokens,
            own_tokens,
            pl.BlockSpec((8, count), lambda i: (0, 0)),
        ],
        out_specs=[own_tokens, captions, captions, pl.BlockSpec((8, 128), lambda i: (0, 0))],
        out_shape=[
            jax.ShapeDtypeStruct((count, 128), BF16),
            jax.ShapeDtypeStruct((texts, 128), BF16),
            jax.ShapeDtypeStruct((texts, 128), BF16),
            jax.ShapeDtypeStruct((8, 128), F32),
        ],
        scratch_shapes=[pltpu.VMEM((texts, 128), F32), pltpu.VMEM((texts, 128), F32)],
        compiler_params=pltpu.CompilerParams(vmem_limit_bytes=VMEM_LIMIT),
        cost_estimate=pl.CostEstimate(flops=flops, bytes_accessed=12 * count * 128, transcendentals=count * texts),
    )(gates.reshape(pairs, 1, halves), packed, text_packed, text_packed, row, grad, cross, stats)


def self_back_kernel(
    head_dim, first, most, scale,
    q_ref, k_ref, v_ref, column_ref, row_ref, grad_ref, self_ref, stats_ref, more_ref,
    dq_ref, dk_ref, dv_ref, dk_sum, dv_sum,
):
    count = q_ref.shape[0]
    dk_sum[...] = jnp.zeros_like(dk_sum)
    dv_sum[...] = jnp.zeros_like(dv_sum)
    picks = head_picks(head_dim)

    def part(at, rows, spans):
        grad = grad_ref[pl.ds(at, rows), :]
        delta = exact_transposed(picks, grad.astype(F32) * self_ref[pl.ds(at, rows), :])
        dq = rows_back(
            head_dim, q_ref[pl.ds(at, rows), :], grad, delta, stats_ref[:, pl.ds(at, rows)], 0,
            k_ref, v_ref, dk_sum, dv_sum, spans,
        )
        dq_ref[pl.ds(at, rows), :] = (dq * scale + more_ref[pl.ds(at, rows), :].astype(F32)).astype(BF16)

    def clean(block, carry):
        bias = jnp.where(column_ref[first:most, :] == 0, 0.0, MASKED)
        part(
            pl.multiple_of(block * QBLOCK, QBLOCK), QBLOCK,
            [(0, first, lambda scores: scores), (first, most, lambda scores: scores + bias)],
        )
        return carry

    lax.fori_loop(0, first // QBLOCK, clean, 0)
    image = row_ref[0:1, first:count]
    part(first, count - first, [(0, count, lambda scores: jnp.where(column_ref[...] == image, scores, MASKED))])
    dk_ref[...] = (dk_sum[...] * (1.0 / LOG2E)).astype(BF16)
    dv_ref[...] = dv_sum[...].astype(BF16)


def self_back(pair, packed, column, row, grad, own, stats, more, head_dim, scale):
    count = packed.shape[0]
    pairs = packed.shape[1] // 384
    tokens = pl.BlockSpec((count, 128), lambda i: (0, pair))
    out = pl.BlockSpec((count, 128), lambda i: (0, 0))
    most = min(round_up(FIRST_MOST, 128), count)
    flops = 10 * count * count * 128
    return pl.pallas_call(
        functools.partial(self_back_kernel, head_dim, FIRST_PATCHES, most, scale),
        grid=(1,),
        in_specs=[
            tokens,
            pl.BlockSpec((count, 128), lambda i: (0, pairs + pair)),
            pl.BlockSpec((count, 128), lambda i: (0, 2 * pairs + pair)),
            pl.BlockSpec((count, 1), lambda i: (0, 0)),
            pl.BlockSpec((1, count), lambda i: (0, 0)),
            tokens,
            out,
            pl.BlockSpec((8, count), lambda i: (0, 0)),
            out,
        ],
        out_specs=[out, out, out],
        out_shape=[jax.ShapeDtypeStruct((count, 128), BF16)] * 3,
        scratch_shapes=[pltpu.VMEM((count, 128), F32), pltpu.VMEM((count, 128), F32)],
        compiler_params=pltpu.CompilerParams(vmem_limit_bytes=VMEM_LIMIT),
        cost_estimate=pl.CostEstimate(flops=flops, bytes_accessed=30 * count * 128, transcendentals=2 * count * count),
    )(packed, packed, packed, column, row, grad, own, stats, more)


def swiglu_kernel(core_ref, gate_ref, up_ref, out_ref, moved_ref):
    gate = gate_ref[...]
    half = 0.5 * gate
    value = ((half + half * jnp.tanh(half)) * up_ref[...]).astype(BF16)
    out_ref[...] = value
    moved_ref[...] = value


def swiglu(gate_up, core, deep, narrow):
    rows, double = gate_up.shape
    width = double // 2
    blocks = 2 * deep * narrow
    block = width // blocks

    def moved_place(i, core_ref):
        z, c, f = i // (2 * narrow), (i // narrow) % 2, i % narrow
        return (0, ((c + core_ref[0]) % 2) * (deep * narrow) + f * deep + z)

    return pl.pallas_call(
        swiglu_kernel,
        grid_spec=pltpu.PrefetchScalarGridSpec(
            num_scalar_prefetch=1,
            grid=(blocks,),
            in_specs=[
                pl.BlockSpec((rows, block), lambda i, core_ref: (0, i)),
                pl.BlockSpec((rows, block), lambda i, core_ref: (0, blocks + i)),
            ],
            out_specs=[
                pl.BlockSpec((rows, block), lambda i, core_ref: (0, i)),
                pl.BlockSpec((rows, block), moved_place),
            ],
        ),
        out_shape=[jax.ShapeDtypeStruct((rows, width), BF16)] * 2,
        compiler_params=pltpu.CompilerParams(vmem_limit_bytes=VMEM_LIMIT),
        cost_estimate=pl.CostEstimate(flops=6 * rows * width, bytes_accessed=12 * rows * width, transcendentals=rows * width),
    )(core.reshape(1), gate_up, gate_up)


def fsdp_share_kernel(narrow, x_ref, out_ref, send_sem, recv_sem):
    me = lax.axis_index("fsdp")
    barrier = pltpu.get_barrier_semaphore()
    for step in range(1, narrow):
        pl.semaphore_signal(
            barrier, inc=1, device_id={"fsdp": lax.rem(me + step, narrow)}, device_id_type=pl.DeviceIdType.MESH
        )
    pl.semaphore_wait(barrier, narrow - 1)
    copies = []
    for step in range(1, narrow):
        copy = pltpu.make_async_remote_copy(
            src_ref=x_ref,
            dst_ref=out_ref.at[me],
            send_sem=send_sem.at[step],
            recv_sem=recv_sem.at[step],
            device_id={"fsdp": lax.rem(me + step, narrow)},
            device_id_type=pl.DeviceIdType.MESH,
        )
        copy.start()
        copies.append(copy)
    out_ref[me] = x_ref[...]
    for copy in copies:
        copy.wait()


def fsdp_share(value, narrow, collective_id):
    return pl.pallas_call(
        functools.partial(fsdp_share_kernel, narrow),
        in_specs=[pl.BlockSpec(memory_space=pltpu.VMEM)],
        out_specs=pl.BlockSpec(memory_space=pltpu.VMEM),
        out_shape=jax.ShapeDtypeStruct((narrow,) + value.shape, value.dtype),
        scratch_shapes=[pltpu.SemaphoreType.DMA((narrow,)), pltpu.SemaphoreType.DMA((narrow,))],
        compiler_params=pltpu.CompilerParams(collective_id=collective_id, has_side_effects=True),
        cost_estimate=pl.CostEstimate(flops=0, bytes_accessed=8 * narrow * value.size, transcendentals=0),
    )(value)


def place_rows(items, x_ref, chunk, base):
    rows = [(ref, row) for ref in items for row in range(ref.shape[0])]
    at = 0
    while at < len(rows):
        ref, row = rows[at]
        off = at % chunk
        take = min(ref.shape[0] - row, chunk - off)
        x_ref[at // chunk, base + off : base + off + take, :] = ref[row : row + take, :]
        at += take
    while at < x_ref.shape[0] * chunk:
        off = at % chunk
        x_ref[at // chunk, base + off : base + chunk, :] = jnp.zeros((chunk - off, 128), F32)
        at += chunk - off


def finish_kernel(narrow, wide, sum_rows, sum_count, plan, *refs):
    plans, outs = len(plan), len(plan) + 2
    scratch = refs[-7:]
    items, results = refs[: -7 - outs], refs[-7 - outs : -7]
    out_ref, kept_ref, x_ref, first_ref, second_ref, sends, recvs = scratch
    place_rows(items[:sum_count], x_ref, sum_rows, 0)
    place_rows(items[sum_count:], x_ref, x_ref.shape[1] - sum_rows, sum_rows)
    me = lax.axis_index("fsdp")
    group = lax.axis_index("z") * 2 + lax.axis_index("core")
    rows = x_ref.shape[1]
    rest = rows - sum_rows
    barrier = pltpu.get_barrier_semaphore()
    places = [{"fsdp": lax.rem(me + step, narrow)} for step in range(1, narrow)]
    peers = [lax.rem(group + step, wide) for step in range(1, wide)]
    partners = [{"z": peer // 2, "core": peer % 2} for peer in peers]
    for place in places + partners:
        pl.semaphore_signal(barrier, inc=1, device_id=place, device_id_type=pl.DeviceIdType.MESH)
    pl.semaphore_wait(barrier, narrow + wide - 2)

    def send_all(targets, source, target, base):
        copies = []
        for i, place in enumerate(targets):
            copy = pltpu.make_async_remote_copy(
                src_ref=source(i),
                dst_ref=target,
                send_sem=sends.at[base + i],
                recv_sem=recvs.at[base + i],
                device_id=place,
                device_id_type=pl.DeviceIdType.MESH,
            )
            copy.start()
            copies.append(copy)
        return copies

    copies = send_all(places, lambda i: x_ref.at[lax.rem(me + i + 1, narrow)], first_ref.at[me], 0)
    first_ref[me] = x_ref[me]
    for copy in copies:
        copy.wait()
    total = first_ref[0]
    for i in range(1, narrow):
        total = total + first_ref[i]
    second_ref[group] = total
    copies = send_all(partners, lambda i: second_ref.at[group], second_ref.at[group], narrow)
    for copy in copies:
        copy.wait()
    total = second_ref[0, :sum_rows, :]
    for i in range(1, wide):
        total = total + second_ref[i, :sum_rows, :]
    out_ref[me] = total
    for i in range(wide):
        kept_ref[me, i] = second_ref[i, sum_rows:, :]
    copies = send_all(places, lambda i: out_ref.at[me], out_ref.at[me], narrow + wide)
    copies += send_all(places, lambda i: kept_ref.at[me], kept_ref.at[me], 2 * narrow + wide)
    for copy in copies:
        copy.wait()
    for result, source_rows in zip(results[:plans], plan):
        lanes = result.shape[1] // 128
        for i, source in enumerate(source_rows):
            result[i // lanes : i // lanes + 1, i % lanes * 128 : (i % lanes + 1) * 128] = out_ref[
                source // sum_rows, source % sum_rows : source % sum_rows + 1, :
            ]
    slots_ref, cond_ref = results[plans:]
    images = slots_ref.shape[1]
    width = slots_ref.shape[2] // 128
    lanes = width // 4
    targets = [
        (slots_ref, image, part * lanes + lane)
        for part in range(4) for image in range(images) for lane in range(lanes)
    ] + [(cond_ref, image, lane) for image in range(images) for lane in range(cond_ref.shape[2] // 128)]

    def unpack(g, carry):
        for at, (target, image, lane) in enumerate(targets):
            row = kept_ref[at // rest, g, at % rest : at % rest + 1, :]
            target[g, image : image + 1, lane * 128 : (lane + 1) * 128] = row
        return carry

    lax.fori_loop(0, wide, unpack, 0)


def finish(summed, kept, plan, images, narrow, wide, collective_id):
    sum_total = sum(item.shape[0] for item in summed)
    kept_total = sum(item.shape[0] for item in kept)
    sum_rows = round_up(-(-sum_total // narrow), 8)
    kept_rows = round_up(-(-kept_total // narrow), 8)
    rows = sum_rows + kept_rows
    count = 3 * narrow + wide
    cond_width = kept[-1].shape[0] * 128 // images
    slot_width = (kept_total - kept[-1].shape[0]) * 128 // images
    vmem = pl.BlockSpec(memory_space=pltpu.VMEM)
    shapes = [shape for shape, _ in plan] + [(wide, images, slot_width), (wide, images, cond_width)]
    return pl.pallas_call(
        functools.partial(finish_kernel, narrow, wide, sum_rows, len(summed), [source for _, source in plan]),
        in_specs=[vmem] * (len(summed) + len(kept)),
        out_specs=[vmem] * len(shapes),
        out_shape=[jax.ShapeDtypeStruct(shape, F32) for shape in shapes],
        scratch_shapes=[
            pltpu.VMEM((narrow, sum_rows, 128), F32),
            pltpu.VMEM((narrow, wide, kept_rows, 128), F32),
            pltpu.VMEM((narrow, rows, 128), F32),
            pltpu.VMEM((narrow, rows, 128), F32),
            pltpu.VMEM((wide, rows, 128), F32),
            pltpu.SemaphoreType.DMA((count,)),
            pltpu.SemaphoreType.DMA((count,)),
        ],
        compiler_params=pltpu.CompilerParams(collective_id=collective_id, has_side_effects=True),
    )(*summed, *kept)


def exchange(blocks, axis):
    return lax.all_to_all(blocks, axis, 0, 0, tiled=True)


def core_swap(value):
    return lax.ppermute(value, "core", [(0, 1), (1, 0)])


def by_core(low, high):
    first = lax.axis_index("core") == 0
    return jnp.where(first, low, high), jnp.where(first, high, low)


def in_core_order(own, other):
    first = lax.axis_index("core") == 0
    return jnp.where(first, own, other), jnp.where(first, other, own)


def chip_sum(own_left, other_left, right):
    came = core_swap(outer_sum(other_left, right).astype(BF16))
    return (outer_sum(own_left, right) + came.astype(F32)).astype(BF16)


def fsdp_sum(both):
    return lax.psum_scatter(both, "fsdp", scatter_dimension=0, tiled=True)


def z_pieces(blocks, deep):
    me = lax.axis_index("z")
    return [lax.dynamic_index_in_dim(blocks, me, 0, keepdims=False)] + [
        lax.ppermute(
            lax.dynamic_index_in_dim(blocks, me ^ step, 0, keepdims=False), "z", [(i, i ^ step) for i in range(deep)]
        )
        for step in range(1, deep)
    ]


def added(pieces):
    return functools.reduce(jnp.add, [piece.astype(F32) for piece in pieces])


def to_all(block, narrow):
    return [
        lax.ppermute(block, "fsdp", [(i, i ^ step) for i in range(narrow)]) for step in range(1, narrow)
    ]


def relative(blocks, me, axis):
    return jnp.concatenate(
        [lax.dynamic_slice_in_dim(blocks, me ^ step, 1, axis) for step in range(blocks.shape[axis])], axis=axis
    )


def device_columns(value, deep, narrow):
    rows, width = value.shape
    block = width // (2 * deep * narrow)
    core = lax.axis_index("core")
    target = jnp.arange(width, dtype=jnp.int32)
    c, f, z, r = (
        target // (narrow * deep * block), target // (deep * block) % narrow, target // block % deep, target % block,
    )
    c = (c + core) % 2
    source = ((z * 2 + c) * narrow + f) * block + r
    pick = (jnp.arange(width, dtype=jnp.int32)[:, None] == source[None, :]).astype(BF16)
    moved = low_product(value, pick).astype(BF16)
    return moved[:, : width // 2], moved[:, width // 2 :]


def whole_weight(shard):
    rows = shard.shape[0] // 2
    half = lax.dynamic_slice_in_dim(shard, lax.axis_index("core") * rows, rows, 0)
    return lax.all_gather(half, ("fsdp", "core"), axis=0, tiled=True)


def shards(
    tokens,
    cotangent,
    text_states,
    conditioning,
    image_sizes,
    ada_weight,
    ada_bias,
    qkv_weight,
    out_weight,
    text_weight,
    gate_up_weight,
    down_weight,
    norm_gains,
    norm_shifts,
    text_gain,
    head_gate,
):
    model_width = tokens.shape[2]
    head_count = head_gate.shape[0]
    head_dim = model_width // head_count
    image_count = text_states.shape[1]
    caption_local = text_states.shape[2]
    caption_width = text_states.shape[3]
    local_tok = tokens.shape[1]
    deep = lax.axis_size("z")
    narrow = lax.axis_size("fsdp")
    wide = 2 * deep
    me = lax.axis_index("fsdp")
    group_tok = local_tok * narrow
    caption_full = caption_local * narrow
    score_scale = head_dim ** (-0.5)
    text_total = image_count * caption_full
    text_local = image_count * caption_local
    part = model_width // narrow
    part_pad = round_up(part, 128)
    heads_here = head_count // narrow
    pairs = part_pad // 128
    halves = 128 // head_dim

    group_sizes = image_sizes[0]
    position = me * local_tok + jnp.arange(local_tok, dtype=jnp.int32)
    image_index = token_layout(group_sizes, position, image_count)[0]
    key_image, key_row, key_col = token_layout(
        group_sizes, jnp.arange(group_tok, dtype=jnp.int32), image_count
    )
    member = [(image_index == i).astype(F32)[:, None] for i in range(image_count)]
    cosine, sine = rope_tables(key_row, key_col, head_dim)

    cond_low = jax.nn.silu(conditioning[0].astype(F32)).astype(BF16)
    cond_rows = ada_weight.shape[0]
    cond_part = lax.dynamic_slice_in_dim(cond_low, me * cond_rows, cond_rows, 1)
    modulation_part = low_product(cond_part, ada_weight)
    modulation = (
        jnp.sum(fsdp_share(modulation_part.reshape(-1, 128), narrow, 0), axis=0).reshape(modulation_part.shape)
        + ada_bias
    )

    def per_token(index):
        rows = modulation[:, index * model_width : (index + 1) * model_width]
        return functools.reduce(
            jnp.add, [member[i] * rows[i : i + 1, :] for i in range(image_count)]
        )

    def per_image(value):
        return [jnp.sum(member[i] * value, axis=0).reshape(-1, 128) for i in range(image_count)]

    token_in = tokens[0].astype(F32)
    token_inverse = inverse_rms(token_in)
    tokens_all = lax.all_gather(tokens[0], "fsdp", axis=0, tiled=True)
    def widened(value, slots):
        if part == part_pad:
            return value
        lead = value.shape[:-1]
        value = value.reshape(*lead, slots, part)
        pads = [(0, 0)] * (len(lead) + 1) + [(0, part_pad - part)]
        return jnp.pad(value, pads).reshape(*lead, slots * part_pad)

    def narrowed(value, slots):
        if part == part_pad:
            return value
        lead = value.shape[:-1]
        return value.reshape(*lead, slots, part_pad)[..., :part].reshape(*lead, slots * part)

    def own_columns(value):
        return widened(lax.dynamic_slice_in_dim(value, me * part, part, value.ndim - 1), 1)

    qkv_rows = qkv_weight.shape[0] // 2
    qkv_half = lax.dynamic_slice_in_dim(qkv_weight, lax.axis_index("core") * qkv_rows, qkv_rows, 0)
    qkv_half = exchange(
        qkv_half.reshape(qkv_rows, 3, narrow, part).transpose(2, 0, 1, 3).reshape(narrow, qkv_rows, 3 * part), "fsdp"
    )
    own_qkv = widened(
        jnp.concatenate(in_core_order(qkv_half, core_swap(qkv_half)), axis=1).reshape(model_width, 3 * part), 3
    )

    full_out = whole_weight(out_weight)
    full_gate_up = whole_weight(gate_up_weight)
    full_down = whole_weight(down_weight)

    text_in = text_states[0].astype(F32).reshape(text_local, caption_width)
    text_inverse = inverse_rms(text_in)
    text_low = (text_in * text_inverse * text_gain).astype(BF16)
    text_cols = caption_width // narrow
    text_slice = (
        exchange(text_low.reshape(text_local, narrow, text_cols).transpose(1, 0, 2), "fsdp")
        .reshape(narrow, image_count, caption_local, text_cols)
        .transpose(1, 0, 2, 3)
        .reshape(text_total, text_cols)
    )
    own_text_weight = (
        text_weight.reshape(text_cols, 2, narrow, part).transpose(2, 0, 1, 3).reshape(narrow, text_cols, 2 * part)
    )
    relative_text_weight = (
        relative(own_text_weight, me, 0).transpose(1, 0, 2).reshape(text_cols, 2 * model_width)
    )
    text_partial = jnp.stack([low_product(text_slice, own_text_weight[i]).astype(BF16) for i in range(narrow)])
    text_partial, tokens_all, relative_text_weight = lax.optimization_barrier(
        (text_partial, tokens_all, relative_text_weight)
    )
    text_projected = widened(jnp.sum(exchange(text_partial, "fsdp").astype(F32), axis=0), 2)
    text_parts = fsdp_share(column_stats(text_projected, part, part_pad, 1), narrow, 1)
    text_means = text_parts[:, 0, :]
    text_mean = jnp.mean(text_means, axis=0)
    text_square = jnp.sum(text_parts[:, 1, :], axis=0) + part * jnp.sum((text_means - text_mean) ** 2, axis=0)
    text_key_inverse = lax.rsqrt(text_square / model_width + EPS)[:, None]
    text_unit = (text_projected[:, :part_pad] - text_mean[:, None]) * text_key_inverse
    text_gains = own_columns(norm_gains[4])
    text_packed = jnp.concatenate(
        [(text_unit * text_gains).astype(BF16), text_projected[:, part_pad:].astype(BF16)], axis=1
    )

    wide_tokens = tokens_all.astype(F32)
    wide_scale = functools.reduce(
        jnp.add,
        [(key_image == i).astype(F32)[:, None] * modulation[i : i + 1, :model_width] for i in range(image_count)],
    )
    normed_all = (wide_tokens * inverse_rms(wide_tokens) * norm_gains[0] * (1.0 + wide_scale)).astype(BF16)

    projected = low_product(normed_all, own_qkv)
    stats_all = fsdp_share(column_stats(projected, part, part_pad, 2), narrow, 2)
    head_gains = own_columns(norm_gains[2:4])
    packed = make_heads(
        projected, stats_all, cosine, sine, head_gains, own_columns(norm_shifts), part, score_scale * LOG2E
    )
    gate_tanh = jnp.tanh(head_gate)
    own_gates = lax.dynamic_slice_in_dim(gate_tanh, me * heads_here, heads_here, 0)
    own_gates = jnp.concatenate([own_gates, jnp.ones((pairs * halves - heads_here,), F32)])
    column = key_image[:, None]
    row = key_image[None, :]
    attended = [
        attend(pair, own_gates, packed, text_packed, column, row, head_dim, image_count) for pair in range(pairs)
    ]
    mixed_pairs = [exchange(one[0].reshape(narrow, local_tok, 128), "fsdp") for one in attended]
    self_outs = [one[1] for one in attended]
    cross_outs = [one[2] for one in attended]
    stats = [one[3] for one in attended]
    mixed_low = (
        narrowed(jnp.concatenate(mixed_pairs, axis=2), 1).transpose(1, 0, 2).reshape(local_tok, model_width)
    )

    branch = low_product(mixed_low, full_out)
    branch_inverse = inverse_rms(branch)
    branch_unit = branch * branch_inverse
    gate_attend = jnp.tanh(per_token(1))
    hidden = token_in + gate_attend * (branch_unit * norm_gains[1])
    hidden_inverse = inverse_rms(hidden)
    hidden_unit = hidden * hidden_inverse
    scale_feed = 1.0 + per_token(2)
    normed_feed_low = (hidden_unit * norm_gains[5] * scale_feed).astype(BF16)
    gate_up = low_product(normed_feed_low, full_gate_up)
    hidden_units = gate_up.shape[1] // 2
    gate_half = gate_up[:, :hidden_units]
    up_half = gate_up[:, hidden_units:]
    sigmoid = jax.nn.sigmoid(gate_half)
    if hidden_units // (wide * narrow) % 128 == 0:
        activated_low, moved = swiglu(gate_up, lax.axis_index("core"), deep, narrow)
        down_columns = (moved[:, : hidden_units // 2], moved[:, hidden_units // 2 :])
    else:
        activated_low = (gate_half * sigmoid * up_half).astype(BF16)
        down_columns = device_columns(activated_low, deep, narrow)
    down_out = low_product(activated_low, full_down)
    down_inverse = inverse_rms(down_out)
    down_unit = down_out * down_inverse
    gate_feed = jnp.tanh(per_token(3))
    down_normed = down_unit * norm_gains[6]
    result = (hidden + gate_feed * down_normed).astype(BF16)

    grad_result = cotangent[0].astype(F32)
    grad_down_y = grad_result * gate_feed
    grad_gain_six = jnp.sum(grad_down_y * down_unit, axis=0)
    grad_gate_feed = per_image(grad_result * down_normed * (1.0 - gate_feed * gate_feed))
    grad_down_low = norm_pull(grad_down_y * norm_gains[6], down_unit, down_inverse).astype(BF16)
    grad_activated = times_transposed(grad_down_low, full_down)
    grad_gate_low = (grad_activated * up_half * sigmoid * (1.0 + gate_half * (1.0 - sigmoid))).astype(BF16)
    grad_up_low = (grad_activated * gate_half * sigmoid).astype(BF16)
    grad_gate_up_low = jnp.concatenate([grad_gate_low, grad_up_low], axis=1)
    grad_normed_feed = times_transposed(grad_gate_up_low, full_gate_up)
    grad_feed_y = grad_normed_feed * scale_feed
    grad_gain_five = jnp.sum(grad_feed_y * hidden_unit, axis=0)
    grad_scale_feed = per_image(grad_normed_feed * hidden_unit * norm_gains[5])
    grad_hidden = grad_result + norm_pull(grad_feed_y * norm_gains[5], hidden_unit, hidden_inverse)
    grad_branch_y = grad_hidden * gate_attend
    grad_gain_one = jnp.sum(grad_branch_y * branch_unit, axis=0)
    grad_gate_attend = per_image(
        grad_hidden * branch_unit * norm_gains[1] * (1.0 - gate_attend * gate_attend)
    )
    grad_branch_low = norm_pull(grad_branch_y * norm_gains[1], branch_unit, branch_inverse).astype(BF16)
    grad_mixed = times_transposed(grad_branch_low, full_out).astype(BF16)
    grad_blocks = widened(grad_mixed.reshape(local_tok, narrow, part).transpose(1, 0, 2), 1)
    grad_heads = exchange(grad_blocks, "fsdp").reshape(group_tok, part_pad)
    def by_z(value):
        return value.reshape(deep, -1, value.shape[1])

    down_both = chip_sum(*down_columns, grad_down_low)
    feed_columns = device_columns(normed_feed_low, deep, narrow)
    gate_both = chip_sum(*feed_columns, grad_gate_low)
    up_both = chip_sum(*feed_columns, grad_up_low)
    out_both = chip_sum(*device_columns(mixed_low, deep, narrow), grad_branch_low)
    down_part = fsdp_sum(down_both)
    grad_heads, gate_both, up_both, out_both, down_part = lax.optimization_barrier(
        (grad_heads, gate_both, up_both, out_both, down_part)
    )
    gate_part = fsdp_sum(gate_both)
    out_part = fsdp_sum(out_both)
    up_part = fsdp_sum(up_both)
    came_downs = exchange(by_z(down_part), "z")
    crossed = [
        cross_back(
            pair, own_gates, packed, text_packed, row, grad_heads, cross_outs[pair], stats[pair],
            head_dim, image_count, score_scale,
        )
        for pair in range(pairs)
    ]
    dtk = jnp.concatenate([one[1] for one in crossed], axis=1)
    dtv = jnp.concatenate([one[2] for one in crossed], axis=1)
    gate_sums = jnp.stack([one[3] for one in crossed])

    grad_text_keys = dtk.astype(F32)
    own_gain_four = jnp.sum(grad_text_keys * text_unit, axis=0)
    grad_text_unit = grad_text_keys * text_gains
    text_sums = jnp.stack([jnp.sum(grad_text_unit, axis=1), jnp.sum(grad_text_unit * text_unit, axis=1)])
    text_sums = jnp.sum(
        fsdp_share(jnp.pad(text_sums, ((0, 6), (0, 0))), narrow, 3), axis=0
    ) * (1.0 / model_width)
    grad_text_key_in = (grad_text_unit - text_sums[0][:, None] - text_unit * text_sums[1][:, None]) * text_key_inverse
    grad_text_own = jnp.concatenate(
        [narrowed(grad_text_key_in.astype(BF16), 1), narrowed(dtv, 1)], axis=1
    )
    def self_pair(pair):
        return self_back(
            pair, packed, column, row, grad_heads, self_outs[pair], stats[pair], crossed[pair][0], head_dim, score_scale
        )

    came_texts = to_all(grad_text_own, narrow)
    backs = [self_pair(0)]
    first, came_downs, *came_texts = lax.optimization_barrier((backs[0][0], came_downs, *came_texts))
    grad_down_weight = jnp.sum(came_downs.astype(F32), axis=0)
    backs[0] = (first, *backs[0][1:])
    grad_text_columns = jnp.concatenate([grad_text_own, *came_texts], axis=1)
    text_half = text_cols // 2
    own_text, other_text = by_core(text_slice[:, :text_half], text_slice[:, text_half:])
    came_text = core_swap(outer_sum(other_text, grad_text_columns).astype(BF16))
    text_both = (outer_sum(own_text, grad_text_columns) + came_text.astype(F32)).astype(BF16)
    grad_heads, text_both, first = lax.optimization_barrier((grad_heads, text_both, backs[0][0]))
    backs[0] = (first, *backs[0][1:])
    came_text_z = exchange(by_z(text_both), "z")
    backs.append(self_pair(1))
    if pairs > 2:
        grad_heads, gate_part, up_part, second = lax.optimization_barrier(
            (grad_heads, gate_part, up_part, backs[1][0])
        )
        backs[1] = (second, *backs[1][1:])
        backs += [self_pair(pair) for pair in range(2, pairs)]
    gate_pieces = z_pieces(by_z(gate_part), deep)
    last, came_text_z, up_part, out_part, *gate_pieces = lax.optimization_barrier(
        (backs[-1][0], came_text_z, up_part, out_part, *gate_pieces)
    )
    up_width = up_part.shape[1]
    up_pieces = z_pieces(by_z(jnp.concatenate([up_part, out_part], axis=1)), deep)
    backs[-1] = (last, *backs[-1][1:])
    text_part = jnp.sum(came_text_z.astype(F32), axis=0).astype(BF16)
    everyone = ("z", "core", "fsdp")
    grad_text_weight = lax.ppermute(
        text_part,
        everyone,
        [
            ((z * 2 + c) * narrow + f, f * wide + c * deep + z)
            for z in range(deep) for c in range(2) for f in range(narrow)
        ],
    )
    last, grad_text_columns = lax.optimization_barrier((backs[-1][0], grad_text_columns))
    backs[-1] = (last, *backs[-1][1:])
    grad_text_slice = times_transposed(grad_text_columns, relative_text_weight).astype(BF16)
    came_text = exchange(
        grad_text_slice.reshape(image_count, narrow, caption_local, text_cols)
        .transpose(1, 0, 2, 3)
        .reshape(narrow, text_local, text_cols),
        "fsdp",
    )
    own_gate_grad = jnp.sum(gate_sums[:, 0, :].reshape(pairs * halves, head_dim), axis=1)[:heads_here]
    grad_head_gate = lax.dynamic_update_slice_in_dim(
        jnp.zeros((head_count,), F32), own_gate_grad, me * heads_here, 0
    ) * (1.0 - gate_tanh * gate_tanh)
    grad_projected_low, head_sums = heads_back(
        list(zip(*backs)), projected, stats_all, cosine, sine, head_gains, part,
        lambda value: fsdp_share(value, narrow, 4),
    )
    grad_projected_low, came_text, *up_pieces = lax.optimization_barrier(
        (grad_projected_low, came_text, *up_pieces)
    )
    grad_gate_up_weight = jnp.concatenate(
        [added(gate_pieces), added([piece[:, :up_width] for piece in up_pieces])], axis=1
    )
    grad_out_weight = added([piece[:, up_width:] for piece in up_pieces])
    partial_normed, grad_text_weight = lax.optimization_barrier(
        (times_transposed(grad_projected_low, own_qkv).astype(BF16), grad_text_weight)
    )
    grad_normed = lax.psum_scatter(partial_normed, "fsdp", scatter_dimension=0, tiled=True)

    def lane_rows(value):
        return value.reshape(-1, 128)

    group = lax.axis_index("z") * 2 + lax.axis_index("core")
    columns_here = jnp.stack(
        [narrowed(value, 1) for value in (head_sums[0], head_sums[2], own_gain_four, head_sums[1], head_sums[3])]
    )
    here = (jnp.arange(narrow, dtype=jnp.int32) == me)[None, :, None]
    placed = lane_rows(jnp.where(here, columns_here[:, None, :], 0.0))
    cond_rows_here = lane_rows(jnp.where(me == 0, cond_low.astype(F32), 0.0))
    gate_row = jnp.pad(grad_head_gate, (0, 128 - head_count)).reshape(1, 128)
    ready = [lane_rows(grad_gain_one), lane_rows(grad_gain_five), lane_rows(grad_gain_six), placed, gate_row]
    later = [*grad_gate_attend, *grad_scale_feed, *grad_gate_feed, cond_rows_here]
    ready = lax.optimization_barrier(tuple(ready))
    qkv_grad = outer_sum(normed_all, grad_projected_low).astype(BF16).reshape(deep, 2, model_width // wide, 3 * part_pad)
    place = (lax.axis_index("z") * 2 + lax.axis_index("core")) * narrow + me
    grad_text_weight = (
        relative(grad_text_weight.reshape(-1, narrow, 2 * part), place // wide, 1)
        .reshape(-1, narrow, 2, part)
        .transpose(0, 2, 1, 3)
        .reshape(-1, 2 * model_width)
        .astype(F32)
    )
    own_grad, other_grad = by_core(qkv_grad[:, 0], qkv_grad[:, 1])
    own_grad = (own_grad.astype(F32) + core_swap(other_grad).astype(F32)).astype(BF16)
    own_pieces = z_pieces(own_grad, deep)
    came_text, *own_pieces = lax.optimization_barrier((came_text, *own_pieces))
    grad_text_normed = (
        came_text
        .transpose(1, 0, 2)
        .reshape(text_local, caption_width)
        .astype(F32)
    )
    text_state_unit = text_in * text_inverse
    grad_text_gain = jnp.sum(grad_text_normed * text_state_unit, axis=0)
    grad_text = (
        norm_pull(grad_text_normed * text_gain, text_state_unit, text_inverse)
        .astype(BF16)
        .reshape(image_count, caption_local, caption_width)
    )

    own_grad = added(own_pieces)
    grad_qkv_weight = (
        exchange(narrowed(own_grad.astype(BF16), 3).reshape(narrow, -1, 3 * part), "fsdp")
        .reshape(narrow, -1, 3, part)
        .transpose(1, 2, 0, 3)
        .reshape(-1, 3 * model_width)
        .astype(F32)
    )
    grad_normed, grad_qkv_weight, grad_text, grad_text_gain = lax.optimization_barrier(
        (grad_normed, grad_qkv_weight, grad_text, grad_text_gain)
    )
    grad_normed = grad_normed.astype(F32)

    token_unit = token_in * token_inverse
    scale_attend = 1.0 + per_token(0)
    grad_normed_y = grad_normed * scale_attend
    grad_gain_zero = jnp.sum(grad_normed_y * token_unit, axis=0)
    grad_scale_attend = per_image(grad_normed * token_unit * norm_gains[0])
    grad_tokens = (
        grad_hidden + norm_pull(grad_normed_y * norm_gains[0], token_unit, token_inverse)
    ).astype(BF16)
    lanes_of_row = model_width // 128
    def row_range(first, count):
        return list(range(first * lanes_of_row, (first + count) * lanes_of_row))

    gate_at = 9 * lanes_of_row
    text_rows = caption_width // 128
    grad_gains, grad_shifts, gate_row, grad_text_gain, slots, cond_slots = finish(
        [lane_rows(grad_gain_zero), *ready, lane_rows(grad_text_gain)],
        [*grad_scale_attend, *later],
        [
            (norm_gains.shape, row_range(0, 2) + row_range(4, 3) + row_range(2, 2)),
            (norm_shifts.shape, row_range(7, 2)),
            ((1, 128), [gate_at]),
            ((text_rows, 128), list(range(gate_at + 1, gate_at + 1 + text_rows))),
        ],
        image_count, narrow, wide, 5,
    )
    slots = slots.reshape(wide * image_count, -1)
    cond_slots = cond_slots.reshape(wide * image_count, -1)
    grad_head_gate = gate_row[0, :head_count]
    grad_text_gain = grad_text_gain.reshape(-1)
    ada_rows = cond_rows // wide
    own_cond = lax.dynamic_slice_in_dim(cond_slots, (group * narrow + me) * ada_rows, ada_rows, 1)
    grad_ada_weight = exact_outer(own_cond, slots)
    grad_ada_bias = jnp.sum(slots, axis=0)
    return (
        result[None],
        grad_tokens[None],
        grad_text[None],
        grad_ada_weight,
        grad_qkv_weight,
        grad_out_weight,
        grad_text_weight,
        grad_gate_up_weight,
        grad_down_weight,
        grad_ada_bias,
        grad_gains,
        grad_shifts,
        grad_text_gain,
        grad_head_gate,
    )


def solution(mesh):
    wide, narrow = mesh.devices.shape
    fine = Mesh(mesh.devices.reshape(wide // 2, 2, narrow), ("z", "core", "fsdp"))
    groups = ("z", "core")
    every = ("z", "core", "fsdp")
    placed = (
        P(groups, "fsdp", None),
        P(groups, "fsdp", None),
        P(groups, None, "fsdp", None),
        P(groups, None, None),
        P(groups, None, None),
        P("fsdp", None),
        P(),
        P("fsdp", None),
        P("fsdp", None),
        P("fsdp", None),
        P("fsdp", None),
        P("fsdp", None),
        P(),
        P(),
        P(),
        P(),
    )
    return jax.shard_map(
        shards,
        mesh=fine,
        in_specs=placed,
        out_specs=(
            P(groups, "fsdp", None),
            P(groups, "fsdp", None),
            P(groups, None, "fsdp", None),
            P(every, None),
            P(every, None),
            P(every, None),
            P(every, None),
            P(every, None),
            P(every, None),
            P(),
            P(),
            P(),
            P(),
            P(),
        ),
        check_vma=False,
    )
```

```python
import functools

import jax
import jax.numpy as jnp
from jax import lax
from jax.experimental import pallas as pl
from jax.experimental.pallas import tpu as pltpu
from jax.sharding import Mesh
from jax.sharding import PartitionSpec as P

EPS = 1e-05
HIGHEST_PRECISION = lax.Precision.HIGHEST
MASKED = -1e30
LOG2E = 1.4426950408889634
FIRST_PATCHES = 16 * 12**2
FIRST_MOST = FIRST_PATCHES + 96
QBLOCK = 256
BF16 = jnp.bfloat16
F32 = jnp.float32
VMEM_LIMIT = 60 * 1024 * 1024


def round_up(value, step):
    return -(-value // step) * step


def low_product(left, right):
    return jnp.dot(left, right, preferred_element_type=F32)


def times_transposed(left, right):
    return lax.dot_general(left, right, (((1,), (1,)), ((), ())), preferred_element_type=F32)


def outer_sum(left, right):
    return lax.dot_general(left, right, (((0,), (0,)), ((), ())), preferred_element_type=F32)


def exact_outer(left, right):
    return lax.dot_general(
        left, right, (((0,), (0,)), ((), ())), precision=HIGHEST_PRECISION, preferred_element_type=F32
    )


def exact_transposed(left, right):
    return lax.dot_general(
        left, right, (((1,), (1,)), ((), ())), precision=HIGHEST_PRECISION, preferred_element_type=F32
    )


def row_mean(value):
    return jnp.mean(value, axis=-1, keepdims=True)


def inverse_rms(value):
    return lax.rsqrt(row_mean(value * value) + EPS)


def norm_pull(grad, unit, inverse):
    return (grad - unit * row_mean(grad * unit)) * inverse


def token_layout(image_sizes, position, image_count):
    start = jnp.int32(0)
    image_index = jnp.full(position.shape, image_count, jnp.int32)
    token_row = jnp.zeros(position.shape, jnp.int32)
    token_col = jnp.zeros(position.shape, jnp.int32)
    for i in range(image_count):
        width = image_sizes[i, 1] + 1
        end = start + image_sizes[i, 0] * width
        inside = (position >= start) & (position < end)
        offset = position - start
        image_index = jnp.where(inside, i, image_index)
        token_row = jnp.where(inside, offset // width, token_row)
        token_col = jnp.where(inside, offset % width, token_col)
        start = end
    return image_index, token_row, token_col


def rope_tables(token_row, token_col, head_dim):
    quarter = head_dim // 4
    pair = (jnp.arange(128, dtype=jnp.int32) % head_dim) // 2
    frequency = 10000.0 ** (-(pair % quarter).astype(F32) / quarter)
    place = jnp.where(
        (pair < quarter)[None, :], token_row.astype(F32)[:, None], token_col.astype(F32)[:, None]
    )
    angles = place * frequency[None, :]
    even = (jnp.arange(128, dtype=jnp.int32) % 2 == 0)[None, :]
    return jnp.cos(angles), jnp.where(even, -jnp.sin(angles), jnp.sin(angles))


def swap_pairs(value):
    width = value.shape[1]
    even = lax.broadcasted_iota(jnp.int32, value.shape, 1) % 2 == 0
    return jnp.where(even, pltpu.roll(value, width - 1, 1), pltpu.roll(value, 1, 1))


def wide_table(table, width):
    return jnp.concatenate([table] * (width // table.shape[1]), axis=1)


def pack_columns(columns):
    rows = columns[0].shape[0]
    lane = lax.broadcasted_iota(jnp.int32, (rows, 128), 1)
    packed = jnp.zeros((rows, 128), F32)
    for i, column in enumerate(columns):
        packed = jnp.where(lane == i, column, packed)
    return jnp.transpose(packed)[:8, :]


def as_columns(rows_list):
    width = rows_list[0].shape[1]
    stacked = jnp.concatenate(
        rows_list + [jnp.zeros((128 - len(rows_list), width), F32)], axis=0
    )
    return jnp.transpose(stacked)


def real_lanes(shape, part):
    return lax.broadcasted_iota(jnp.int32, shape, 1) < part


def own_stats(value, part):
    mean = jnp.sum(value, axis=1, keepdims=True) * (1.0 / part)
    centred = value - mean
    if value.shape[1] != part:
        centred = jnp.where(real_lanes(value.shape, part), centred, 0.0)
    return mean, jnp.sum(centred * centred, axis=1, keepdims=True)


def joined_stats(stats_ref, part, slot):
    narrow = stats_ref.shape[0]
    means = [stats_ref[i, 2 * slot : 2 * slot + 1, :] for i in range(narrow)]
    squares = [stats_ref[i, 2 * slot + 1 : 2 * slot + 2, :] for i in range(narrow)]
    mean = functools.reduce(jnp.add, means) * (1.0 / narrow)
    square = functools.reduce(jnp.add, squares)
    square = square + part * functools.reduce(jnp.add, [(m - mean) * (m - mean) for m in means])
    return mean, lax.rsqrt(square * (1.0 / (narrow * part)) + EPS)


def stats_kernel(part, slots, projected_ref, out_ref):
    padded = projected_ref.shape[1] // slots
    columns = []
    for slot in range(slots):
        columns += own_stats(projected_ref[:, slot * padded : (slot + 1) * padded], part)
    out_ref[...] = pack_columns(columns)


def column_stats(projected, part, padded, slots):
    rows = projected.shape[0]
    return pl.pallas_call(
        functools.partial(stats_kernel, part, slots),
        grid=(pl.cdiv(rows, QBLOCK),),
        in_specs=[pl.BlockSpec((QBLOCK, slots * padded), lambda i: (i, 0))],
        out_specs=pl.BlockSpec((8, QBLOCK), lambda i: (0, i)),
        out_shape=jax.ShapeDtypeStruct((8, rows), F32),
        compiler_params=pltpu.CompilerParams(vmem_limit_bytes=VMEM_LIMIT),
        cost_estimate=pl.CostEstimate(flops=10 * rows * slots * padded, bytes_accessed=4 * rows * slots * padded, transcendentals=0),
    )(projected)


def heads_kernel(part, query_scale, projected_ref, stats_ref, cos_ref, sin_ref, gains_ref, shifts_ref, out_ref):
    padded = projected_ref.shape[1] // 3
    cosine = wide_table(cos_ref[...], padded)
    sine = wide_table(sin_ref[...], padded)
    columns = as_columns([*joined_stats(stats_ref, part, 0), *joined_stats(stats_ref, part, 1)])
    for slot in range(3):
        place = slice(slot * padded, (slot + 1) * padded)
        value = projected_ref[:, place]
        if slot < 2:
            value = (value - columns[:, 2 * slot : 2 * slot + 1]) * columns[:, 2 * slot + 1 : 2 * slot + 2]
            value = value * gains_ref[slot : slot + 1, :] + shifts_ref[slot : slot + 1, :]
            value = value * cosine + swap_pairs(value) * sine
            if slot == 0:
                value = value * query_scale
        out_ref[:, place] = value.astype(BF16)


def make_heads(projected, stats, cosine, sine, gains, shifts, part, query_scale):
    rows, triple = projected.shape
    padded = triple // 3
    narrow = stats.shape[0]
    return pl.pallas_call(
        functools.partial(heads_kernel, part, query_scale),
        grid=(pl.cdiv(rows, QBLOCK),),
        in_specs=[
            pl.BlockSpec((QBLOCK, triple), lambda i: (i, 0)),
            pl.BlockSpec((narrow, 8, QBLOCK), lambda i: (0, 0, i)),
            pl.BlockSpec((QBLOCK, 128), lambda i: (i, 0)),
            pl.BlockSpec((QBLOCK, 128), lambda i: (i, 0)),
            pl.BlockSpec((2, padded), lambda i: (0, 0)),
            pl.BlockSpec((2, padded), lambda i: (0, 0)),
        ],
        out_specs=pl.BlockSpec((QBLOCK, triple), lambda i: (i, 0)),
        out_shape=jax.ShapeDtypeStruct((rows, triple), BF16),
        compiler_params=pltpu.CompilerParams(vmem_limit_bytes=VMEM_LIMIT),
        cost_estimate=pl.CostEstimate(flops=40 * rows * triple, bytes_accessed=6 * rows * triple, transcendentals=0),
    )(projected, stats, cosine, sine, gains, shifts)


def turned_back(refs, cosine, sine):
    grad = jnp.concatenate([ref[...].astype(F32) for ref in refs], axis=1)
    return grad * cosine - swap_pairs(grad) * sine


def grad_stats_kernel(rows, part, pairs, *refs):
    dq_refs, dk_refs = refs[:pairs], refs[pairs : 2 * pairs]
    projected_ref, stats_ref, cos_ref, sin_ref, gains_ref, out_ref, sums_ref = refs[2 * pairs :]
    step = pl.program_id(0)
    padded = 128 * pairs
    cosine = wide_table(cos_ref[...], padded)
    sine = wide_table(sin_ref[...], padded)
    height = cos_ref.shape[0]
    inside = step * height + lax.broadcasted_iota(jnp.int32, (height, 1), 0) < rows

    @pl.when(step == 0)
    def _():
        sums_ref[...] = jnp.zeros_like(sums_ref)

    columns = as_columns([*joined_stats(stats_ref, part, 0), *joined_stats(stats_ref, part, 1)])
    packed = []
    for slot, grads in enumerate((dq_refs, dk_refs)):
        grad = jnp.where(inside, turned_back(grads, cosine, sine), 0.0)
        unit = (projected_ref[:, slot * padded : (slot + 1) * padded] - columns[:, 2 * slot : 2 * slot + 1])
        unit = jnp.where(inside, unit * columns[:, 2 * slot + 1 : 2 * slot + 2], 0.0)
        both = grad * unit
        sums_ref[2 * slot : 2 * slot + 1, :] += jnp.sum(both, axis=0, keepdims=True)
        sums_ref[2 * slot + 1 : 2 * slot + 2, :] += jnp.sum(grad, axis=0, keepdims=True)
        gain = gains_ref[slot : slot + 1, :]
        packed.append(jnp.sum(grad * gain, axis=1, keepdims=True))
        packed.append(jnp.sum(both * gain, axis=1, keepdims=True))
    out_ref[...] = pack_columns(packed)


def heads_back_kernel(part, pairs, *refs):
    dq_refs, dk_refs, dv_refs = refs[:pairs], refs[pairs : 2 * pairs], refs[2 * pairs : 3 * pairs]
    projected_ref, stats_ref, totals_ref, cos_ref, sin_ref, gains_ref, out_ref = refs[3 * pairs :]
    padded = 128 * pairs
    narrow = stats_ref.shape[0]
    cosine = wide_table(cos_ref[...], padded)
    sine = wide_table(sin_ref[...], padded)
    means = [
        functools.reduce(jnp.add, [totals_ref[i, j : j + 1, :] for i in range(narrow)]) * (1.0 / (narrow * part))
        for j in range(4)
    ]
    columns = as_columns([*joined_stats(stats_ref, part, 0), *joined_stats(stats_ref, part, 1), *means])
    for slot, grads in enumerate((dq_refs, dk_refs)):
        grad = turned_back(grads, cosine, sine) * gains_ref[slot : slot + 1, :]
        inverse = columns[:, 2 * slot + 1 : 2 * slot + 2]
        unit = (projected_ref[:, slot * padded : (slot + 1) * padded] - columns[:, 2 * slot : 2 * slot + 1]) * inverse
        grad = grad - columns[:, 4 + 2 * slot : 5 + 2 * slot] - unit * columns[:, 5 + 2 * slot : 6 + 2 * slot]
        grad = grad * inverse
        if padded != part:
            grad = jnp.where(real_lanes(grad.shape, part), grad, 0.0)
        out_ref[:, slot * padded : (slot + 1) * padded] = grad.astype(BF16)
    for pair, ref in enumerate(dv_refs):
        out_ref[:, 2 * padded + 128 * pair : 2 * padded + 128 * (pair + 1)] = ref[...]


def heads_back(grads, projected, stats, cosine, sine, gains, part, share):
    rows, triple = projected.shape
    padded = triple // 3
    pairs = padded // 128
    narrow = stats.shape[0]
    pair_spec = pl.BlockSpec((QBLOCK, 128), lambda i: (i, 0))
    two_spec = pl.BlockSpec((QBLOCK, 2 * padded), lambda i: (i, 0))
    stat_spec = pl.BlockSpec((narrow, 8, QBLOCK), lambda i: (0, 0, i))
    gain_spec = pl.BlockSpec((2, padded), lambda i: (0, 0))
    own, sums = pl.pallas_call(
        functools.partial(grad_stats_kernel, rows, part, pairs),
        grid=(pl.cdiv(rows, QBLOCK),),
        in_specs=[pair_spec] * (2 * pairs) + [two_spec, stat_spec, pair_spec, pair_spec, gain_spec],
        out_specs=[
            pl.BlockSpec((8, QBLOCK), lambda i: (0, i)),
            pl.BlockSpec((8, padded), lambda i: (0, 0)),
        ],
        out_shape=[jax.ShapeDtypeStruct((8, rows), F32), jax.ShapeDtypeStruct((8, padded), F32)],
        compiler_params=pltpu.CompilerParams(vmem_limit_bytes=VMEM_LIMIT),
        cost_estimate=pl.CostEstimate(flops=4 * rows * triple, bytes_accessed=rows * triple // 16, transcendentals=0),
    )(*grads[0], *grads[1], projected, stats, cosine, sine, gains)
    totals = share(own)
    out = pl.pallas_call(
        functools.partial(heads_back_kernel, part, pairs),
        grid=(pl.cdiv(rows, QBLOCK),),
        in_specs=[pair_spec] * (3 * pairs) + [two_spec, stat_spec, stat_spec, pair_spec, pair_spec, gain_spec],
        out_specs=pl.BlockSpec((QBLOCK, triple), lambda i: (i, 0)),
        out_shape=jax.ShapeDtypeStruct((rows, triple), BF16),
        compiler_params=pltpu.CompilerParams(vmem_limit_bytes=VMEM_LIMIT),
        cost_estimate=pl.CostEstimate(flops=4 * rows * triple, bytes_accessed=rows * triple // 16, transcendentals=0),
    )(*grads[0], *grads[1], *grads[2], projected, stats, totals, cosine, sine, gains)
    return out, sums


def head_lanes(rows, half, head_dim):
    lane = lax.broadcasted_iota(jnp.int32, (rows, 128), 1)
    return (lane >= half * head_dim) & (lane < (half + 1) * head_dim)


def softmax_product(pieces):
    maximum = functools.reduce(jnp.maximum, [jnp.max(s, axis=1, keepdims=True) for s, _ in pieces])
    total, result = 0.0, 0.0
    for scores, values in pieces:
        weight = jnp.exp2(scores - maximum)
        total = total + jnp.sum(weight, axis=1, keepdims=True)
        result = result + low_product(weight.astype(BF16), values)
    return result * (1.0 / total), maximum + jnp.log2(total)


def attend_kernel(
    head_dim, first, most, caption, image_count,
    gate_ref, q_ref, k_ref, v_ref, tk_ref, tv_ref, column_ref, row_ref,
    mixed_ref, self_ref, cross_ref, stats_ref,
):
    count = q_ref.shape[0]
    halves = 128 // head_dim

    def emit(at, rows, outs):
        lanes = [head_lanes(rows, half, head_dim) for half in range(halves)]
        own, cross, gated = 0.0, 0.0, 0.0
        columns = []
        for half, (own_out, own_total, cross_out, cross_total) in enumerate(outs):
            gate = gate_ref[0, half]
            own = own + jnp.where(lanes[half], own_out, 0.0)
            cross = cross + jnp.where(lanes[half], cross_out, 0.0)
            gated = gated + jnp.where(lanes[half], gate * cross_out, 0.0)
            columns += [own_total, cross_total]
        self_ref[pl.ds(at, rows), :] = own
        cross_ref[pl.ds(at, rows), :] = cross
        mixed_ref[pl.ds(at, rows), :] = (own + gated).astype(BF16)
        lane = lax.broadcasted_iota(jnp.int32, (rows, 128), 1)
        packed = jnp.zeros((rows, 128), F32)
        for i, column in enumerate(columns):
            packed = jnp.where(lane == i, column, packed)
        stats_ref[:, pl.ds(at, rows)] = jnp.transpose(packed)[:8, :]

    def clean(block, carry):
        at = pl.multiple_of(block * QBLOCK, QBLOCK)
        queries = q_ref[pl.ds(at, QBLOCK), :]
        outs = []
        for half in range(halves):
            q = jnp.where(head_lanes(QBLOCK, half, head_dim), queries, jnp.zeros_like(queries))
            bias = jnp.where(row_ref[0:1, first:most] == 0, 0.0, MASKED)
            own_out, own_total = softmax_product([
                (times_transposed(q, k_ref[0:first, :]), v_ref[0:first, :]),
                (times_transposed(q, k_ref[first:most, :]) + bias, v_ref[first:most, :]),
            ])
            cross_out, cross_total = softmax_product(
                [(times_transposed(q, tk_ref[0:caption, :]), tv_ref[0:caption, :])]
            )
            outs.append((own_out, own_total, cross_out, cross_total))
        emit(at, QBLOCK, outs)
        return carry

    lax.fori_loop(0, first // QBLOCK, clean, 0)
    rest = count - first
    queries = q_ref[first:count, :]
    image = column_ref[first:count, :]
    outs = []
    for half in range(halves):
        q = jnp.where(head_lanes(rest, half, head_dim), queries, jnp.zeros_like(queries))
        own_out, own_total = softmax_product([
            (jnp.where(image == row_ref[0:1, :], times_transposed(q, k_ref[...]), MASKED), v_ref[...])
        ])
        scores = times_transposed(q, tk_ref[...])
        owner = lax.broadcasted_iota(jnp.int32, (1, scores.shape[1]), 1) // caption
        scores = jnp.where((image == owner) | (image == image_count), scores, MASKED)
        cross_out, cross_total = softmax_product([(scores, tv_ref[...])])
        outs.append((own_out, own_total, cross_out, cross_total))
    emit(first, rest, outs)


def attend(pair, gates, packed, text_packed, column, row, head_dim, image_count):
    count, texts = packed.shape[0], text_packed.shape[0]
    pairs = packed.shape[1] // 384
    halves = 128 // head_dim
    out = pl.BlockSpec((count, 128), lambda i: (0, 0))
    most = min(round_up(FIRST_MOST, 128), count)
    flops = 4 * count * (count + texts) * 128
    return pl.pallas_call(
        functools.partial(
            attend_kernel, head_dim, FIRST_PATCHES, most, texts // image_count, image_count
        ),
        grid=(1,),
        in_specs=[
            pl.BlockSpec((None, 1, halves), lambda i: (pair, 0, 0), memory_space=pltpu.SMEM),
            pl.BlockSpec((count, 128), lambda i: (0, pair)),
            pl.BlockSpec((count, 128), lambda i: (0, pairs + pair)),
            pl.BlockSpec((count, 128), lambda i: (0, 2 * pairs + pair)),
            pl.BlockSpec((texts, 128), lambda i: (0, pair)),
            pl.BlockSpec((texts, 128), lambda i: (0, pairs + pair)),
            pl.BlockSpec((count, 1), lambda i: (0, 0)),
            pl.BlockSpec((1, count), lambda i: (0, 0)),
        ],
        out_specs=[out, out, out, pl.BlockSpec((8, count), lambda i: (0, 0))],
        out_shape=[
            jax.ShapeDtypeStruct((count, 128), BF16),
            jax.ShapeDtypeStruct((count, 128), F32),
            jax.ShapeDtypeStruct((count, 128), F32),
            jax.ShapeDtypeStruct((8, count), F32),
        ],
        compiler_params=pltpu.CompilerParams(vmem_limit_bytes=VMEM_LIMIT),
        cost_estimate=pl.CostEstimate(flops=flops, bytes_accessed=20 * count * 128, transcendentals=2 * count * count),
    )(gates.reshape(pairs, 1, halves), packed, packed, packed, text_packed, text_packed, column, row)


def gate_lanes(gate_ref, head_dim):
    lane = lax.broadcasted_iota(jnp.int32, (1, 128), 1)
    gates = jnp.zeros((1, 128), F32)
    for half in range(128 // head_dim):
        gates = jnp.where(lane // head_dim == half, gate_ref[0, half], gates)
    return gates


def head_picks(head_dim):
    return (
        lax.broadcasted_iota(jnp.int32, (8, 128), 1) // head_dim
        == lax.broadcasted_iota(jnp.int32, (8, 128), 0)
    ).astype(F32)


def rows_back(head_dim, queries, outs, delta, stats, offset, keys, values, key_sum, value_sum, spans):
    rows = queries.shape[0]
    halves = 128 // head_dim
    zero = jnp.zeros((rows, 128), BF16)
    lanes = [head_lanes(rows, half, head_dim) for half in range(halves)]
    q_heads = [jnp.where(lane, queries, zero) for lane in lanes]
    out_heads = [jnp.where(lane, outs, zero) for lane in lanes]
    q_stack = jnp.concatenate(q_heads, axis=0)
    out_stack = jnp.concatenate(out_heads, axis=0)
    dq = [0.0] * halves
    for low, high, mask in spans:
        key_part = keys[low:high, :]
        value_part = values[low:high, :]
        probs, grads = [], []
        for half in range(halves):
            scores = mask(times_transposed(key_part, q_heads[half]))
            prob = jnp.exp2(scores - stats[2 * half + offset : 2 * half + offset + 1, :])
            dprob = times_transposed(value_part, out_heads[half])
            dscore = (prob * (dprob - delta[half : half + 1, :])).astype(BF16)
            probs.append(prob.astype(BF16))
            grads.append(dscore)
            dq[half] = dq[half] + outer_sum(dscore, key_part)
        value_sum[low:high, :] += low_product(jnp.concatenate(probs, axis=1), out_stack)
        key_sum[low:high, :] += low_product(jnp.concatenate(grads, axis=1), q_stack)
    total = 0.0
    for half in range(halves):
        total = total + jnp.where(lanes[half], dq[half], 0.0)
    return total


def cross_back_kernel(
    head_dim, first, caption, image_count, scale,
    gate_ref, q_ref, tk_ref, tv_ref, row_ref, grad_ref, cross_ref, stats_ref,
    dq_ref, dtk_ref, dtv_ref, gate_grad_ref, dtk_sum, dtv_sum,
):
    count = q_ref.shape[0]
    for total in (dtk_sum, dtv_sum, gate_grad_ref):
        total[...] = jnp.zeros_like(total)
    gates = gate_lanes(gate_ref, head_dim)
    picks = head_picks(head_dim)

    def part(at, rows, spans):
        wide = grad_ref[pl.ds(at, rows), :].astype(F32)
        cross = cross_ref[pl.ds(at, rows), :]
        gate_grad_ref[0:1, :] += jnp.sum(wide * cross, axis=0, keepdims=True)
        gated = (wide * gates).astype(BF16)
        delta = exact_transposed(picks, gated.astype(F32) * cross)
        dq = rows_back(
            head_dim, q_ref[pl.ds(at, rows), :], gated, delta, stats_ref[:, pl.ds(at, rows)], 1,
            tk_ref, tv_ref, dtk_sum, dtv_sum, spans,
        )
        dq_ref[pl.ds(at, rows), :] = (dq * scale).astype(BF16)

    def clean(block, carry):
        part(pl.multiple_of(block * QBLOCK, QBLOCK), QBLOCK, [(0, caption, lambda scores: scores)])
        return carry

    lax.fori_loop(0, first // QBLOCK, clean, 0)
    image = row_ref[0:1, first:count]
    owner = lax.broadcasted_iota(jnp.int32, (tk_ref.shape[0], 1), 0) // caption
    allowed = (owner == image) | (image == image_count)
    part(first, count - first, [(0, tk_ref.shape[0], lambda scores: jnp.where(allowed, scores, MASKED))])
    dtk_ref[...] = (dtk_sum[...] * (1.0 / LOG2E)).astype(BF16)
    dtv_ref[...] = dtv_sum[...].astype(BF16)


def cross_back(pair, gates, packed, text_packed, row, grad, cross, stats, head_dim, image_count, scale):
    count, texts = packed.shape[0], text_packed.shape[0]
    pairs = packed.shape[1] // 384
    halves = 128 // head_dim
    tokens = pl.BlockSpec((count, 128), lambda i: (0, pair))
    own_tokens = pl.BlockSpec((count, 128), lambda i: (0, 0))
    captions = pl.BlockSpec((texts, 128), lambda i: (0, 0))
    flops = 10 * count * texts * 128
    return pl.pallas_call(
        functools.partial(cross_back_kernel, head_dim, FIRST_PATCHES, texts // image_count, image_count, scale),
        grid=(1,),
        in_specs=[
            pl.BlockSpec((None, 1, halves), lambda i: (pair, 0, 0), memory_space=pltpu.SMEM),
            tokens,
            pl.BlockSpec((texts, 128), lambda i: (0, pair)),
            pl.BlockSpec((texts, 128), lambda i: (0, pairs + pair)),
            pl.BlockSpec((1, count), lambda i: (0, 0)),
            tokens,
            own_tokens,
            pl.BlockSpec((8, count), lambda i: (0, 0)),
        ],
        out_specs=[own_tokens, captions, captions, pl.BlockSpec((8, 128), lambda i: (0, 0))],
        out_shape=[
            jax.ShapeDtypeStruct((count, 128), BF16),
            jax.ShapeDtypeStruct((texts, 128), BF16),
            jax.ShapeDtypeStruct((texts, 128), BF16),
            jax.ShapeDtypeStruct((8, 128), F32),
        ],
        scratch_shapes=[pltpu.VMEM((texts, 128), F32), pltpu.VMEM((texts, 128), F32)],
        compiler_params=pltpu.CompilerParams(vmem_limit_bytes=VMEM_LIMIT),
        cost_estimate=pl.CostEstimate(flops=flops, bytes_accessed=12 * count * 128, transcendentals=count * texts),
    )(gates.reshape(pairs, 1, halves), packed, text_packed, text_packed, row, grad, cross, stats)


def self_back_kernel(
    head_dim, first, most, scale,
    q_ref, k_ref, v_ref, column_ref, row_ref, grad_ref, self_ref, stats_ref, more_ref,
    dq_ref, dk_ref, dv_ref, dk_sum, dv_sum,
):
    count = q_ref.shape[0]
    dk_sum[...] = jnp.zeros_like(dk_sum)
    dv_sum[...] = jnp.zeros_like(dv_sum)
    picks = head_picks(head_dim)

    def part(at, rows, spans):
        grad = grad_ref[pl.ds(at, rows), :]
        delta = exact_transposed(picks, grad.astype(F32) * self_ref[pl.ds(at, rows), :])
        dq = rows_back(
            head_dim, q_ref[pl.ds(at, rows), :], grad, delta, stats_ref[:, pl.ds(at, rows)], 0,
            k_ref, v_ref, dk_sum, dv_sum, spans,
        )
        dq_ref[pl.ds(at, rows), :] = (dq * scale + more_ref[pl.ds(at, rows), :].astype(F32)).astype(BF16)

    def clean(block, carry):
        bias = jnp.where(column_ref[first:most, :] == 0, 0.0, MASKED)
        part(
            pl.multiple_of(block * QBLOCK, QBLOCK), QBLOCK,
            [(0, first, lambda scores: scores), (first, most, lambda scores: scores + bias)],
        )
        return carry

    lax.fori_loop(0, first // QBLOCK, clean, 0)
    image = row_ref[0:1, first:count]
    part(first, count - first, [(0, count, lambda scores: jnp.where(column_ref[...] == image, scores, MASKED))])
    dk_ref[...] = (dk_sum[...] * (1.0 / LOG2E)).astype(BF16)
    dv_ref[...] = dv_sum[...].astype(BF16)


def self_back(pair, packed, column, row, grad, own, stats, more, head_dim, scale):
    count = packed.shape[0]
    pairs = packed.shape[1] // 384
    tokens = pl.BlockSpec((count, 128), lambda i: (0, pair))
    out = pl.BlockSpec((count, 128), lambda i: (0, 0))
    most = min(round_up(FIRST_MOST, 128), count)
    flops = 10 * count * count * 128
    return pl.pallas_call(
        functools.partial(self_back_kernel, head_dim, FIRST_PATCHES, most, scale),
        grid=(1,),
        in_specs=[
            tokens,
            pl.BlockSpec((count, 128), lambda i: (0, pairs + pair)),
            pl.BlockSpec((count, 128), lambda i: (0, 2 * pairs + pair)),
            pl.BlockSpec((count, 1), lambda i: (0, 0)),
            pl.BlockSpec((1, count), lambda i: (0, 0)),
            tokens,
            out,
            pl.BlockSpec((8, count), lambda i: (0, 0)),
            out,
        ],
        out_specs=[out, out, out],
        out_shape=[jax.ShapeDtypeStruct((count, 128), BF16)] * 3,
        scratch_shapes=[pltpu.VMEM((count, 128), F32), pltpu.VMEM((count, 128), F32)],
        compiler_params=pltpu.CompilerParams(vmem_limit_bytes=VMEM_LIMIT),
        cost_estimate=pl.CostEstimate(flops=flops, bytes_accessed=30 * count * 128, transcendentals=2 * count * count),
    )(packed, packed, packed, column, row, grad, own, stats, more)


def swiglu_kernel(core_ref, gate_ref, up_ref, out_ref, moved_ref):
    gate = gate_ref[...]
    half = 0.5 * gate
    value = ((half + half * jnp.tanh(half)) * up_ref[...]).astype(BF16)
    out_ref[...] = value
    moved_ref[...] = value


def swiglu(gate_up, core, deep, narrow):
    rows, double = gate_up.shape
    width = double // 2
    blocks = 2 * deep * narrow
    block = width // blocks

    def moved_place(i, core_ref):
        z, c, f = i // (2 * narrow), (i // narrow) % 2, i % narrow
        return (0, ((c + core_ref[0]) % 2) * (deep * narrow) + f * deep + z)

    return pl.pallas_call(
        swiglu_kernel,
        grid_spec=pltpu.PrefetchScalarGridSpec(
            num_scalar_prefetch=1,
            grid=(blocks,),
            in_specs=[
                pl.BlockSpec((rows, block), lambda i, core_ref: (0, i)),
                pl.BlockSpec((rows, block), lambda i, core_ref: (0, blocks + i)),
            ],
            out_specs=[
                pl.BlockSpec((rows, block), lambda i, core_ref: (0, i)),
                pl.BlockSpec((rows, block), moved_place),
            ],
        ),
        out_shape=[jax.ShapeDtypeStruct((rows, width), BF16)] * 2,
        compiler_params=pltpu.CompilerParams(vmem_limit_bytes=VMEM_LIMIT),
        cost_estimate=pl.CostEstimate(flops=6 * rows * width, bytes_accessed=12 * rows * width, transcendentals=rows * width),
    )(core.reshape(1), gate_up, gate_up)


def fsdp_share_kernel(narrow, x_ref, out_ref, send_sem, recv_sem):
    me = lax.axis_index("fsdp")
    barrier = pltpu.get_barrier_semaphore()
    for step in range(1, narrow):
        pl.semaphore_signal(
            barrier, inc=1, device_id={"fsdp": lax.rem(me + step, narrow)}, device_id_type=pl.DeviceIdType.MESH
        )
    pl.semaphore_wait(barrier, narrow - 1)
    copies = []
    for step in range(1, narrow):
        copy = pltpu.make_async_remote_copy(
            src_ref=x_ref,
            dst_ref=out_ref.at[me],
            send_sem=send_sem.at[step],
            recv_sem=recv_sem.at[step],
            device_id={"fsdp": lax.rem(me + step, narrow)},
            device_id_type=pl.DeviceIdType.MESH,
        )
        copy.start()
        copies.append(copy)
    out_ref[me] = x_ref[...]
    for copy in copies:
        copy.wait()


def fsdp_share(value, narrow, collective_id):
    return pl.pallas_call(
        functools.partial(fsdp_share_kernel, narrow),
        in_specs=[pl.BlockSpec(memory_space=pltpu.VMEM)],
        out_specs=pl.BlockSpec(memory_space=pltpu.VMEM),
        out_shape=jax.ShapeDtypeStruct((narrow,) + value.shape, value.dtype),
        scratch_shapes=[pltpu.SemaphoreType.DMA((narrow,)), pltpu.SemaphoreType.DMA((narrow,))],
        compiler_params=pltpu.CompilerParams(collective_id=collective_id, has_side_effects=True),
        cost_estimate=pl.CostEstimate(flops=0, bytes_accessed=8 * narrow * value.size, transcendentals=0),
    )(value)


def place_rows(items, x_ref, chunk, base):
    rows = [(ref, row) for ref in items for row in range(ref.shape[0])]
    at = 0
    while at < len(rows):
        ref, row = rows[at]
        off = at % chunk
        take = min(ref.shape[0] - row, chunk - off)
        x_ref[at // chunk, base + off : base + off + take, :] = ref[row : row + take, :]
        at += take
    while at < x_ref.shape[0] * chunk:
        off = at % chunk
        x_ref[at // chunk, base + off : base + chunk, :] = jnp.zeros((chunk - off, 128), F32)
        at += chunk - off


def finish_kernel(narrow, wide, sum_rows, sum_count, plan, *refs):
    plans, outs = len(plan), len(plan) + 2
    scratch = refs[-7:]
    items, results = refs[: -7 - outs], refs[-7 - outs : -7]
    out_ref, kept_ref, x_ref, first_ref, second_ref, sends, recvs = scratch
    place_rows(items[:sum_count], x_ref, sum_rows, 0)
    place_rows(items[sum_count:], x_ref, x_ref.shape[1] - sum_rows, sum_rows)
    me = lax.axis_index("fsdp")
    group = lax.axis_index("z") * 2 + lax.axis_index("core")
    rows = x_ref.shape[1]
    rest = rows - sum_rows
    barrier = pltpu.get_barrier_semaphore()
    places = [{"fsdp": lax.rem(me + step, narrow)} for step in range(1, narrow)]
    peers = [lax.rem(group + step, wide) for step in range(1, wide)]
    partners = [{"z": peer // 2, "core": peer % 2} for peer in peers]
    for place in places + partners:
        pl.semaphore_signal(barrier, inc=1, device_id=place, device_id_type=pl.DeviceIdType.MESH)
    pl.semaphore_wait(barrier, narrow + wide - 2)

    def send_all(targets, source, target, base):
        copies = []
        for i, place in enumerate(targets):
            copy = pltpu.make_async_remote_copy(
                src_ref=source(i),
                dst_ref=target,
                send_sem=sends.at[base + i],
                recv_sem=recvs.at[base + i],
                device_id=place,
                device_id_type=pl.DeviceIdType.MESH,
            )
            copy.start()
            copies.append(copy)
        return copies

    copies = send_all(places, lambda i: x_ref.at[lax.rem(me + i + 1, narrow)], first_ref.at[me], 0)
    first_ref[me] = x_ref[me]
    for copy in copies:
        copy.wait()
    total = first_ref[0]
    for i in range(1, narrow):
        total = total + first_ref[i]
    second_ref[group] = total
    copies = send_all(partners, lambda i: second_ref.at[group], second_ref.at[group], narrow)
    for copy in copies:
        copy.wait()
    total = second_ref[0, :sum_rows, :]
    for i in range(1, wide):
        total = total + second_ref[i, :sum_rows, :]
    out_ref[me] = total
    for i in range(wide):
        kept_ref[me, i] = second_ref[i, sum_rows:, :]
    copies = send_all(places, lambda i: out_ref.at[me], out_ref.at[me], narrow + wide)
    copies += send_all(places, lambda i: kept_ref.at[me], kept_ref.at[me], 2 * narrow + wide)
    for copy in copies:
        copy.wait()
    for result, source_rows in zip(results[:plans], plan):
        lanes = result.shape[1] // 128
        for i, source in enumerate(source_rows):
            result[i // lanes : i // lanes + 1, i % lanes * 128 : (i % lanes + 1) * 128] = out_ref[
                source // sum_rows, source % sum_rows : source % sum_rows + 1, :
            ]
    slots_ref, cond_ref = results[plans:]
    images = slots_ref.shape[1]
    width = slots_ref.shape[2] // 128
    lanes = width // 4
    targets = [
        (slots_ref, image, part * lanes + lane)
        for part in range(4) for image in range(images) for lane in range(lanes)
    ] + [(cond_ref, image, lane) for image in range(images) for lane in range(cond_ref.shape[2] // 128)]

    def unpack(g, carry):
        for at, (target, image, lane) in enumerate(targets):
            row = kept_ref[at // rest, g, at % rest : at % rest + 1, :]
            target[g, image : image + 1, lane * 128 : (lane + 1) * 128] = row
        return carry

    lax.fori_loop(0, wide, unpack, 0)


def finish(summed, kept, plan, images, narrow, wide, collective_id):
    sum_total = sum(item.shape[0] for item in summed)
    kept_total = sum(item.shape[0] for item in kept)
    sum_rows = round_up(-(-sum_total // narrow), 8)
    kept_rows = round_up(-(-kept_total // narrow), 8)
    rows = sum_rows + kept_rows
    count = 3 * narrow + wide
    cond_width = kept[-1].shape[0] * 128 // images
    slot_width = (kept_total - kept[-1].shape[0]) * 128 // images
    vmem = pl.BlockSpec(memory_space=pltpu.VMEM)
    shapes = [shape for shape, _ in plan] + [(wide, images, slot_width), (wide, images, cond_width)]
    return pl.pallas_call(
        functools.partial(finish_kernel, narrow, wide, sum_rows, len(summed), [source for _, source in plan]),
        in_specs=[vmem] * (len(summed) + len(kept)),
        out_specs=[vmem] * len(shapes),
        out_shape=[jax.ShapeDtypeStruct(shape, F32) for shape in shapes],
        scratch_shapes=[
            pltpu.VMEM((narrow, sum_rows, 128), F32),
            pltpu.VMEM((narrow, wide, kept_rows, 128), F32),
            pltpu.VMEM((narrow, rows, 128), F32),
            pltpu.VMEM((narrow, rows, 128), F32),
            pltpu.VMEM((wide, rows, 128), F32),
            pltpu.SemaphoreType.DMA((count,)),
            pltpu.SemaphoreType.DMA((count,)),
        ],
        compiler_params=pltpu.CompilerParams(collective_id=collective_id, has_side_effects=True),
    )(*summed, *kept)


def exchange(blocks, axis):
    return lax.all_to_all(blocks, axis, 0, 0, tiled=True)


def core_swap(value):
    return lax.ppermute(value, "core", [(0, 1), (1, 0)])


def by_core(low, high):
    first = lax.axis_index("core") == 0
    return jnp.where(first, low, high), jnp.where(first, high, low)


def in_core_order(own, other):
    first = lax.axis_index("core") == 0
    return jnp.where(first, own, other), jnp.where(first, other, own)


def chip_sum(own_left, other_left, right):
    came = core_swap(outer_sum(other_left, right).astype(BF16))
    return (outer_sum(own_left, right) + came.astype(F32)).astype(BF16)


def fsdp_sum(both):
    return lax.psum_scatter(both, "fsdp", scatter_dimension=0, tiled=True)


def z_pieces(blocks, deep):
    me = lax.axis_index("z")
    return [lax.dynamic_index_in_dim(blocks, me, 0, keepdims=False)] + [
        lax.ppermute(
            lax.dynamic_index_in_dim(blocks, me ^ step, 0, keepdims=False), "z", [(i, i ^ step) for i in range(deep)]
        )
        for step in range(1, deep)
    ]


def added(pieces):
    return functools.reduce(jnp.add, [piece.astype(F32) for piece in pieces])


def to_all(block, narrow):
    return [
        lax.ppermute(block, "fsdp", [(i, i ^ step) for i in range(narrow)]) for step in range(1, narrow)
    ]


def relative(blocks, me, axis):
    return jnp.concatenate(
        [lax.dynamic_slice_in_dim(blocks, me ^ step, 1, axis) for step in range(blocks.shape[axis])], axis=axis
    )


def device_columns(value, deep, narrow):
    rows, width = value.shape
    block = width // (2 * deep * narrow)
    core = lax.axis_index("core")
    target = jnp.arange(width, dtype=jnp.int32)
    c, f, z, r = (
        target // (narrow * deep * block), target // (deep * block) % narrow, target // block % deep, target % block,
    )
    c = (c + core) % 2
    source = ((z * 2 + c) * narrow + f) * block + r
    pick = (jnp.arange(width, dtype=jnp.int32)[:, None] == source[None, :]).astype(BF16)
    moved = low_product(value, pick).astype(BF16)
    return moved[:, : width // 2], moved[:, width // 2 :]


def whole_weight(shard):
    rows = shard.shape[0] // 2
    half = lax.dynamic_slice_in_dim(shard, lax.axis_index("core") * rows, rows, 0)
    return lax.all_gather(half, ("fsdp", "core"), axis=0, tiled=True)


def shards(
    tokens,
    cotangent,
    text_states,
    conditioning,
    image_sizes,
    ada_weight,
    ada_bias,
    qkv_weight,
    out_weight,
    text_weight,
    gate_up_weight,
    down_weight,
    norm_gains,
    norm_shifts,
    text_gain,
    head_gate,
):
    model_width = tokens.shape[2]
    head_count = head_gate.shape[0]
    head_dim = model_width // head_count
    image_count = text_states.shape[1]
    caption_local = text_states.shape[2]
    caption_width = text_states.shape[3]
    local_tok = tokens.shape[1]
    deep = lax.axis_size("z")
    narrow = lax.axis_size("fsdp")
    wide = 2 * deep
    me = lax.axis_index("fsdp")
    group_tok = local_tok * narrow
    caption_full = caption_local * narrow
    score_scale = head_dim ** (-0.5)
    text_total = image_count * caption_full
    text_local = image_count * caption_local
    part = model_width // narrow
    part_pad = round_up(part, 128)
    heads_here = head_count // narrow
    pairs = part_pad // 128
    halves = 128 // head_dim

    group_sizes = image_sizes[0]
    position = me * local_tok + jnp.arange(local_tok, dtype=jnp.int32)
    image_index = token_layout(group_sizes, position, image_count)[0]
    key_image, key_row, key_col = token_layout(
        group_sizes, jnp.arange(group_tok, dtype=jnp.int32), image_count
    )
    member = [(image_index == i).astype(F32)[:, None] for i in range(image_count)]
    cosine, sine = rope_tables(key_row, key_col, head_dim)

    cond_low = jax.nn.silu(conditioning[0].astype(F32)).astype(BF16)
    cond_rows = ada_weight.shape[0]
    cond_part = lax.dynamic_slice_in_dim(cond_low, me * cond_rows, cond_rows, 1)
    modulation_part = low_product(cond_part, ada_weight)
    modulation = (
        jnp.sum(fsdp_share(modulation_part.reshape(-1, 128), narrow, 0), axis=0).reshape(modulation_part.shape)
        + ada_bias
    )

    def per_token(index):
        rows = modulation[:, index * model_width : (index + 1) * model_width]
        return functools.reduce(
            jnp.add, [member[i] * rows[i : i + 1, :] for i in range(image_count)]
        )

    def per_image(value):
        return [jnp.sum(member[i] * value, axis=0).reshape(-1, 128) for i in range(image_count)]

    token_in = tokens[0].astype(F32)
    token_inverse = inverse_rms(token_in)
    tokens_all = lax.all_gather(tokens[0], "fsdp", axis=0, tiled=True)
    def widened(value, slots):
        if part == part_pad:
            return value
        lead = value.shape[:-1]
        value = value.reshape(*lead, slots, part)
        pads = [(0, 0)] * (len(lead) + 1) + [(0, part_pad - part)]
        return jnp.pad(value, pads).reshape(*lead, slots * part_pad)

    def narrowed(value, slots):
        if part == part_pad:
            return value
        lead = value.shape[:-1]
        return value.reshape(*lead, slots, part_pad)[..., :part].reshape(*lead, slots * part)

    def own_columns(value):
        return widened(lax.dynamic_slice_in_dim(value, me * part, part, value.ndim - 1), 1)

    qkv_rows = qkv_weight.shape[0] // 2
    qkv_half = lax.dynamic_slice_in_dim(qkv_weight, lax.axis_index("core") * qkv_rows, qkv_rows, 0)
    qkv_half = exchange(
        qkv_half.reshape(qkv_rows, 3, narrow, part).transpose(2, 0, 1, 3).reshape(narrow, qkv_rows, 3 * part), "fsdp"
    )
    own_qkv = widened(
        jnp.concatenate(in_core_order(qkv_half, core_swap(qkv_half)), axis=1).reshape(model_width, 3 * part), 3
    )

    full_out = whole_weight(out_weight)
    full_gate_up = whole_weight(gate_up_weight)
    full_down = whole_weight(down_weight)

    text_in = text_states[0].astype(F32).reshape(text_local, caption_width)
    text_inverse = inverse_rms(text_in)
    text_low = (text_in * text_inverse * text_gain).astype(BF16)
    text_cols = caption_width // narrow
    text_slice = (
        exchange(text_low.reshape(text_local, narrow, text_cols).transpose(1, 0, 2), "fsdp")
        .reshape(narrow, image_count, caption_local, text_cols)
        .transpose(1, 0, 2, 3)
        .reshape(text_total, text_cols)
    )
    own_text_weight = (
        text_weight.reshape(text_cols, 2, narrow, part).transpose(2, 0, 1, 3).reshape(narrow, text_cols, 2 * part)
    )
    text_partial = jnp.stack([low_product(text_slice, own_text_weight[i]).astype(BF16) for i in range(narrow)])
    text_partial, tokens_all = lax.optimization_barrier((text_partial, tokens_all))
    text_projected = widened(jnp.sum(exchange(text_partial, "fsdp").astype(F32), axis=0), 2)
    text_parts = fsdp_share(column_stats(text_projected, part, part_pad, 1), narrow, 1)
    text_means = text_parts[:, 0, :]
    text_mean = jnp.mean(text_means, axis=0)
    text_square = jnp.sum(text_parts[:, 1, :], axis=0) + part * jnp.sum((text_means - text_mean) ** 2, axis=0)
    text_key_inverse = lax.rsqrt(text_square / model_width + EPS)[:, None]
    text_unit = (text_projected[:, :part_pad] - text_mean[:, None]) * text_key_inverse
    text_gains = own_columns(norm_gains[4])
    text_packed = jnp.concatenate(
        [(text_unit * text_gains).astype(BF16), text_projected[:, part_pad:].astype(BF16)], axis=1
    )

    wide_tokens = tokens_all.astype(F32)
    wide_scale = functools.reduce(
        jnp.add,
        [(key_image == i).astype(F32)[:, None] * modulation[i : i + 1, :model_width] for i in range(image_count)],
    )
    normed_all = (wide_tokens * inverse_rms(wide_tokens) * norm_gains[0] * (1.0 + wide_scale)).astype(BF16)

    projected = low_product(normed_all, own_qkv)
    stats_all = fsdp_share(column_stats(projected, part, part_pad, 2), narrow, 2)
    head_gains = own_columns(norm_gains[2:4])
    packed = make_heads(
        projected, stats_all, cosine, sine, head_gains, own_columns(norm_shifts), part, score_scale * LOG2E
    )
    gate_tanh = jnp.tanh(head_gate)
    own_gates = lax.dynamic_slice_in_dim(gate_tanh, me * heads_here, heads_here, 0)
    own_gates = jnp.concatenate([own_gates, jnp.ones((pairs * halves - heads_here,), F32)])
    column = key_image[:, None]
    row = key_image[None, :]
    attended = [
        attend(pair, own_gates, packed, text_packed, column, row, head_dim, image_count) for pair in range(pairs)
    ]
    mixed_pairs = [exchange(one[0].reshape(narrow, local_tok, 128), "fsdp") for one in attended]
    self_outs = [one[1] for one in attended]
    cross_outs = [one[2] for one in attended]
    stats = [one[3] for one in attended]
    mixed_low = (
        narrowed(jnp.concatenate(mixed_pairs, axis=2), 1).transpose(1, 0, 2).reshape(local_tok, model_width)
    )

    branch = low_product(mixed_low, full_out)
    branch_inverse = inverse_rms(branch)
    branch_unit = branch * branch_inverse
    gate_attend = jnp.tanh(per_token(1))
    hidden = token_in + gate_attend * (branch_unit * norm_gains[1])
    hidden_inverse = inverse_rms(hidden)
    hidden_unit = hidden * hidden_inverse
    scale_feed = 1.0 + per_token(2)
    normed_feed_low = (hidden_unit * norm_gains[5] * scale_feed).astype(BF16)
    gate_up = low_product(normed_feed_low, full_gate_up)
    hidden_units = gate_up.shape[1] // 2
    gate_half = gate_up[:, :hidden_units]
    up_half = gate_up[:, hidden_units:]
    sigmoid = jax.nn.sigmoid(gate_half)
    if hidden_units // (wide * narrow) % 128 == 0:
        activated_low, moved = swiglu(gate_up, lax.axis_index("core"), deep, narrow)
        down_columns = (moved[:, : hidden_units // 2], moved[:, hidden_units // 2 :])
    else:
        activated_low = (gate_half * sigmoid * up_half).astype(BF16)
        down_columns = device_columns(activated_low, deep, narrow)
    down_out = low_product(activated_low, full_down)
    down_inverse = inverse_rms(down_out)
    down_unit = down_out * down_inverse
    gate_feed = jnp.tanh(per_token(3))
    down_normed = down_unit * norm_gains[6]
    result = (hidden + gate_feed * down_normed).astype(BF16)

    grad_result = cotangent[0].astype(F32)
    grad_down_y = grad_result * gate_feed
    grad_gain_six = jnp.sum(grad_down_y * down_unit, axis=0)
    grad_gate_feed = per_image(grad_result * down_normed * (1.0 - gate_feed * gate_feed))
    grad_down_low = norm_pull(grad_down_y * norm_gains[6], down_unit, down_inverse).astype(BF16)
    grad_activated = times_transposed(grad_down_low, full_down)
    grad_gate_low = (grad_activated * up_half * sigmoid * (1.0 + gate_half * (1.0 - sigmoid))).astype(BF16)
    grad_up_low = (grad_activated * gate_half * sigmoid).astype(BF16)
    grad_gate_up_low = jnp.concatenate([grad_gate_low, grad_up_low], axis=1)
    grad_normed_feed = times_transposed(grad_gate_up_low, full_gate_up)
    grad_feed_y = grad_normed_feed * scale_feed
    grad_gain_five = jnp.sum(grad_feed_y * hidden_unit, axis=0)
    grad_scale_feed = per_image(grad_normed_feed * hidden_unit * norm_gains[5])
    grad_hidden = grad_result + norm_pull(grad_feed_y * norm_gains[5], hidden_unit, hidden_inverse)
    grad_branch_y = grad_hidden * gate_attend
    grad_gain_one = jnp.sum(grad_branch_y * branch_unit, axis=0)
    grad_gate_attend = per_image(
        grad_hidden * branch_unit * norm_gains[1] * (1.0 - gate_attend * gate_attend)
    )
    grad_branch_low = norm_pull(grad_branch_y * norm_gains[1], branch_unit, branch_inverse).astype(BF16)
    grad_mixed = times_transposed(grad_branch_low, full_out).astype(BF16)
    grad_blocks = widened(grad_mixed.reshape(local_tok, narrow, part).transpose(1, 0, 2), 1)
    grad_heads = exchange(grad_blocks, "fsdp").reshape(group_tok, part_pad)
    def by_z(value):
        return value.reshape(deep, -1, value.shape[1])

    down_both = chip_sum(*down_columns, grad_down_low)
    feed_columns = device_columns(normed_feed_low, deep, narrow)
    gate_both = chip_sum(*feed_columns, grad_gate_low)
    up_both = chip_sum(*feed_columns, grad_up_low)
    out_both = chip_sum(*device_columns(mixed_low, deep, narrow), grad_branch_low)
    down_part = fsdp_sum(down_both)
    grad_heads, gate_both, up_both, out_both, down_part = lax.optimization_barrier(
        (grad_heads, gate_both, up_both, out_both, down_part)
    )
    gate_part = fsdp_sum(gate_both)
    out_part = fsdp_sum(out_both)
    up_part = fsdp_sum(up_both)
    came_downs = exchange(by_z(down_part), "z")
    crossed = [
        cross_back(
            pair, own_gates, packed, text_packed, row, grad_heads, cross_outs[pair], stats[pair],
            head_dim, image_count, score_scale,
        )
        for pair in range(pairs)
    ]
    dtk = jnp.concatenate([one[1] for one in crossed], axis=1)
    dtv = jnp.concatenate([one[2] for one in crossed], axis=1)
    gate_sums = jnp.stack([one[3] for one in crossed])

    grad_text_keys = dtk.astype(F32)
    own_gain_four = jnp.sum(grad_text_keys * text_unit, axis=0)
    grad_text_unit = grad_text_keys * text_gains
    text_sums = jnp.stack([jnp.sum(grad_text_unit, axis=1), jnp.sum(grad_text_unit * text_unit, axis=1)])
    text_sums = jnp.sum(
        fsdp_share(jnp.pad(text_sums, ((0, 6), (0, 0))), narrow, 3), axis=0
    ) * (1.0 / model_width)
    grad_text_key_in = (grad_text_unit - text_sums[0][:, None] - text_unit * text_sums[1][:, None]) * text_key_inverse
    grad_text_own = jnp.concatenate(
        [narrowed(grad_text_key_in.astype(BF16), 1), narrowed(dtv, 1)], axis=1
    )
    def self_pair(pair):
        return self_back(
            pair, packed, column, row, grad_heads, self_outs[pair], stats[pair], crossed[pair][0], head_dim, score_scale
        )

    came_texts = to_all(grad_text_own, narrow)
    backs = [self_pair(0)]
    first, came_downs, *came_texts = lax.optimization_barrier((backs[0][0], came_downs, *came_texts))
    grad_down_weight = jnp.sum(came_downs.astype(F32), axis=0)
    backs[0] = (first, *backs[0][1:])
    grad_text_columns = jnp.concatenate([grad_text_own, *came_texts], axis=1)
    text_half = text_cols // 2
    own_text, other_text = by_core(text_slice[:, :text_half], text_slice[:, text_half:])
    came_text = core_swap(outer_sum(other_text, grad_text_columns).astype(BF16))
    text_both = (outer_sum(own_text, grad_text_columns) + came_text.astype(F32)).astype(BF16)
    grad_heads, text_both, first = lax.optimization_barrier((grad_heads, text_both, backs[0][0]))
    backs[0] = (first, *backs[0][1:])
    came_text_z = exchange(by_z(text_both), "z")
    backs.append(self_pair(1))
    if pairs > 2:
        grad_heads, gate_part, up_part, second = lax.optimization_barrier(
            (grad_heads, gate_part, up_part, backs[1][0])
        )
        backs[1] = (second, *backs[1][1:])
        backs += [self_pair(pair) for pair in range(2, pairs)]
    gate_pieces = z_pieces(by_z(gate_part), deep)
    last, came_text_z, up_part, out_part, *gate_pieces = lax.optimization_barrier(
        (backs[-1][0], came_text_z, up_part, out_part, *gate_pieces)
    )
    up_width = up_part.shape[1]
    up_pieces = z_pieces(by_z(jnp.concatenate([up_part, out_part], axis=1)), deep)
    backs[-1] = (last, *backs[-1][1:])
    text_part = jnp.sum(came_text_z.astype(F32), axis=0).astype(BF16)
    everyone = ("z", "core", "fsdp")
    grad_text_weight = lax.ppermute(
        text_part,
        everyone,
        [
            ((z * 2 + c) * narrow + f, f * wide + c * deep + z)
            for z in range(deep) for c in range(2) for f in range(narrow)
        ],
    )
    own_gate_grad = jnp.sum(gate_sums[:, 0, :].reshape(pairs * halves, head_dim), axis=1)[:heads_here]
    grad_head_gate = lax.dynamic_update_slice_in_dim(
        jnp.zeros((head_count,), F32), own_gate_grad, me * heads_here, 0
    ) * (1.0 - gate_tanh * gate_tanh)
    grad_projected_low, head_sums = heads_back(
        list(zip(*backs)), projected, stats_all, cosine, sine, head_gains, part,
        lambda value: fsdp_share(value, narrow, 4),
    )
    grad_projected_low, *up_pieces = lax.optimization_barrier((grad_projected_low, *up_pieces))
    grad_gate_up_weight = jnp.concatenate(
        [added(gate_pieces), added([piece[:, :up_width] for piece in up_pieces])], axis=1
    )
    grad_out_weight = added([piece[:, up_width:] for piece in up_pieces])
    partial_normed, grad_text_weight = lax.optimization_barrier(
        (times_transposed(grad_projected_low, own_qkv).astype(BF16), grad_text_weight)
    )
    grad_normed = lax.psum_scatter(partial_normed, "fsdp", scatter_dimension=0, tiled=True)

    def lane_rows(value):
        return value.reshape(-1, 128)

    group = lax.axis_index("z") * 2 + lax.axis_index("core")
    columns_here = jnp.stack(
        [narrowed(value, 1) for value in (head_sums[0], head_sums[2], own_gain_four, head_sums[1], head_sums[3])]
    )
    here = (jnp.arange(narrow, dtype=jnp.int32) == me)[None, :, None]
    placed = lane_rows(jnp.where(here, columns_here[:, None, :], 0.0))
    cond_rows_here = lane_rows(jnp.where(me == 0, cond_low.astype(F32), 0.0))
    gate_row = jnp.pad(grad_head_gate, (0, 128 - head_count)).reshape(1, 128)
    ready = [lane_rows(grad_gain_one), lane_rows(grad_gain_five), lane_rows(grad_gain_six), placed, gate_row]
    later = [*grad_gate_attend, *grad_scale_feed, *grad_gate_feed, cond_rows_here]
    ready = lax.optimization_barrier(tuple(ready))
    qkv_grad = outer_sum(normed_all, grad_projected_low).astype(BF16).reshape(deep, 2, model_width // wide, 3 * part_pad)
    own_grad, other_grad = by_core(qkv_grad[:, 0], qkv_grad[:, 1])
    own_grad = (own_grad.astype(F32) + core_swap(other_grad).astype(F32)).astype(BF16)
    own_pieces = z_pieces(own_grad, deep)
    own_pieces[0], grad_text_columns, grad_text_weight = lax.optimization_barrier(
        (own_pieces[0], grad_text_columns, grad_text_weight)
    )
    ordered = relative(grad_text_columns.reshape(text_total, narrow, 2 * part), me, 1)
    grad_text_ordered = (
        ordered.reshape(text_total, narrow, 2, part).transpose(0, 2, 1, 3).reshape(text_total, 2 * model_width)
    )
    grad_text_slice = times_transposed(grad_text_ordered, text_weight).astype(BF16)
    came_text = exchange(
        grad_text_slice.reshape(image_count, narrow, caption_local, text_cols)
        .transpose(1, 0, 2, 3)
        .reshape(narrow, text_local, text_cols),
        "fsdp",
    )
    place = (lax.axis_index("z") * 2 + lax.axis_index("core")) * narrow + me
    grad_text_weight = (
        relative(grad_text_weight.reshape(-1, narrow, 2 * part), place // wide, 1)
        .reshape(-1, narrow, 2, part)
        .transpose(0, 2, 1, 3)
        .reshape(-1, 2 * model_width)
        .astype(F32)
    )
    grad_text_normed = (
        came_text
        .transpose(1, 0, 2)
        .reshape(text_local, caption_width)
        .astype(F32)
    )
    text_state_unit = text_in * text_inverse
    grad_text_gain = jnp.sum(grad_text_normed * text_state_unit, axis=0)
    grad_text = (
        norm_pull(grad_text_normed * text_gain, text_state_unit, text_inverse)
        .astype(BF16)
        .reshape(image_count, caption_local, caption_width)
    )

    grad_text, grad_text_gain, grad_text_weight, *own_pieces = lax.optimization_barrier(
        (grad_text, grad_text_gain, grad_text_weight, *own_pieces)
    )
    own_grad = added(own_pieces)
    own_exchanged = exchange(narrowed(own_grad.astype(BF16), 3).reshape(narrow, -1, 3 * part), "fsdp")
    grad_normed, own_exchanged = lax.optimization_barrier((grad_normed, own_exchanged))
    grad_qkv_weight = (
        own_exchanged.reshape(narrow, -1, 3, part)
        .transpose(1, 2, 0, 3)
        .reshape(-1, 3 * model_width)
        .astype(F32)
    )
    grad_normed = grad_normed.astype(F32)

    token_unit = token_in * token_inverse
    scale_attend = 1.0 + per_token(0)
    grad_normed_y = grad_normed * scale_attend
    grad_gain_zero = jnp.sum(grad_normed_y * token_unit, axis=0)
    grad_scale_attend = per_image(grad_normed * token_unit * norm_gains[0])
    grad_tokens = (
        grad_hidden + norm_pull(grad_normed_y * norm_gains[0], token_unit, token_inverse)
    ).astype(BF16)
    lanes_of_row = model_width // 128
    def row_range(first, count):
        return list(range(first * lanes_of_row, (first + count) * lanes_of_row))

    gate_at = 9 * lanes_of_row
    text_rows = caption_width // 128
    grad_gains, grad_shifts, gate_row, grad_text_gain, slots, cond_slots = finish(
        [lane_rows(grad_gain_zero), *ready, lane_rows(grad_text_gain)],
        [*grad_scale_attend, *later],
        [
            (norm_gains.shape, row_range(0, 2) + row_range(4, 3) + row_range(2, 2)),
            (norm_shifts.shape, row_range(7, 2)),
            ((1, 128), [gate_at]),
            ((text_rows, 128), list(range(gate_at + 1, gate_at + 1 + text_rows))),
        ],
        image_count, narrow, wide, 5,
    )
    slots = slots.reshape(wide * image_count, -1)
    cond_slots = cond_slots.reshape(wide * image_count, -1)
    grad_head_gate = gate_row[0, :head_count]
    grad_text_gain = grad_text_gain.reshape(-1)
    ada_rows = cond_rows // wide
    own_cond = lax.dynamic_slice_in_dim(cond_slots, (group * narrow + me) * ada_rows, ada_rows, 1)
    grad_ada_weight = exact_outer(own_cond, slots)
    grad_ada_bias = jnp.sum(slots, axis=0)
    return (
        result[None],
        grad_tokens[None],
        grad_text[None],
        grad_ada_weight,
        grad_qkv_weight,
        grad_out_weight,
        grad_text_weight,
        grad_gate_up_weight,
        grad_down_weight,
        grad_ada_bias,
        grad_gains,
        grad_shifts,
        grad_text_gain,
        grad_head_gate,
    )


def solution(mesh):
    wide, narrow = mesh.devices.shape
    fine = Mesh(mesh.devices.reshape(wide // 2, 2, narrow), ("z", "core", "fsdp"))
    groups = ("z", "core")
    every = ("z", "core", "fsdp")
    placed = (
        P(groups, "fsdp", None),
        P(groups, "fsdp", None),
        P(groups, None, "fsdp", None),
        P(groups, None, None),
        P(groups, None, None),
        P("fsdp", None),
        P(),
        P("fsdp", None),
        P("fsdp", None),
        P("fsdp", None),
        P("fsdp", None),
        P("fsdp", None),
        P(),
        P(),
        P(),
        P(),
    )
    return jax.shard_map(
        shards,
        mesh=fine,
        in_specs=placed,
        out_specs=(
            P(groups, "fsdp", None),
            P(groups, "fsdp", None),
            P(groups, None, "fsdp", None),
            P(every, None),
            P(every, None),
            P(every, None),
            P(every, None),
            P(every, None),
            P(every, None),
            P(),
            P(),
            P(),
            P(),
            P(),
        ),
        check_vma=False,
    )
```

```python
import functools

import jax
import jax.numpy as jnp
from jax import lax
from jax.experimental import pallas as pl
from jax.experimental.pallas import tpu as pltpu
from jax.sharding import Mesh
from jax.sharding import PartitionSpec as P

EPS = 1e-05
HIGHEST_PRECISION = lax.Precision.HIGHEST
MASKED = -1e30
LOG2E = 1.4426950408889634
FIRST_PATCHES = 16 * 12**2
FIRST_MOST = FIRST_PATCHES + 96
QBLOCK = 256
ROW_BLOCK = 384
BF16 = jnp.bfloat16
F32 = jnp.float32
VMEM_LIMIT = 60 * 1024 * 1024


def round_up(value, step):
    return -(-value // step) * step


def low_product(left, right):
    return jnp.dot(left, right, preferred_element_type=F32)


def times_transposed(left, right):
    return lax.dot_general(left, right, (((1,), (1,)), ((), ())), preferred_element_type=F32)


def outer_sum(left, right):
    return lax.dot_general(left, right, (((0,), (0,)), ((), ())), preferred_element_type=F32)


def exact_outer(left, right):
    return lax.dot_general(
        left, right, (((0,), (0,)), ((), ())), precision=HIGHEST_PRECISION, preferred_element_type=F32
    )


def exact_transposed(left, right):
    return lax.dot_general(
        left, right, (((1,), (1,)), ((), ())), precision=HIGHEST_PRECISION, preferred_element_type=F32
    )


def row_mean(value):
    return jnp.mean(value, axis=-1, keepdims=True)


def inverse_rms(value):
    return lax.rsqrt(row_mean(value * value) + EPS)


def norm_pull(grad, unit, inverse):
    return (grad - unit * row_mean(grad * unit)) * inverse


def token_layout(image_sizes, position, image_count):
    start = jnp.int32(0)
    image_index = jnp.full(position.shape, image_count, jnp.int32)
    token_row = jnp.zeros(position.shape, jnp.int32)
    token_col = jnp.zeros(position.shape, jnp.int32)
    for i in range(image_count):
        width = image_sizes[i, 1] + 1
        end = start + image_sizes[i, 0] * width
        inside = (position >= start) & (position < end)
        offset = position - start
        image_index = jnp.where(inside, i, image_index)
        token_row = jnp.where(inside, offset // width, token_row)
        token_col = jnp.where(inside, offset % width, token_col)
        start = end
    return image_index, token_row, token_col


def rope_tables(token_row, token_col, head_dim):
    quarter = head_dim // 4
    pair = (jnp.arange(128, dtype=jnp.int32) % head_dim) // 2
    frequency = 10000.0 ** (-(pair % quarter).astype(F32) / quarter)
    place = jnp.where(
        (pair < quarter)[None, :], token_row.astype(F32)[:, None], token_col.astype(F32)[:, None]
    )
    angles = place * frequency[None, :]
    even = (jnp.arange(128, dtype=jnp.int32) % 2 == 0)[None, :]
    return jnp.cos(angles), jnp.where(even, -jnp.sin(angles), jnp.sin(angles))


def swap_pairs(value):
    width = value.shape[1]
    even = lax.broadcasted_iota(jnp.int32, value.shape, 1) % 2 == 0
    return jnp.where(even, pltpu.roll(value, width - 1, 1), pltpu.roll(value, 1, 1))


def wide_table(table, width):
    return jnp.concatenate([table] * (width // table.shape[1]), axis=1)


def pack_columns(columns):
    rows = columns[0].shape[0]
    lane = lax.broadcasted_iota(jnp.int32, (rows, 128), 1)
    packed = jnp.zeros((rows, 128), F32)
    for i, column in enumerate(columns):
        packed = jnp.where(lane == i, column, packed)
    return jnp.transpose(packed)[:8, :]


def as_columns(rows_list):
    width = rows_list[0].shape[1]
    stacked = jnp.concatenate(
        rows_list + [jnp.zeros((128 - len(rows_list), width), F32)], axis=0
    )
    return jnp.transpose(stacked)


def real_lanes(shape, part):
    return lax.broadcasted_iota(jnp.int32, shape, 1) < part


def own_stats(value, part):
    mean = jnp.sum(value, axis=1, keepdims=True) * (1.0 / part)
    centred = value - mean
    if value.shape[1] != part:
        centred = jnp.where(real_lanes(value.shape, part), centred, 0.0)
    return mean, jnp.sum(centred * centred, axis=1, keepdims=True)


def joined_stats(stats_ref, part, slot):
    narrow = stats_ref.shape[0]
    means = [stats_ref[i, 2 * slot : 2 * slot + 1, :] for i in range(narrow)]
    squares = [stats_ref[i, 2 * slot + 1 : 2 * slot + 2, :] for i in range(narrow)]
    mean = functools.reduce(jnp.add, means) * (1.0 / narrow)
    square = functools.reduce(jnp.add, squares)
    square = square + part * functools.reduce(jnp.add, [(m - mean) * (m - mean) for m in means])
    return mean, lax.rsqrt(square * (1.0 / (narrow * part)) + EPS)


def stats_kernel(part, slots, projected_ref, out_ref):
    padded = projected_ref.shape[1] // slots
    columns = []
    for slot in range(slots):
        columns += own_stats(projected_ref[:, slot * padded : (slot + 1) * padded], part)
    out_ref[...] = pack_columns(columns)


def column_stats(projected, part, padded, slots):
    rows = projected.shape[0]
    return pl.pallas_call(
        functools.partial(stats_kernel, part, slots),
        grid=(pl.cdiv(rows, ROW_BLOCK),),
        in_specs=[pl.BlockSpec((ROW_BLOCK, slots * padded), lambda i: (i, 0))],
        out_specs=pl.BlockSpec((8, ROW_BLOCK), lambda i: (0, i)),
        out_shape=jax.ShapeDtypeStruct((8, rows), F32),
        compiler_params=pltpu.CompilerParams(vmem_limit_bytes=VMEM_LIMIT),
        cost_estimate=pl.CostEstimate(flops=10 * rows * slots * padded, bytes_accessed=4 * rows * slots * padded, transcendentals=0),
    )(projected)


def heads_kernel(part, query_scale, projected_ref, stats_ref, cos_ref, sin_ref, gains_ref, shifts_ref, out_ref):
    padded = projected_ref.shape[1] // 3
    cosine = wide_table(cos_ref[...], padded)
    sine = wide_table(sin_ref[...], padded)
    columns = as_columns([*joined_stats(stats_ref, part, 0), *joined_stats(stats_ref, part, 1)])
    for slot in range(3):
        place = slice(slot * padded, (slot + 1) * padded)
        value = projected_ref[:, place]
        if slot < 2:
            value = (value - columns[:, 2 * slot : 2 * slot + 1]) * columns[:, 2 * slot + 1 : 2 * slot + 2]
            value = value * gains_ref[slot : slot + 1, :] + shifts_ref[slot : slot + 1, :]
            value = value * cosine + swap_pairs(value) * sine
            if slot == 0:
                value = value * query_scale
        out_ref[:, place] = value.astype(BF16)


def make_heads(projected, stats, cosine, sine, gains, shifts, part, query_scale):
    rows, triple = projected.shape
    padded = triple // 3
    narrow = stats.shape[0]
    return pl.pallas_call(
        functools.partial(heads_kernel, part, query_scale),
        grid=(pl.cdiv(rows, ROW_BLOCK),),
        in_specs=[
            pl.BlockSpec((ROW_BLOCK, triple), lambda i: (i, 0)),
            pl.BlockSpec((narrow, 8, ROW_BLOCK), lambda i: (0, 0, i)),
            pl.BlockSpec((ROW_BLOCK, 128), lambda i: (i, 0)),
            pl.BlockSpec((ROW_BLOCK, 128), lambda i: (i, 0)),
            pl.BlockSpec((2, padded), lambda i: (0, 0)),
            pl.BlockSpec((2, padded), lambda i: (0, 0)),
        ],
        out_specs=pl.BlockSpec((ROW_BLOCK, triple), lambda i: (i, 0)),
        out_shape=jax.ShapeDtypeStruct((rows, triple), BF16),
        compiler_params=pltpu.CompilerParams(vmem_limit_bytes=VMEM_LIMIT),
        cost_estimate=pl.CostEstimate(flops=40 * rows * triple, bytes_accessed=6 * rows * triple, transcendentals=0),
    )(projected, stats, cosine, sine, gains, shifts)


def turned_back(refs, cosine, sine):
    grad = jnp.concatenate([ref[...].astype(F32) for ref in refs], axis=1)
    return grad * cosine - swap_pairs(grad) * sine


def grad_stats_kernel(rows, part, pairs, *refs):
    dq_refs, dk_refs = refs[:pairs], refs[pairs : 2 * pairs]
    projected_ref, stats_ref, cos_ref, sin_ref, gains_ref, out_ref, sums_ref = refs[2 * pairs :]
    step = pl.program_id(0)
    padded = 128 * pairs
    cosine = wide_table(cos_ref[...], padded)
    sine = wide_table(sin_ref[...], padded)
    height = cos_ref.shape[0]
    inside = step * height + lax.broadcasted_iota(jnp.int32, (height, 1), 0) < rows

    @pl.when(step == 0)
    def _():
        sums_ref[...] = jnp.zeros_like(sums_ref)

    columns = as_columns([*joined_stats(stats_ref, part, 0), *joined_stats(stats_ref, part, 1)])
    packed = []
    for slot, grads in enumerate((dq_refs, dk_refs)):
        grad = jnp.where(inside, turned_back(grads, cosine, sine), 0.0)
        unit = (projected_ref[:, slot * padded : (slot + 1) * padded] - columns[:, 2 * slot : 2 * slot + 1])
        unit = jnp.where(inside, unit * columns[:, 2 * slot + 1 : 2 * slot + 2], 0.0)
        both = grad * unit
        sums_ref[2 * slot : 2 * slot + 1, :] += jnp.sum(both, axis=0, keepdims=True)
        sums_ref[2 * slot + 1 : 2 * slot + 2, :] += jnp.sum(grad, axis=0, keepdims=True)
        gain = gains_ref[slot : slot + 1, :]
        packed.append(jnp.sum(grad * gain, axis=1, keepdims=True))
        packed.append(jnp.sum(both * gain, axis=1, keepdims=True))
    out_ref[...] = pack_columns(packed)


def heads_back_kernel(part, pairs, *refs):
    dq_refs, dk_refs, dv_refs = refs[:pairs], refs[pairs : 2 * pairs], refs[2 * pairs : 3 * pairs]
    projected_ref, stats_ref, totals_ref, cos_ref, sin_ref, gains_ref, out_ref = refs[3 * pairs :]
    padded = 128 * pairs
    narrow = stats_ref.shape[0]
    cosine = wide_table(cos_ref[...], padded)
    sine = wide_table(sin_ref[...], padded)
    means = [
        functools.reduce(jnp.add, [totals_ref[i, j : j + 1, :] for i in range(narrow)]) * (1.0 / (narrow * part))
        for j in range(4)
    ]
    columns = as_columns([*joined_stats(stats_ref, part, 0), *joined_stats(stats_ref, part, 1), *means])
    for slot, grads in enumerate((dq_refs, dk_refs)):
        grad = turned_back(grads, cosine, sine) * gains_ref[slot : slot + 1, :]
        inverse = columns[:, 2 * slot + 1 : 2 * slot + 2]
        unit = (projected_ref[:, slot * padded : (slot + 1) * padded] - columns[:, 2 * slot : 2 * slot + 1]) * inverse
        grad = grad - columns[:, 4 + 2 * slot : 5 + 2 * slot] - unit * columns[:, 5 + 2 * slot : 6 + 2 * slot]
        grad = grad * inverse
        if padded != part:
            grad = jnp.where(real_lanes(grad.shape, part), grad, 0.0)
        out_ref[:, slot * padded : (slot + 1) * padded] = grad.astype(BF16)
    for pair, ref in enumerate(dv_refs):
        out_ref[:, 2 * padded + 128 * pair : 2 * padded + 128 * (pair + 1)] = ref[...]


def heads_back(grads, projected, stats, cosine, sine, gains, part, share):
    rows, triple = projected.shape
    padded = triple // 3
    pairs = padded // 128
    narrow = stats.shape[0]
    pair_spec = pl.BlockSpec((ROW_BLOCK, 128), lambda i: (i, 0))
    two_spec = pl.BlockSpec((ROW_BLOCK, 2 * padded), lambda i: (i, 0))
    stat_spec = pl.BlockSpec((narrow, 8, ROW_BLOCK), lambda i: (0, 0, i))
    gain_spec = pl.BlockSpec((2, padded), lambda i: (0, 0))
    own, sums = pl.pallas_call(
        functools.partial(grad_stats_kernel, rows, part, pairs),
        grid=(pl.cdiv(rows, ROW_BLOCK),),
        in_specs=[pair_spec] * (2 * pairs) + [two_spec, stat_spec, pair_spec, pair_spec, gain_spec],
        out_specs=[
            pl.BlockSpec((8, ROW_BLOCK), lambda i: (0, i)),
            pl.BlockSpec((8, padded), lambda i: (0, 0)),
        ],
        out_shape=[jax.ShapeDtypeStruct((8, rows), F32), jax.ShapeDtypeStruct((8, padded), F32)],
        compiler_params=pltpu.CompilerParams(vmem_limit_bytes=VMEM_LIMIT),
        cost_estimate=pl.CostEstimate(flops=4 * rows * triple, bytes_accessed=rows * triple // 16, transcendentals=0),
    )(*grads[0], *grads[1], projected, stats, cosine, sine, gains)
    totals = share(own)
    out = pl.pallas_call(
        functools.partial(heads_back_kernel, part, pairs),
        grid=(pl.cdiv(rows, ROW_BLOCK),),
        in_specs=[pair_spec] * (3 * pairs) + [two_spec, stat_spec, stat_spec, pair_spec, pair_spec, gain_spec],
        out_specs=pl.BlockSpec((ROW_BLOCK, triple), lambda i: (i, 0)),
        out_shape=jax.ShapeDtypeStruct((rows, triple), BF16),
        compiler_params=pltpu.CompilerParams(vmem_limit_bytes=VMEM_LIMIT),
        cost_estimate=pl.CostEstimate(flops=4 * rows * triple, bytes_accessed=rows * triple // 16, transcendentals=0),
    )(*grads[0], *grads[1], *grads[2], projected, stats, totals, cosine, sine, gains)
    return out, sums


def head_lanes(rows, half, head_dim):
    lane = lax.broadcasted_iota(jnp.int32, (rows, 128), 1)
    return (lane >= half * head_dim) & (lane < (half + 1) * head_dim)


def softmax_product(pieces):
    maximum = functools.reduce(jnp.maximum, [jnp.max(s, axis=1, keepdims=True) for s, _ in pieces])
    total, result = 0.0, 0.0
    for scores, values in pieces:
        weight = jnp.exp2(scores - maximum)
        total = total + jnp.sum(weight, axis=1, keepdims=True)
        result = result + low_product(weight.astype(BF16), values)
    return result * (1.0 / total), maximum + jnp.log2(total)


def attend_kernel(
    head_dim, first, most, caption, image_count,
    gate_ref, q_ref, k_ref, v_ref, tk_ref, tv_ref, column_ref, row_ref,
    mixed_ref, self_ref, cross_ref, stats_ref,
):
    count = q_ref.shape[0]
    halves = 128 // head_dim

    def emit(at, rows, outs):
        lanes = [head_lanes(rows, half, head_dim) for half in range(halves)]
        own, cross, gated = 0.0, 0.0, 0.0
        columns = []
        for half, (own_out, own_total, cross_out, cross_total) in enumerate(outs):
            gate = gate_ref[0, half]
            own = own + jnp.where(lanes[half], own_out, 0.0)
            cross = cross + jnp.where(lanes[half], cross_out, 0.0)
            gated = gated + jnp.where(lanes[half], gate * cross_out, 0.0)
            columns += [own_total, cross_total]
        self_ref[pl.ds(at, rows), :] = own
        cross_ref[pl.ds(at, rows), :] = cross
        mixed_ref[pl.ds(at, rows), :] = (own + gated).astype(BF16)
        lane = lax.broadcasted_iota(jnp.int32, (rows, 128), 1)
        packed = jnp.zeros((rows, 128), F32)
        for i, column in enumerate(columns):
            packed = jnp.where(lane == i, column, packed)
        stats_ref[:, pl.ds(at, rows)] = jnp.transpose(packed)[:8, :]

    def clean(block, carry):
        at = pl.multiple_of(block * QBLOCK, QBLOCK)
        queries = q_ref[pl.ds(at, QBLOCK), :]
        outs = []
        for half in range(halves):
            q = jnp.where(head_lanes(QBLOCK, half, head_dim), queries, jnp.zeros_like(queries))
            bias = jnp.where(row_ref[0:1, first:most] == 0, 0.0, MASKED)
            own_out, own_total = softmax_product([
                (times_transposed(q, k_ref[0:first, :]), v_ref[0:first, :]),
                (times_transposed(q, k_ref[first:most, :]) + bias, v_ref[first:most, :]),
            ])
            cross_out, cross_total = softmax_product(
                [(times_transposed(q, tk_ref[0:caption, :]), tv_ref[0:caption, :])]
            )
            outs.append((own_out, own_total, cross_out, cross_total))
        emit(at, QBLOCK, outs)
        return carry

    lax.fori_loop(0, first // QBLOCK, clean, 0)
    rest = count - first
    queries = q_ref[first:count, :]
    image = column_ref[first:count, :]
    outs = []
    for half in range(halves):
        q = jnp.where(head_lanes(rest, half, head_dim), queries, jnp.zeros_like(queries))
        own_out, own_total = softmax_product([
            (jnp.where(image == row_ref[0:1, :], times_transposed(q, k_ref[...]), MASKED), v_ref[...])
        ])
        scores = times_transposed(q, tk_ref[...])
        owner = lax.broadcasted_iota(jnp.int32, (1, scores.shape[1]), 1) // caption
        scores = jnp.where((image == owner) | (image == image_count), scores, MASKED)
        cross_out, cross_total = softmax_product([(scores, tv_ref[...])])
        outs.append((own_out, own_total, cross_out, cross_total))
    emit(first, rest, outs)


def attend(pair, gates, packed, text_packed, column, row, head_dim, image_count):
    count, texts = packed.shape[0], text_packed.shape[0]
    pairs = packed.shape[1] // 384
    halves = 128 // head_dim
    out = pl.BlockSpec((count, 128), lambda i: (0, 0))
    most = min(round_up(FIRST_MOST, 128), count)
    flops = 4 * count * (count + texts) * 128
    return pl.pallas_call(
        functools.partial(
            attend_kernel, head_dim, FIRST_PATCHES, most, texts // image_count, image_count
        ),
        grid=(1,),
        in_specs=[
            pl.BlockSpec((None, 1, halves), lambda i: (pair, 0, 0), memory_space=pltpu.SMEM),
            pl.BlockSpec((count, 128), lambda i: (0, pair)),
            pl.BlockSpec((count, 128), lambda i: (0, pairs + pair)),
            pl.BlockSpec((count, 128), lambda i: (0, 2 * pairs + pair)),
            pl.BlockSpec((texts, 128), lambda i: (0, pair)),
            pl.BlockSpec((texts, 128), lambda i: (0, pairs + pair)),
            pl.BlockSpec((count, 1), lambda i: (0, 0)),
            pl.BlockSpec((1, count), lambda i: (0, 0)),
        ],
        out_specs=[out, out, out, pl.BlockSpec((8, count), lambda i: (0, 0))],
        out_shape=[
            jax.ShapeDtypeStruct((count, 128), BF16),
            jax.ShapeDtypeStruct((count, 128), F32),
            jax.ShapeDtypeStruct((count, 128), F32),
            jax.ShapeDtypeStruct((8, count), F32),
        ],
        compiler_params=pltpu.CompilerParams(vmem_limit_bytes=VMEM_LIMIT),
        cost_estimate=pl.CostEstimate(flops=flops, bytes_accessed=20 * count * 128, transcendentals=2 * count * count),
    )(gates.reshape(pairs, 1, halves), packed, packed, packed, text_packed, text_packed, column, row)


def gate_lanes(gate_ref, head_dim):
    lane = lax.broadcasted_iota(jnp.int32, (1, 128), 1)
    gates = jnp.zeros((1, 128), F32)
    for half in range(128 // head_dim):
        gates = jnp.where(lane // head_dim == half, gate_ref[0, half], gates)
    return gates


def head_picks(head_dim):
    return (
        lax.broadcasted_iota(jnp.int32, (8, 128), 1) // head_dim
        == lax.broadcasted_iota(jnp.int32, (8, 128), 0)
    ).astype(F32)


def rows_back(head_dim, queries, outs, delta, stats, offset, keys, values, key_sum, value_sum, spans):
    rows = queries.shape[0]
    halves = 128 // head_dim
    zero = jnp.zeros((rows, 128), BF16)
    lanes = [head_lanes(rows, half, head_dim) for half in range(halves)]
    q_heads = [jnp.where(lane, queries, zero) for lane in lanes]
    out_heads = [jnp.where(lane, outs, zero) for lane in lanes]
    q_stack = jnp.concatenate(q_heads, axis=0)
    out_stack = jnp.concatenate(out_heads, axis=0)
    dq = [0.0] * halves
    for low, high, mask in spans:
        key_part = keys[low:high, :]
        value_part = values[low:high, :]
        probs, grads = [], []
        for half in range(halves):
            scores = mask(times_transposed(key_part, q_heads[half]))
            prob = jnp.exp2(scores - stats[2 * half + offset : 2 * half + offset + 1, :])
            dprob = times_transposed(value_part, out_heads[half])
            dscore = (prob * (dprob - delta[half : half + 1, :])).astype(BF16)
            probs.append(prob.astype(BF16))
            grads.append(dscore)
            dq[half] = dq[half] + outer_sum(dscore, key_part)
        value_sum[low:high, :] += low_product(jnp.concatenate(probs, axis=1), out_stack)
        key_sum[low:high, :] += low_product(jnp.concatenate(grads, axis=1), q_stack)
    total = 0.0
    for half in range(halves):
        total = total + jnp.where(lanes[half], dq[half], 0.0)
    return total


def cross_back_kernel(
    head_dim, first, caption, image_count, scale,
    gate_ref, q_ref, tk_ref, tv_ref, row_ref, grad_ref, cross_ref, stats_ref,
    dq_ref, dtk_ref, dtv_ref, gate_grad_ref, dtk_sum, dtv_sum,
):
    count = q_ref.shape[0]
    for total in (dtk_sum, dtv_sum, gate_grad_ref):
        total[...] = jnp.zeros_like(total)
    gates = gate_lanes(gate_ref, head_dim)
    picks = head_picks(head_dim)

    def part(at, rows, spans):
        wide = grad_ref[pl.ds(at, rows), :].astype(F32)
        cross = cross_ref[pl.ds(at, rows), :]
        gate_grad_ref[0:1, :] += jnp.sum(wide * cross, axis=0, keepdims=True)
        gated = (wide * gates).astype(BF16)
        delta = exact_transposed(picks, gated.astype(F32) * cross)
        dq = rows_back(
            head_dim, q_ref[pl.ds(at, rows), :], gated, delta, stats_ref[:, pl.ds(at, rows)], 1,
            tk_ref, tv_ref, dtk_sum, dtv_sum, spans,
        )
        dq_ref[pl.ds(at, rows), :] = (dq * scale).astype(BF16)

    def clean(block, carry):
        part(pl.multiple_of(block * QBLOCK, QBLOCK), QBLOCK, [(0, caption, lambda scores: scores)])
        return carry

    lax.fori_loop(0, first // QBLOCK, clean, 0)
    image = row_ref[0:1, first:count]
    owner = lax.broadcasted_iota(jnp.int32, (tk_ref.shape[0], 1), 0) // caption
    allowed = (owner == image) | (image == image_count)
    part(first, count - first, [(0, tk_ref.shape[0], lambda scores: jnp.where(allowed, scores, MASKED))])
    dtk_ref[...] = (dtk_sum[...] * (1.0 / LOG2E)).astype(BF16)
    dtv_ref[...] = dtv_sum[...].astype(BF16)


def cross_back(pair, gates, packed, text_packed, row, grad, cross, stats, head_dim, image_count, scale):
    count, texts = packed.shape[0], text_packed.shape[0]
    pairs = packed.shape[1] // 384
    halves = 128 // head_dim
    tokens = pl.BlockSpec((count, 128), lambda i: (0, pair))
    own_tokens = pl.BlockSpec((count, 128), lambda i: (0, 0))
    captions = pl.BlockSpec((texts, 128), lambda i: (0, 0))
    flops = 10 * count * texts * 128
    return pl.pallas_call(
        functools.partial(cross_back_kernel, head_dim, FIRST_PATCHES, texts // image_count, image_count, scale),
        grid=(1,),
        in_specs=[
            pl.BlockSpec((None, 1, halves), lambda i: (pair, 0, 0), memory_space=pltpu.SMEM),
            tokens,
            pl.BlockSpec((texts, 128), lambda i: (0, pair)),
            pl.BlockSpec((texts, 128), lambda i: (0, pairs + pair)),
            pl.BlockSpec((1, count), lambda i: (0, 0)),
            tokens,
            own_tokens,
            pl.BlockSpec((8, count), lambda i: (0, 0)),
        ],
        out_specs=[own_tokens, captions, captions, pl.BlockSpec((8, 128), lambda i: (0, 0))],
        out_shape=[
            jax.ShapeDtypeStruct((count, 128), BF16),
            jax.ShapeDtypeStruct((texts, 128), BF16),
            jax.ShapeDtypeStruct((texts, 128), BF16),
            jax.ShapeDtypeStruct((8, 128), F32),
        ],
        scratch_shapes=[pltpu.VMEM((texts, 128), F32), pltpu.VMEM((texts, 128), F32)],
        compiler_params=pltpu.CompilerParams(vmem_limit_bytes=VMEM_LIMIT),
        cost_estimate=pl.CostEstimate(flops=flops, bytes_accessed=12 * count * 128, transcendentals=count * texts),
    )(gates.reshape(pairs, 1, halves), packed, text_packed, text_packed, row, grad, cross, stats)


def self_back_kernel(
    head_dim, first, most, scale,
    q_ref, k_ref, v_ref, column_ref, row_ref, grad_ref, self_ref, stats_ref, more_ref,
    dq_ref, dk_ref, dv_ref, dk_sum, dv_sum,
):
    count = q_ref.shape[0]
    dk_sum[...] = jnp.zeros_like(dk_sum)
    dv_sum[...] = jnp.zeros_like(dv_sum)
    picks = head_picks(head_dim)

    def part(at, rows, spans):
        grad = grad_ref[pl.ds(at, rows), :]
        delta = exact_transposed(picks, grad.astype(F32) * self_ref[pl.ds(at, rows), :])
        dq = rows_back(
            head_dim, q_ref[pl.ds(at, rows), :], grad, delta, stats_ref[:, pl.ds(at, rows)], 0,
            k_ref, v_ref, dk_sum, dv_sum, spans,
        )
        dq_ref[pl.ds(at, rows), :] = (dq * scale + more_ref[pl.ds(at, rows), :].astype(F32)).astype(BF16)

    def clean(block, carry):
        bias = jnp.where(column_ref[first:most, :] == 0, 0.0, MASKED)
        part(
            pl.multiple_of(block * QBLOCK, QBLOCK), QBLOCK,
            [(0, first, lambda scores: scores), (first, most, lambda scores: scores + bias)],
        )
        return carry

    lax.fori_loop(0, first // QBLOCK, clean, 0)
    image = row_ref[0:1, first:count]
    part(first, count - first, [(0, count, lambda scores: jnp.where(column_ref[...] == image, scores, MASKED))])
    dk_ref[...] = (dk_sum[...] * (1.0 / LOG2E)).astype(BF16)
    dv_ref[...] = dv_sum[...].astype(BF16)


def self_back(pair, packed, column, row, grad, own, stats, more, head_dim, scale):
    count = packed.shape[0]
    pairs = packed.shape[1] // 384
    tokens = pl.BlockSpec((count, 128), lambda i: (0, pair))
    out = pl.BlockSpec((count, 128), lambda i: (0, 0))
    most = min(round_up(FIRST_MOST, 128), count)
    flops = 10 * count * count * 128
    return pl.pallas_call(
        functools.partial(self_back_kernel, head_dim, FIRST_PATCHES, most, scale),
        grid=(1,),
        in_specs=[
            tokens,
            pl.BlockSpec((count, 128), lambda i: (0, pairs + pair)),
            pl.BlockSpec((count, 128), lambda i: (0, 2 * pairs + pair)),
            pl.BlockSpec((count, 1), lambda i: (0, 0)),
            pl.BlockSpec((1, count), lambda i: (0, 0)),
            tokens,
            out,
            pl.BlockSpec((8, count), lambda i: (0, 0)),
            out,
        ],
        out_specs=[out, out, out],
        out_shape=[jax.ShapeDtypeStruct((count, 128), BF16)] * 3,
        scratch_shapes=[pltpu.VMEM((count, 128), F32), pltpu.VMEM((count, 128), F32)],
        compiler_params=pltpu.CompilerParams(vmem_limit_bytes=VMEM_LIMIT),
        cost_estimate=pl.CostEstimate(flops=flops, bytes_accessed=30 * count * 128, transcendentals=2 * count * count),
    )(packed, packed, packed, column, row, grad, own, stats, more)


def swiglu_kernel(core_ref, gate_ref, up_ref, out_ref, moved_ref):
    gate = gate_ref[...]
    half = 0.5 * gate
    value = ((half + half * jnp.tanh(half)) * up_ref[...]).astype(BF16)
    out_ref[...] = value
    moved_ref[...] = value


def swiglu(gate_up, core, deep, narrow):
    rows, double = gate_up.shape
    width = double // 2
    blocks = 2 * deep * narrow
    block = width // blocks

    def moved_place(i, core_ref):
        z, c, f = i // (2 * narrow), (i // narrow) % 2, i % narrow
        return (0, ((c + core_ref[0]) % 2) * (deep * narrow) + f * deep + z)

    return pl.pallas_call(
        swiglu_kernel,
        grid_spec=pltpu.PrefetchScalarGridSpec(
            num_scalar_prefetch=1,
            grid=(blocks,),
            in_specs=[
                pl.BlockSpec((rows, block), lambda i, core_ref: (0, i)),
                pl.BlockSpec((rows, block), lambda i, core_ref: (0, blocks + i)),
            ],
            out_specs=[
                pl.BlockSpec((rows, block), lambda i, core_ref: (0, i)),
                pl.BlockSpec((rows, block), moved_place),
            ],
        ),
        out_shape=[jax.ShapeDtypeStruct((rows, width), BF16)] * 2,
        compiler_params=pltpu.CompilerParams(vmem_limit_bytes=VMEM_LIMIT),
        cost_estimate=pl.CostEstimate(flops=6 * rows * width, bytes_accessed=12 * rows * width, transcendentals=rows * width),
    )(core.reshape(1), gate_up, gate_up)


def fsdp_share_kernel(narrow, x_ref, out_ref, send_sem, recv_sem):
    me = lax.axis_index("fsdp")
    barrier = pltpu.get_barrier_semaphore()
    for step in range(1, narrow):
        pl.semaphore_signal(
            barrier, inc=1, device_id={"fsdp": lax.rem(me + step, narrow)}, device_id_type=pl.DeviceIdType.MESH
        )
    pl.semaphore_wait(barrier, narrow - 1)
    copies = []
    for step in range(1, narrow):
        copy = pltpu.make_async_remote_copy(
            src_ref=x_ref,
            dst_ref=out_ref.at[me],
            send_sem=send_sem.at[step],
            recv_sem=recv_sem.at[step],
            device_id={"fsdp": lax.rem(me + step, narrow)},
            device_id_type=pl.DeviceIdType.MESH,
        )
        copy.start()
        copies.append(copy)
    out_ref[me] = x_ref[...]
    for copy in copies:
        copy.wait()


def fsdp_share(value, narrow, collective_id):
    return pl.pallas_call(
        functools.partial(fsdp_share_kernel, narrow),
        in_specs=[pl.BlockSpec(memory_space=pltpu.VMEM)],
        out_specs=pl.BlockSpec(memory_space=pltpu.VMEM),
        out_shape=jax.ShapeDtypeStruct((narrow,) + value.shape, value.dtype),
        scratch_shapes=[pltpu.SemaphoreType.DMA((narrow,)), pltpu.SemaphoreType.DMA((narrow,))],
        compiler_params=pltpu.CompilerParams(collective_id=collective_id, has_side_effects=True),
        cost_estimate=pl.CostEstimate(flops=0, bytes_accessed=8 * narrow * value.size, transcendentals=0),
    )(value)


def place_rows(items, x_ref, chunk, base):
    rows = [(ref, row) for ref in items for row in range(ref.shape[0])]
    at = 0
    while at < len(rows):
        ref, row = rows[at]
        off = at % chunk
        take = min(ref.shape[0] - row, chunk - off)
        x_ref[at // chunk, base + off : base + off + take, :] = ref[row : row + take, :]
        at += take
    while at < x_ref.shape[0] * chunk:
        off = at % chunk
        x_ref[at // chunk, base + off : base + chunk, :] = jnp.zeros((chunk - off, 128), F32)
        at += chunk - off


def finish_kernel(narrow, wide, sum_rows, sum_count, plan, *refs):
    plans, outs = len(plan), len(plan) + 2
    scratch = refs[-7:]
    items, results = refs[: -7 - outs], refs[-7 - outs : -7]
    out_ref, kept_ref, x_ref, first_ref, second_ref, sends, recvs = scratch
    place_rows(items[:sum_count], x_ref, sum_rows, 0)
    place_rows(items[sum_count:], x_ref, x_ref.shape[1] - sum_rows, sum_rows)
    me = lax.axis_index("fsdp")
    group = lax.axis_index("z") * 2 + lax.axis_index("core")
    rows = x_ref.shape[1]
    rest = rows - sum_rows
    barrier = pltpu.get_barrier_semaphore()
    places = [{"fsdp": lax.rem(me + step, narrow)} for step in range(1, narrow)]
    peers = [lax.rem(group + step, wide) for step in range(1, wide)]
    partners = [{"z": peer // 2, "core": peer % 2} for peer in peers]
    for place in places + partners:
        pl.semaphore_signal(barrier, inc=1, device_id=place, device_id_type=pl.DeviceIdType.MESH)
    pl.semaphore_wait(barrier, narrow + wide - 2)

    def send_all(targets, source, target, base):
        copies = []
        for i, place in enumerate(targets):
            copy = pltpu.make_async_remote_copy(
                src_ref=source(i),
                dst_ref=target,
                send_sem=sends.at[base + i],
                recv_sem=recvs.at[base + i],
                device_id=place,
                device_id_type=pl.DeviceIdType.MESH,
            )
            copy.start()
            copies.append(copy)
        return copies

    copies = send_all(places, lambda i: x_ref.at[lax.rem(me + i + 1, narrow)], first_ref.at[me], 0)
    first_ref[me] = x_ref[me]
    for copy in copies:
        copy.wait()
    total = first_ref[0]
    for i in range(1, narrow):
        total = total + first_ref[i]
    second_ref[group] = total
    copies = send_all(partners, lambda i: second_ref.at[group], second_ref.at[group], narrow)
    for copy in copies:
        copy.wait()
    total = second_ref[0, :sum_rows, :]
    for i in range(1, wide):
        total = total + second_ref[i, :sum_rows, :]
    out_ref[me] = total
    for i in range(wide):
        kept_ref[me, i] = second_ref[i, sum_rows:, :]
    copies = send_all(places, lambda i: out_ref.at[me], out_ref.at[me], narrow + wide)
    copies += send_all(places, lambda i: kept_ref.at[me], kept_ref.at[me], 2 * narrow + wide)
    for copy in copies:
        copy.wait()
    for result, source_rows in zip(results[:plans], plan):
        lanes = result.shape[1] // 128
        for i, source in enumerate(source_rows):
            result[i // lanes : i // lanes + 1, i % lanes * 128 : (i % lanes + 1) * 128] = out_ref[
                source // sum_rows, source % sum_rows : source % sum_rows + 1, :
            ]
    slots_ref, cond_ref = results[plans:]
    images = slots_ref.shape[1]
    width = slots_ref.shape[2] // 128
    lanes = width // 4
    targets = [
        (slots_ref, image, part * lanes + lane)
        for part in range(4) for image in range(images) for lane in range(lanes)
    ] + [(cond_ref, image, lane) for image in range(images) for lane in range(cond_ref.shape[2] // 128)]

    def unpack(g, carry):
        for at, (target, image, lane) in enumerate(targets):
            row = kept_ref[at // rest, g, at % rest : at % rest + 1, :]
            target[g, image : image + 1, lane * 128 : (lane + 1) * 128] = row
        return carry

    lax.fori_loop(0, wide, unpack, 0)


def finish(summed, kept, plan, images, narrow, wide, collective_id):
    sum_total = sum(item.shape[0] for item in summed)
    kept_total = sum(item.shape[0] for item in kept)
    sum_rows = round_up(-(-sum_total // narrow), 8)
    kept_rows = round_up(-(-kept_total // narrow), 8)
    rows = sum_rows + kept_rows
    count = 3 * narrow + wide
    cond_width = kept[-1].shape[0] * 128 // images
    slot_width = (kept_total - kept[-1].shape[0]) * 128 // images
    vmem = pl.BlockSpec(memory_space=pltpu.VMEM)
    shapes = [shape for shape, _ in plan] + [(wide, images, slot_width), (wide, images, cond_width)]
    return pl.pallas_call(
        functools.partial(finish_kernel, narrow, wide, sum_rows, len(summed), [source for _, source in plan]),
        in_specs=[vmem] * (len(summed) + len(kept)),
        out_specs=[vmem] * len(shapes),
        out_shape=[jax.ShapeDtypeStruct(shape, F32) for shape in shapes],
        scratch_shapes=[
            pltpu.VMEM((narrow, sum_rows, 128), F32),
            pltpu.VMEM((narrow, wide, kept_rows, 128), F32),
            pltpu.VMEM((narrow, rows, 128), F32),
            pltpu.VMEM((narrow, rows, 128), F32),
            pltpu.VMEM((wide, rows, 128), F32),
            pltpu.SemaphoreType.DMA((count,)),
            pltpu.SemaphoreType.DMA((count,)),
        ],
        compiler_params=pltpu.CompilerParams(collective_id=collective_id, has_side_effects=True),
    )(*summed, *kept)


def exchange(blocks, axis):
    return lax.all_to_all(blocks, axis, 0, 0, tiled=True)


def core_swap(value):
    return lax.ppermute(value, "core", [(0, 1), (1, 0)])


def by_core(low, high):
    first = lax.axis_index("core") == 0
    return jnp.where(first, low, high), jnp.where(first, high, low)


def in_core_order(own, other):
    first = lax.axis_index("core") == 0
    return jnp.where(first, own, other), jnp.where(first, other, own)


def chip_sum(own_left, other_left, right):
    came = core_swap(outer_sum(other_left, right).astype(BF16))
    return (outer_sum(own_left, right) + came.astype(F32)).astype(BF16)


def fsdp_sum(both):
    return lax.psum_scatter(both, "fsdp", scatter_dimension=0, tiled=True)


def z_pieces(blocks, deep):
    me = lax.axis_index("z")
    return [lax.dynamic_index_in_dim(blocks, me, 0, keepdims=False)] + [
        lax.ppermute(
            lax.dynamic_index_in_dim(blocks, me ^ step, 0, keepdims=False), "z", [(i, i ^ step) for i in range(deep)]
        )
        for step in range(1, deep)
    ]


def added(pieces):
    return functools.reduce(jnp.add, [piece.astype(F32) for piece in pieces])


def to_all(block, narrow):
    return [
        lax.ppermute(block, "fsdp", [(i, i ^ step) for i in range(narrow)]) for step in range(1, narrow)
    ]


def relative(blocks, me, axis):
    return jnp.concatenate(
        [lax.dynamic_slice_in_dim(blocks, me ^ step, 1, axis) for step in range(blocks.shape[axis])], axis=axis
    )


def device_columns(value, deep, narrow):
    rows, width = value.shape
    block = width // (2 * deep * narrow)
    core = lax.axis_index("core")
    target = jnp.arange(width, dtype=jnp.int32)
    c, f, z, r = (
        target // (narrow * deep * block), target // (deep * block) % narrow, target // block % deep, target % block,
    )
    c = (c + core) % 2
    source = ((z * 2 + c) * narrow + f) * block + r
    pick = (jnp.arange(width, dtype=jnp.int32)[:, None] == source[None, :]).astype(BF16)
    moved = low_product(value, pick).astype(BF16)
    return moved[:, : width // 2], moved[:, width // 2 :]


def whole_weight(shard):
    rows = shard.shape[0] // 2
    half = lax.dynamic_slice_in_dim(shard, lax.axis_index("core") * rows, rows, 0)
    return lax.all_gather(half, ("fsdp", "core"), axis=0, tiled=True)


def shards(
    tokens,
    cotangent,
    text_states,
    conditioning,
    image_sizes,
    ada_weight,
    ada_bias,
    qkv_weight,
    out_weight,
    text_weight,
    gate_up_weight,
    down_weight,
    norm_gains,
    norm_shifts,
    text_gain,
    head_gate,
):
    model_width = tokens.shape[2]
    head_count = head_gate.shape[0]
    head_dim = model_width // head_count
    image_count = text_states.shape[1]
    caption_local = text_states.shape[2]
    caption_width = text_states.shape[3]
    local_tok = tokens.shape[1]
    deep = lax.axis_size("z")
    narrow = lax.axis_size("fsdp")
    wide = 2 * deep
    me = lax.axis_index("fsdp")
    group_tok = local_tok * narrow
    caption_full = caption_local * narrow
    score_scale = head_dim ** (-0.5)
    text_total = image_count * caption_full
    text_local = image_count * caption_local
    part = model_width // narrow
    part_pad = round_up(part, 128)
    heads_here = head_count // narrow
    pairs = part_pad // 128
    halves = 128 // head_dim

    group_sizes = image_sizes[0]
    position = me * local_tok + jnp.arange(local_tok, dtype=jnp.int32)
    image_index = token_layout(group_sizes, position, image_count)[0]
    key_image, key_row, key_col = token_layout(
        group_sizes, jnp.arange(group_tok, dtype=jnp.int32), image_count
    )
    member = [(image_index == i).astype(F32)[:, None] for i in range(image_count)]
    cosine, sine = rope_tables(key_row, key_col, head_dim)

    cond_low = jax.nn.silu(conditioning[0].astype(F32)).astype(BF16)
    cond_rows = ada_weight.shape[0]
    cond_part = lax.dynamic_slice_in_dim(cond_low, me * cond_rows, cond_rows, 1)
    modulation_part = low_product(cond_part, ada_weight)
    modulation = (
        jnp.sum(fsdp_share(modulation_part.reshape(-1, 128), narrow, 0), axis=0).reshape(modulation_part.shape)
        + ada_bias
    )

    def per_token(index):
        rows = modulation[:, index * model_width : (index + 1) * model_width]
        return functools.reduce(
            jnp.add, [member[i] * rows[i : i + 1, :] for i in range(image_count)]
        )

    def per_image(value):
        return [jnp.sum(member[i] * value, axis=0).reshape(-1, 128) for i in range(image_count)]

    token_in = tokens[0].astype(F32)
    token_inverse = inverse_rms(token_in)
    tokens_all = lax.all_gather(tokens[0], "fsdp", axis=0, tiled=True)
    def widened(value, slots):
        if part == part_pad:
            return value
        lead = value.shape[:-1]
        value = value.reshape(*lead, slots, part)
        pads = [(0, 0)] * (len(lead) + 1) + [(0, part_pad - part)]
        return jnp.pad(value, pads).reshape(*lead, slots * part_pad)

    def narrowed(value, slots):
        if part == part_pad:
            return value
        lead = value.shape[:-1]
        return value.reshape(*lead, slots, part_pad)[..., :part].reshape(*lead, slots * part)

    def own_columns(value):
        return widened(lax.dynamic_slice_in_dim(value, me * part, part, value.ndim - 1), 1)

    qkv_rows = qkv_weight.shape[0] // 2
    qkv_half = lax.dynamic_slice_in_dim(qkv_weight, lax.axis_index("core") * qkv_rows, qkv_rows, 0)
    qkv_half = exchange(
        qkv_half.reshape(qkv_rows, 3, narrow, part).transpose(2, 0, 1, 3).reshape(narrow, qkv_rows, 3 * part), "fsdp"
    )
    own_qkv = widened(
        jnp.concatenate(in_core_order(qkv_half, core_swap(qkv_half)), axis=1).reshape(model_width, 3 * part), 3
    )

    full_out = whole_weight(out_weight)
    full_gate_up = whole_weight(gate_up_weight)
    full_down = whole_weight(down_weight)

    text_in = text_states[0].astype(F32).reshape(text_local, caption_width)
    text_inverse = inverse_rms(text_in)
    text_low = (text_in * text_inverse * text_gain).astype(BF16)
    text_cols = caption_width // narrow
    text_slice = (
        exchange(text_low.reshape(text_local, narrow, text_cols).transpose(1, 0, 2), "fsdp")
        .reshape(narrow, image_count, caption_local, text_cols)
        .transpose(1, 0, 2, 3)
        .reshape(text_total, text_cols)
    )
    own_text_weight = (
        text_weight.reshape(text_cols, 2, narrow, part).transpose(2, 0, 1, 3).reshape(narrow, text_cols, 2 * part)
    )
    text_partial = jnp.stack([low_product(text_slice, own_text_weight[i]).astype(BF16) for i in range(narrow)])
    text_partial, tokens_all = lax.optimization_barrier((text_partial, tokens_all))
    text_projected = widened(jnp.sum(exchange(text_partial, "fsdp").astype(F32), axis=0), 2)
    text_parts = fsdp_share(column_stats(text_projected, part, part_pad, 1), narrow, 1)
    text_means = text_parts[:, 0, :]
    text_mean = jnp.mean(text_means, axis=0)
    text_square = jnp.sum(text_parts[:, 1, :], axis=0) + part * jnp.sum((text_means - text_mean) ** 2, axis=0)
    text_key_inverse = lax.rsqrt(text_square / model_width + EPS)[:, None]
    text_unit = (text_projected[:, :part_pad] - text_mean[:, None]) * text_key_inverse
    text_gains = own_columns(norm_gains[4])
    text_packed = jnp.concatenate(
        [(text_unit * text_gains).astype(BF16), text_projected[:, part_pad:].astype(BF16)], axis=1
    )

    wide_tokens = tokens_all.astype(F32)
    wide_scale = functools.reduce(
        jnp.add,
        [(key_image == i).astype(F32)[:, None] * modulation[i : i + 1, :model_width] for i in range(image_count)],
    )
    normed_all = (wide_tokens * inverse_rms(wide_tokens) * norm_gains[0] * (1.0 + wide_scale)).astype(BF16)

    projected = low_product(normed_all, own_qkv)
    stats_all = fsdp_share(column_stats(projected, part, part_pad, 2), narrow, 2)
    head_gains = own_columns(norm_gains[2:4])
    packed = make_heads(
        projected, stats_all, cosine, sine, head_gains, own_columns(norm_shifts), part, score_scale * LOG2E
    )
    gate_tanh = jnp.tanh(head_gate)
    own_gates = lax.dynamic_slice_in_dim(gate_tanh, me * heads_here, heads_here, 0)
    own_gates = jnp.concatenate([own_gates, jnp.ones((pairs * halves - heads_here,), F32)])
    column = key_image[:, None]
    row = key_image[None, :]
    attended = [
        attend(pair, own_gates, packed, text_packed, column, row, head_dim, image_count) for pair in range(pairs)
    ]
    mixed_pairs = [exchange(one[0].reshape(narrow, local_tok, 128), "fsdp") for one in attended]
    self_outs = [one[1] for one in attended]
    cross_outs = [one[2] for one in attended]
    stats = [one[3] for one in attended]
    mixed_low = (
        narrowed(jnp.concatenate(mixed_pairs, axis=2), 1).transpose(1, 0, 2).reshape(local_tok, model_width)
    )

    branch = low_product(mixed_low, full_out)
    branch_inverse = inverse_rms(branch)
    branch_unit = branch * branch_inverse
    gate_attend = jnp.tanh(per_token(1))
    hidden = token_in + gate_attend * (branch_unit * norm_gains[1])
    hidden_inverse = inverse_rms(hidden)
    hidden_unit = hidden * hidden_inverse
    scale_feed = 1.0 + per_token(2)
    normed_feed_low = (hidden_unit * norm_gains[5] * scale_feed).astype(BF16)
    gate_up = low_product(normed_feed_low, full_gate_up)
    hidden_units = gate_up.shape[1] // 2
    gate_half = gate_up[:, :hidden_units]
    up_half = gate_up[:, hidden_units:]
    sigmoid = jax.nn.sigmoid(gate_half)
    if hidden_units // (wide * narrow) % 128 == 0:
        activated_low, moved = swiglu(gate_up, lax.axis_index("core"), deep, narrow)
        down_columns = (moved[:, : hidden_units // 2], moved[:, hidden_units // 2 :])
    else:
        activated_low = (gate_half * sigmoid * up_half).astype(BF16)
        down_columns = device_columns(activated_low, deep, narrow)
    down_out = low_product(activated_low, full_down)
    down_inverse = inverse_rms(down_out)
    down_unit = down_out * down_inverse
    gate_feed = jnp.tanh(per_token(3))
    down_normed = down_unit * norm_gains[6]
    result = (hidden + gate_feed * down_normed).astype(BF16)

    grad_result = cotangent[0].astype(F32)
    grad_down_y = grad_result * gate_feed
    grad_gain_six = jnp.sum(grad_down_y * down_unit, axis=0)
    grad_gate_feed = per_image(grad_result * down_normed * (1.0 - gate_feed * gate_feed))
    grad_down_low = norm_pull(grad_down_y * norm_gains[6], down_unit, down_inverse).astype(BF16)
    grad_activated = times_transposed(grad_down_low, full_down)
    grad_gate_low = (grad_activated * up_half * sigmoid * (1.0 + gate_half * (1.0 - sigmoid))).astype(BF16)
    grad_up_low = (grad_activated * gate_half * sigmoid).astype(BF16)
    grad_gate_up_low = jnp.concatenate([grad_gate_low, grad_up_low], axis=1)
    grad_normed_feed = times_transposed(grad_gate_up_low, full_gate_up)
    grad_feed_y = grad_normed_feed * scale_feed
    grad_gain_five = jnp.sum(grad_feed_y * hidden_unit, axis=0)
    grad_scale_feed = per_image(grad_normed_feed * hidden_unit * norm_gains[5])
    grad_hidden = grad_result + norm_pull(grad_feed_y * norm_gains[5], hidden_unit, hidden_inverse)
    grad_branch_y = grad_hidden * gate_attend
    grad_gain_one = jnp.sum(grad_branch_y * branch_unit, axis=0)
    grad_gate_attend = per_image(
        grad_hidden * branch_unit * norm_gains[1] * (1.0 - gate_attend * gate_attend)
    )
    grad_branch_low = norm_pull(grad_branch_y * norm_gains[1], branch_unit, branch_inverse).astype(BF16)
    grad_mixed = times_transposed(grad_branch_low, full_out).astype(BF16)
    grad_blocks = widened(grad_mixed.reshape(local_tok, narrow, part).transpose(1, 0, 2), 1)
    grad_heads = exchange(grad_blocks, "fsdp").reshape(group_tok, part_pad)
    def by_z(value):
        return value.reshape(deep, -1, value.shape[1])

    down_both = chip_sum(*down_columns, grad_down_low)
    feed_columns = device_columns(normed_feed_low, deep, narrow)
    gate_both = chip_sum(*feed_columns, grad_gate_low)
    up_both = chip_sum(*feed_columns, grad_up_low)
    out_both = chip_sum(*device_columns(mixed_low, deep, narrow), grad_branch_low)
    down_part = fsdp_sum(down_both)
    grad_heads, gate_both, up_both, out_both, down_part = lax.optimization_barrier(
        (grad_heads, gate_both, up_both, out_both, down_part)
    )
    gate_part = fsdp_sum(gate_both)
    out_part = fsdp_sum(out_both)
    up_part = fsdp_sum(up_both)
    came_downs = exchange(by_z(down_part), "z")
    crossed = [
        cross_back(
            pair, own_gates, packed, text_packed, row, grad_heads, cross_outs[pair], stats[pair],
            head_dim, image_count, score_scale,
        )
        for pair in range(pairs)
    ]
    dtk = jnp.concatenate([one[1] for one in crossed], axis=1)
    dtv = jnp.concatenate([one[2] for one in crossed], axis=1)
    gate_sums = jnp.stack([one[3] for one in crossed])

    grad_text_keys = dtk.astype(F32)
    own_gain_four = jnp.sum(grad_text_keys * text_unit, axis=0)
    grad_text_unit = grad_text_keys * text_gains
    text_sums = jnp.stack([jnp.sum(grad_text_unit, axis=1), jnp.sum(grad_text_unit * text_unit, axis=1)])
    text_sums = jnp.sum(
        fsdp_share(jnp.pad(text_sums, ((0, 6), (0, 0))), narrow, 3), axis=0
    ) * (1.0 / model_width)
    grad_text_key_in = (grad_text_unit - text_sums[0][:, None] - text_unit * text_sums[1][:, None]) * text_key_inverse
    grad_text_own = jnp.concatenate(
        [narrowed(grad_text_key_in.astype(BF16), 1), narrowed(dtv, 1)], axis=1
    )
    def self_pair(pair):
        return self_back(
            pair, packed, column, row, grad_heads, self_outs[pair], stats[pair], crossed[pair][0], head_dim, score_scale
        )

    came_texts = to_all(grad_text_own, narrow)
    backs = [self_pair(0)]
    first, came_downs, *came_texts = lax.optimization_barrier((backs[0][0], came_downs, *came_texts))
    grad_down_weight = jnp.sum(came_downs.astype(F32), axis=0)
    backs[0] = (first, *backs[0][1:])
    grad_text_columns = jnp.concatenate([grad_text_own, *came_texts], axis=1)
    text_half = text_cols // 2
    own_text, other_text = by_core(text_slice[:, :text_half], text_slice[:, text_half:])
    came_text = core_swap(outer_sum(other_text, grad_text_columns).astype(BF16))
    text_both = (outer_sum(own_text, grad_text_columns) + came_text.astype(F32)).astype(BF16)
    grad_heads, text_both, first = lax.optimization_barrier((grad_heads, text_both, backs[0][0]))
    backs[0] = (first, *backs[0][1:])
    came_text_z = exchange(by_z(text_both), "z")
    backs.append(self_pair(1))
    if pairs > 2:
        grad_heads, gate_part, up_part, second = lax.optimization_barrier(
            (grad_heads, gate_part, up_part, backs[1][0])
        )
        backs[1] = (second, *backs[1][1:])
        backs += [self_pair(pair) for pair in range(2, pairs)]
    gate_pieces = z_pieces(by_z(gate_part), deep)
    last, came_text_z, up_part, out_part, *gate_pieces = lax.optimization_barrier(
        (backs[-1][0], came_text_z, up_part, out_part, *gate_pieces)
    )
    up_width = up_part.shape[1]
    up_pieces = z_pieces(by_z(jnp.concatenate([up_part, out_part], axis=1)), deep)
    backs[-1] = (last, *backs[-1][1:])
    text_part = jnp.sum(came_text_z.astype(F32), axis=0).astype(BF16)
    everyone = ("z", "core", "fsdp")
    grad_text_weight = lax.ppermute(
        text_part,
        everyone,
        [
            ((z * 2 + c) * narrow + f, f * wide + c * deep + z)
            for z in range(deep) for c in range(2) for f in range(narrow)
        ],
    )
    own_gate_grad = jnp.sum(gate_sums[:, 0, :].reshape(pairs * halves, head_dim), axis=1)[:heads_here]
    grad_head_gate = lax.dynamic_update_slice_in_dim(
        jnp.zeros((head_count,), F32), own_gate_grad, me * heads_here, 0
    ) * (1.0 - gate_tanh * gate_tanh)
    grad_projected_low, head_sums = heads_back(
        list(zip(*backs)), projected, stats_all, cosine, sine, head_gains, part,
        lambda value: fsdp_share(value, narrow, 4),
    )
    grad_projected_low, *up_pieces = lax.optimization_barrier((grad_projected_low, *up_pieces))
    grad_gate_up_weight = jnp.concatenate(
        [added(gate_pieces), added([piece[:, :up_width] for piece in up_pieces])], axis=1
    )
    grad_out_weight = added([piece[:, up_width:] for piece in up_pieces])
    partial_normed, grad_text_weight = lax.optimization_barrier(
        (times_transposed(grad_projected_low, own_qkv).astype(BF16), grad_text_weight)
    )
    grad_normed = lax.psum_scatter(partial_normed, "fsdp", scatter_dimension=0, tiled=True)

    def lane_rows(value):
        return value.reshape(-1, 128)

    group = lax.axis_index("z") * 2 + lax.axis_index("core")
    columns_here = jnp.stack(
        [narrowed(value, 1) for value in (head_sums[0], head_sums[2], own_gain_four, head_sums[1], head_sums[3])]
    )
    here = (jnp.arange(narrow, dtype=jnp.int32) == me)[None, :, None]
    placed = lane_rows(jnp.where(here, columns_here[:, None, :], 0.0))
    cond_rows_here = lane_rows(jnp.where(me == 0, cond_low.astype(F32), 0.0))
    gate_row = jnp.pad(grad_head_gate, (0, 128 - head_count)).reshape(1, 128)
    ready = [lane_rows(grad_gain_one), lane_rows(grad_gain_five), lane_rows(grad_gain_six), placed, gate_row]
    later = [*grad_gate_attend, *grad_scale_feed, *grad_gate_feed, cond_rows_here]
    ready = lax.optimization_barrier(tuple(ready))
    qkv_grad = outer_sum(normed_all, grad_projected_low).astype(BF16).reshape(deep, 2, model_width // wide, 3 * part_pad)
    own_grad, other_grad = by_core(qkv_grad[:, 0], qkv_grad[:, 1])
    own_grad = (own_grad.astype(F32) + core_swap(other_grad).astype(F32)).astype(BF16)
    own_pieces = z_pieces(own_grad, deep)
    own_pieces[0], grad_text_columns, grad_text_weight = lax.optimization_barrier(
        (own_pieces[0], grad_text_columns, grad_text_weight)
    )
    ordered = relative(grad_text_columns.reshape(text_total, narrow, 2 * part), me, 1)
    grad_text_ordered = (
        ordered.reshape(text_total, narrow, 2, part).transpose(0, 2, 1, 3).reshape(text_total, 2 * model_width)
    )
    grad_text_slice = times_transposed(grad_text_ordered, text_weight).astype(BF16)
    came_text = exchange(
        grad_text_slice.reshape(image_count, narrow, caption_local, text_cols)
        .transpose(1, 0, 2, 3)
        .reshape(narrow, text_local, text_cols),
        "fsdp",
    )
    place = (lax.axis_index("z") * 2 + lax.axis_index("core")) * narrow + me
    grad_text_weight = (
        relative(grad_text_weight.reshape(-1, narrow, 2 * part), place // wide, 1)
        .reshape(-1, narrow, 2, part)
        .transpose(0, 2, 1, 3)
        .reshape(-1, 2 * model_width)
        .astype(F32)
    )
    grad_text_normed = (
        came_text
        .transpose(1, 0, 2)
        .reshape(text_local, caption_width)
        .astype(F32)
    )
    text_state_unit = text_in * text_inverse
    grad_text_gain = jnp.sum(grad_text_normed * text_state_unit, axis=0)
    grad_text = (
        norm_pull(grad_text_normed * text_gain, text_state_unit, text_inverse)
        .astype(BF16)
        .reshape(image_count, caption_local, caption_width)
    )

    grad_text, grad_text_gain, grad_text_weight, *own_pieces = lax.optimization_barrier(
        (grad_text, grad_text_gain, grad_text_weight, *own_pieces)
    )
    own_grad = added(own_pieces)
    own_exchanged = exchange(narrowed(own_grad.astype(BF16), 3).reshape(narrow, -1, 3 * part), "fsdp")
    grad_normed, own_exchanged = lax.optimization_barrier((grad_normed, own_exchanged))
    grad_qkv_weight = (
        own_exchanged.reshape(narrow, -1, 3, part)
        .transpose(1, 2, 0, 3)
        .reshape(-1, 3 * model_width)
        .astype(F32)
    )
    grad_normed = grad_normed.astype(F32)

    token_unit = token_in * token_inverse
    scale_attend = 1.0 + per_token(0)
    grad_normed_y = grad_normed * scale_attend
    grad_gain_zero = jnp.sum(grad_normed_y * token_unit, axis=0)
    grad_scale_attend = per_image(grad_normed * token_unit * norm_gains[0])
    grad_tokens = (
        grad_hidden + norm_pull(grad_normed_y * norm_gains[0], token_unit, token_inverse)
    ).astype(BF16)
    lanes_of_row = model_width // 128
    def row_range(first, count):
        return list(range(first * lanes_of_row, (first + count) * lanes_of_row))

    gate_at = 9 * lanes_of_row
    text_rows = caption_width // 128
    grad_gains, grad_shifts, gate_row, grad_text_gain, slots, cond_slots = finish(
        [lane_rows(grad_gain_zero), *ready, lane_rows(grad_text_gain)],
        [*grad_scale_attend, *later],
        [
            (norm_gains.shape, row_range(0, 2) + row_range(4, 3) + row_range(2, 2)),
            (norm_shifts.shape, row_range(7, 2)),
            ((1, 128), [gate_at]),
            ((text_rows, 128), list(range(gate_at + 1, gate_at + 1 + text_rows))),
        ],
        image_count, narrow, wide, 5,
    )
    slots = slots.reshape(wide * image_count, -1)
    cond_slots = cond_slots.reshape(wide * image_count, -1)
    grad_head_gate = gate_row[0, :head_count]
    grad_text_gain = grad_text_gain.reshape(-1)
    ada_rows = cond_rows // wide
    own_cond = lax.dynamic_slice_in_dim(cond_slots, (group * narrow + me) * ada_rows, ada_rows, 1)
    grad_ada_weight = exact_outer(own_cond, slots)
    grad_ada_bias = jnp.sum(slots, axis=0)
    return (
        result[None],
        grad_tokens[None],
        grad_text[None],
        grad_ada_weight,
        grad_qkv_weight,
        grad_out_weight,
        grad_text_weight,
        grad_gate_up_weight,
        grad_down_weight,
        grad_ada_bias,
        grad_gains,
        grad_shifts,
        grad_text_gain,
        grad_head_gate,
    )


def solution(mesh):
    wide, narrow = mesh.devices.shape
    fine = Mesh(mesh.devices.reshape(wide // 2, 2, narrow), ("z", "core", "fsdp"))
    groups = ("z", "core")
    every = ("z", "core", "fsdp")
    placed = (
        P(groups, "fsdp", None),
        P(groups, "fsdp", None),
        P(groups, None, "fsdp", None),
        P(groups, None, None),
        P(groups, None, None),
        P("fsdp", None),
        P(),
        P("fsdp", None),
        P("fsdp", None),
        P("fsdp", None),
        P("fsdp", None),
        P("fsdp", None),
        P(),
        P(),
        P(),
        P(),
    )
    return jax.shard_map(
        shards,
        mesh=fine,
        in_specs=placed,
        out_specs=(
            P(groups, "fsdp", None),
            P(groups, "fsdp", None),
            P(groups, None, "fsdp", None),
            P(every, None),
            P(every, None),
            P(every, None),
            P(every, None),
            P(every, None),
            P(every, None),
            P(),
            P(),
            P(),
            P(),
            P(),
        ),
        check_vma=False,
    )
```
